32 devices in a mesh: dp: 4 (over y, core), seq: 8 (over z, x).
Axes of the slice: x: 2, y: 2, z: 4, core: 2. Of those that a mesh axis runs over, the one named last changes fastest.
Arguments:
- query_rows: bfloat16 [512, 8, 2048], P('seq', 'dp'), may hold values from -6 to 6
- key_rows: bfloat16 [512, 8, 2048], P('seq', 'dp'), may hold values from -6 to 6
- value_rows: bfloat16 [512, 8, 2048], P('seq', 'dp'), may hold values from -6 to 6
- region_lengths: int32 [8], P('dp'), may hold values from 64 to 512, as said below
- norm_gain: float32 [2048], replicated, may hold values from 0.1 to 1.9
- conv_weight: bfloat16 [9, 128, 128], replicated, may hold values from -0.1875 to 0.1875
- cotangent: bfloat16 [8, 32, 256, 128], P('dp', 'seq'), may hold values from -6 to 6
Outputs:
- decoded: bfloat16 [8, 32, 256, 128], P('dp', 'seq')
- weight_grad: float32 [9, 128, 128], replicated
The draws below stay inside these ranges and needn't reach their ends.
Inputs may be any that keep to these rules, and one draw needn't show every extreme that they name: Region r's tokens fill its first region_lengths[r] slots; in every draw some region fills all 512 slots.
All inputs are finite; a program needn't handle non-finite values.
Results may differ from the reference program's by a relative error of at most 0.0063.
Values may be sent and summed in bfloat16 or wider, within the bound.
No kernel may reach another device: no remote copies, remote signals or barrier semaphores. Data moves between devices by JAX's collectives and lax.ppermute only.
A program may use at most 64 MiB of HBM per device.

```python
import math
import jax
import jax.numpy as jnp
from jax import lax

D = 2048
HEADS = 16
PATCH = 4
TOK_DEV = 64
HD = 128
CH = 128
CAP = 512
REGIONS = 8
ROWS_PIX = 32
COLS_PIX = 256
N_SEQ = 8


def paired_rows(key):
    whole_shape = (CAP, REGIONS, D)
    query_vals = jnp.clip(jax.random.normal(jax.random.fold_in(key, 11), whole_shape, jnp.float32), -6.0, 6.0)
    key_vals = jnp.clip(jax.random.normal(jax.random.fold_in(key, 12), whole_shape, jnp.float32), -6.0, 6.0)
    return (query_vals, key_vals)


def draw_query_rows(key, part):
    return paired_rows(key)[0].astype(jnp.bfloat16)


def draw_key_rows(key, part):
    return paired_rows(key)[1].astype(jnp.bfloat16)


def draw_region_lengths(key, part):
    values = jax.random.randint(jax.random.fold_in(key, 21), (REGIONS,), CAP // 8, CAP + 1)
    longest = jax.random.randint(jax.random.fold_in(key, 22), (), 0, REGIONS)
    return jnp.where(jnp.arange(REGIONS) == longest, CAP, values).astype(jnp.int32)


def block_scale(own_key, shape, cuts, least, high):
    gain, own = 1.0, jax.random.fold_in(own_key, 6)
    for dim, shards_of in cuts:
        heights = jnp.exp(jax.random.uniform(jax.random.fold_in(own, dim), (shards_of,), jnp.float32, least / len(cuts), high / len(cuts)))
        gain = gain * jnp.repeat(heights, shape[dim] // shards_of).reshape([-1 if axis == dim else 1 for axis in range(len(shape))])
    return gain


def bell_draw(own_key, extent, spread, most, split=(), held_as=jnp.bfloat16):
    entries = jax.random.normal(own_key, extent, jnp.float32) * spread
    if len(split) > 0:
        entries = block_scale(own_key, extent, split, -0.22, 0.18) * entries
    return jnp.clip(entries, min=-most, max=most).astype(held_as)


def setup_inputs(seed: int = 0) -> dict:
    key_of = jax.random.split(jax.random.key(seed), 8)
    return {
        "query_rows": draw_query_rows(jax.random.fold_in(key_of[7], 71), 0),
        "key_rows": draw_key_rows(jax.random.fold_in(key_of[7], 71), 0),
        "value_rows": bell_draw(key_of[2], (CAP, REGIONS, D), 1.0, 6.0, ((0, 8), (1, 4))),
        "region_lengths": draw_region_lengths(jax.random.fold_in(key_of[7], 71), 0),
        "norm_gain": jnp.clip(1.0 + 0.18 * jax.random.normal(key_of[4], (D,), jnp.float32), 0.1, 1.9),
        "conv_weight": bell_draw(key_of[5], (9, CH, CH), (9 * CH) ** -0.5, 0.1875),
        "cotangent": bell_draw(key_of[6], (REGIONS, ROWS_PIX, COLS_PIX, CH), 1.0, 6.0, ((0, 4), (1, 8))),
    }


def attend_one(packed):
    query_mat, key_mat, value_mat, key_count = packed
    scores = jnp.dot(query_mat, key_mat.T, preferred_element_type=jnp.float32) * (1.0 / math.sqrt(HD))
    key_valid = jnp.arange(CAP, dtype=jnp.int32) < key_count
    scores = jnp.where(key_valid[None, :], scores, -1e+30)
    top_score = lax.optimization_barrier(jnp.max(scores, axis=1, keepdims=True))
    powers = jnp.exp(scores - top_score)
    totals = lax.optimization_barrier(jnp.sum(powers, axis=1, keepdims=True))
    mixed = jnp.dot(powers.astype(jnp.bfloat16), value_mat, preferred_element_type=jnp.float32) / totals
    return mixed.astype(jnp.bfloat16)

def reference(query_rows, key_rows, value_rows, region_lengths, norm_gain, conv_weight, cotangent):
    item_total = REGIONS * HEADS

    def heads_major(source):
        return source.reshape(CAP, item_total, HD).transpose(1, 0, 2)
    counts = jnp.repeat(region_lengths, HEADS)
    attended = lax.map(attend_one, (heads_major(query_rows), heads_major(key_rows), heads_major(value_rows), counts))
    attended = attended.transpose(1, 0, 2).reshape(CAP, REGIONS, D)
    values32 = attended.astype(jnp.float32)
    mean_val = lax.optimization_barrier(jnp.mean(values32, axis=-1, keepdims=True))
    centered = values32 - mean_val
    variance = lax.optimization_barrier(jnp.mean(centered * centered, axis=-1, keepdims=True))
    normed = centered * lax.rsqrt(variance + 1e-05) * norm_gain
    positions = jnp.arange(CAP, dtype=jnp.int32)
    token_live = positions[:, None] < region_lengths[None, :]
    normed = jnp.where(token_live[:, :, None], normed, 0.0).astype(jnp.bfloat16)
    image = normed.reshape(N_SEQ, TOK_DEV, REGIONS, PATCH, PATCH, CH).transpose(2, 0, 3, 1, 4, 5)
    image = image.reshape(REGIONS, ROWS_PIX, COLS_PIX, CH)
    padded = jnp.pad(image, ((0, 0), (1, 1), (1, 1), (0, 0)))
    cot_flat = cotangent.reshape(-1, CH)
    accum = jnp.zeros((REGIONS * ROWS_PIX * COLS_PIX, CH), jnp.float32)
    grads = []
    for tap_number in range(9):
        row_shift, col_shift = divmod(tap_number, 3)
        window = padded[:, row_shift:row_shift + ROWS_PIX, col_shift:col_shift + COLS_PIX, :].reshape(-1, CH)
        accum = accum + jnp.dot(window, conv_weight[tap_number], preferred_element_type=jnp.float32)
        grads.append(jnp.dot(window.T, cot_flat, preferred_element_type=jnp.float32))
    decoded = accum.reshape(REGIONS, ROWS_PIX, COLS_PIX, CH).astype(jnp.bfloat16)
    factor = 1.0 / math.sqrt(PATCH * COLS_PIX)
    weight_grad = jnp.stack(grads) * factor
    return (decoded, weight_grad)
```

```python
import functools
import math

import jax
import jax.numpy as jnp
from jax import lax
from jax.experimental import pallas as pl
from jax.experimental.pallas import tpu as pltpu
from jax.sharding import PartitionSpec as P

HEADS = 16
PATCH = 4
RIM = 8
VMEM_LIMIT = 48 * 1024 * 1024

VMEM = functools.partial(pl.BlockSpec, memory_space=pltpu.VMEM)
SMEM = functools.partial(pl.BlockSpec, memory_space=pltpu.SMEM)


def call(kernel, name, out_shape, in_specs, scratch=(), flops=0, moved=0, exps=0):
    many = isinstance(out_shape, (list, tuple))
    return pl.pallas_call(
        kernel,
        out_shape=out_shape,
        in_specs=in_specs,
        out_specs=[VMEM() for _ in out_shape] if many else VMEM(),
        scratch_shapes=list(scratch),
        compiler_params=pltpu.CompilerParams(vmem_limit_bytes=VMEM_LIMIT),
        cost_estimate=pl.CostEstimate(flops=flops, bytes_accessed=moved, transcendentals=exps),
        name=name,
    )


def pack_kernel(regions, heads, per_device, *refs):
    sources, out_ref = refs[:-1], refs[-1]
    width = sources[0].shape[2] // heads
    for which, ref in enumerate(sources):
        for head in range(heads):
            block = ref[:, :, head * width : (head + 1) * width].astype(jnp.float32)
            for region in range(regions):
                item = head * regions + region
                out_ref[item // per_device, which, item % per_device] = block[:, region, :].astype(
                    jnp.bfloat16
                )


def attend_kernel(block_rows, lengths_ref, packed_ref, out_ref):
    sources, _, per_device, tokens, width = packed_ref.shape
    capacity = sources * tokens
    blocks = capacity // block_rows
    per_block = block_rows // tokens
    factor = math.log2(math.e) / math.sqrt(width)
    columns = lax.broadcasted_iota(jnp.int32, (1, capacity), 1)
    for item in range(per_device):
        length = lengths_ref[item]
        key_valid = columns < length
        for block in range(blocks):
            rows = slice(block * per_block, (block + 1) * per_block)

            @pl.when(block * block_rows < length)
            def _(item=item, rows=rows, key_valid=key_valid):
                query = packed_ref[rows, 0, item].reshape(block_rows, width)
                keys = packed_ref[:, 1, item].reshape(capacity, width)
                values = packed_ref[:, 2, item].reshape(capacity, width)
                scores = lax.dot_general(
                    query, keys, (((1,), (1,)), ((), ())), preferred_element_type=jnp.float32
                )
                scores = jnp.where(key_valid, scores * factor, -1e30)
                powers = jnp.exp2(scores - jnp.max(scores, axis=1, keepdims=True))
                totals = jnp.sum(powers, axis=1, keepdims=True)
                mixed = jnp.dot(
                    powers.astype(jnp.bfloat16), values, preferred_element_type=jnp.float32
                )
                mixed = (mixed / totals).astype(jnp.bfloat16)
                out_ref[rows, item] = mixed.reshape(per_block, tokens, width)

            @pl.when(block * block_rows >= length)
            def _(item=item, rows=rows):
                out_ref[rows, item] = jnp.zeros((per_block, tokens, width), jnp.bfloat16)


def three_windows(padded, columns):
    return jnp.concatenate(
        [padded[RIM - 1 + shift : RIM - 1 + shift + columns].astype(jnp.bfloat16) for shift in range(3)],
        axis=1,
    )


def norm_kernel(
    chunk_rows,
    lengths_ref,
    base_ref,
    attended_ref,
    gain_ref,
    cot_ref,
    cot_before_ref,
    cot_after_ref,
    image_ref,
    first_ref,
    last_ref,
    grad_ref,
    pixels,
    windows,
    cots,
    grads,
):
    heads, regions, tokens, width = attended_ref.shape
    columns = tokens * PATCH
    features = heads * width
    position = base_ref[0] + lax.broadcasted_iota(jnp.int32, (tokens, 1), 0)
    pixels[:, :, :RIM, :] = jnp.zeros((regions, PATCH, RIM, width), jnp.float32)
    pixels[:, :, RIM + columns :, :] = jnp.zeros((regions, PATCH, RIM, width), jnp.float32)
    for region in range(regions):
        total = jnp.zeros((tokens, width), jnp.float32)
        for head in range(heads):
            total = total + attended_ref[head, region].astype(jnp.float32)
        mean = jnp.sum(total, axis=1, keepdims=True) * (1.0 / features)
        total = jnp.zeros((tokens, width), jnp.float32)
        for head in range(heads):
            centered = attended_ref[head, region].astype(jnp.float32) - mean
            total = total + centered * centered
        variance = jnp.sum(total, axis=1, keepdims=True) * (1.0 / features)
        spread = lax.rsqrt(variance + 1e-05)
        live = position < lengths_ref[region]
        for head in range(heads):
            centered = attended_ref[head, region].astype(jnp.float32) - mean
            normed = jnp.where(live, centered * spread * gain_ref[head : head + 1, :], 0.0)
            row, column = divmod(head, PATCH)
            pixels[region, row, pl.ds(RIM + column, tokens, stride=PATCH), :] = normed
        for row in range(PATCH):
            window = three_windows(pixels[region, row], columns)
            middle = window[:, width : 2 * width]
            image_ref[region, row] = middle
            if row == 0:
                first_ref[region] = middle
            if row == PATCH - 1:
                last_ref[region] = middle
            start = (region * PATCH + row) * columns
            windows[start : start + columns, :] = window
            below = cot_ref[region, row + 1] if row < PATCH - 1 else cot_after_ref[region]
            above = cot_ref[region, row - 1] if row > 0 else cot_before_ref[region]
            cots[start : start + columns, :] = jnp.concatenate(
                [below, cot_ref[region, row], above], axis=1
            )
    product = lax.dot_general(
        windows[...], cots[...], (((0,), (0,)), ((), ())), preferred_element_type=jnp.float32
    )
    for down in range(3):
        for across in range(3):
            tap = 3 * down + across
            grads[tap * width : (tap + 1) * width, :] = product[
                across * width : (across + 1) * width, down * width : (down + 1) * width
            ]
    filled = 9 * width
    if filled < grads.shape[0]:
        grads[filled:, :] = jnp.zeros((grads.shape[0] - filled, width), jnp.float32)
    for chunk in range(grad_ref.shape[0]):
        grad_ref[chunk] = grads[chunk * chunk_rows : (chunk + 1) * chunk_rows, :].astype(jnp.bfloat16)


def decode_kernel(image_ref, before_ref, after_ref, weight_ref, out_ref, padded):
    regions, rows, columns, width = image_ref.shape
    padded[:RIM, :] = jnp.zeros((RIM, width), jnp.float32)
    padded[RIM + columns :, :] = jnp.zeros((RIM, width), jnp.float32)
    for region in range(regions):
        strips = []
        for row in range(-1, rows + 1):
            if row < 0:
                source = before_ref[region]
            elif row == rows:
                source = after_ref[region]
            else:
                source = image_ref[region, row]
            padded[RIM : RIM + columns, :] = source.astype(jnp.float32)
            strips.append(three_windows(padded[...], columns))
            if len(strips) == 3:
                total = jnp.dot(strips[0], weight_ref[0], preferred_element_type=jnp.float32)
                for down in (1, 2):
                    total = total + jnp.dot(
                        strips[down], weight_ref[down], preferred_element_type=jnp.float32
                    )
                out_ref[region, row - 1] = total.astype(jnp.bfloat16)
                strips.pop(0)


def sum_kernel(factor, parts_ref, out_ref):
    total = parts_ref[0].astype(jnp.float32)
    for part in range(1, parts_ref.shape[0]):
        total = total + parts_ref[part].astype(jnp.float32)
    total = (total * factor).astype(jnp.bfloat16)
    for part in range(out_ref.shape[0]):
        out_ref[part] = total


def spread_kernel(parts_ref, out_ref):
    rows = parts_ref.shape[1]
    for part in range(parts_ref.shape[0]):
        start = part * rows
        kept = min(rows, out_ref.shape[0] - start)
        if kept > 0:
            out_ref[start : start + kept, :] = parts_ref[part, :kept, :].astype(jnp.float32)


def swap(parts, axes):
    return lax.all_to_all(parts, axes, split_axis=0, concat_axis=0, tiled=True)


def body(query_rows, key_rows, value_rows, region_lengths, norm_gain, conv_weight, cotangent):
    tokens, regions, model_width = query_rows.shape
    width = model_width // HEADS
    seq_count = lax.axis_size("seq")
    seq_index = lax.axis_index("seq")
    everyone = lax.axis_size("dp") * seq_count
    columns = tokens * PATCH
    capacity = seq_count * tokens
    per_device = regions * HEADS // seq_count
    up = [(i, i + 1) for i in range(seq_count - 1)]
    down = [(j, i) for i, j in up]
    local_bytes = 2 * query_rows.size

    packed = call(
        functools.partial(pack_kernel, regions, HEADS, per_device),
        "pack",
        jax.ShapeDtypeStruct((seq_count, 3, per_device, tokens, width), jnp.bfloat16),
        [VMEM()] * 3,
        moved=6 * local_bytes,
    )(query_rows, key_rows, value_rows)
    packed = swap(packed, "seq")

    cot_before = lax.ppermute(cotangent[:, PATCH - 1], "seq", up)
    cot_after = lax.ppermute(cotangent[:, 0], "seq", down)

    items = seq_index * per_device + jnp.arange(per_device, dtype=jnp.int32)
    item_lengths = jnp.sum(
        jnp.where(
            (items % regions)[:, None] == jnp.arange(regions, dtype=jnp.int32)[None, :],
            region_lengths[None, :],
            0,
        ),
        axis=1,
    )
    block_rows = min(256, capacity)
    mixed = call(
        functools.partial(attend_kernel, block_rows),
        "attend",
        jax.ShapeDtypeStruct((seq_count, per_device, tokens, width), jnp.bfloat16),
        [SMEM(), VMEM()],
        flops=4 * per_device * capacity * capacity * width,
        moved=4 * local_bytes,
        exps=per_device * capacity * capacity,
    )(item_lengths, packed)
    attended = swap(mixed, "seq").reshape(HEADS, regions, tokens, width)

    chunk_rows = -(-9 * width // everyone)
    pixel_rows = regions * PATCH * columns
    conv_flops = 18 * pixel_rows * width * width
    row_shape = jax.ShapeDtypeStruct((regions, columns, width), jnp.bfloat16)
    image, first, last, grad_parts = call(
        functools.partial(norm_kernel, chunk_rows),
        "norm_and_gradient",
        [
            jax.ShapeDtypeStruct((regions, PATCH, columns, width), jnp.bfloat16),
            row_shape,
            row_shape,
            jax.ShapeDtypeStruct((everyone, chunk_rows, width), jnp.bfloat16),
        ],
        [SMEM(), SMEM()] + [VMEM()] * 5,
        scratch=[
            pltpu.VMEM((regions, PATCH, columns + 2 * RIM, width), jnp.float32),
            pltpu.VMEM((pixel_rows, 3 * width), jnp.bfloat16),
            pltpu.VMEM((pixel_rows, 3 * width), jnp.bfloat16),
            pltpu.VMEM((everyone * chunk_rows, width), jnp.float32),
        ],
        flops=conv_flops,
        moved=4 * local_bytes,
    )(
        region_lengths,
        (seq_index * tokens).reshape(1),
        attended,
        norm_gain.reshape(HEADS, width),
        cotangent,
        cot_before,
        cot_after,
    )
    grad_parts = swap(grad_parts, ("dp", "seq"))
    before = lax.ppermute(last, "seq", up)
    after = lax.ppermute(first, "seq", down)
    sums = call(
        functools.partial(sum_kernel, 1.0 / math.sqrt(PATCH * columns)),
        "sum_parts",
        jax.ShapeDtypeStruct(grad_parts.shape, jnp.bfloat16),
        [VMEM()],
        moved=4 * grad_parts.size,
    )(grad_parts)
    sums = swap(sums, ("dp", "seq"))
    decoded = call(
        decode_kernel,
        "decode",
        jax.ShapeDtypeStruct(cotangent.shape, jnp.bfloat16),
        [VMEM()] * 4,
        scratch=[pltpu.VMEM((columns + 2 * RIM, width), jnp.float32)],
        flops=conv_flops,
        moved=2 * local_bytes,
    )(image, before, after, conv_weight.reshape(3, 3 * width, width))
    weight_grad = call(
        spread_kernel,
        "spread_sums",
        jax.ShapeDtypeStruct((9 * width, width), jnp.float32),
        [VMEM()],
        moved=6 * grad_parts.size,
    )(sums)
    return (decoded, weight_grad.reshape(conv_weight.shape))


def solution(mesh):
    placed = (
        P("seq", "dp", None),
        P("seq", "dp", None),
        P("seq", "dp", None),
        P("dp"),
        P(),
        P(),
        P("dp", "seq", None, None),
    )
    return jax.shard_map(
        body,
        mesh=mesh,
        in_specs=placed,
        out_specs=(P("dp", "seq", None, None), P()),
        check_vma=False,
    )
```

```python
import functools
import math

import jax
import jax.numpy as jnp
from jax import lax
from jax.experimental import pallas as pl
from jax.experimental.pallas import tpu as pltpu
from jax.sharding import PartitionSpec as P

HEADS = 16
PATCH = 4
RIM = 8
VMEM_LIMIT = 48 * 1024 * 1024
VMEM_WHOLE = 60 * 1024 * 1024

VMEM = functools.partial(pl.BlockSpec, memory_space=pltpu.VMEM)
HBM = functools.partial(pl.BlockSpec, memory_space=pltpu.HBM)
ANY = functools.partial(pl.BlockSpec, memory_space=pl.ANY)
SMEM = functools.partial(pl.BlockSpec, memory_space=pltpu.SMEM)


def call(kernel, name, out_shape, in_specs, out_specs=None, scratch=(), flops=0, moved=0, exps=0, grant=VMEM_LIMIT):
    many = isinstance(out_shape, (list, tuple))
    return pl.pallas_call(
        kernel,
        out_shape=out_shape,
        in_specs=in_specs,
        out_specs=out_specs or ([VMEM() for _ in out_shape] if many else VMEM()),
        scratch_shapes=list(scratch),
        compiler_params=pltpu.CompilerParams(vmem_limit_bytes=grant),
        cost_estimate=pl.CostEstimate(flops=flops, bytes_accessed=moved, transcendentals=exps),
        name=name,
    )


def pack_kernel(
    regions, heads, per_device, query_ref, key_ref, value_ref, cot_ref, out_ref, first_ref, last_ref, held, ready, sems
):
    width = held.shape[3] // heads
    copies = [
        pltpu.make_async_copy(ref, held.at[which], sems.at[which])
        for which, ref in enumerate((query_ref, key_ref, value_ref))
    ]
    rows = cot_ref.shape[1]
    edges = [
        pltpu.make_async_copy(cot_ref.at[:, 0], first_ref, sems.at[3]),
        pltpu.make_async_copy(cot_ref.at[:, rows - 1], last_ref, sems.at[4]),
    ]
    for copy in copies + edges:
        copy.start()
    for which, copy in enumerate(copies):
        copy.wait()
        for head in range(heads):
            block = held[which, :, :, head * width : (head + 1) * width].astype(jnp.float32)
            for region in range(regions):
                item = head * regions + region
                ready[item // per_device, which, item % per_device] = block[:, region, :].astype(
                    jnp.bfloat16
                )
        store = pltpu.make_async_copy(ready.at[:, which], out_ref.at[:, which], sems.at[5 + which])
        store.start()
        edges.append(store)
    for copy in edges:
        copy.wait()


def attend_kernel(block_rows, group, lengths_ref, packed_ref, before_ref, after_ref, out_ref):
    del before_ref, after_ref
    sources, _, per_device, tokens, width = packed_ref.shape
    capacity = sources * tokens
    per_block = block_rows // tokens
    factor = math.log2(math.e) / math.sqrt(width)
    slots = lax.broadcasted_iota(jnp.int32, (capacity, block_rows), 0)
    for lead in range(group):
        length = lengths_ref[lead]
        items = range(lead, per_device, group)
        for block in range(capacity // block_rows):
            rows = slice(block * per_block, (block + 1) * per_block)

            @pl.when(block * block_rows < length)
            def _(items=items, rows=rows, length=length):
                key_valid = slots < length
                for item in items:
                    query = packed_ref[rows, 0, item].reshape(block_rows, width)
                    keys = packed_ref[:, 1, item].reshape(capacity, width)
                    values = packed_ref[:, 2, item].reshape(capacity, width)
                    scores = lax.dot_general(
                        keys, query, (((1,), (1,)), ((), ())), preferred_element_type=jnp.float32
                    )
                    scores = jnp.where(key_valid, scores * factor, -1e30)
                    powers = jnp.exp2(scores - jnp.max(scores, axis=0, keepdims=True))
                    totals = jnp.sum(powers, axis=0, keepdims=True)
                    mixed = lax.dot_general(
                        values,
                        powers.astype(jnp.bfloat16),
                        (((0,), (0,)), ((), ())),
                        preferred_element_type=jnp.float32,
                    )
                    mixed = (mixed / totals).T.astype(jnp.bfloat16)
                    out_ref[rows, item] = mixed.reshape(per_block, tokens, width)

            @pl.when(block * block_rows >= length)
            def _(items=items, rows=rows):
                for item in items:
                    out_ref[rows, item] = jnp.zeros((per_block, tokens, width), jnp.bfloat16)


def three_windows(padded, columns):
    return jnp.concatenate(
        [padded[RIM - 1 + shift : RIM - 1 + shift + columns].astype(jnp.bfloat16) for shift in range(3)],
        axis=1,
    )


def norm_kernel(
    chunk_rows,
    lengths_ref,
    base_ref,
    attended_ref,
    gain_ref,
    cot_ref,
    cot_before_ref,
    cot_after_ref,
    image_ref,
    first_ref,
    last_ref,
    grad_ref,
    pixels,
    windows,
    cots,
    grads,
):
    heads, regions, tokens, width = attended_ref.shape
    columns = tokens * PATCH
    features = heads * width
    position = base_ref[0] + lax.broadcasted_iota(jnp.int32, (tokens, 1), 0)
    pixels[:, :, :RIM, :] = jnp.zeros((regions, PATCH, RIM, width), jnp.float32)
    pixels[:, :, RIM + columns :, :] = jnp.zeros((regions, PATCH, RIM, width), jnp.float32)
    for region in range(regions):
        total = jnp.zeros((tokens, width), jnp.float32)
        for head in range(heads):
            total = total + attended_ref[head, region].astype(jnp.float32)
        mean = jnp.sum(total, axis=1, keepdims=True) * (1.0 / features)
        total = jnp.zeros((tokens, width), jnp.float32)
        for head in range(heads):
            centered = attended_ref[head, region].astype(jnp.float32) - mean
            total = total + centered * centered
        variance = jnp.sum(total, axis=1, keepdims=True) * (1.0 / features)
        spread = lax.rsqrt(variance + 1e-05)
        live = position < lengths_ref[region]
        for head in range(heads):
            centered = attended_ref[head, region].astype(jnp.float32) - mean
            normed = jnp.where(live, centered * spread * gain_ref[head : head + 1, :], 0.0)
            row, column = divmod(head, PATCH)
            pixels[region, row, pl.ds(RIM + column, tokens, stride=PATCH), :] = normed
        for row in range(PATCH):
            window = three_windows(pixels[region, row], columns)
            middle = window[:, width : 2 * width]
            image_ref[region, row] = middle
            if row == 0:
                first_ref[region] = middle
            if row == PATCH - 1:
                last_ref[region] = middle
            start = (region * PATCH + row) * columns
            windows[start : start + columns, :] = window
            below = cot_ref[region, row + 1] if row < PATCH - 1 else cot_after_ref[region]
            above = cot_ref[region, row - 1] if row > 0 else cot_before_ref[region]
            cots[start : start + columns, :] = jnp.concatenate(
                [below, cot_ref[region, row], above], axis=1
            )
    product = lax.dot_general(
        windows[...], cots[...], (((0,), (0,)), ((), ())), preferred_element_type=jnp.float32
    )
    for down in range(3):
        for across in range(3):
            tap = 3 * down + across
            grads[tap * width : (tap + 1) * width, :] = product[
                across * width : (across + 1) * width, down * width : (down + 1) * width
            ]
    filled = 9 * width
    if filled < grads.shape[0]:
        grads[filled:, :] = jnp.zeros((grads.shape[0] - filled, width), jnp.float32)
    for chunk in range(grad_ref.shape[0]):
        grad_ref[chunk] = grads[chunk * chunk_rows : (chunk + 1) * chunk_rows, :].astype(jnp.bfloat16)


def decode_kernel(image_ref, before_ref, after_ref, weight_ref, out_ref, padded):
    regions, rows, columns, width = image_ref.shape
    padded[:RIM, :] = jnp.zeros((RIM, width), jnp.float32)
    padded[RIM + columns :, :] = jnp.zeros((RIM, width), jnp.float32)
    for region in range(regions):
        strips = []
        for row in range(-1, rows + 1):
            if row < 0:
                source = before_ref[region]
            elif row == rows:
                source = after_ref[region]
            else:
                source = image_ref[region, row]
            padded[RIM : RIM + columns, :] = source.astype(jnp.float32)
            strips.append(three_windows(padded[...], columns))
            if len(strips) == 3:
                total = jnp.dot(strips[0], weight_ref[0], preferred_element_type=jnp.float32)
                for down in (1, 2):
                    total = total + jnp.dot(
                        strips[down], weight_ref[down], preferred_element_type=jnp.float32
                    )
                out_ref[region, row - 1] = total.astype(jnp.bfloat16)
                strips.pop(0)


def sum_kernel(factor, parts_ref, before_ref, after_ref, out_ref):
    del before_ref, after_ref
    total = parts_ref[0].astype(jnp.float32)
    for part in range(1, parts_ref.shape[0]):
        total = total + parts_ref[part].astype(jnp.float32)
    total = (total * factor).astype(jnp.bfloat16)
    for part in range(out_ref.shape[0]):
        out_ref[part] = total


def spread_kernel(parts_ref, out_ref):
    rows = parts_ref.shape[1]
    for part in range(parts_ref.shape[0]):
        start = part * rows
        kept = min(rows, out_ref.shape[0] - start)
        if kept > 0:
            out_ref[start : start + kept, :] = parts_ref[part, :kept, :].astype(jnp.float32)


def swap(parts, axes):
    return lax.all_to_all(parts, axes, split_axis=0, concat_axis=0, tiled=True)


def body(query_rows, key_rows, value_rows, region_lengths, norm_gain, conv_weight, cotangent):
    tokens, regions, model_width = query_rows.shape
    width = model_width // HEADS
    seq_count = lax.axis_size("seq")
    seq_index = lax.axis_index("seq")
    everyone = lax.axis_size("dp") * seq_count
    columns = tokens * PATCH
    capacity = seq_count * tokens
    per_device = regions * HEADS // seq_count
    up = [(i, i + 1) for i in range(seq_count - 1)]
    down = [(j, i) for i, j in up]
    local_bytes = 2 * query_rows.size

    edge_shape = jax.ShapeDtypeStruct((regions, columns, width), jnp.bfloat16)
    packed, cot_first, cot_last = call(
        functools.partial(pack_kernel, regions, HEADS, per_device),
        "pack",
        [
            jax.ShapeDtypeStruct((seq_count, 3, per_device, tokens, width), jnp.bfloat16),
            edge_shape,
            edge_shape,
        ],
        [HBM()] * 4,
        out_specs=[HBM()] * 3,
        scratch=[
            pltpu.VMEM((3,) + query_rows.shape, jnp.bfloat16),
            pltpu.VMEM((seq_count, 3, per_device, tokens, width), jnp.bfloat16),
            pltpu.SemaphoreType.DMA((8,)),
        ],
        moved=6 * local_bytes,
        grant=VMEM_WHOLE,
    )(query_rows, key_rows, value_rows, cotangent)
    packed = swap(packed, "seq")
    cot_before = lax.ppermute(cot_last, "seq", up)
    cot_after = lax.ppermute(cot_first, "seq", down)

    items = seq_index * per_device + jnp.arange(per_device, dtype=jnp.int32)
    item_lengths = jnp.sum(
        jnp.where(
            (items % regions)[:, None] == jnp.arange(regions, dtype=jnp.int32)[None, :],
            region_lengths[None, :],
            0,
        ),
        axis=1,
    )
    block_rows = min(256, capacity)
    group = regions if per_device % regions == 0 else per_device
    mixed = call(
        functools.partial(attend_kernel, block_rows, group),
        "attend",
        jax.ShapeDtypeStruct((seq_count, per_device, tokens, width), jnp.bfloat16),
        [SMEM(), VMEM(), ANY(), ANY()],
        flops=4 * per_device * capacity * capacity * width,
        moved=4 * local_bytes,
        exps=per_device * capacity * capacity,
    )(item_lengths, packed, cot_before, cot_after)
    attended = swap(mixed, "seq").reshape(HEADS, regions, tokens, width)

    chunk_rows = -(-9 * width // everyone)
    pixel_rows = regions * PATCH * columns
    conv_flops = 18 * pixel_rows * width * width
    image, first, last, grad_parts = call(
        functools.partial(norm_kernel, chunk_rows),
        "norm_and_gradient",
        [
            jax.ShapeDtypeStruct((regions, PATCH, columns, width), jnp.bfloat16),
            edge_shape,
            edge_shape,
            jax.ShapeDtypeStruct((everyone, chunk_rows, width), jnp.bfloat16),
        ],
        [SMEM(), SMEM()] + [VMEM()] * 5,
        scratch=[
            pltpu.VMEM((regions, PATCH, columns + 2 * RIM, width), jnp.float32),
            pltpu.VMEM((pixel_rows, 3 * width), jnp.bfloat16),
            pltpu.VMEM((pixel_rows, 3 * width), jnp.bfloat16),
            pltpu.VMEM((everyone * chunk_rows, width), jnp.float32),
        ],
        flops=conv_flops,
        moved=4 * local_bytes,
    )(
        region_lengths,
        (seq_index * tokens).reshape(1),
        attended,
        norm_gain.reshape(HEADS, width),
        cotangent,
        cot_before,
        cot_after,
    )
    grad_parts = swap(grad_parts, ("dp", "seq"))
    before = lax.ppermute(last, "seq", up)
    after = lax.ppermute(first, "seq", down)
    sums = call(
        functools.partial(sum_kernel, 1.0 / math.sqrt(PATCH * columns)),
        "sum_parts",
        jax.ShapeDtypeStruct(grad_parts.shape, jnp.bfloat16),
        [VMEM(), ANY(), ANY()],
        moved=4 * grad_parts.size,
    )(grad_parts, before, after)
    sums = swap(sums, ("dp", "seq"))
    decoded = call(
        decode_kernel,
        "decode",
        jax.ShapeDtypeStruct(cotangent.shape, jnp.bfloat16),
        [VMEM()] * 4,
        scratch=[pltpu.VMEM((columns + 2 * RIM, width), jnp.float32)],
        flops=conv_flops,
        moved=2 * local_bytes,
    )(image, before, after, conv_weight.reshape(3, 3 * width, width))
    weight_grad = call(
        spread_kernel,
        "spread_sums",
        jax.ShapeDtypeStruct((9 * width, width), jnp.float32),
        [VMEM()],
        moved=6 * grad_parts.size,
    )(sums)
    return (decoded, weight_grad.reshape(conv_weight.shape))


def solution(mesh):
    placed = (
        P("seq", "dp", None),
        P("seq", "dp", None),
        P("seq", "dp", None),
        P("dp"),
        P(),
        P(),
        P("dp", "seq", None, None),
    )
    return jax.shard_map(
        body,
        mesh=mesh,
        in_specs=placed,
        out_specs=(P("dp", "seq", None, None), P()),
        check_vma=False,
    )
```

```python
import functools
import math

import jax
import jax.numpy as jnp
from jax import lax
from jax.experimental import pallas as pl
from jax.experimental.pallas import tpu as pltpu
from jax.sharding import PartitionSpec as P

HEADS = 16
PATCH = 4
RIM = 8
VMEM_LIMIT = 48 * 1024 * 1024
VMEM_WHOLE = 60 * 1024 * 1024

VMEM = functools.partial(pl.BlockSpec, memory_space=pltpu.VMEM)
HBM = functools.partial(pl.BlockSpec, memory_space=pltpu.HBM)
ANY = functools.partial(pl.BlockSpec, memory_space=pl.ANY)
SMEM = functools.partial(pl.BlockSpec, memory_space=pltpu.SMEM)


def call(kernel, name, out_shape, in_specs, out_specs=None, scratch=(), flops=0, moved=0, exps=0, grant=VMEM_LIMIT):
    many = isinstance(out_shape, (list, tuple))
    return pl.pallas_call(
        kernel,
        out_shape=out_shape,
        in_specs=in_specs,
        out_specs=out_specs or ([VMEM() for _ in out_shape] if many else VMEM()),
        scratch_shapes=list(scratch),
        compiler_params=pltpu.CompilerParams(vmem_limit_bytes=grant),
        cost_estimate=pl.CostEstimate(flops=flops, bytes_accessed=moved, transcendentals=exps),
        name=name,
    )


def pack_kernel(
    regions,
    heads,
    per_device,
    query_ref,
    key_ref,
    value_ref,
    cot_ref,
    out_ref,
    first_ref,
    last_ref,
    held,
    ready,
    edges,
    sems,
):
    width = held.shape[3] // heads
    rows = cot_ref.shape[1]
    loads = [
        pltpu.make_async_copy(ref, held.at[which], sems.at[which])
        for which, ref in enumerate((query_ref, key_ref, value_ref))
    ]
    loads.append(pltpu.make_async_copy(cot_ref.at[:, 0], edges.at[0], sems.at[3]))
    loads.append(pltpu.make_async_copy(cot_ref.at[:, rows - 1], edges.at[1], sems.at[4]))
    for load in loads:
        load.start()
    stores = []
    for which in range(3):
        loads[which].wait()
        for head in range(heads):
            block = held[which, :, :, head * width : (head + 1) * width].astype(jnp.float32)
            for region in range(regions):
                item = head * regions + region
                ready[item // per_device, which, item % per_device] = block[:, region, :].astype(
                    jnp.bfloat16
                )
        stores.append(
            pltpu.make_async_copy(ready.at[:, which], out_ref.at[:, which], sems.at[5 + which])
        )
        stores[-1].start()
        if which == 0:
            for edge, ref in enumerate((first_ref, last_ref)):
                loads[3 + edge].wait()
                stores.append(pltpu.make_async_copy(edges.at[edge], ref, sems.at[8 + edge]))
                stores[-1].start()
    for store in stores:
        store.wait()


def attend_kernel(
    block_rows, group, lengths_ref, packed_ref, before_ref, after_ref, out_ref, mixed_ref, sems
):
    del before_ref, after_ref
    sources, _, per_device, tokens, width = packed_ref.shape
    capacity = sources * tokens
    per_block = block_rows // tokens
    blocks = capacity // block_rows
    factor = math.log2(math.e) / math.sqrt(width)
    slots = lax.broadcasted_iota(jnp.int32, (1, capacity), 1)

    def rows_of(block):
        return slice(block * per_block, (block + 1) * per_block)

    def clear(item, block):
        mixed_ref[rows_of(block), item] = jnp.zeros((per_block, tokens, width), jnp.bfloat16)

    def score(item, block):
        query = packed_ref[rows_of(block), 0, item].reshape(block_rows, width)
        keys = packed_ref[:, 1, item].reshape(capacity, width)
        return lax.dot_general(
            query, keys, (((1,), (1,)), ((), ())), preferred_element_type=jnp.float32
        )

    def finish(item, block, scores, key_valid):
        values = packed_ref[:, 2, item].reshape(capacity, width)
        scores = jnp.where(key_valid, scores * factor, -1e30)
        powers = jnp.exp2(scores - jnp.max(scores, axis=1, keepdims=True))
        totals = jnp.sum(powers, axis=1, keepdims=True)
        mixed = jnp.dot(powers.astype(jnp.bfloat16), values, preferred_element_type=jnp.float32)
        mixed = (mixed / totals).astype(jnp.bfloat16)
        mixed_ref[rows_of(block), item] = mixed.reshape(per_block, tokens, width)

    def attend(tasks, length):
        key_valid = slots < length
        waiting = None
        for item, block in tasks:
            scores = score(item, block)
            if waiting is not None:
                finish(*waiting, key_valid)
            waiting = (item, block, scores)
        finish(*waiting, key_valid)

    stores = []
    for lead in range(group):
        length = lengths_ref[lead]
        items = list(range(lead, per_device, group))
        for block in range(0, blocks, 2):
            pair = list(range(block, min(block + 2, blocks)))
            start = block * block_rows

            @pl.when(length > start + block_rows)
            def _(items=items, pair=pair, length=length):
                attend([(item, one) for one in pair for item in items], length)

            @pl.when((length > start) & (length <= start + block_rows))
            def _(items=items, pair=pair, length=length):
                attend([(item, pair[0]) for item in items], length)
                for one in pair[1:]:
                    for item in items:
                        clear(item, one)

            @pl.when(length <= start)
            def _(items=items, pair=pair):
                for one in pair:
                    for item in items:
                        clear(item, one)

            rows = slice(pair[0] * per_block, (pair[-1] + 1) * per_block)
            for item in items:
                store = pltpu.make_async_copy(
                    mixed_ref.at[rows, item], out_ref.at[rows, item], sems.at[len(stores)]
                )
                store.start()
                stores.append(store)
    for store in stores:
        store.wait()


def three_windows(padded, columns):
    return jnp.concatenate(
        [padded[RIM - 1 + shift : RIM - 1 + shift + columns].astype(jnp.bfloat16) for shift in range(3)],
        axis=1,
    )


def norm_kernel(
    chunk_rows,
    lengths_ref,
    base_ref,
    attended_ref,
    gain_ref,
    cot_ref,
    cot_before_ref,
    cot_after_ref,
    image_ref,
    first_ref,
    last_ref,
    grad_ref,
    pixels,
    windows,
    cots,
    grads,
):
    heads, regions, tokens, width = attended_ref.shape
    columns = tokens * PATCH
    features = heads * width
    position = base_ref[0] + lax.broadcasted_iota(jnp.int32, (tokens, 1), 0)
    pixels[:, :, :RIM, :] = jnp.zeros((regions, PATCH, RIM, width), jnp.float32)
    pixels[:, :, RIM + columns :, :] = jnp.zeros((regions, PATCH, RIM, width), jnp.float32)
    for region in range(regions):
        total = jnp.zeros((tokens, width), jnp.float32)
        for head in range(heads):
            total = total + attended_ref[head, region].astype(jnp.float32)
        mean = jnp.sum(total, axis=1, keepdims=True) * (1.0 / features)
        total = jnp.zeros((tokens, width), jnp.float32)
        for head in range(heads):
            centered = attended_ref[head, region].astype(jnp.float32) - mean
            total = total + centered * centered
        variance = jnp.sum(total, axis=1, keepdims=True) * (1.0 / features)
        spread = lax.rsqrt(variance + 1e-05)
        live = position < lengths_ref[region]
        for head in range(heads):
            centered = attended_ref[head, region].astype(jnp.float32) - mean
            normed = jnp.where(live, centered * spread * gain_ref[head : head + 1, :], 0.0)
            row, column = divmod(head, PATCH)
            pixels[region, row, pl.ds(RIM + column, tokens, stride=PATCH), :] = normed
        for row in range(PATCH):
            window = three_windows(pixels[region, row], columns)
            middle = window[:, width : 2 * width]
            image_ref[region, row] = middle
            if row == 0:
                first_ref[region] = middle
            if row == PATCH - 1:
                last_ref[region] = middle
            start = (region * PATCH + row) * columns
            windows[start : start + columns, :] = window
            below = cot_ref[region, row + 1] if row < PATCH - 1 else cot_after_ref[region]
            above = cot_ref[region, row - 1] if row > 0 else cot_before_ref[region]
            cots[start : start + columns, :] = jnp.concatenate(
                [below, cot_ref[region, row], above], axis=1
            )
    product = lax.dot_general(
        windows[...], cots[...], (((0,), (0,)), ((), ())), preferred_element_type=jnp.float32
    )
    for down in range(3):
        for across in range(3):
            tap = 3 * down + across
            grads[tap * width : (tap + 1) * width, :] = product[
                across * width : (across + 1) * width, down * width : (down + 1) * width
            ]
    filled = 9 * width
    if filled < grads.shape[0]:
        grads[filled:, :] = jnp.zeros((grads.shape[0] - filled, width), jnp.float32)
    for chunk in range(grad_ref.shape[0]):
        grad_ref[chunk] = grads[chunk * chunk_rows : (chunk + 1) * chunk_rows, :].astype(jnp.bfloat16)


def decode_kernel(image_ref, before_ref, after_ref, weight_ref, out_ref, padded):
    regions, rows, columns, width = image_ref.shape
    padded[:RIM, :] = jnp.zeros((RIM, width), jnp.float32)
    padded[RIM + columns :, :] = jnp.zeros((RIM, width), jnp.float32)
    for region in range(regions):
        strips = []
        for row in range(-1, rows + 1):
            if row < 0:
                source = before_ref[region]
            elif row == rows:
                source = after_ref[region]
            else:
                source = image_ref[region, row]
            padded[RIM : RIM + columns, :] = source.astype(jnp.float32)
            strips.append(three_windows(padded[...], columns))
            if len(strips) == 3:
                total = jnp.dot(strips[0], weight_ref[0], preferred_element_type=jnp.float32)
                for down in (1, 2):
                    total = total + jnp.dot(
                        strips[down], weight_ref[down], preferred_element_type=jnp.float32
                    )
                out_ref[region, row - 1] = total.astype(jnp.bfloat16)
                strips.pop(0)


def sum_kernel(factor, parts_ref, *refs):
    out_ref = refs[-1]
    total = parts_ref[0].astype(jnp.float32)
    for part in range(1, parts_ref.shape[0]):
        total = total + parts_ref[part].astype(jnp.float32)
    if factor is not None:
        total = total * factor
    total = total.astype(jnp.bfloat16)
    for part in range(out_ref.shape[0]):
        out_ref[part] = total


def spread_kernel(parts_ref, out_ref):
    rows = parts_ref.shape[1]
    for part in range(parts_ref.shape[0]):
        start = part * rows
        kept = min(rows, out_ref.shape[0] - start)
        if kept > 0:
            out_ref[start : start + kept, :] = parts_ref[part, :kept, :].astype(jnp.float32)


def swap(parts, axes, groups=None):
    return lax.all_to_all(
        parts, axes, split_axis=0, concat_axis=0, axis_index_groups=groups, tiled=True
    )


def planes_and_columns(outer, seq_count):
    inner = 1
    while seq_count % (2 * inner) == 0 and (2 * inner) ** 2 <= seq_count:
        inner *= 2
    planes = [
        [o * seq_count + start + i for o in range(outer) for i in range(inner)]
        for start in range(0, seq_count, inner)
    ]
    columns = [list(column) for column in zip(*planes)]
    return planes, columns


def body(query_rows, key_rows, value_rows, region_lengths, norm_gain, conv_weight, cotangent):
    tokens, regions, model_width = query_rows.shape
    width = model_width // HEADS
    seq_count = lax.axis_size("seq")
    seq_index = lax.axis_index("seq")
    planes, lines = planes_and_columns(lax.axis_size("dp"), seq_count)
    columns = tokens * PATCH
    capacity = seq_count * tokens
    per_device = regions * HEADS // seq_count
    up = [(i, i + 1) for i in range(seq_count - 1)]
    down = [(j, i) for i, j in up]
    local_bytes = 2 * query_rows.size

    edge_shape = jax.ShapeDtypeStruct((regions, columns, width), jnp.bfloat16)
    packed, cot_first, cot_last = call(
        functools.partial(pack_kernel, regions, HEADS, per_device),
        "pack",
        [
            jax.ShapeDtypeStruct((seq_count, 3, per_device, tokens, width), jnp.bfloat16),
            edge_shape,
            edge_shape,
        ],
        [HBM()] * 4,
        out_specs=[HBM()] * 3,
        scratch=[
            pltpu.VMEM((3,) + query_rows.shape, jnp.bfloat16),
            pltpu.VMEM((seq_count, 3, per_device, tokens, width), jnp.bfloat16),
            pltpu.VMEM((2,) + edge_shape.shape, jnp.bfloat16),
            pltpu.SemaphoreType.DMA((10,)),
        ],
        moved=6 * local_bytes,
        grant=VMEM_WHOLE,
    )(query_rows, key_rows, value_rows, cotangent)
    packed = swap(packed, "seq")
    cot_before = lax.ppermute(cot_last, "seq", up)
    cot_after = lax.ppermute(cot_first, "seq", down)

    items = seq_index * per_device + jnp.arange(per_device, dtype=jnp.int32)
    item_lengths = jnp.sum(
        jnp.where(
            (items % regions)[:, None] == jnp.arange(regions, dtype=jnp.int32)[None, :],
            region_lengths[None, :],
            0,
        ),
        axis=1,
    )
    block_rows = min(256, capacity)
    group = regions if per_device % regions == 0 else per_device
    mixed = call(
        functools.partial(attend_kernel, block_rows, group),
        "attend",
        jax.ShapeDtypeStruct((seq_count, per_device, tokens, width), jnp.bfloat16),
        [SMEM(), VMEM(), ANY(), ANY()],
        out_specs=HBM(),
        scratch=[
            pltpu.VMEM((seq_count, per_device, tokens, width), jnp.bfloat16),
            pltpu.SemaphoreType.DMA((per_device * -(-capacity // block_rows),)),
        ],
        flops=4 * per_device * capacity * capacity * width,
        moved=4 * local_bytes,
        exps=per_device * capacity * capacity,
    )(item_lengths, packed, cot_before, cot_after)
    attended = swap(mixed, "seq").reshape(HEADS, regions, tokens, width)

    chunk_rows = -(-9 * width // len(lines))
    pixel_rows = regions * PATCH * columns
    conv_flops = 18 * pixel_rows * width * width
    image, first, last, grad_parts = call(
        functools.partial(norm_kernel, chunk_rows),
        "norm_and_gradient",
        [
            jax.ShapeDtypeStruct((regions, PATCH, columns, width), jnp.bfloat16),
            edge_shape,
            edge_shape,
            jax.ShapeDtypeStruct((len(lines), chunk_rows, width), jnp.bfloat16),
        ],
        [SMEM(), SMEM()] + [VMEM()] * 5,
        scratch=[
            pltpu.VMEM((regions, PATCH, columns + 2 * RIM, width), jnp.float32),
            pltpu.VMEM((pixel_rows, 3 * width), jnp.bfloat16),
            pltpu.VMEM((pixel_rows, 3 * width), jnp.bfloat16),
            pltpu.VMEM((len(lines) * chunk_rows, width), jnp.float32),
        ],
        flops=conv_flops,
        moved=4 * local_bytes,
    )(
        region_lengths,
        (seq_index * tokens).reshape(1),
        attended,
        norm_gain.reshape(HEADS, width),
        cotangent,
        cot_before,
        cot_after,
    )
    grad_parts = swap(grad_parts, ("dp", "seq"), planes)
    before = lax.ppermute(last, "seq", up)
    after = lax.ppermute(first, "seq", down)
    plane_sums = call(
        functools.partial(sum_kernel, None),
        "sum_plane",
        jax.ShapeDtypeStruct((len(planes), chunk_rows, width), jnp.bfloat16),
        [VMEM()],
        moved=4 * grad_parts.size,
    )(grad_parts)
    plane_sums = swap(plane_sums, ("dp", "seq"), lines)
    sums = call(
        functools.partial(sum_kernel, 1.0 / math.sqrt(PATCH * columns)),
        "sum_planes",
        jax.ShapeDtypeStruct(grad_parts.shape, jnp.bfloat16),
        [VMEM(), ANY(), ANY()],
        moved=4 * grad_parts.size,
    )(plane_sums, before, after)
    sums = swap(sums, ("dp", "seq"), planes)
    decoded = call(
        decode_kernel,
        "decode",
        jax.ShapeDtypeStruct(cotangent.shape, jnp.bfloat16),
        [VMEM()] * 4,
        scratch=[pltpu.VMEM((columns + 2 * RIM, width), jnp.float32)],
        flops=conv_flops,
        moved=2 * local_bytes,
    )(image, before, after, conv_weight.reshape(3, 3 * width, width))
    weight_grad = call(
        spread_kernel,
        "spread_sums",
        jax.ShapeDtypeStruct((9 * width, width), jnp.float32),
        [VMEM()],
        moved=6 * grad_parts.size,
    )(sums)
    return (decoded, weight_grad.reshape(conv_weight.shape))


def solution(mesh):
    placed = (
        P("seq", "dp", None),
        P("seq", "dp", None),
        P("seq", "dp", None),
        P("dp"),
        P(),
        P(),
        P("dp", "seq", None, None),
    )
    return jax.shard_map(
        body,
        mesh=mesh,
        in_specs=placed,
        out_specs=(P("dp", "seq", None, None), P()),
        check_vma=False,
    )
```

```python
import functools
import math

import jax
import jax.numpy as jnp
from jax import lax
from jax.experimental import pallas as pl
from jax.experimental.pallas import tpu as pltpu
from jax.sharding import PartitionSpec as P

HEADS = 16
PATCH = 4
RIM = 8
VMEM_LIMIT = 48 * 1024 * 1024
VMEM_WHOLE = 60 * 1024 * 1024

VMEM = functools.partial(pl.BlockSpec, memory_space=pltpu.VMEM)
HBM = functools.partial(pl.BlockSpec, memory_space=pltpu.HBM)
ANY = functools.partial(pl.BlockSpec, memory_space=pl.ANY)
SMEM = functools.partial(pl.BlockSpec, memory_space=pltpu.SMEM)


def call(kernel, name, out_shape, in_specs, out_specs=None, scratch=(), flops=0, moved=0, exps=0, grant=VMEM_LIMIT):
    many = isinstance(out_shape, (list, tuple))
    return pl.pallas_call(
        kernel,
        out_shape=out_shape,
        in_specs=in_specs,
        out_specs=out_specs or ([VMEM() for _ in out_shape] if many else VMEM()),
        scratch_shapes=list(scratch),
        compiler_params=pltpu.CompilerParams(vmem_limit_bytes=grant),
        cost_estimate=pl.CostEstimate(flops=flops, bytes_accessed=moved, transcendentals=exps),
        name=name,
    )


def pack_kernel(
    regions,
    heads,
    per_device,
    index_ref,
    query_ref,
    key_ref,
    value_ref,
    cot_ref,
    *refs,
):
    held, ready, edges, sems = refs[-4:]
    first_ref, last_ref = refs[-6:-4]
    out_refs = refs[:-6]
    width = held.shape[3] // heads
    rows = cot_ref.shape[1]
    loads = [
        pltpu.make_async_copy(ref, held.at[which], sems.at[which])
        for which, ref in enumerate((query_ref, key_ref, value_ref))
    ]
    loads.append(pltpu.make_async_copy(cot_ref.at[:, 0], edges.at[0], sems.at[3]))
    loads.append(pltpu.make_async_copy(cot_ref.at[:, rows - 1], edges.at[1], sems.at[4]))
    for load in loads:
        load.start()
    stores = []
    for which in range(3):
        loads[which].wait()
        for head in range(heads):
            block = held[which, :, :, head * width : (head + 1) * width].astype(jnp.float32)
            for region in range(regions):
                item = head * regions + region
                slot = lax.bitwise_xor(index_ref[0], item // per_device)
                ready[slot, which, item % per_device] = block[:, region, :].astype(jnp.bfloat16)
        for number, ref in enumerate(out_refs):
            stores.append(
                pltpu.make_async_copy(
                    ready.at[number, which], ref.at[which], sems.at[7 + 3 * number + which]
                )
            )
            stores[-1].start()
        if which == 0:
            for edge, ref in enumerate((first_ref, last_ref)):
                loads[3 + edge].wait()
                stores.append(pltpu.make_async_copy(edges.at[edge], ref, sems.at[5 + edge]))
                stores[-1].start()
    for store in stores:
        store.wait()


def attend_kernel(block_rows, group, index_ref, lengths_ref, *refs):
    out_ref, packed_ref, mixed_ref, load_sems, sems = refs[-5:]
    loads = [
        pltpu.make_async_copy(
            ref, packed_ref.at[lax.bitwise_xor(index_ref[0], number)], load_sems.at[number]
        )
        for number, ref in enumerate(refs[:-5])
    ]
    for load in loads:
        load.start()
    for load in loads:
        load.wait()
    sources, _, per_device, tokens, width = packed_ref.shape
    capacity = sources * tokens
    per_block = block_rows // tokens
    blocks = capacity // block_rows
    factor = math.log2(math.e) / math.sqrt(width)
    slots = lax.broadcasted_iota(jnp.int32, (1, capacity), 1)

    def rows_of(block):
        return slice(block * per_block, (block + 1) * per_block)

    def clear(item, block):
        mixed_ref[rows_of(block), item] = jnp.zeros((per_block, tokens, width), jnp.bfloat16)

    def score(item, block):
        query = packed_ref[rows_of(block), 0, item].reshape(block_rows, width)
        keys = packed_ref[:, 1, item].reshape(capacity, width)
        return lax.dot_general(
            query, keys, (((1,), (1,)), ((), ())), preferred_element_type=jnp.float32
        )

    def finish(item, block, scores, key_valid):
        values = packed_ref[:, 2, item].reshape(capacity, width)
        scores = jnp.where(key_valid, scores * factor, -1e30)
        powers = jnp.exp2(scores - jnp.max(scores, axis=1, keepdims=True))
        totals = jnp.sum(powers, axis=1, keepdims=True)
        mixed = jnp.dot(powers.astype(jnp.bfloat16), values, preferred_element_type=jnp.float32)
        mixed = (mixed / totals).astype(jnp.bfloat16)
        mixed_ref[rows_of(block), item] = mixed.reshape(per_block, tokens, width)

    def attend(tasks, length):
        key_valid = slots < length
        waiting = None
        for item, block in tasks:
            scores = score(item, block)
            if waiting is not None:
                finish(*waiting, key_valid)
            waiting = (item, block, scores)
        finish(*waiting, key_valid)

    stores = []
    for lead in range(group):
        length = lengths_ref[lead]
        items = list(range(lead, per_device, group))
        for block in range(0, blocks, 2):
            pair = list(range(block, min(block + 2, blocks)))
            start = block * block_rows

            @pl.when(length > start + block_rows)
            def _(items=items, pair=pair, length=length):
                attend([(item, one) for one in pair for item in items], length)

            @pl.when((length > start) & (length <= start + block_rows))
            def _(items=items, pair=pair, length=length):
                attend([(item, pair[0]) for item in items], length)
                for one in pair[1:]:
                    for item in items:
                        clear(item, one)

            @pl.when(length <= start)
            def _(items=items, pair=pair):
                for one in pair:
                    for item in items:
                        clear(item, one)

            rows = slice(pair[0] * per_block, (pair[-1] + 1) * per_block)
            for item in items:
                store = pltpu.make_async_copy(
                    mixed_ref.at[rows, item], out_ref.at[rows, item], sems.at[len(stores)]
                )
                store.start()
                stores.append(store)
    for store in stores:
        store.wait()


def three_windows(padded, columns):
    return jnp.concatenate(
        [padded[RIM - 1 + shift : RIM - 1 + shift + columns].astype(jnp.bfloat16) for shift in range(3)],
        axis=1,
    )


def norm_kernel(
    chunk_rows,
    lengths_ref,
    base_ref,
    attended_ref,
    gain_ref,
    cot_ref,
    cot_before_ref,
    cot_after_ref,
    image_ref,
    first_ref,
    last_ref,
    grad_ref,
    pixels,
    windows,
    cots,
    grads,
):
    heads, regions, tokens, width = attended_ref.shape
    columns = tokens * PATCH
    features = heads * width
    position = base_ref[0] + lax.broadcasted_iota(jnp.int32, (tokens, 1), 0)
    pixels[:, :, :RIM, :] = jnp.zeros((regions, PATCH, RIM, width), jnp.float32)
    pixels[:, :, RIM + columns :, :] = jnp.zeros((regions, PATCH, RIM, width), jnp.float32)
    for region in range(regions):
        total = jnp.zeros((tokens, width), jnp.float32)
        for head in range(heads):
            total = total + attended_ref[head, region].astype(jnp.float32)
        mean = jnp.sum(total, axis=1, keepdims=True) * (1.0 / features)
        total = jnp.zeros((tokens, width), jnp.float32)
        for head in range(heads):
            centered = attended_ref[head, region].astype(jnp.float32) - mean
            total = total + centered * centered
        variance = jnp.sum(total, axis=1, keepdims=True) * (1.0 / features)
        spread = lax.rsqrt(variance + 1e-05)
        live = position < lengths_ref[region]
        for head in range(heads):
            centered = attended_ref[head, region].astype(jnp.float32) - mean
            normed = jnp.where(live, centered * spread * gain_ref[head : head + 1, :], 0.0)
            row, column = divmod(head, PATCH)
            pixels[region, row, pl.ds(RIM + column, tokens, stride=PATCH), :] = normed
        for row in range(PATCH):
            window = three_windows(pixels[region, row], columns)
            middle = window[:, width : 2 * width]
            image_ref[region, row] = middle
            if row == 0:
                first_ref[region] = middle
            if row == PATCH - 1:
                last_ref[region] = middle
            start = (region * PATCH + row) * columns
            windows[start : start + columns, :] = window
            below = cot_ref[region, row + 1] if row < PATCH - 1 else cot_after_ref[region]
            above = cot_ref[region, row - 1] if row > 0 else cot_before_ref[region]
            cots[start : start + columns, :] = jnp.concatenate(
                [below, cot_ref[region, row], above], axis=1
            )
    product = lax.dot_general(
        windows[...], cots[...], (((0,), (0,)), ((), ())), preferred_element_type=jnp.float32
    )
    for down in range(3):
        for across in range(3):
            tap = 3 * down + across
            grads[tap * width : (tap + 1) * width, :] = product[
                across * width : (across + 1) * width, down * width : (down + 1) * width
            ]
    filled = 9 * width
    if filled < grads.shape[0]:
        grads[filled:, :] = jnp.zeros((grads.shape[0] - filled, width), jnp.float32)
    for chunk in range(grad_ref.shape[0]):
        grad_ref[chunk] = grads[chunk * chunk_rows : (chunk + 1) * chunk_rows, :].astype(jnp.bfloat16)


def decode_kernel(image_ref, before_ref, after_ref, weight_ref, out_ref, padded):
    regions, rows, columns, width = image_ref.shape
    padded[:RIM, :] = jnp.zeros((RIM, width), jnp.float32)
    padded[RIM + columns :, :] = jnp.zeros((RIM, width), jnp.float32)
    for region in range(regions):
        strips = []
        for row in range(-1, rows + 1):
            if row < 0:
                source = before_ref[region]
            elif row == rows:
                source = after_ref[region]
            else:
                source = image_ref[region, row]
            padded[RIM : RIM + columns, :] = source.astype(jnp.float32)
            strips.append(three_windows(padded[...], columns))
            if len(strips) == 3:
                total = jnp.dot(strips[0], weight_ref[0], preferred_element_type=jnp.float32)
                for down in (1, 2):
                    total = total + jnp.dot(
                        strips[down], weight_ref[down], preferred_element_type=jnp.float32
                    )
                out_ref[region, row - 1] = total.astype(jnp.bfloat16)
                strips.pop(0)


def sum_kernel(factor, parts_ref, *refs):
    out_ref = refs[-1]
    total = parts_ref[0].astype(jnp.float32)
    for part in range(1, parts_ref.shape[0]):
        total = total + parts_ref[part].astype(jnp.float32)
    total = (total * factor).astype(jnp.bfloat16)
    for part in range(out_ref.shape[0]):
        out_ref[part] = total


def spread_kernel(parts_ref, out_ref):
    rows = parts_ref.shape[1]
    for part in range(parts_ref.shape[0]):
        start = part * rows
        kept = min(rows, out_ref.shape[0] - start)
        if kept > 0:
            out_ref[start : start + kept, :] = parts_ref[part, :kept, :].astype(jnp.float32)


def swap(parts, axes):
    return lax.all_to_all(parts, axes, split_axis=0, concat_axis=0, tiled=True)


def body(query_rows, key_rows, value_rows, region_lengths, norm_gain, conv_weight, cotangent):
    tokens, regions, model_width = query_rows.shape
    width = model_width // HEADS
    seq_count = lax.axis_size("seq")
    seq_index = lax.axis_index("seq")
    everyone = lax.axis_size("dp") * seq_count
    columns = tokens * PATCH
    capacity = seq_count * tokens
    per_device = regions * HEADS // seq_count
    up = [(i, i + 1) for i in range(seq_count - 1)]
    down = [(j, i) for i, j in up]
    local_bytes = 2 * query_rows.size

    edge_shape = jax.ShapeDtypeStruct((regions, columns, width), jnp.bfloat16)
    chunk_shape = jax.ShapeDtypeStruct((3, per_device, tokens, width), jnp.bfloat16)
    index = seq_index.reshape(1)
    *packed, cot_first, cot_last = call(
        functools.partial(pack_kernel, regions, HEADS, per_device),
        "pack",
        [chunk_shape] * seq_count + [edge_shape] * 2,
        [SMEM()] + [HBM()] * 4,
        out_specs=[HBM()] * (seq_count + 2),
        scratch=[
            pltpu.VMEM((3,) + query_rows.shape, jnp.bfloat16),
            pltpu.VMEM((seq_count,) + chunk_shape.shape, jnp.bfloat16),
            pltpu.VMEM((2,) + edge_shape.shape, jnp.bfloat16),
            pltpu.SemaphoreType.DMA((7 + 3 * seq_count,)),
        ],
        moved=6 * local_bytes,
        grant=VMEM_WHOLE,
    )(index, query_rows, key_rows, value_rows, cotangent)
    half = seq_count // 2
    for distance in list(range(half, seq_count)) + list(range(1, half)):
        pairs = [(i, i ^ distance) for i in range(seq_count)]
        packed[distance] = lax.ppermute(packed[distance], "seq", pairs)
    cot_before = lax.ppermute(cot_last, "seq", up)
    cot_after = lax.ppermute(cot_first, "seq", down)

    items = seq_index * per_device + jnp.arange(per_device, dtype=jnp.int32)
    item_lengths = jnp.sum(
        jnp.where(
            (items % regions)[:, None] == jnp.arange(regions, dtype=jnp.int32)[None, :],
            region_lengths[None, :],
            0,
        ),
        axis=1,
    )
    block_rows = min(256, capacity)
    group = regions if per_device % regions == 0 else per_device
    mixed = call(
        functools.partial(attend_kernel, block_rows, group),
        "attend",
        jax.ShapeDtypeStruct((seq_count, per_device, tokens, width), jnp.bfloat16),
        [SMEM(), SMEM()] + [ANY()] * seq_count,
        out_specs=HBM(),
        scratch=[
            pltpu.VMEM((seq_count,) + chunk_shape.shape, jnp.bfloat16),
            pltpu.VMEM((seq_count, per_device, tokens, width), jnp.bfloat16),
            pltpu.SemaphoreType.DMA((seq_count,)),
            pltpu.SemaphoreType.DMA((per_device * -(-capacity // block_rows),)),
        ],
        flops=4 * per_device * capacity * capacity * width,
        moved=4 * local_bytes,
        exps=per_device * capacity * capacity,
    )(index, item_lengths, *packed)
    attended = swap(mixed, "seq").reshape(HEADS, regions, tokens, width)

    chunk_rows = -(-9 * width // everyone)
    pixel_rows = regions * PATCH * columns
    conv_flops = 18 * pixel_rows * width * width
    image, first, last, grad_parts = call(
        functools.partial(norm_kernel, chunk_rows),
        "norm_and_gradient",
        [
            jax.ShapeDtypeStruct((regions, PATCH, columns, width), jnp.bfloat16),
            edge_shape,
            edge_shape,
            jax.ShapeDtypeStruct((everyone, chunk_rows, width), jnp.bfloat16),
        ],
        [SMEM(), SMEM()] + [VMEM()] * 5,
        scratch=[
            pltpu.VMEM((regions, PATCH, columns + 2 * RIM, width), jnp.float32),
            pltpu.VMEM((pixel_rows, 3 * width), jnp.bfloat16),
            pltpu.VMEM((pixel_rows, 3 * width), jnp.bfloat16),
            pltpu.VMEM((everyone * chunk_rows, width), jnp.float32),
        ],
        flops=conv_flops,
        moved=4 * local_bytes,
    )(
        region_lengths,
        (seq_index * tokens).reshape(1),
        attended,
        norm_gain.reshape(HEADS, width),
        cotangent,
        cot_before,
        cot_after,
    )
    grad_parts = swap(grad_parts, ("dp", "seq"))
    before = lax.ppermute(last, "seq", up)
    after = lax.ppermute(first, "seq", down)
    sums = call(
        functools.partial(sum_kernel, 1.0 / math.sqrt(PATCH * columns)),
        "sum_parts",
        jax.ShapeDtypeStruct(grad_parts.shape, jnp.bfloat16),
        [VMEM(), ANY(), ANY()],
        moved=4 * grad_parts.size,
    )(grad_parts, before, after)
    sums = swap(sums, ("dp", "seq"))
    decoded = call(
        decode_kernel,
        "decode",
        jax.ShapeDtypeStruct(cotangent.shape, jnp.bfloat16),
        [VMEM()] * 4,
        scratch=[pltpu.VMEM((columns + 2 * RIM, width), jnp.float32)],
        flops=conv_flops,
        moved=2 * local_bytes,
    )(image, before, after, conv_weight.reshape(3, 3 * width, width))
    weight_grad = call(
        spread_kernel,
        "spread_sums",
        jax.ShapeDtypeStruct((9 * width, width), jnp.float32),
        [VMEM()],
        moved=6 * grad_parts.size,
    )(sums)
    return (decoded, weight_grad.reshape(conv_weight.shape))


def solution(mesh):
    placed = (
        P("seq", "dp", None),
        P("seq", "dp", None),
        P("seq", "dp", None),
        P("dp"),
        P(),
        P(),
        P("dp", "seq", None, None),
    )
    return jax.shard_map(
        body,
        mesh=mesh,
        in_specs=placed,
        out_specs=(P("dp", "seq", None, None), P()),
        check_vma=False,
    )
```

```python
import functools
import math

import jax
import jax.numpy as jnp
from jax import lax
from jax.experimental import pallas as pl
from jax.experimental.pallas import tpu as pltpu
from jax.sharding import PartitionSpec as P

HEADS = 16
PATCH = 4
RIM = 8
VMEM_LIMIT = 48 * 1024 * 1024
VMEM_WHOLE = 60 * 1024 * 1024

VMEM = functools.partial(pl.BlockSpec, memory_space=pltpu.VMEM)
HBM = functools.partial(pl.BlockSpec, memory_space=pltpu.HBM)
ANY = functools.partial(pl.BlockSpec, memory_space=pl.ANY)
SMEM = functools.partial(pl.BlockSpec, memory_space=pltpu.SMEM)


def call(kernel, name, out_shape, in_specs, out_specs=None, scratch=(), flops=0, moved=0, exps=0, grant=VMEM_LIMIT):
    many = isinstance(out_shape, (list, tuple))
    return pl.pallas_call(
        kernel,
        out_shape=out_shape,
        in_specs=in_specs,
        out_specs=out_specs or ([VMEM() for _ in out_shape] if many else VMEM()),
        scratch_shapes=list(scratch),
        compiler_params=pltpu.CompilerParams(vmem_limit_bytes=grant),
        cost_estimate=pl.CostEstimate(flops=flops, bytes_accessed=moved, transcendentals=exps),
        name=name,
    )


def pack_kernel(
    regions,
    heads,
    per_device,
    index_ref,
    query_ref,
    key_ref,
    value_ref,
    cot_ref,
    *refs,
):
    held, ready, edges, sems = refs[-4:]
    edge_refs = refs[-6:-4]
    out_refs = refs[:-6]
    width = held.shape[3] // heads
    rows = cot_ref.shape[1]
    loads = [
        pltpu.make_async_copy(ref, held.at[which], sems.at[which])
        for which, ref in enumerate((query_ref, key_ref, value_ref))
    ]
    odd = lax.rem(index_ref[0], 2)
    for edge, row in enumerate(((1 - odd) * (rows - 1), odd * (rows - 1))):
        loads.append(pltpu.make_async_copy(cot_ref.at[:, row], edges.at[edge], sems.at[3 + edge]))
    for load in loads:
        load.start()
    stores = []
    for which in range(3):
        loads[which].wait()
        for head in range(heads):
            block = held[which, :, :, head * width : (head + 1) * width].astype(jnp.float32)
            for region in range(regions):
                item = head * regions + region
                slot = lax.bitwise_xor(index_ref[0], item // per_device)
                ready[slot, which, item % per_device] = block[:, region, :].astype(jnp.bfloat16)
        for number, ref in enumerate(out_refs):
            stores.append(
                pltpu.make_async_copy(
                    ready.at[number, which], ref.at[which], sems.at[7 + 3 * number + which]
                )
            )
            stores[-1].start()
        if which == 0:
            for edge, ref in enumerate(edge_refs):
                loads[3 + edge].wait()
                stores.append(pltpu.make_async_copy(edges.at[edge], ref, sems.at[5 + edge]))
                stores[-1].start()
    for store in stores:
        store.wait()


def attend_kernel(block_rows, group, order, index_ref, lengths_ref, *refs):
    out_ref, mixed_ref, sems = refs[-3:]
    chunks = dict(zip(order, refs[:-3]))
    index = index_ref[0]
    sources = len(chunks)
    _, per_device, tokens, width = chunks[0].shape
    capacity = sources * tokens
    per_block = block_rows // tokens
    blocks = capacity // block_rows
    factor = math.log2(math.e) / math.sqrt(width)
    columns = lax.broadcasted_iota(jnp.int32, (1, capacity), 1)
    slots = columns
    for distance in range(sources):
        here = (columns >= distance * tokens) & (columns < (distance + 1) * tokens)
        moved = (lax.bitwise_xor(index, distance) - distance) * tokens
        slots = jnp.where(here, columns + moved, slots)

    def rows_of(which, item, distances):
        return jnp.concatenate([chunks[distance][which, item] for distance in distances], axis=0)

    def distances_of(block):
        return range(block * per_block, (block + 1) * per_block)

    def start_of(block, span):
        return lax.bitwise_xor(lax.div(index, span), block) * span

    def clear(item, block):
        for distance in distances_of(block):
            mixed_ref[lax.bitwise_xor(index, distance), item] = jnp.zeros(
                (tokens, width), jnp.bfloat16
            )

    def score(item, block):
        return lax.dot_general(
            rows_of(0, item, distances_of(block)),
            rows_of(1, item, range(sources)),
            (((1,), (1,)), ((), ())),
            preferred_element_type=jnp.float32,
        )

    def finish(item, block, scores, key_valid):
        scores = jnp.where(key_valid, scores * factor, -1e30)
        powers = jnp.exp2(scores - jnp.max(scores, axis=1, keepdims=True))
        totals = jnp.sum(powers, axis=1, keepdims=True)
        mixed = jnp.dot(
            powers.astype(jnp.bfloat16),
            rows_of(2, item, range(sources)),
            preferred_element_type=jnp.float32,
        )
        mixed = (mixed / totals).astype(jnp.bfloat16)
        for number, distance in enumerate(distances_of(block)):
            mixed_ref[lax.bitwise_xor(index, distance), item] = mixed[
                number * tokens : (number + 1) * tokens
            ]

    def attend(items, live, dead, length):
        key_valid = slots < length
        waiting = None
        for block in live:
            for item in items:
                scores = score(item, block)
                if waiting is not None:
                    finish(*waiting, key_valid)
                waiting = (item, block, scores)
        if waiting is not None:
            finish(*waiting, key_valid)
        for block in dead:
            for item in items:
                clear(item, block)

    stores = []
    for lead in range(group):
        length = lengths_ref[lead]
        items = list(range(lead, per_device, group))
        for block in range(0, blocks, 2):
            pair = list(range(block, min(block + 2, blocks)))
            alive = [length > start_of(one, per_block) * tokens for one in pair]
            for case in range(2 ** len(pair)):
                live = [one for bit, one in enumerate(pair) if case >> bit & 1]
                dead = [one for one in pair if one not in live]
                chosen = None
                for bit in range(len(pair)):
                    test = alive[bit] if case >> bit & 1 else jnp.logical_not(alive[bit])
                    chosen = test if chosen is None else chosen & test

                @pl.when(chosen)
                def _(items=items, live=live, dead=dead, length=length):
                    attend(items, live, dead, length)

            span = per_block * len(pair)
            rows = pl.ds(start_of(block // len(pair), span), span)
            for item in items:
                store = pltpu.make_async_copy(
                    mixed_ref.at[rows, item], out_ref.at[rows, item], sems.at[len(stores)]
                )
                store.start()
                stores.append(store)
    for store in stores:
        store.wait()


def three_windows(padded, columns):
    return jnp.concatenate(
        [padded[RIM - 1 + shift : RIM - 1 + shift + columns].astype(jnp.bfloat16) for shift in range(3)],
        axis=1,
    )


def around(odd, near, far):
    return jnp.where(odd == 1, near, far), jnp.where(odd == 1, far, near)


def norm_kernel(
    chunk_rows,
    lengths_ref,
    index_ref,
    attended_ref,
    gain_ref,
    cot_ref,
    cot_near_ref,
    cot_far_ref,
    image_ref,
    near_ref,
    far_ref,
    grad_ref,
    pixels,
    windows,
    cots,
    grads,
):
    heads, regions, tokens, width = attended_ref.shape
    columns = tokens * PATCH
    features = heads * width
    odd = lax.rem(index_ref[0], 2)
    position = index_ref[0] * tokens + lax.broadcasted_iota(jnp.int32, (tokens, 1), 0)
    pixels[:, :, :RIM, :] = jnp.zeros((regions, PATCH, RIM, width), jnp.float32)
    pixels[:, :, RIM + columns :, :] = jnp.zeros((regions, PATCH, RIM, width), jnp.float32)
    for region in range(regions):
        total = jnp.zeros((tokens, width), jnp.float32)
        for head in range(heads):
            total = total + attended_ref[head, region].astype(jnp.float32)
        mean = jnp.sum(total, axis=1, keepdims=True) * (1.0 / features)
        total = jnp.zeros((tokens, width), jnp.float32)
        for head in range(heads):
            centered = attended_ref[head, region].astype(jnp.float32) - mean
            total = total + centered * centered
        variance = jnp.sum(total, axis=1, keepdims=True) * (1.0 / features)
        spread = lax.rsqrt(variance + 1e-05)
        live = position < lengths_ref[region]
        for head in range(heads):
            centered = attended_ref[head, region].astype(jnp.float32) - mean
            normed = jnp.where(live, centered * spread * gain_ref[head : head + 1, :], 0.0)
            row, column = divmod(head, PATCH)
            pixels[region, row, pl.ds(RIM + column, tokens, stride=PATCH), :] = normed
        cot_before, cot_after = around(odd, cot_near_ref[region], cot_far_ref[region])
        for row in range(PATCH):
            window = three_windows(pixels[region, row], columns)
            middle = window[:, width : 2 * width]
            image_ref[region, row] = middle
            start = (region * PATCH + row) * columns
            windows[start : start + columns, :] = window
            below = cot_ref[region, row + 1] if row < PATCH - 1 else cot_after
            above = cot_ref[region, row - 1] if row > 0 else cot_before
            cots[start : start + columns, :] = jnp.concatenate(
                [below, cot_ref[region, row], above], axis=1
            )
        near_ref[region] = image_ref[region, (1 - odd) * (PATCH - 1)]
        far_ref[region] = image_ref[region, odd * (PATCH - 1)]
    product = lax.dot_general(
        windows[...], cots[...], (((0,), (0,)), ((), ())), preferred_element_type=jnp.float32
    )
    for down in range(3):
        for across in range(3):
            tap = 3 * down + across
            grads[tap * width : (tap + 1) * width, :] = product[
                across * width : (across + 1) * width, down * width : (down + 1) * width
            ]
    filled = 9 * width
    if filled < grads.shape[0]:
        grads[filled:, :] = jnp.zeros((grads.shape[0] - filled, width), jnp.float32)
    for chunk in range(grad_ref.shape[0]):
        grad_ref[chunk] = grads[chunk * chunk_rows : (chunk + 1) * chunk_rows, :].astype(jnp.bfloat16)


def decode_kernel(index_ref, image_ref, near_ref, far_ref, weight_ref, out_ref, padded):
    regions, rows, columns, width = image_ref.shape
    padded[:RIM, :] = jnp.zeros((RIM, width), jnp.float32)
    padded[RIM + columns :, :] = jnp.zeros((RIM, width), jnp.float32)
    for region in range(regions):
        strips = []
        before, after = around(lax.rem(index_ref[0], 2), near_ref[region], far_ref[region])
        for row in range(-1, rows + 1):
            if row < 0:
                source = before
            elif row == rows:
                source = after
            else:
                source = image_ref[region, row]
            padded[RIM : RIM + columns, :] = source.astype(jnp.float32)
            strips.append(three_windows(padded[...], columns))
            if len(strips) == 3:
                total = jnp.dot(strips[0], weight_ref[0], preferred_element_type=jnp.float32)
                for down in (1, 2):
                    total = total + jnp.dot(
                        strips[down], weight_ref[down], preferred_element_type=jnp.float32
                    )
                out_ref[region, row - 1] = total.astype(jnp.bfloat16)
                strips.pop(0)


def sum_kernel(count, factor, *refs):
    out_ref = refs[-1]
    if count == 1:
        parts = [refs[0].at[part] for part in range(refs[0].shape[0])]
    else:
        parts = refs[:count]
    totals = [part[...].astype(jnp.float32) for part in parts]
    while len(totals) > 1:
        paired = [one + other for one, other in zip(totals[::2], totals[1::2])]
        totals = paired + totals[2 * len(paired) :]
    total = totals[0]
    if factor is not None:
        total = total * factor
    total = total.astype(jnp.bfloat16)
    if out_ref.ndim == 2:
        out_ref[...] = total
    else:
        for part in range(out_ref.shape[0]):
            out_ref[part] = total


def spread_kernel(parts_ref, out_ref):
    rows = parts_ref.shape[1]
    for part in range(parts_ref.shape[0]):
        start = part * rows
        kept = min(rows, out_ref.shape[0] - start)
        if kept > 0:
            out_ref[start : start + kept, :] = parts_ref[part, :kept, :].astype(jnp.float32)


def swap(parts, axes, groups=None):
    return lax.all_to_all(
        parts, axes, split_axis=0, concat_axis=0, axis_index_groups=groups, tiled=True
    )


def trade(values, distance):
    pairs = [(i, i ^ distance) for i in range(lax.axis_size("seq"))]
    return lax.ppermute(values, "seq", pairs)


def planes_of(outer, seq_count):
    inner = 1
    while seq_count % (2 * inner) == 0 and (2 * inner) ** 2 <= seq_count:
        inner *= 2
    planes = [
        [o * seq_count + start + i for o in range(outer) for i in range(inner)]
        for start in range(0, seq_count, inner)
    ]
    return inner, planes


def body(query_rows, key_rows, value_rows, region_lengths, norm_gain, conv_weight, cotangent):
    tokens, regions, model_width = query_rows.shape
    width = model_width // HEADS
    seq_count = lax.axis_size("seq")
    seq_index = lax.axis_index("seq")
    inner, planes = planes_of(lax.axis_size("dp"), seq_count)
    plane_size = len(planes[0])
    columns = tokens * PATCH
    capacity = seq_count * tokens
    per_device = regions * HEADS // seq_count
    far_pairs = [(i, i + 1) for i in range(1, seq_count - 1, 2)]
    far_pairs = far_pairs + [(j, i) for i, j in far_pairs]
    local_bytes = 2 * query_rows.size

    edge_shape = jax.ShapeDtypeStruct((regions, columns, width), jnp.bfloat16)
    chunk_shape = jax.ShapeDtypeStruct((3, per_device, tokens, width), jnp.bfloat16)
    index = seq_index.reshape(1)
    *packed, cot_near, cot_far = call(
        functools.partial(pack_kernel, regions, HEADS, per_device),
        "pack",
        [chunk_shape] * seq_count + [edge_shape] * 2,
        [SMEM()] + [HBM()] * 4,
        out_specs=[HBM()] * (seq_count + 2),
        scratch=[
            pltpu.VMEM((3,) + query_rows.shape, jnp.bfloat16),
            pltpu.VMEM((seq_count,) + chunk_shape.shape, jnp.bfloat16),
            pltpu.VMEM((2,) + edge_shape.shape, jnp.bfloat16),
            pltpu.SemaphoreType.DMA((7 + 3 * seq_count,)),
        ],
        moved=6 * local_bytes,
        grant=VMEM_WHOLE,
    )(index, query_rows, key_rows, value_rows, cotangent)
    half = seq_count // 2
    order = list(range(half, seq_count)) + list(range(1, half)) + [0]
    for distance in order[:-1]:
        packed[distance] = trade(packed[distance], distance)
    cot_near = trade(cot_near, 1)
    cot_far = lax.ppermute(cot_far, "seq", far_pairs)

    items = seq_index * per_device + jnp.arange(per_device, dtype=jnp.int32)
    item_lengths = jnp.sum(
        jnp.where(
            (items % regions)[:, None] == jnp.arange(regions, dtype=jnp.int32)[None, :],
            region_lengths[None, :],
            0,
        ),
        axis=1,
    )
    block_rows = min(256, capacity)
    group = regions if per_device % regions == 0 else per_device
    mixed = call(
        functools.partial(attend_kernel, block_rows, group, order),
        "attend",
        jax.ShapeDtypeStruct((seq_count, per_device, tokens, width), jnp.bfloat16),
        [SMEM(), SMEM()] + [VMEM()] * seq_count,
        out_specs=HBM(),
        scratch=[
            pltpu.VMEM((seq_count, per_device, tokens, width), jnp.bfloat16),
            pltpu.SemaphoreType.DMA((per_device * -(-capacity // block_rows),)),
        ],
        flops=4 * per_device * capacity * capacity * width,
        moved=4 * local_bytes,
        exps=per_device * capacity * capacity,
    )(index, item_lengths, *[packed[distance] for distance in order])
    attended = swap(mixed, "seq").reshape(HEADS, regions, tokens, width)

    chunk_rows = -(-9 * width // plane_size)
    pixel_rows = regions * PATCH * columns
    conv_flops = 18 * pixel_rows * width * width
    image, near, far, grad_parts = call(
        functools.partial(norm_kernel, chunk_rows),
        "norm_and_gradient",
        [
            jax.ShapeDtypeStruct((regions, PATCH, columns, width), jnp.bfloat16),
            edge_shape,
            edge_shape,
            jax.ShapeDtypeStruct((plane_size, chunk_rows, width), jnp.bfloat16),
        ],
        [SMEM(), SMEM()] + [VMEM()] * 5,
        scratch=[
            pltpu.VMEM((regions, PATCH, columns + 2 * RIM, width), jnp.float32),
            pltpu.VMEM((pixel_rows, 3 * width), jnp.bfloat16),
            pltpu.VMEM((pixel_rows, 3 * width), jnp.bfloat16),
            pltpu.VMEM((plane_size * chunk_rows, width), jnp.float32),
        ],
        flops=conv_flops,
        moved=4 * local_bytes,
    )(
        region_lengths,
        index,
        attended,
        norm_gain.reshape(HEADS, width),
        cotangent,
        cot_near,
        cot_far,
    )
    grad_parts = swap(grad_parts, ("dp", "seq"), planes)
    near = trade(near, 1)
    far = lax.ppermute(far, "seq", far_pairs)
    plane_sum = call(
        functools.partial(sum_kernel, 1, None),
        "sum_plane",
        jax.ShapeDtypeStruct((chunk_rows, width), jnp.bfloat16),
        [VMEM()],
        moved=2 * grad_parts.size,
    )(grad_parts)
    plane_sums = [plane_sum] + [trade(plane_sum, inner * step) for step in range(1, len(planes))]
    sums = call(
        functools.partial(sum_kernel, len(planes), 1.0 / math.sqrt(PATCH * columns)),
        "sum_planes",
        jax.ShapeDtypeStruct(grad_parts.shape, jnp.bfloat16),
        [VMEM()] * len(planes) + [ANY(), ANY()],
        moved=4 * grad_parts.size,
    )(*plane_sums, near, far)
    sums = swap(sums, ("dp", "seq"), planes)
    decoded = call(
        decode_kernel,
        "decode",
        jax.ShapeDtypeStruct(cotangent.shape, jnp.bfloat16),
        [SMEM()] + [VMEM()] * 4,
        scratch=[pltpu.VMEM((columns + 2 * RIM, width), jnp.float32)],
        flops=conv_flops,
        moved=2 * local_bytes,
    )(index, image, near, far, conv_weight.reshape(3, 3 * width, width))
    weight_grad = call(
        spread_kernel,
        "spread_sums",
        jax.ShapeDtypeStruct((9 * width, width), jnp.float32),
        [VMEM()],
        moved=6 * grad_parts.size,
    )(sums)
    return (decoded, weight_grad.reshape(conv_weight.shape))


def solution(mesh):
    placed = (
        P("seq", "dp", None),
        P("seq", "dp", None),
        P("seq", "dp", None),
        P("dp"),
        P(),
        P(),
        P("dp", "seq", None, None),
    )
    return jax.shard_map(
        body,
        mesh=mesh,
        in_specs=placed,
        out_specs=(P("dp", "seq", None, None), P()),
        check_vma=False,
    )
```

```python
import functools
import math

import jax
import jax.numpy as jnp
from jax import lax
from jax.experimental import pallas as pl
from jax.experimental.pallas import tpu as pltpu
from jax.sharding import PartitionSpec as P

HEADS = 16
PATCH = 4
RIM = 8
VMEM_LIMIT = 48 * 1024 * 1024
VMEM_WHOLE = 60 * 1024 * 1024

VMEM = functools.partial(pl.BlockSpec, memory_space=pltpu.VMEM)
HBM = functools.partial(pl.BlockSpec, memory_space=pltpu.HBM)
ANY = functools.partial(pl.BlockSpec, memory_space=pl.ANY)
SMEM = functools.partial(pl.BlockSpec, memory_space=pltpu.SMEM)


def call(kernel, name, out_shape, in_specs, out_specs=None, scratch=(), flops=0, moved=0, exps=0, grant=VMEM_LIMIT):
    many = isinstance(out_shape, (list, tuple))
    return pl.pallas_call(
        kernel,
        out_shape=out_shape,
        in_specs=in_specs,
        out_specs=out_specs or ([VMEM() for _ in out_shape] if many else VMEM()),
        scratch_shapes=list(scratch),
        compiler_params=pltpu.CompilerParams(vmem_limit_bytes=grant),
        cost_estimate=pl.CostEstimate(flops=flops, bytes_accessed=moved, transcendentals=exps),
        name=name,
    )


def unpack_items(held, which, regions, per_device, owner):
    width = held.shape[3] // HEADS
    aligned = per_device % regions == 0
    items = []
    for place in range(per_device):
        if aligned and place % regions:
            region = place % regions
        else:
            item = owner * per_device + place
            head = lax.div(item, regions)
            region = 0 if aligned else lax.rem(item, regions)
            start = pl.multiple_of(head * width, width)
            block = held[which, :, :, pl.ds(start, width)].astype(jnp.float32)
        value = block[:, 0, :]
        for other in range(1, regions):
            if aligned:
                value = block[:, other, :] if region == other else value
            else:
                value = jnp.where(region == other, block[:, other, :], value)
        items.append(value.astype(jnp.bfloat16))
    return items


def pack_kernel(
    regions, per_device, index_ref, query_ref, key_ref, value_ref, cot_ref, *refs
):
    held, ready, edges, sems = refs[-4:]
    edge_refs = refs[-6:-4]
    out_refs = refs[:-6]
    rows = cot_ref.shape[1]
    loads = [
        pltpu.make_async_copy(ref, held.at[which], sems.at[which])
        for which, ref in enumerate((query_ref, key_ref, value_ref))
    ]
    odd = lax.rem(index_ref[0], 2)
    for edge, row in enumerate(((1 - odd) * (rows - 1), odd * (rows - 1))):
        loads.append(pltpu.make_async_copy(cot_ref.at[:, row], edges.at[edge], sems.at[3 + edge]))
    for load in loads:
        load.start()
    stores = []
    for which in range(3):
        loads[which].wait()
        for number, ref in enumerate(out_refs):
            owner = lax.bitwise_xor(index_ref[0], number + 1)
            for place, value in enumerate(unpack_items(held, which, regions, per_device, owner)):
                ready[number, which, place] = value
            stores.append(
                pltpu.make_async_copy(
                    ready.at[number, which], ref.at[which], sems.at[7 + 3 * number + which]
                )
            )
            stores[-1].start()
        if which == 0:
            for edge, ref in enumerate(edge_refs):
                loads[3 + edge].wait()
                stores.append(pltpu.make_async_copy(edges.at[edge], ref, sems.at[5 + edge]))
                stores[-1].start()
    for store in stores:
        store.wait()


def own_kernel(regions, per_device, index_ref, query_ref, key_ref, value_ref, out_ref, held, sems):
    tokens, width = out_ref.shape[2:]
    span = max(1, per_device // regions) * width
    index = index_ref[0]
    start = lax.div(index * per_device, regions) * width
    loads = []
    for which, ref in enumerate((query_ref, key_ref, value_ref)):
        columns = pl.ds(pl.multiple_of(start, width), span)
        loads.append(
            pltpu.make_async_copy(ref.at[:, :, columns], held.at[which], sems.at[which])
        )
        loads[-1].start()
    for which, load in enumerate(loads):
        load.wait()
        for head in range(span // width):
            block = held[which, :, :, head * width : (head + 1) * width].astype(jnp.float32)
            if per_device % regions:
                value = block[:, 0, :]
                for other in range(1, regions):
                    value = jnp.where(lax.rem(index, regions) == other, block[:, other, :], value)
                out_ref[which, head] = value.astype(jnp.bfloat16)
            else:
                for region in range(regions):
                    out_ref[which, head * regions + region] = block[:, region, :].astype(
                        jnp.bfloat16
                    )


def attend_kernel(block_rows, group, order, index_ref, lengths_ref, *refs):
    chunks = dict(zip(order, refs))
    out_refs = refs[len(order) :]
    index = index_ref[0]
    sources = len(chunks)
    _, per_device, tokens, width = chunks[0].shape
    capacity = sources * tokens
    per_block = block_rows // tokens
    blocks = capacity // block_rows
    factor = math.log2(math.e) / math.sqrt(width)
    columns = lax.broadcasted_iota(jnp.int32, (1, capacity), 1)
    slots = columns
    for distance in range(sources):
        here = (columns >= distance * tokens) & (columns < (distance + 1) * tokens)
        moved = (lax.bitwise_xor(index, distance) - distance) * tokens
        slots = jnp.where(here, columns + moved, slots)

    def rows_of(which, item, distances):
        return jnp.concatenate([chunks[distance][which, item] for distance in distances], axis=0)

    def distances_of(block):
        return range(block * per_block, (block + 1) * per_block)

    def start_of(block, span):
        return lax.bitwise_xor(lax.div(index, span), block) * span

    def clear(item, block):
        for distance in distances_of(block):
            out_refs[distance][item] = jnp.zeros((tokens, width), jnp.bfloat16)

    def score(item, block):
        return lax.dot_general(
            rows_of(0, item, distances_of(block)),
            rows_of(1, item, range(sources)),
            (((1,), (1,)), ((), ())),
            preferred_element_type=jnp.float32,
        )

    def finish(item, block, scores, key_valid):
        scores = jnp.where(key_valid, scores * factor, -1e30)
        powers = jnp.exp2(scores - jnp.max(scores, axis=1, keepdims=True))
        totals = jnp.sum(powers, axis=1, keepdims=True)
        mixed = jnp.dot(
            powers.astype(jnp.bfloat16),
            rows_of(2, item, range(sources)),
            preferred_element_type=jnp.float32,
        )
        mixed = (mixed / totals).astype(jnp.bfloat16)
        for number, distance in enumerate(distances_of(block)):
            out_refs[distance][item] = mixed[number * tokens : (number + 1) * tokens]

    def attend(items, live, dead, length):
        key_valid = slots < length
        waiting = None
        for block in live:
            for item in items:
                scores = score(item, block)
                if waiting is not None:
                    finish(*waiting, key_valid)
                waiting = (item, block, scores)
        if waiting is not None:
            finish(*waiting, key_valid)
        for block in dead:
            for item in items:
                clear(item, block)

    for lead in range(group):
        length = lengths_ref[lead]
        items = list(range(lead, per_device, group))
        for block in range(0, blocks, 2):
            pair = list(range(block, min(block + 2, blocks)))
            alive = [length > start_of(one, per_block) * tokens for one in pair]
            for case in range(2 ** len(pair)):
                live = [one for bit, one in enumerate(pair) if case >> bit & 1]
                dead = [one for one in pair if one not in live]
                chosen = None
                for bit in range(len(pair)):
                    test = alive[bit] if case >> bit & 1 else jnp.logical_not(alive[bit])
                    chosen = test if chosen is None else chosen & test

                @pl.when(chosen)
                def _(items=items, live=live, dead=dead, length=length):
                    attend(items, live, dead, length)


def three_windows(padded, columns):
    return jnp.concatenate(
        [padded[RIM - 1 + shift : RIM - 1 + shift + columns].astype(jnp.bfloat16) for shift in range(3)],
        axis=1,
    )


def around(odd, near, far):
    return jnp.where(odd == 1, near, far), jnp.where(odd == 1, far, near)


def norm_kernel(
    chunk_rows,
    lengths_ref,
    index_ref,
    gain_ref,
    cot_ref,
    cot_near_ref,
    cot_far_ref,
    *refs,
):
    image_ref, near_ref, far_ref, grad_ref, attended, pixels, windows, cots, grads = refs[-9:]
    for distance, ref in enumerate(refs[:-9]):
        attended[lax.bitwise_xor(index_ref[0], distance)] = ref[...]
    heads = gain_ref.shape[0]
    regions = image_ref.shape[0]
    _, per_device, tokens, width = attended.shape

    def load(head, region):
        owner, place = divmod(head * regions + region, per_device)
        return attended[owner, place].astype(jnp.float32)

    columns = tokens * PATCH
    features = heads * width
    odd = lax.rem(index_ref[0], 2)
    position = index_ref[0] * tokens + lax.broadcasted_iota(jnp.int32, (tokens, 1), 0)
    pixels[:, :, :RIM, :] = jnp.zeros((regions, PATCH, RIM, width), jnp.float32)
    pixels[:, :, RIM + columns :, :] = jnp.zeros((regions, PATCH, RIM, width), jnp.float32)
    for region in range(regions):
        total = jnp.zeros((tokens, width), jnp.float32)
        for head in range(heads):
            total = total + load(head, region)
        mean = jnp.sum(total, axis=1, keepdims=True) * (1.0 / features)
        total = jnp.zeros((tokens, width), jnp.float32)
        for head in range(heads):
            centered = load(head, region) - mean
            total = total + centered * centered
        variance = jnp.sum(total, axis=1, keepdims=True) * (1.0 / features)
        spread = lax.rsqrt(variance + 1e-05)
        live = position < lengths_ref[region]
        for head in range(heads):
            centered = load(head, region) - mean
            normed = jnp.where(live, centered * spread * gain_ref[head : head + 1, :], 0.0)
            row, column = divmod(head, PATCH)
            pixels[region, row, pl.ds(RIM + column, tokens, stride=PATCH), :] = normed
        cot_before, cot_after = around(odd, cot_near_ref[region], cot_far_ref[region])
        for row in range(PATCH):
            window = three_windows(pixels[region, row], columns)
            middle = window[:, width : 2 * width]
            image_ref[region, row] = middle
            start = (region * PATCH + row) * columns
            windows[start : start + columns, :] = window
            below = cot_ref[region, row + 1] if row < PATCH - 1 else cot_after
            above = cot_ref[region, row - 1] if row > 0 else cot_before
            cots[start : start + columns, :] = jnp.concatenate(
                [below, cot_ref[region, row], above], axis=1
            )
        near_ref[region] = image_ref[region, (1 - odd) * (PATCH - 1)]
        far_ref[region] = image_ref[region, odd * (PATCH - 1)]
        part = slice(region * PATCH * columns, (region + 1) * PATCH * columns)
        term = lax.dot_general(
            windows[part, :],
            cots[part, :],
            (((0,), (0,)), ((), ())),
            preferred_element_type=jnp.float32,
        )
        product = term if region == 0 else product + term
    for down in range(3):
        for across in range(3):
            tap = 3 * down + across
            grads[tap * width : (tap + 1) * width, :] = product[
                across * width : (across + 1) * width, down * width : (down + 1) * width
            ]
    filled = 9 * width
    if filled < grads.shape[0]:
        grads[filled:, :] = jnp.zeros((grads.shape[0] - filled, width), jnp.float32)
    for chunk in range(grad_ref.shape[0]):
        grad_ref[chunk] = grads[chunk * chunk_rows : (chunk + 1) * chunk_rows, :].astype(jnp.bfloat16)


def decode_kernel(index_ref, image_ref, near_ref, far_ref, weight_ref, out_ref, padded):
    regions, rows, columns, width = image_ref.shape
    padded[:RIM, :] = jnp.zeros((RIM, width), jnp.float32)
    padded[RIM + columns :, :] = jnp.zeros((RIM, width), jnp.float32)
    for region in range(regions):
        strips = []
        before, after = around(lax.rem(index_ref[0], 2), near_ref[region], far_ref[region])
        for row in range(-1, rows + 1):
            if row < 0:
                source = before
            elif row == rows:
                source = after
            else:
                source = image_ref[region, row]
            padded[RIM : RIM + columns, :] = source.astype(jnp.float32)
            strips.append(three_windows(padded[...], columns))
            if len(strips) == 3:
                total = jnp.dot(strips[0], weight_ref[0], preferred_element_type=jnp.float32)
                for down in (1, 2):
                    total = total + jnp.dot(
                        strips[down], weight_ref[down], preferred_element_type=jnp.float32
                    )
                out_ref[region, row - 1] = total.astype(jnp.bfloat16)
                strips.pop(0)


def sum_kernel(count, factor, *refs):
    out_ref = refs[-1]
    if count == 1:
        parts = [refs[0].at[part] for part in range(refs[0].shape[0])]
    else:
        parts = refs[:count]
    totals = [part[...].astype(jnp.float32) for part in parts]
    while len(totals) > 1:
        paired = [one + other for one, other in zip(totals[::2], totals[1::2])]
        totals = paired + totals[2 * len(paired) :]
    total = totals[0]
    if factor is not None:
        total = total * factor
    total = total.astype(jnp.bfloat16)
    if out_ref.ndim == 2:
        out_ref[...] = total
    else:
        for part in range(out_ref.shape[0]):
            out_ref[part] = total


def spread_kernel(parts_ref, out_ref):
    rows = parts_ref.shape[1]
    for part in range(parts_ref.shape[0]):
        start = part * rows
        kept = min(rows, out_ref.shape[0] - start)
        if kept > 0:
            out_ref[start : start + kept, :] = parts_ref[part, :kept, :].astype(jnp.float32)


def swap(parts, axes, groups=None):
    return lax.all_to_all(
        parts, axes, split_axis=0, concat_axis=0, axis_index_groups=groups, tiled=True
    )


def trade(values, distance):
    pairs = [(i, i ^ distance) for i in range(lax.axis_size("seq"))]
    return lax.ppermute(values, "seq", pairs)


def planes_of(outer, seq_count):
    inner = 1
    while seq_count % (2 * inner) == 0 and (2 * inner) ** 2 <= seq_count:
        inner *= 2
    planes = [
        [o * seq_count + start + i for o in range(outer) for i in range(inner)]
        for start in range(0, seq_count, inner)
    ]
    return inner, planes


def body(query_rows, key_rows, value_rows, region_lengths, norm_gain, conv_weight, cotangent):
    tokens, regions, model_width = query_rows.shape
    width = model_width // HEADS
    seq_count = lax.axis_size("seq")
    seq_index = lax.axis_index("seq")
    inner, planes = planes_of(lax.axis_size("dp"), seq_count)
    plane_size = len(planes[0])
    columns = tokens * PATCH
    capacity = seq_count * tokens
    per_device = regions * HEADS // seq_count
    far_pairs = [(i, i + 1) for i in range(1, seq_count - 1, 2)]
    far_pairs = far_pairs + [(j, i) for i, j in far_pairs]
    local_bytes = 2 * query_rows.size

    edge_shape = jax.ShapeDtypeStruct((regions, columns, width), jnp.bfloat16)
    chunk_shape = jax.ShapeDtypeStruct((3, per_device, tokens, width), jnp.bfloat16)
    index = seq_index.reshape(1)
    *leaving, cot_near, cot_far = call(
        functools.partial(pack_kernel, regions, per_device),
        "pack",
        [chunk_shape] * (seq_count - 1) + [edge_shape] * 2,
        [SMEM()] + [HBM()] * 4,
        out_specs=[HBM()] * (seq_count + 1),
        scratch=[
            pltpu.VMEM((3,) + query_rows.shape, jnp.bfloat16),
            pltpu.VMEM((seq_count - 1,) + chunk_shape.shape, jnp.bfloat16),
            pltpu.VMEM((2,) + edge_shape.shape, jnp.bfloat16),
            pltpu.SemaphoreType.DMA((7 + 3 * (seq_count - 1),)),
        ],
        moved=6 * local_bytes,
        grant=VMEM_WHOLE,
    )(index, query_rows, key_rows, value_rows, cotangent)
    order = list(range(1, seq_count)) + [0]
    packed = [trade(chunk, distance) for distance, chunk in zip(order, leaving)]
    own = call(
        functools.partial(own_kernel, regions, per_device),
        "own_chunk",
        chunk_shape,
        [SMEM()] + [HBM()] * 3,
        scratch=[
            pltpu.VMEM((3, tokens, regions, max(1, per_device // regions) * width), jnp.bfloat16),
            pltpu.SemaphoreType.DMA((3,)),
        ],
        moved=12 * chunk_shape.size,
    )(index, query_rows, key_rows, value_rows)
    cot_near = trade(cot_near, 1)
    cot_far = lax.ppermute(cot_far, "seq", far_pairs)

    items = seq_index * per_device + jnp.arange(per_device, dtype=jnp.int32)
    item_lengths = jnp.sum(
        jnp.where(
            (items % regions)[:, None] == jnp.arange(regions, dtype=jnp.int32)[None, :],
            region_lengths[None, :],
            0,
        ),
        axis=1,
    )
    block_rows = min(256, capacity)
    group = regions if per_device % regions == 0 else per_device
    mixed = call(
        functools.partial(attend_kernel, block_rows, group, order),
        "attend",
        [jax.ShapeDtypeStruct((per_device, tokens, width), jnp.bfloat16)] * seq_count,
        [SMEM(), SMEM()] + [VMEM()] * seq_count,
        flops=4 * per_device * capacity * capacity * width,
        moved=4 * local_bytes,
        exps=per_device * capacity * capacity,
    )(index, item_lengths, *packed, own)
    attended = [mixed[0]] + [trade(mixed[distance], distance) for distance in order[:-1]]

    chunk_rows = -(-9 * width // plane_size)
    pixel_rows = regions * PATCH * columns
    conv_flops = 18 * pixel_rows * width * width
    image, near, far, grad_parts = call(
        functools.partial(norm_kernel, chunk_rows),
        "norm_and_gradient",
        [
            jax.ShapeDtypeStruct((regions, PATCH, columns, width), jnp.bfloat16),
            edge_shape,
            edge_shape,
            jax.ShapeDtypeStruct((plane_size, chunk_rows, width), jnp.bfloat16),
        ],
        [SMEM(), SMEM()] + [VMEM()] * (4 + seq_count),
        scratch=[
            pltpu.VMEM((seq_count,) + mixed[0].shape, jnp.bfloat16),
            pltpu.VMEM((regions, PATCH, columns + 2 * RIM, width), jnp.float32),
            pltpu.VMEM((pixel_rows, 3 * width), jnp.bfloat16),
            pltpu.VMEM((pixel_rows, 3 * width), jnp.bfloat16),
            pltpu.VMEM((plane_size * chunk_rows, width), jnp.float32),
        ],
        flops=conv_flops,
        moved=4 * local_bytes,
    )(
        region_lengths,
        index,
        norm_gain.reshape(HEADS, width),
        cotangent,
        cot_near,
        cot_far,
        *attended,
    )
    grad_parts = swap(grad_parts, ("dp", "seq"), planes)
    near = trade(near, 1)
    far = lax.ppermute(far, "seq", far_pairs)
    plane_sum = call(
        functools.partial(sum_kernel, 1, None),
        "sum_plane",
        jax.ShapeDtypeStruct((chunk_rows, width), jnp.bfloat16),
        [VMEM()],
        moved=2 * grad_parts.size,
    )(grad_parts)
    plane_sums = [plane_sum] + [trade(plane_sum, inner * step) for step in range(1, len(planes))]
    sums = call(
        functools.partial(sum_kernel, len(planes), 1.0 / math.sqrt(PATCH * columns)),
        "sum_planes",
        jax.ShapeDtypeStruct(grad_parts.shape, jnp.bfloat16),
        [VMEM()] * len(planes) + [ANY(), ANY()],
        moved=4 * grad_parts.size,
    )(*plane_sums, near, far)
    sums = swap(sums, ("dp", "seq"), planes)
    decoded = call(
        decode_kernel,
        "decode",
        jax.ShapeDtypeStruct(cotangent.shape, jnp.bfloat16),
        [SMEM()] + [VMEM()] * 4,
        scratch=[pltpu.VMEM((columns + 2 * RIM, width), jnp.float32)],
        flops=conv_flops,
        moved=2 * local_bytes,
    )(index, image, near, far, conv_weight.reshape(3, 3 * width, width))
    weight_grad = call(
        spread_kernel,
        "spread_sums",
        jax.ShapeDtypeStruct((9 * width, width), jnp.float32),
        [VMEM()],
        moved=6 * grad_parts.size,
    )(sums)
    return (decoded, weight_grad.reshape(conv_weight.shape))


def solution(mesh):
    placed = (
        P("seq", "dp", None),
        P("seq", "dp", None),
        P("seq", "dp", None),
        P("dp"),
        P(),
        P(),
        P("dp", "seq", None, None),
    )
    return jax.shard_map(
        body,
        mesh=mesh,
        in_specs=placed,
        out_specs=(P("dp", "seq", None, None), P()),
        check_vma=False,
    )
```

```python
import functools
import math

import jax
import jax.numpy as jnp
from jax import lax
from jax.experimental import pallas as pl
from jax.experimental.pallas import tpu as pltpu
from jax.sharding import PartitionSpec as P

HEADS = 16
PATCH = 4
RIM = 8
VMEM_LIMIT = 48 * 1024 * 1024
VMEM_WHOLE = 60 * 1024 * 1024

VMEM = functools.partial(pl.BlockSpec, memory_space=pltpu.VMEM)
HBM = functools.partial(pl.BlockSpec, memory_space=pltpu.HBM)
ANY = functools.partial(pl.BlockSpec, memory_space=pl.ANY)
SMEM = functools.partial(pl.BlockSpec, memory_space=pltpu.SMEM)


def call(kernel, name, out_shape, in_specs, out_specs=None, scratch=(), flops=0, moved=0, exps=0, grant=VMEM_LIMIT):
    many = isinstance(out_shape, (list, tuple))
    return pl.pallas_call(
        kernel,
        out_shape=out_shape,
        in_specs=in_specs,
        out_specs=out_specs or ([VMEM() for _ in out_shape] if many else VMEM()),
        scratch_shapes=list(scratch),
        compiler_params=pltpu.CompilerParams(vmem_limit_bytes=grant),
        cost_estimate=pl.CostEstimate(flops=flops, bytes_accessed=moved, transcendentals=exps),
        name=name,
    )


def unpack_items(held, which, regions, per_device, owner):
    width = held.shape[3] // HEADS
    aligned = per_device % regions == 0
    items = []
    for place in range(per_device):
        if aligned and place % regions:
            region = place % regions
        else:
            item = owner * per_device + place
            head = lax.div(item, regions)
            region = 0 if aligned else lax.rem(item, regions)
            start = pl.multiple_of(head * width, width)
            block = held[which, :, :, pl.ds(start, width)].astype(jnp.float32)
        value = block[:, 0, :]
        for other in range(1, regions):
            if aligned:
                value = block[:, other, :] if region == other else value
            else:
                value = jnp.where(region == other, block[:, other, :], value)
        items.append(value.astype(jnp.bfloat16))
    return items


def pack_kernel(
    regions, per_device, index_ref, query_ref, key_ref, value_ref, cot_ref, *refs
):
    held, ready, edges, sems = refs[-4:]
    edge_refs = refs[-6:-4]
    out_refs = refs[:-6]
    rows = cot_ref.shape[1]
    loads = [
        pltpu.make_async_copy(ref, held.at[which], sems.at[which])
        for which, ref in enumerate((query_ref, key_ref, value_ref))
    ]
    odd = lax.rem(index_ref[0], 2)
    for edge, row in enumerate(((1 - odd) * (rows - 1), odd * (rows - 1))):
        loads.append(pltpu.make_async_copy(cot_ref.at[:, row], edges.at[edge], sems.at[3 + edge]))
    for load in loads:
        load.start()
    stores = []
    for which in range(3):
        loads[which].wait()
        for number, ref in enumerate(out_refs):
            owner = lax.bitwise_xor(index_ref[0], number + 1)
            for place, value in enumerate(unpack_items(held, which, regions, per_device, owner)):
                ready[number, which, place] = value
            stores.append(
                pltpu.make_async_copy(
                    ready.at[number, which], ref.at[which], sems.at[7 + 3 * number + which]
                )
            )
            stores[-1].start()
        if which == 0:
            for edge, ref in enumerate(edge_refs):
                loads[3 + edge].wait()
                stores.append(pltpu.make_async_copy(edges.at[edge], ref, sems.at[5 + edge]))
                stores[-1].start()
    for store in stores:
        store.wait()


def own_kernel(regions, per_device, index_ref, query_ref, key_ref, value_ref, out_ref, held, sems):
    tokens, width = out_ref.shape[2:]
    span = max(1, per_device // regions) * width
    index = index_ref[0]
    start = lax.div(index * per_device, regions) * width
    loads = []
    for which, ref in enumerate((query_ref, key_ref, value_ref)):
        columns = pl.ds(pl.multiple_of(start, width), span)
        loads.append(
            pltpu.make_async_copy(ref.at[:, :, columns], held.at[which], sems.at[which])
        )
        loads[-1].start()
    for which, load in enumerate(loads):
        load.wait()
        for head in range(span // width):
            block = held[which, :, :, head * width : (head + 1) * width].astype(jnp.float32)
            if per_device % regions:
                value = block[:, 0, :]
                for other in range(1, regions):
                    value = jnp.where(lax.rem(index, regions) == other, block[:, other, :], value)
                out_ref[which, head] = value.astype(jnp.bfloat16)
            else:
                for region in range(regions):
                    out_ref[which, head * regions + region] = block[:, region, :].astype(
                        jnp.bfloat16
                    )


def attend_kernel(block_rows, group, order, index_ref, lengths_ref, *refs):
    chunks = dict(zip(order, refs))
    out_refs = refs[len(order) :]
    index = index_ref[0]
    sources = len(chunks)
    _, per_device, tokens, width = chunks[0].shape
    capacity = sources * tokens
    per_block = block_rows // tokens
    blocks = capacity // block_rows
    factor = math.log2(math.e) / math.sqrt(width)
    columns = lax.broadcasted_iota(jnp.int32, (1, capacity), 1)
    slots = columns
    for distance in range(sources):
        here = (columns >= distance * tokens) & (columns < (distance + 1) * tokens)
        moved = (lax.bitwise_xor(index, distance) - distance) * tokens
        slots = jnp.where(here, columns + moved, slots)

    def rows_of(which, item, distances):
        return jnp.concatenate([chunks[distance][which, item] for distance in distances], axis=0)

    def distances_of(block):
        return range(block * per_block, (block + 1) * per_block)

    def start_of(block, span):
        return lax.bitwise_xor(lax.div(index, span), block) * span

    def clear(item, block):
        for distance in distances_of(block):
            out_refs[distance][item] = jnp.zeros((tokens, width), jnp.bfloat16)

    def score(item, block):
        return lax.dot_general(
            rows_of(0, item, distances_of(block)),
            rows_of(1, item, range(sources)),
            (((1,), (1,)), ((), ())),
            preferred_element_type=jnp.float32,
        )

    def finish(item, block, scores, key_valid):
        scores = jnp.where(key_valid, scores * factor, -1e30)
        powers = jnp.exp2(scores - jnp.max(scores, axis=1, keepdims=True))
        totals = jnp.sum(powers, axis=1, keepdims=True)
        mixed = jnp.dot(
            powers.astype(jnp.bfloat16),
            rows_of(2, item, range(sources)),
            preferred_element_type=jnp.float32,
        )
        mixed = (mixed / totals).astype(jnp.bfloat16)
        for number, distance in enumerate(distances_of(block)):
            out_refs[distance][item] = mixed[number * tokens : (number + 1) * tokens]

    def attend(items, live, dead, length):
        key_valid = slots < length
        waiting = None
        for block in live:
            for item in items:
                scores = score(item, block)
                if waiting is not None:
                    finish(*waiting, key_valid)
                waiting = (item, block, scores)
        if waiting is not None:
            finish(*waiting, key_valid)
        for block in dead:
            for item in items:
                clear(item, block)

    for lead in range(group):
        length = lengths_ref[lead]
        items = list(range(lead, per_device, group))
        for block in range(0, blocks, 2):
            pair = list(range(block, min(block + 2, blocks)))
            alive = [length > start_of(one, per_block) * tokens for one in pair]
            for case in range(2 ** len(pair)):
                live = [one for bit, one in enumerate(pair) if case >> bit & 1]
                dead = [one for one in pair if one not in live]
                chosen = None
                for bit in range(len(pair)):
                    test = alive[bit] if case >> bit & 1 else jnp.logical_not(alive[bit])
                    chosen = test if chosen is None else chosen & test

                @pl.when(chosen)
                def _(items=items, live=live, dead=dead, length=length):
                    attend(items, live, dead, length)


def three_windows(padded, columns):
    return jnp.concatenate(
        [padded[RIM - 1 + shift : RIM - 1 + shift + columns].astype(jnp.bfloat16) for shift in range(3)],
        axis=1,
    )


def around(odd, near, far):
    return jnp.where(odd == 1, near, far), jnp.where(odd == 1, far, near)


def turn_kernel(index_ref, cot_ref, near_ref, far_ref, out_ref):
    regions, rows, columns, width = cot_ref.shape
    for region in range(regions):
        before, after = around(lax.rem(index_ref[0], 2), near_ref[region], far_ref[region])
        for row in range(-1, rows + 1):
            value = before if row < 0 else after if row == rows else cot_ref[region, row]
            turned = value.T
            for down in range(3):
                image_row = row - 1 + down
                if 0 <= image_row < rows:
                    start = (region * rows + image_row) * columns
                    out_ref[down * width : (down + 1) * width, start : start + columns] = turned


def norm_kernel(chunk_rows, lengths_ref, index_ref, gain_ref, turned_ref, *refs):
    attended, pixels, windows, grads = refs[-4:]
    sources = attended.shape[0]
    chunks = refs[:sources]
    image_ref, near_ref, far_ref = refs[sources : sources + 3]
    grad_refs = refs[sources + 3 : -4]
    for distance, ref in enumerate(chunks):
        attended[lax.bitwise_xor(index_ref[0], distance)] = ref[...]
    heads = gain_ref.shape[0]
    regions = image_ref.shape[0]
    _, per_device, tokens, width = attended.shape

    def load(head, region):
        owner, place = divmod(head * regions + region, per_device)
        return attended[owner, place].astype(jnp.float32)

    columns = tokens * PATCH
    features = heads * width
    odd = lax.rem(index_ref[0], 2)
    position = index_ref[0] * tokens + lax.broadcasted_iota(jnp.int32, (tokens, 1), 0)
    pixels[:, :, :RIM, :] = jnp.zeros((regions, PATCH, RIM, width), jnp.float32)
    pixels[:, :, RIM + columns :, :] = jnp.zeros((regions, PATCH, RIM, width), jnp.float32)
    for region in range(regions):
        total = jnp.zeros((tokens, width), jnp.float32)
        for head in range(heads):
            total = total + load(head, region)
        mean = jnp.sum(total, axis=1, keepdims=True) * (1.0 / features)
        total = jnp.zeros((tokens, width), jnp.float32)
        for head in range(heads):
            centered = load(head, region) - mean
            total = total + centered * centered
        variance = jnp.sum(total, axis=1, keepdims=True) * (1.0 / features)
        spread = lax.rsqrt(variance + 1e-05)
        live = position < lengths_ref[region]
        for head in range(heads):
            centered = load(head, region) - mean
            normed = jnp.where(live, centered * spread * gain_ref[head : head + 1, :], 0.0)
            row, column = divmod(head, PATCH)
            pixels[region, row, pl.ds(RIM + column, tokens, stride=PATCH), :] = normed
        for row in range(PATCH):
            window = three_windows(pixels[region, row], columns)
            image_ref[region, row] = window[:, width : 2 * width]
            start = (region * PATCH + row) * columns
            windows[start : start + columns, :] = window
        near_ref[region] = image_ref[region, (1 - odd) * (PATCH - 1)]
        far_ref[region] = image_ref[region, odd * (PATCH - 1)]
        part = slice(region * PATCH * columns, (region + 1) * PATCH * columns)
        term = jnp.dot(turned_ref[:, part], windows[part, :], preferred_element_type=jnp.float32)
        product = term if region == 0 else product + term
    for down in range(3):
        for across in range(3):
            tap = 3 * down + across
            grads[tap * width : (tap + 1) * width, :] = product[
                down * width : (down + 1) * width, across * width : (across + 1) * width
            ].T
    filled = 9 * width
    if filled < grads.shape[0]:
        grads[filled:, :] = jnp.zeros((grads.shape[0] - filled, width), jnp.float32)
    for distance, ref in enumerate(grad_refs):
        start = lax.bitwise_xor(index_ref[1], distance) * chunk_rows
        rows = pl.ds(pl.multiple_of(start, chunk_rows), chunk_rows)
        ref[...] = grads[rows, :].astype(jnp.bfloat16)


def decode_kernel(index_ref, image_ref, near_ref, far_ref, weight_ref, out_ref, padded):
    regions, rows, columns, width = image_ref.shape
    padded[:RIM, :] = jnp.zeros((RIM, width), jnp.float32)
    padded[RIM + columns :, :] = jnp.zeros((RIM, width), jnp.float32)
    for region in range(regions):
        strips = []
        before, after = around(lax.rem(index_ref[0], 2), near_ref[region], far_ref[region])
        for row in range(-1, rows + 1):
            if row < 0:
                source = before
            elif row == rows:
                source = after
            else:
                source = image_ref[region, row]
            padded[RIM : RIM + columns, :] = source.astype(jnp.float32)
            strips.append(three_windows(padded[...], columns))
            if len(strips) == 3:
                total = jnp.dot(strips[0], weight_ref[0], preferred_element_type=jnp.float32)
                for down in (1, 2):
                    total = total + jnp.dot(
                        strips[down], weight_ref[down], preferred_element_type=jnp.float32
                    )
                out_ref[region, row - 1] = total.astype(jnp.bfloat16)
                strips.pop(0)


def sum_kernel(count, factor, *refs):
    out_ref = refs[-1]
    totals = [ref[...].astype(jnp.float32) for ref in refs[:count]]
    while len(totals) > 1:
        paired = [one + other for one, other in zip(totals[::2], totals[1::2])]
        totals = paired + totals[2 * len(paired) :]
    out_ref[...] = (totals[0] * factor).astype(jnp.bfloat16)


def spread_kernel(index_ref, *refs):
    out_ref = refs[-1]
    chunk_rows = refs[0].shape[0]
    for distance, ref in enumerate(refs[:-1]):
        start = lax.bitwise_xor(index_ref[1], distance) * chunk_rows
        rows = pl.ds(pl.multiple_of(start, chunk_rows), chunk_rows)
        out_ref[rows, :] = ref[...].astype(jnp.float32)


def trade(values, distance):
    pairs = [(i, i ^ distance) for i in range(lax.axis_size("seq"))]
    return lax.ppermute(values, "seq", pairs)


def inner_size(seq_count):
    inner = 1
    while seq_count % (2 * inner) == 0 and (2 * inner) ** 2 <= seq_count:
        inner *= 2
    return inner


def trade_in_plane(values, distance, inner):
    seq_count = lax.axis_size("seq")
    pairs = []
    for outer in range(lax.axis_size("dp")):
        for seq in range(seq_count):
            partner, lane = divmod((outer * inner + seq % inner) ^ distance, inner)
            pairs.append((outer * seq_count + seq, partner * seq_count + seq - seq % inner + lane))
    return lax.ppermute(values, ("dp", "seq"), pairs)


def body(query_rows, key_rows, value_rows, region_lengths, norm_gain, conv_weight, cotangent):
    tokens, regions, model_width = query_rows.shape
    width = model_width // HEADS
    seq_count = lax.axis_size("seq")
    seq_index = lax.axis_index("seq")
    inner = inner_size(seq_count)
    plane_size = lax.axis_size("dp") * inner
    plane_index = lax.axis_index("dp") * inner + lax.rem(seq_index, inner)
    columns = tokens * PATCH
    capacity = seq_count * tokens
    per_device = regions * HEADS // seq_count
    far_pairs = [(i, i + 1) for i in range(1, seq_count - 1, 2)]
    far_pairs = far_pairs + [(j, i) for i, j in far_pairs]
    local_bytes = 2 * query_rows.size

    edge_shape = jax.ShapeDtypeStruct((regions, columns, width), jnp.bfloat16)
    chunk_shape = jax.ShapeDtypeStruct((3, per_device, tokens, width), jnp.bfloat16)
    index = jnp.stack([seq_index, plane_index]).astype(jnp.int32)
    *leaving, cot_near, cot_far = call(
        functools.partial(pack_kernel, regions, per_device),
        "pack",
        [chunk_shape] * (seq_count - 1) + [edge_shape] * 2,
        [SMEM()] + [HBM()] * 4,
        out_specs=[HBM()] * (seq_count + 1),
        scratch=[
            pltpu.VMEM((3,) + query_rows.shape, jnp.bfloat16),
            pltpu.VMEM((seq_count - 1,) + chunk_shape.shape, jnp.bfloat16),
            pltpu.VMEM((2,) + edge_shape.shape, jnp.bfloat16),
            pltpu.SemaphoreType.DMA((7 + 3 * (seq_count - 1),)),
        ],
        moved=6 * local_bytes,
        grant=VMEM_WHOLE,
    )(index, query_rows, key_rows, value_rows, cotangent)
    order = list(range(1, seq_count)) + [0]
    packed = [trade(chunk, distance) for distance, chunk in zip(order, leaving)]
    own = call(
        functools.partial(own_kernel, regions, per_device),
        "own_chunk",
        chunk_shape,
        [SMEM()] + [HBM()] * 3,
        scratch=[
            pltpu.VMEM((3, tokens, regions, max(1, per_device // regions) * width), jnp.bfloat16),
            pltpu.SemaphoreType.DMA((3,)),
        ],
        moved=12 * chunk_shape.size,
    )(index, query_rows, key_rows, value_rows)
    cot_near = trade(cot_near, 1)
    cot_far = lax.ppermute(cot_far, "seq", far_pairs)

    items = seq_index * per_device + jnp.arange(per_device, dtype=jnp.int32)
    item_lengths = jnp.sum(
        jnp.where(
            (items % regions)[:, None] == jnp.arange(regions, dtype=jnp.int32)[None, :],
            region_lengths[None, :],
            0,
        ),
        axis=1,
    )
    block_rows = min(256, capacity)
    group = regions if per_device % regions == 0 else per_device
    mixed = call(
        functools.partial(attend_kernel, block_rows, group, order),
        "attend",
        [jax.ShapeDtypeStruct((per_device, tokens, width), jnp.bfloat16)] * seq_count,
        [SMEM(), SMEM()] + [VMEM()] * seq_count,
        flops=4 * per_device * capacity * capacity * width,
        moved=4 * local_bytes,
        exps=per_device * capacity * capacity,
    )(index, item_lengths, *packed, own)
    attended = [mixed[0]] + [trade(mixed[distance], distance) for distance in order[:-1]]

    turned = call(
        turn_kernel,
        "turn_cotangent",
        jax.ShapeDtypeStruct((3 * width, cotangent.size // width), jnp.bfloat16),
        [SMEM()] + [VMEM()] * 3,
        moved=8 * cotangent.size,
    )(index, cotangent, cot_near, cot_far)
    chunk_rows = -(-9 * width // (16 * plane_size)) * 16
    pixel_rows = regions * PATCH * columns
    conv_flops = 18 * pixel_rows * width * width
    part_shape = jax.ShapeDtypeStruct((chunk_rows, width), jnp.bfloat16)
    image, near, far, *parts = call(
        functools.partial(norm_kernel, chunk_rows),
        "norm_and_gradient",
        [jax.ShapeDtypeStruct((regions, PATCH, columns, width), jnp.bfloat16)]
        + [edge_shape] * 2
        + [part_shape] * plane_size,
        [SMEM(), SMEM()] + [VMEM()] * (2 + seq_count),
        scratch=[
            pltpu.VMEM((seq_count,) + mixed[0].shape, jnp.bfloat16),
            pltpu.VMEM((regions, PATCH, columns + 2 * RIM, width), jnp.float32),
            pltpu.VMEM((pixel_rows, 3 * width), jnp.bfloat16),
            pltpu.VMEM((plane_size * chunk_rows, width), jnp.float32),
        ],
        flops=conv_flops,
        moved=4 * local_bytes,
    )(region_lengths, index, norm_gain.reshape(HEADS, width), turned, *attended)
    distances = range(1, plane_size)
    parts[1:] = [trade_in_plane(parts[distance], distance, inner) for distance in distances]
    near = trade(near, 1)
    far = lax.ppermute(far, "seq", far_pairs)
    plane_sum = call(
        functools.partial(sum_kernel, plane_size, 1.0),
        "sum_plane",
        part_shape,
        [VMEM()] * plane_size,
        moved=4 * plane_size * chunk_rows * width,
    )(*parts)
    plane_sums = [plane_sum] + [
        trade(plane_sum, distance) for distance in range(inner, seq_count, inner)
    ]
    total = call(
        functools.partial(sum_kernel, len(plane_sums), 1.0 / math.sqrt(PATCH * columns)),
        "sum_planes",
        part_shape,
        [VMEM()] * len(plane_sums) + [ANY(), ANY()],
        moved=4 * len(plane_sums) * chunk_rows * width,
    )(*plane_sums, near, far)
    totals = [total] + [trade_in_plane(total, distance, inner) for distance in distances]
    decoded = call(
        decode_kernel,
        "decode",
        jax.ShapeDtypeStruct(cotangent.shape, jnp.bfloat16),
        [SMEM()] + [VMEM()] * 4,
        scratch=[pltpu.VMEM((columns + 2 * RIM, width), jnp.float32)],
        flops=conv_flops,
        moved=2 * local_bytes,
    )(index, image, near, far, conv_weight.reshape(3, 3 * width, width))
    weight_grad = call(
        spread_kernel,
        "spread_sums",
        jax.ShapeDtypeStruct((plane_size * chunk_rows, width), jnp.float32),
        [SMEM()] + [VMEM()] * plane_size,
        moved=6 * plane_size * chunk_rows * width,
    )(index, *totals)
    return (decoded, weight_grad[: 9 * width].reshape(conv_weight.shape))


def solution(mesh):
    placed = (
        P("seq", "dp", None),
        P("seq", "dp", None),
        P("seq", "dp", None),
        P("dp"),
        P(),
        P(),
        P("dp", "seq", None, None),
    )
    return jax.shard_map(
        body,
        mesh=mesh,
        in_specs=placed,
        out_specs=(P("dp", "seq", None, None), P()),
        check_vma=False,
    )
```

```python
import functools
import math

import jax
import jax.numpy as jnp
from jax import lax
from jax.experimental import pallas as pl
from jax.experimental.pallas import tpu as pltpu
from jax.sharding import PartitionSpec as P

HEADS = 16
PATCH = 4
RIM = 8
VMEM_LIMIT = 48 * 1024 * 1024
VMEM_WHOLE = 60 * 1024 * 1024

VMEM = functools.partial(pl.BlockSpec, memory_space=pltpu.VMEM)
HBM = functools.partial(pl.BlockSpec, memory_space=pltpu.HBM)
ANY = functools.partial(pl.BlockSpec, memory_space=pl.ANY)
SMEM = functools.partial(pl.BlockSpec, memory_space=pltpu.SMEM)


def call(kernel, name, out_shape, in_specs, out_specs=None, scratch=(), flops=0, moved=0, exps=0, grant=VMEM_LIMIT):
    many = isinstance(out_shape, (list, tuple))
    return pl.pallas_call(
        kernel,
        out_shape=out_shape,
        in_specs=in_specs,
        out_specs=out_specs or ([VMEM() for _ in out_shape] if many else VMEM()),
        scratch_shapes=list(scratch),
        compiler_params=pltpu.CompilerParams(vmem_limit_bytes=grant),
        cost_estimate=pl.CostEstimate(flops=flops, bytes_accessed=moved, transcendentals=exps),
        name=name,
    )


def unpack_items(held, which, regions, per_device, owner):
    width = held.shape[3] // HEADS
    aligned = per_device % regions == 0
    items = []
    for place in range(per_device):
        if aligned and place % regions:
            region = place % regions
        else:
            item = owner * per_device + place
            head = lax.div(item, regions)
            region = 0 if aligned else lax.rem(item, regions)
            start = pl.multiple_of(head * width, width)
            block = held[which, :, :, pl.ds(start, width)].astype(jnp.float32)
        value = block[:, 0, :]
        for other in range(1, regions):
            if aligned:
                value = block[:, other, :] if region == other else value
            else:
                value = jnp.where(region == other, block[:, other, :], value)
        items.append(value.astype(jnp.bfloat16))
    return items


def pack_kernel(
    regions, per_device, index_ref, query_ref, key_ref, value_ref, cot_ref, *refs
):
    held, ready, edges, sems = refs[-4:]
    edge_refs = refs[-6:-4]
    out_refs = refs[:-6]
    rows = cot_ref.shape[1]
    loads = [
        pltpu.make_async_copy(ref, held.at[which], sems.at[which])
        for which, ref in enumerate((query_ref, key_ref, value_ref))
    ]
    odd = lax.rem(index_ref[0], 2)
    for edge, row in enumerate(((1 - odd) * (rows - 1), odd * (rows - 1))):
        loads.append(pltpu.make_async_copy(cot_ref.at[:, row], edges.at[edge], sems.at[3 + edge]))
    for load in loads:
        load.start()
    stores = []
    for which in range(3):
        loads[which].wait()
        for number, ref in enumerate(out_refs):
            owner = lax.bitwise_xor(index_ref[0], number + 1)
            for place, value in enumerate(unpack_items(held, which, regions, per_device, owner)):
                ready[number, which, place] = value
            stores.append(
                pltpu.make_async_copy(
                    ready.at[number, which], ref.at[which], sems.at[7 + 3 * number + which]
                )
            )
            stores[-1].start()
        if which == 0:
            for edge, ref in enumerate(edge_refs):
                loads[3 + edge].wait()
                stores.append(pltpu.make_async_copy(edges.at[edge], ref, sems.at[5 + edge]))
                stores[-1].start()
    for store in stores:
        store.wait()


def own_kernel(regions, per_device, index_ref, query_ref, key_ref, value_ref, out_ref, held, sems):
    tokens, width = out_ref.shape[2:]
    span = max(1, per_device // regions) * width
    index = index_ref[0]
    start = lax.div(index * per_device, regions) * width
    loads = []
    for which, ref in enumerate((query_ref, key_ref, value_ref)):
        columns = pl.ds(pl.multiple_of(start, width), span)
        loads.append(
            pltpu.make_async_copy(ref.at[:, :, columns], held.at[which], sems.at[which])
        )
        loads[-1].start()
    for which, load in enumerate(loads):
        load.wait()
        for head in range(span // width):
            block = held[which, :, :, head * width : (head + 1) * width].astype(jnp.float32)
            if per_device % regions:
                value = block[:, 0, :]
                for other in range(1, regions):
                    value = jnp.where(lax.rem(index, regions) == other, block[:, other, :], value)
                out_ref[which, head] = value.astype(jnp.bfloat16)
            else:
                for region in range(regions):
                    out_ref[which, head * regions + region] = block[:, region, :].astype(
                        jnp.bfloat16
                    )


def attend_kernel(block_rows, group, order, index_ref, lengths_ref, *refs):
    chunks = dict(zip(order, refs))
    out_refs = refs[len(order) :]
    index = index_ref[0]
    sources = len(chunks)
    _, per_device, tokens, width = chunks[0].shape
    capacity = sources * tokens
    per_block = block_rows // tokens
    blocks = capacity // block_rows
    factor = math.log2(math.e) / math.sqrt(width)
    columns = lax.broadcasted_iota(jnp.int32, (1, capacity), 1)
    slots = columns
    for distance in range(sources):
        here = (columns >= distance * tokens) & (columns < (distance + 1) * tokens)
        moved = (lax.bitwise_xor(index, distance) - distance) * tokens
        slots = jnp.where(here, columns + moved, slots)

    def rows_of(which, item, distances):
        return jnp.concatenate([chunks[distance][which, item] for distance in distances], axis=0)

    def distances_of(block):
        return range(block * per_block, (block + 1) * per_block)

    def start_of(block, span):
        return lax.bitwise_xor(lax.div(index, span), block) * span

    def clear(item, block):
        for distance in distances_of(block):
            out_refs[distance][item] = jnp.zeros((tokens, width), jnp.bfloat16)

    def score(item, block):
        return lax.dot_general(
            rows_of(0, item, distances_of(block)),
            rows_of(1, item, range(sources)),
            (((1,), (1,)), ((), ())),
            preferred_element_type=jnp.float32,
        )

    def finish(item, block, scores, key_valid):
        scores = jnp.where(key_valid, scores * factor, -1e30)
        powers = jnp.exp2(scores - jnp.max(scores, axis=1, keepdims=True))
        totals = jnp.sum(powers, axis=1, keepdims=True)
        mixed = jnp.dot(
            powers.astype(jnp.bfloat16),
            rows_of(2, item, range(sources)),
            preferred_element_type=jnp.float32,
        )
        mixed = (mixed / totals).astype(jnp.bfloat16)
        for number, distance in enumerate(distances_of(block)):
            out_refs[distance][item] = mixed[number * tokens : (number + 1) * tokens]

    def attend(items, live, dead, length):
        key_valid = slots < length
        waiting = None
        for block in live:
            for item in items:
                scores = score(item, block)
                if waiting is not None:
                    finish(*waiting, key_valid)
                waiting = (item, block, scores)
        if waiting is not None:
            finish(*waiting, key_valid)
        for block in dead:
            for item in items:
                clear(item, block)

    for lead in range(group):
        length = lengths_ref[lead]
        items = list(range(lead, per_device, group))
        for block in range(0, blocks, 2):
            pair = list(range(block, min(block + 2, blocks)))
            alive = [length > start_of(one, per_block) * tokens for one in pair]
            for case in range(2 ** len(pair)):
                live = [one for bit, one in enumerate(pair) if case >> bit & 1]
                dead = [one for one in pair if one not in live]
                chosen = None
                for bit in range(len(pair)):
                    test = alive[bit] if case >> bit & 1 else jnp.logical_not(alive[bit])
                    chosen = test if chosen is None else chosen & test

                @pl.when(chosen)
                def _(items=items, live=live, dead=dead, length=length):
                    attend(items, live, dead, length)


def three_windows(padded, columns):
    return jnp.concatenate(
        [padded[RIM - 1 + shift : RIM - 1 + shift + columns].astype(jnp.bfloat16) for shift in range(3)],
        axis=1,
    )


def around(odd, near, far):
    return jnp.where(odd == 1, near, far), jnp.where(odd == 1, far, near)


def turn_kernel(index_ref, cot_ref, near_ref, far_ref, out_ref):
    regions, rows, columns, width = cot_ref.shape
    for region in range(regions):
        before, after = around(lax.rem(index_ref[0], 2), near_ref[region], far_ref[region])
        for row in range(-1, rows + 1):
            value = before if row < 0 else after if row == rows else cot_ref[region, row]
            turned = value.T
            for down in range(3):
                image_row = row - 1 + down
                if 0 <= image_row < rows:
                    start = (region * rows + image_row) * columns
                    out_ref[down * width : (down + 1) * width, start : start + columns] = turned


def norm_kernel(chunk_rows, lengths_ref, index_ref, gain_ref, turned_ref, *refs):
    image_ref, near_ref, far_ref, grad_ref, attended, pixels, windows, grads = refs[-8:]
    for distance, ref in enumerate(refs[:-8]):
        attended[lax.bitwise_xor(index_ref[0], distance)] = ref[...]
    heads = gain_ref.shape[0]
    regions = image_ref.shape[0]
    _, per_device, tokens, width = attended.shape

    def load(head, region):
        owner, place = divmod(head * regions + region, per_device)
        return attended[owner, place].astype(jnp.float32)

    columns = tokens * PATCH
    features = heads * width
    odd = lax.rem(index_ref[0], 2)
    position = index_ref[0] * tokens + lax.broadcasted_iota(jnp.int32, (tokens, 1), 0)
    pixels[:, :, :RIM, :] = jnp.zeros((regions, PATCH, RIM, width), jnp.float32)
    pixels[:, :, RIM + columns :, :] = jnp.zeros((regions, PATCH, RIM, width), jnp.float32)
    for region in range(regions):
        total = jnp.zeros((tokens, width), jnp.float32)
        for head in range(heads):
            total = total + load(head, region)
        mean = jnp.sum(total, axis=1, keepdims=True) * (1.0 / features)
        total = jnp.zeros((tokens, width), jnp.float32)
        for head in range(heads):
            centered = load(head, region) - mean
            total = total + centered * centered
        variance = jnp.sum(total, axis=1, keepdims=True) * (1.0 / features)
        spread = lax.rsqrt(variance + 1e-05)
        live = position < lengths_ref[region]
        for head in range(heads):
            centered = load(head, region) - mean
            normed = jnp.where(live, centered * spread * gain_ref[head : head + 1, :], 0.0)
            row, column = divmod(head, PATCH)
            pixels[region, row, pl.ds(RIM + column, tokens, stride=PATCH), :] = normed
        for row in range(PATCH):
            window = three_windows(pixels[region, row], columns)
            image_ref[region, row] = window[:, width : 2 * width]
            start = (region * PATCH + row) * columns
            windows[start : start + columns, :] = window
        near_ref[region] = image_ref[region, (1 - odd) * (PATCH - 1)]
        far_ref[region] = image_ref[region, odd * (PATCH - 1)]
        part = slice(region * PATCH * columns, (region + 1) * PATCH * columns)
        term = jnp.dot(turned_ref[:, part], windows[part, :], preferred_element_type=jnp.float32)
        product = term if region == 0 else product + term
    for down in range(3):
        for across in range(3):
            tap = 3 * down + across
            grads[tap * width : (tap + 1) * width, :] = product[
                down * width : (down + 1) * width, across * width : (across + 1) * width
            ].T
    filled = 9 * width
    if filled < grads.shape[0]:
        grads[filled:, :] = jnp.zeros((grads.shape[0] - filled, width), jnp.float32)
    for chunk in range(grad_ref.shape[0]):
        grad_ref[chunk] = grads[chunk * chunk_rows : (chunk + 1) * chunk_rows, :].astype(jnp.bfloat16)


def decode_kernel(index_ref, image_ref, near_ref, far_ref, weight_ref, out_ref, done_ref, padded):
    done_ref[...] = jnp.zeros(done_ref.shape, jnp.float32)
    regions, rows, columns, width = image_ref.shape
    padded[:RIM, :] = jnp.zeros((RIM, width), jnp.float32)
    padded[RIM + columns :, :] = jnp.zeros((RIM, width), jnp.float32)
    for region in range(regions):
        strips = []
        before, after = around(lax.rem(index_ref[0], 2), near_ref[region], far_ref[region])
        for row in range(-1, rows + 1):
            if row < 0:
                source = before
            elif row == rows:
                source = after
            else:
                source = image_ref[region, row]
            padded[RIM : RIM + columns, :] = source.astype(jnp.float32)
            strips.append(three_windows(padded[...], columns))
            if len(strips) == 3:
                total = jnp.dot(strips[0], weight_ref[0], preferred_element_type=jnp.float32)
                for down in (1, 2):
                    total = total + jnp.dot(
                        strips[down], weight_ref[down], preferred_element_type=jnp.float32
                    )
                out_ref[region, row - 1] = total.astype(jnp.bfloat16)
                strips.pop(0)


def sum_kernel(count, factor, *refs):
    out_ref = refs[-1]
    totals = [ref[...].astype(jnp.float32) for ref in refs[:count]]
    if count == 1:
        totals = [totals[0][part] for part in range(totals[0].shape[0])]
    while len(totals) > 1:
        paired = [one + other for one, other in zip(totals[::2], totals[1::2])]
        totals = paired + totals[2 * len(paired) :]
    out_ref[...] = (totals[0] * factor).astype(jnp.bfloat16)


def spread_kernel(plane_ref, *refs):
    out_ref = refs[-1]
    chunk_rows = refs[0].shape[0]
    for distance, ref in enumerate(refs[:-1]):
        start = lax.bitwise_xor(plane_ref[0], distance) * chunk_rows
        rows = pl.ds(pl.multiple_of(start, chunk_rows), chunk_rows)
        out_ref[rows, :] = ref[...].astype(jnp.float32)


def trade(values, distance):
    pairs = [(i, i ^ distance) for i in range(lax.axis_size("seq"))]
    return lax.ppermute(values, "seq", pairs)


def inner_size(seq_count):
    inner = 1
    while seq_count % (2 * inner) == 0 and (2 * inner) ** 2 <= seq_count:
        inner *= 2
    return inner


def planes_of(inner):
    outer, seq_count = (lax.axis_size("dp"), lax.axis_size("seq"))
    return [
        [o * seq_count + start + lane for o in range(outer) for lane in range(inner)]
        for start in range(0, seq_count, inner)
    ]


def trade_in_plane(values, distance, inner):
    seq_count = lax.axis_size("seq")
    pairs = []
    for outer in range(lax.axis_size("dp")):
        for seq in range(seq_count):
            partner, lane = divmod((outer * inner + seq % inner) ^ distance, inner)
            pairs.append((outer * seq_count + seq, partner * seq_count + seq - seq % inner + lane))
    return lax.ppermute(values, ("dp", "seq"), pairs)


def body(query_rows, key_rows, value_rows, region_lengths, norm_gain, conv_weight, cotangent):
    tokens, regions, model_width = query_rows.shape
    width = model_width // HEADS
    seq_count = lax.axis_size("seq")
    seq_index = lax.axis_index("seq")
    inner = inner_size(seq_count)
    plane_size = lax.axis_size("dp") * inner
    plane_index = lax.axis_index("dp") * inner + lax.bitwise_and(seq_index, inner - 1)
    columns = tokens * PATCH
    capacity = seq_count * tokens
    per_device = regions * HEADS // seq_count
    far_pairs = [(i, i + 1) for i in range(1, seq_count - 1, 2)]
    far_pairs = far_pairs + [(j, i) for i, j in far_pairs]
    local_bytes = 2 * query_rows.size

    edge_shape = jax.ShapeDtypeStruct((regions, columns, width), jnp.bfloat16)
    chunk_shape = jax.ShapeDtypeStruct((3, per_device, tokens, width), jnp.bfloat16)
    index = seq_index.reshape(1)
    *leaving, cot_near, cot_far = call(
        functools.partial(pack_kernel, regions, per_device),
        "pack",
        [chunk_shape] * (seq_count - 1) + [edge_shape] * 2,
        [SMEM()] + [HBM()] * 4,
        out_specs=[HBM()] * (seq_count + 1),
        scratch=[
            pltpu.VMEM((3,) + query_rows.shape, jnp.bfloat16),
            pltpu.VMEM((seq_count - 1,) + chunk_shape.shape, jnp.bfloat16),
            pltpu.VMEM((2,) + edge_shape.shape, jnp.bfloat16),
            pltpu.SemaphoreType.DMA((7 + 3 * (seq_count - 1),)),
        ],
        moved=6 * local_bytes,
        grant=VMEM_WHOLE,
    )(index, query_rows, key_rows, value_rows, cotangent)
    order = list(range(1, seq_count)) + [0]
    packed = [trade(chunk, distance) for distance, chunk in zip(order, leaving)]
    own = call(
        functools.partial(own_kernel, regions, per_device),
        "own_chunk",
        chunk_shape,
        [SMEM()] + [HBM()] * 3,
        scratch=[
            pltpu.VMEM((3, tokens, regions, max(1, per_device // regions) * width), jnp.bfloat16),
            pltpu.SemaphoreType.DMA((3,)),
        ],
        moved=12 * chunk_shape.size,
    )(index, query_rows, key_rows, value_rows)
    cot_near = trade(cot_near, 1)
    cot_far = lax.ppermute(cot_far, "seq", far_pairs)

    items = seq_index * per_device + jnp.arange(per_device, dtype=jnp.int32)
    item_lengths = jnp.sum(
        jnp.where(
            (items % regions)[:, None] == jnp.arange(regions, dtype=jnp.int32)[None, :],
            region_lengths[None, :],
            0,
        ),
        axis=1,
    )
    block_rows = min(256, capacity)
    group = regions if per_device % regions == 0 else per_device
    mixed = call(
        functools.partial(attend_kernel, block_rows, group, order),
        "attend",
        [jax.ShapeDtypeStruct((per_device, tokens, width), jnp.bfloat16)] * seq_count,
        [SMEM(), SMEM()] + [VMEM()] * seq_count,
        flops=4 * per_device * capacity * capacity * width,
        moved=4 * local_bytes,
        exps=per_device * capacity * capacity,
    )(index, item_lengths, *packed, own)
    attended = [mixed[0]] + [trade(mixed[distance], distance) for distance in order[:-1]]

    turned = call(
        turn_kernel,
        "turn_cotangent",
        jax.ShapeDtypeStruct((3 * width, cotangent.size // width), jnp.bfloat16),
        [SMEM()] + [VMEM()] * 3,
        moved=8 * cotangent.size,
    )(index, cotangent, cot_near, cot_far)
    chunk_rows = -(-9 * width // (16 * plane_size)) * 16
    pixel_rows = regions * PATCH * columns
    conv_flops = 18 * pixel_rows * width * width
    part_shape = jax.ShapeDtypeStruct((chunk_rows, width), jnp.bfloat16)
    image, near, far, parts = call(
        functools.partial(norm_kernel, chunk_rows),
        "norm_and_gradient",
        [jax.ShapeDtypeStruct((regions, PATCH, columns, width), jnp.bfloat16)]
        + [edge_shape] * 2
        + [jax.ShapeDtypeStruct((plane_size, chunk_rows, width), jnp.bfloat16)],
        [SMEM(), SMEM()] + [VMEM()] * (2 + seq_count),
        scratch=[
            pltpu.VMEM((seq_count,) + mixed[0].shape, jnp.bfloat16),
            pltpu.VMEM((regions, PATCH, columns + 2 * RIM, width), jnp.float32),
            pltpu.VMEM((pixel_rows, 3 * width), jnp.bfloat16),
            pltpu.VMEM((plane_size * chunk_rows, width), jnp.float32),
        ],
        flops=conv_flops,
        moved=4 * local_bytes,
    )(region_lengths, index, norm_gain.reshape(HEADS, width), turned, *attended)
    parts = lax.all_to_all(
        parts, ("dp", "seq"), 0, 0, axis_index_groups=planes_of(inner), tiled=True
    )
    near = trade(near, 1)
    far = lax.ppermute(far, "seq", far_pairs)
    plane_sum = call(
        functools.partial(sum_kernel, 1, 1.0),
        "sum_plane",
        part_shape,
        [VMEM()],
        moved=4 * parts.size,
    )(parts)
    plane_sums = [plane_sum] + [
        trade(plane_sum, distance) for distance in range(inner, seq_count, inner)
    ]
    decoded, done = call(
        decode_kernel,
        "decode",
        [
            jax.ShapeDtypeStruct(cotangent.shape, jnp.bfloat16),
            jax.ShapeDtypeStruct((8, width), jnp.float32),
        ],
        [SMEM()] + [VMEM()] * 4,
        scratch=[pltpu.VMEM((columns + 2 * RIM, width), jnp.float32)],
        flops=conv_flops,
        moved=2 * local_bytes,
    )(index, image, near, far, conv_weight.reshape(3, 3 * width, width))
    total = call(
        functools.partial(sum_kernel, len(plane_sums), 1.0 / math.sqrt(PATCH * columns)),
        "sum_planes",
        part_shape,
        [VMEM()] * len(plane_sums) + [ANY()],
        moved=4 * len(plane_sums) * chunk_rows * width,
    )(*plane_sums, done)
    totals = [total] + [trade_in_plane(total, distance, inner) for distance in range(1, plane_size)]
    weight_grad = call(
        spread_kernel,
        "spread_sums",
        jax.ShapeDtypeStruct((plane_size * chunk_rows, width), jnp.float32),
        [SMEM()] + [VMEM()] * plane_size,
        moved=6 * plane_size * chunk_rows * width,
    )(plane_index.reshape(1), *totals)
    return (decoded, weight_grad[: 9 * width].reshape(conv_weight.shape))


def solution(mesh):
    placed = (
        P("seq", "dp", None),
        P("seq", "dp", None),
        P("seq", "dp", None),
        P("dp"),
        P(),
        P(),
        P("dp", "seq", None, None),
    )
    return jax.shard_map(
        body,
        mesh=mesh,
        in_specs=placed,
        out_specs=(P("dp", "seq", None, None), P()),
        check_vma=False,
    )
```

```python
import functools
import math

import jax
import jax.numpy as jnp
from jax import lax
from jax.experimental import pallas as pl
from jax.experimental.pallas import tpu as pltpu
from jax.sharding import PartitionSpec as P

HEADS = 16
PATCH = 4
RIM = 8
VMEM_LIMIT = 48 * 1024 * 1024
VMEM_WHOLE = 60 * 1024 * 1024

VMEM = functools.partial(pl.BlockSpec, memory_space=pltpu.VMEM)
HBM = functools.partial(pl.BlockSpec, memory_space=pltpu.HBM)
ANY = functools.partial(pl.BlockSpec, memory_space=pl.ANY)
SMEM = functools.partial(pl.BlockSpec, memory_space=pltpu.SMEM)


def call(kernel, name, out_shape, in_specs, out_specs=None, scratch=(), flops=0, moved=0, exps=0, grant=VMEM_LIMIT):
    many = isinstance(out_shape, (list, tuple))
    return pl.pallas_call(
        kernel,
        out_shape=out_shape,
        in_specs=in_specs,
        out_specs=out_specs or ([VMEM() for _ in out_shape] if many else VMEM()),
        scratch_shapes=list(scratch),
        compiler_params=pltpu.CompilerParams(vmem_limit_bytes=grant),
        cost_estimate=pl.CostEstimate(flops=flops, bytes_accessed=moved, transcendentals=exps),
        name=name,
    )


def unpack_items(held, which, regions, per_device, owner):
    width = held.shape[3] // HEADS
    aligned = per_device % regions == 0
    items = []
    for place in range(per_device):
        if aligned and place % regions:
            region = place % regions
        else:
            item = owner * per_device + place
            head = lax.div(item, regions)
            region = 0 if aligned else lax.rem(item, regions)
            start = pl.multiple_of(head * width, width)
            block = held[which, :, :, pl.ds(start, width)].astype(jnp.float32)
        value = block[:, 0, :]
        for other in range(1, regions):
            if aligned:
                value = block[:, other, :] if region == other else value
            else:
                value = jnp.where(region == other, block[:, other, :], value)
        items.append(value.astype(jnp.bfloat16))
    return items


def pack_kernel(
    regions, per_device, index_ref, query_ref, key_ref, value_ref, cot_ref, *refs
):
    held, ready, edges, sems = refs[-4:]
    edge_refs = refs[-6:-4]
    out_refs = refs[:-6]
    rows = cot_ref.shape[1]
    loads = [
        pltpu.make_async_copy(ref, held.at[which], sems.at[which])
        for which, ref in enumerate((query_ref, key_ref, value_ref))
    ]
    odd = lax.rem(index_ref[0], 2)
    for edge, row in enumerate(((1 - odd) * (rows - 1), odd * (rows - 1))):
        loads.append(pltpu.make_async_copy(cot_ref.at[:, row], edges.at[edge], sems.at[3 + edge]))
    for load in loads:
        load.start()
    stores = []
    for which in range(3):
        loads[which].wait()
        for number, ref in enumerate(out_refs):
            owner = lax.bitwise_xor(index_ref[0], number + 1)
            for place, value in enumerate(unpack_items(held, which, regions, per_device, owner)):
                ready[number, which, place] = value
            stores.append(
                pltpu.make_async_copy(
                    ready.at[number, which], ref.at[which], sems.at[7 + 3 * number + which]
                )
            )
            stores[-1].start()
        if which == 0:
            for edge, ref in enumerate(edge_refs):
                loads[3 + edge].wait()
                stores.append(pltpu.make_async_copy(edges.at[edge], ref, sems.at[5 + edge]))
                stores[-1].start()
    for store in stores:
        store.wait()


def own_kernel(regions, per_device, index_ref, query_ref, key_ref, value_ref, out_ref, held, sems):
    tokens, width = out_ref.shape[2:]
    span = max(1, per_device // regions) * width
    index = index_ref[0]
    start = lax.div(index * per_device, regions) * width
    loads = []
    for which, ref in enumerate((query_ref, key_ref, value_ref)):
        columns = pl.ds(pl.multiple_of(start, width), span)
        loads.append(
            pltpu.make_async_copy(ref.at[:, :, columns], held.at[which], sems.at[which])
        )
        loads[-1].start()
    for which, load in enumerate(loads):
        load.wait()
        for head in range(span // width):
            block = held[which, :, :, head * width : (head + 1) * width].astype(jnp.float32)
            if per_device % regions:
                value = block[:, 0, :]
                for other in range(1, regions):
                    value = jnp.where(lax.rem(index, regions) == other, block[:, other, :], value)
                out_ref[which, head] = value.astype(jnp.bfloat16)
            else:
                for region in range(regions):
                    out_ref[which, head * regions + region] = block[:, region, :].astype(
                        jnp.bfloat16
                    )


def attend_kernel(block_rows, group, order, index_ref, lengths_ref, *refs):
    chunks = dict(zip(order, refs))
    out_refs = refs[len(order) :]
    index = index_ref[0]
    sources = len(chunks)
    _, per_device, tokens, width = chunks[0].shape
    capacity = sources * tokens
    per_block = block_rows // tokens
    blocks = capacity // block_rows
    factor = math.log2(math.e) / math.sqrt(width)
    columns = lax.broadcasted_iota(jnp.int32, (1, capacity), 1)
    slots = columns
    for distance in range(sources):
        here = (columns >= distance * tokens) & (columns < (distance + 1) * tokens)
        moved = (lax.bitwise_xor(index, distance) - distance) * tokens
        slots = jnp.where(here, columns + moved, slots)

    def rows_of(which, item, distances):
        return jnp.concatenate([chunks[distance][which, item] for distance in distances], axis=0)

    def distances_of(block):
        return range(block * per_block, (block + 1) * per_block)

    def start_of(block, span):
        return lax.bitwise_xor(lax.div(index, span), block) * span

    def clear(item, block):
        for distance in distances_of(block):
            out_refs[distance][item] = jnp.zeros((tokens, width), jnp.bfloat16)

    def score(item, block):
        return lax.dot_general(
            rows_of(0, item, distances_of(block)),
            rows_of(1, item, range(sources)),
            (((1,), (1,)), ((), ())),
            preferred_element_type=jnp.float32,
        )

    def finish(item, block, scores, key_valid):
        scores = jnp.where(key_valid, scores * factor, -1e30)
        powers = jnp.exp2(scores - jnp.max(scores, axis=1, keepdims=True))
        totals = jnp.sum(powers, axis=1, keepdims=True)
        mixed = jnp.dot(
            powers.astype(jnp.bfloat16),
            rows_of(2, item, range(sources)),
            preferred_element_type=jnp.float32,
        )
        mixed = (mixed / totals).astype(jnp.bfloat16)
        for number, distance in enumerate(distances_of(block)):
            out_refs[distance][item] = mixed[number * tokens : (number + 1) * tokens]

    def attend(items, live, dead, length):
        key_valid = slots < length
        waiting = None
        for block in live:
            for item in items:
                scores = score(item, block)
                if waiting is not None:
                    finish(*waiting, key_valid)
                waiting = (item, block, scores)
        if waiting is not None:
            finish(*waiting, key_valid)
        for block in dead:
            for item in items:
                clear(item, block)

    for lead in range(group):
        length = lengths_ref[lead]
        items = list(range(lead, per_device, group))
        for block in range(0, blocks, 2):
            pair = list(range(block, min(block + 2, blocks)))
            alive = [length > start_of(one, per_block) * tokens for one in pair]
            for case in range(2 ** len(pair)):
                live = [one for bit, one in enumerate(pair) if case >> bit & 1]
                dead = [one for one in pair if one not in live]
                chosen = None
                for bit in range(len(pair)):
                    test = alive[bit] if case >> bit & 1 else jnp.logical_not(alive[bit])
                    chosen = test if chosen is None else chosen & test

                @pl.when(chosen)
                def _(items=items, live=live, dead=dead, length=length):
                    attend(items, live, dead, length)


def three_windows(padded, columns):
    return jnp.concatenate(
        [padded[RIM - 1 + shift : RIM - 1 + shift + columns].astype(jnp.bfloat16) for shift in range(3)],
        axis=1,
    )


def rows_at(place, rows):
    return pl.ds(pl.multiple_of(place * rows, rows), rows)


def around(odd, near, far):
    return jnp.where(odd == 1, near, far), jnp.where(odd == 1, far, near)


def turn_kernel(index_ref, cot_ref, near_ref, far_ref, out_ref):
    regions, rows, columns, width = cot_ref.shape
    for region in range(regions):
        before, after = around(lax.rem(index_ref[0], 2), near_ref[region], far_ref[region])
        for row in range(-1, rows + 1):
            value = before if row < 0 else after if row == rows else cot_ref[region, row]
            turned = value.T
            for down in range(3):
                image_row = row - 1 + down
                if 0 <= image_row < rows:
                    start = (region * rows + image_row) * columns
                    out_ref[down * width : (down + 1) * width, start : start + columns] = turned


def norm_kernel(lengths_ref, index_ref, quad_ref, gain_ref, turned_ref, *refs):
    attended, pixels, windows, grads = refs[-4:]
    sources = attended.shape[0]
    image_ref, near_ref, far_ref = refs[sources : sources + 3]
    grad_refs = refs[sources + 3 : -4]
    for distance, ref in enumerate(refs[:sources]):
        attended[lax.bitwise_xor(index_ref[0], distance)] = ref[...]
    heads = gain_ref.shape[0]
    regions = image_ref.shape[0]
    _, per_device, tokens, width = attended.shape

    def load(head, region):
        owner, place = divmod(head * regions + region, per_device)
        return attended[owner, place].astype(jnp.float32)

    columns = tokens * PATCH
    features = heads * width
    odd = lax.rem(index_ref[0], 2)
    position = index_ref[0] * tokens + lax.broadcasted_iota(jnp.int32, (tokens, 1), 0)
    pixels[:, :, :RIM, :] = jnp.zeros((regions, PATCH, RIM, width), jnp.float32)
    pixels[:, :, RIM + columns :, :] = jnp.zeros((regions, PATCH, RIM, width), jnp.float32)
    for region in range(regions):
        total = jnp.zeros((tokens, width), jnp.float32)
        for head in range(heads):
            total = total + load(head, region)
        mean = jnp.sum(total, axis=1, keepdims=True) * (1.0 / features)
        total = jnp.zeros((tokens, width), jnp.float32)
        for head in range(heads):
            centered = load(head, region) - mean
            total = total + centered * centered
        variance = jnp.sum(total, axis=1, keepdims=True) * (1.0 / features)
        spread = lax.rsqrt(variance + 1e-05)
        live = position < lengths_ref[region]
        for head in range(heads):
            centered = load(head, region) - mean
            normed = jnp.where(live, centered * spread * gain_ref[head : head + 1, :], 0.0)
            row, column = divmod(head, PATCH)
            pixels[region, row, pl.ds(RIM + column, tokens, stride=PATCH), :] = normed
        for row in range(PATCH):
            window = three_windows(pixels[region, row], columns)
            image_ref[region, row] = window[:, width : 2 * width]
            start = (region * PATCH + row) * columns
            windows[start : start + columns, :] = window
        near_ref[region] = image_ref[region, (1 - odd) * (PATCH - 1)]
        far_ref[region] = image_ref[region, odd * (PATCH - 1)]
        part = slice(region * PATCH * columns, (region + 1) * PATCH * columns)
        term = jnp.dot(turned_ref[:, part], windows[part, :], preferred_element_type=jnp.float32)
        product = term if region == 0 else product + term
    for down in range(3):
        for across in range(3):
            tap = 3 * down + across
            grads[tap * width : (tap + 1) * width, :] = product[
                down * width : (down + 1) * width, across * width : (across + 1) * width
            ].T
    filled = 9 * width
    if filled < grads.shape[0]:
        grads[filled:, :] = jnp.zeros((grads.shape[0] - filled, width), jnp.float32)
    for distance, ref in enumerate(grad_refs):
        rows = rows_at(lax.bitwise_xor(quad_ref[0], distance), ref.shape[0])
        ref[...] = grads[rows, :].astype(jnp.bfloat16)


def decode_kernel(index_ref, image_ref, near_ref, far_ref, weight_ref, out_ref, padded):
    regions, rows, columns, width = image_ref.shape
    padded[:RIM, :] = jnp.zeros((RIM, width), jnp.float32)
    padded[RIM + columns :, :] = jnp.zeros((RIM, width), jnp.float32)
    for region in range(regions):
        strips = []
        before, after = around(lax.rem(index_ref[0], 2), near_ref[region], far_ref[region])
        for row in range(-1, rows + 1):
            if row < 0:
                source = before
            elif row == rows:
                source = after
            else:
                source = image_ref[region, row]
            padded[RIM : RIM + columns, :] = source.astype(jnp.float32)
            strips.append(three_windows(padded[...], columns))
            if len(strips) == 3:
                total = jnp.dot(strips[0], weight_ref[0], preferred_element_type=jnp.float32)
                for down in (1, 2):
                    total = total + jnp.dot(
                        strips[down], weight_ref[down], preferred_element_type=jnp.float32
                    )
                out_ref[region, row - 1] = total.astype(jnp.bfloat16)
                strips.pop(0)


def add_pairs(terms):
    while len(terms) > 1:
        paired = [one + other for one, other in zip(terms[::2], terms[1::2])]
        terms = paired + terms[2 * len(paired) :]
    return terms[0]


def sum_chips_kernel(core_ref, near_ref, far_ref, *refs):
    keep_ref, send_ref, near_out_ref, far_out_ref, total = refs[-5:]
    total[...] = add_pairs([ref[...].astype(jnp.float32) for ref in refs[:-5]])
    half = keep_ref.shape[0]
    keep_ref[...] = total[rows_at(core_ref[0], half), :]
    send_ref[...] = total[rows_at(1 - core_ref[0], half), :]
    near_out_ref[...] = near_ref[...]
    far_out_ref[...] = far_ref[...]


def sum_kernel(count, factor, *refs):
    total = add_pairs([ref[...].astype(jnp.float32) for ref in refs[:count]])
    refs[-1][...] = (total * factor).astype(jnp.bfloat16)


def join_kernel(core_ref, own_ref, other_ref, out_ref):
    half = own_ref.shape[0]
    out_ref[rows_at(core_ref[0], half), :] = own_ref[...]
    out_ref[rows_at(1 - core_ref[0], half), :] = other_ref[...]


def spread_kernel(quad_ref, *refs):
    out_ref = refs[-1]
    for distance, ref in enumerate(refs[:-1]):
        rows = rows_at(lax.bitwise_xor(quad_ref[0], distance), ref.shape[0])
        out_ref[rows, :] = ref[...].astype(jnp.float32)


def trade(values, distance):
    pairs = [(i, i ^ distance) for i in range(lax.axis_size("seq"))]
    return lax.ppermute(values, "seq", pairs)


def inner_size(seq_count):
    inner = 1
    while seq_count % (2 * inner) == 0 and (2 * inner) ** 2 <= seq_count:
        inner *= 2
    return inner


def trade_chips(values, distance, inner):
    seq_count = lax.axis_size("seq")
    pairs = []
    for outer in range(lax.axis_size("dp")):
        for seq in range(seq_count):
            chip, lane = divmod((outer // 2 * inner + seq % inner) ^ distance, inner)
            partner = (2 * chip + outer % 2) * seq_count + seq - seq % inner + lane
            pairs.append((outer * seq_count + seq, partner))
    return lax.ppermute(values, ("dp", "seq"), pairs)


def trade_cores(values):
    return lax.ppermute(values, "dp", [(i, i ^ 1) for i in range(lax.axis_size("dp"))])


def body(query_rows, key_rows, value_rows, region_lengths, norm_gain, conv_weight, cotangent):
    tokens, regions, model_width = query_rows.shape
    width = model_width // HEADS
    seq_count = lax.axis_size("seq")
    seq_index = lax.axis_index("seq")
    inner = inner_size(seq_count)
    quad_size = lax.axis_size("dp") // 2 * inner
    dp_index = lax.axis_index("dp")
    lane = lax.bitwise_and(seq_index, inner - 1)
    quad = (lax.shift_right_logical(dp_index, 1) * inner + lane).reshape(1)
    core = lax.bitwise_and(dp_index, 1).reshape(1)
    columns = tokens * PATCH
    capacity = seq_count * tokens
    per_device = regions * HEADS // seq_count
    far_pairs = [(i, i + 1) for i in range(1, seq_count - 1, 2)]
    far_pairs = far_pairs + [(j, i) for i, j in far_pairs]
    local_bytes = 2 * query_rows.size

    edge_shape = jax.ShapeDtypeStruct((regions, columns, width), jnp.bfloat16)
    chunk_shape = jax.ShapeDtypeStruct((3, per_device, tokens, width), jnp.bfloat16)
    index = seq_index.reshape(1)
    *leaving, cot_near, cot_far = call(
        functools.partial(pack_kernel, regions, per_device),
        "pack",
        [chunk_shape] * (seq_count - 1) + [edge_shape] * 2,
        [SMEM()] + [HBM()] * 4,
        out_specs=[HBM()] * (seq_count + 1),
        scratch=[
            pltpu.VMEM((3,) + query_rows.shape, jnp.bfloat16),
            pltpu.VMEM((seq_count - 1,) + chunk_shape.shape, jnp.bfloat16),
            pltpu.VMEM((2,) + edge_shape.shape, jnp.bfloat16),
            pltpu.SemaphoreType.DMA((7 + 3 * (seq_count - 1),)),
        ],
        moved=6 * local_bytes,
        grant=VMEM_WHOLE,
    )(index, query_rows, key_rows, value_rows, cotangent)
    order = list(range(1, seq_count)) + [0]
    packed = [trade(chunk, distance) for distance, chunk in zip(order, leaving)]
    own = call(
        functools.partial(own_kernel, regions, per_device),
        "own_chunk",
        chunk_shape,
        [SMEM()] + [HBM()] * 3,
        scratch=[
            pltpu.VMEM((3, tokens, regions, max(1, per_device // regions) * width), jnp.bfloat16),
            pltpu.SemaphoreType.DMA((3,)),
        ],
        moved=12 * chunk_shape.size,
    )(index, query_rows, key_rows, value_rows)
    cot_near = trade(cot_near, 1)
    cot_far = lax.ppermute(cot_far, "seq", far_pairs)

    items = seq_index * per_device + jnp.arange(per_device, dtype=jnp.int32)
    item_lengths = jnp.sum(
        jnp.where(
            (items % regions)[:, None] == jnp.arange(regions, dtype=jnp.int32)[None, :],
            region_lengths[None, :],
            0,
        ),
        axis=1,
    )
    block_rows = min(256, capacity)
    group = regions if per_device % regions == 0 else per_device
    mixed = call(
        functools.partial(attend_kernel, block_rows, group, order),
        "attend",
        [jax.ShapeDtypeStruct((per_device, tokens, width), jnp.bfloat16)] * seq_count,
        [SMEM(), SMEM()] + [VMEM()] * seq_count,
        flops=4 * per_device * capacity * capacity * width,
        moved=4 * local_bytes,
        exps=per_device * capacity * capacity,
    )(index, item_lengths, *packed, own)
    attended = [mixed[0]] + [trade(mixed[distance], distance) for distance in order[:-1]]

    turned = call(
        turn_kernel,
        "turn_cotangent",
        jax.ShapeDtypeStruct((3 * width, cotangent.size // width), jnp.bfloat16),
        [SMEM()] + [VMEM()] * 3,
        moved=8 * cotangent.size,
    )(index, cotangent, cot_near, cot_far)
    chunk_rows = -(-9 * width // (32 * quad_size)) * 32
    pixel_rows = regions * PATCH * columns
    conv_flops = 18 * pixel_rows * width * width
    chunk_moved = 8 * quad_size * chunk_rows * width
    image, near, far, *parts = call(
        norm_kernel,
        "norm_and_gradient",
        [jax.ShapeDtypeStruct((regions, PATCH, columns, width), jnp.bfloat16)]
        + [edge_shape] * 2
        + [jax.ShapeDtypeStruct((chunk_rows, width), jnp.bfloat16)] * quad_size,
        [SMEM()] * 3 + [VMEM()] * (2 + seq_count),
        scratch=[
            pltpu.VMEM((seq_count,) + mixed[0].shape, jnp.bfloat16),
            pltpu.VMEM((regions, PATCH, columns + 2 * RIM, width), jnp.float32),
            pltpu.VMEM((pixel_rows, 3 * width), jnp.bfloat16),
            pltpu.VMEM((quad_size * chunk_rows, width), jnp.float32),
        ],
        flops=conv_flops,
        moved=4 * local_bytes,
    )(region_lengths, index, quad, norm_gain.reshape(HEADS, width), turned, *attended)
    distances = range(1, quad_size)
    parts[1:] = [trade_chips(parts[distance], distance, inner) for distance in distances]
    half_shape = (chunk_rows // 2, width)
    keep, send, near, far = call(
        sum_chips_kernel,
        "sum_chips",
        [jax.ShapeDtypeStruct(half_shape, jnp.float32)] * 2 + [edge_shape] * 2,
        [SMEM()] + [VMEM()] * (2 + quad_size),
        scratch=[pltpu.VMEM((chunk_rows, width), jnp.float32)],
        moved=chunk_moved,
    )(core, near, far, *parts)
    plane_sum = call(
        functools.partial(sum_kernel, 2, 1.0),
        "sum_cores",
        jax.ShapeDtypeStruct(half_shape, jnp.bfloat16),
        [VMEM()] * 2,
        moved=chunk_moved // quad_size,
    )(keep, trade_cores(send))
    near = trade(near, 1)
    far = lax.ppermute(far, "seq", far_pairs)
    plane_sums = [plane_sum] + [
        trade(plane_sum, distance) for distance in range(inner, seq_count, inner)
    ]
    total = call(
        functools.partial(sum_kernel, len(plane_sums), 1.0 / math.sqrt(PATCH * columns)),
        "sum_planes",
        jax.ShapeDtypeStruct(half_shape, jnp.bfloat16),
        [VMEM()] * len(plane_sums) + [ANY()] * 2,
        moved=chunk_moved // quad_size,
    )(*plane_sums, near, far)
    joined = call(
        join_kernel,
        "join_cores",
        jax.ShapeDtypeStruct((chunk_rows, width), jnp.bfloat16),
        [SMEM()] + [VMEM()] * 2,
        moved=chunk_moved // quad_size,
    )(core, total, trade_cores(total))
    totals = [joined] + [trade_chips(joined, distance, inner) for distance in distances]
    decoded = call(
        decode_kernel,
        "decode",
        jax.ShapeDtypeStruct(cotangent.shape, jnp.bfloat16),
        [SMEM()] + [VMEM()] * 4,
        scratch=[pltpu.VMEM((columns + 2 * RIM, width), jnp.float32)],
        flops=conv_flops,
        moved=2 * local_bytes,
    )(index, image, near, far, conv_weight.reshape(3, 3 * width, width))
    weight_grad = call(
        spread_kernel,
        "spread_sums",
        jax.ShapeDtypeStruct((quad_size * chunk_rows, width), jnp.float32),
        [SMEM()] + [VMEM()] * quad_size,
        moved=chunk_moved,
    )(quad, *totals)
    return (decoded, weight_grad[: 9 * width].reshape(conv_weight.shape))


def solution(mesh):
    placed = (
        P("seq", "dp", None),
        P("seq", "dp", None),
        P("seq", "dp", None),
        P("dp"),
        P(),
        P(),
        P("dp", "seq", None, None),
    )
    return jax.shard_map(
        body,
        mesh=mesh,
        in_specs=placed,
        out_specs=(P("dp", "seq", None, None), P()),
        check_vma=False,
    )
```

```python
import functools
import math

import jax
import jax.numpy as jnp
from jax import lax
from jax.experimental import pallas as pl
from jax.experimental.pallas import tpu as pltpu
from jax.sharding import PartitionSpec as P

HEADS = 16
PATCH = 4
RIM = 8
VMEM_LIMIT = 48 * 1024 * 1024
VMEM_WHOLE = 60 * 1024 * 1024

VMEM = functools.partial(pl.BlockSpec, memory_space=pltpu.VMEM)
HBM = functools.partial(pl.BlockSpec, memory_space=pltpu.HBM)
ANY = functools.partial(pl.BlockSpec, memory_space=pl.ANY)
SMEM = functools.partial(pl.BlockSpec, memory_space=pltpu.SMEM)


def call(kernel, name, out_shape, in_specs, out_specs=None, scratch=(), flops=0, moved=0, exps=0, grant=VMEM_LIMIT):
    many = isinstance(out_shape, (list, tuple))
    return pl.pallas_call(
        kernel,
        out_shape=out_shape,
        in_specs=in_specs,
        out_specs=out_specs or ([VMEM() for _ in out_shape] if many else VMEM()),
        scratch_shapes=list(scratch),
        compiler_params=pltpu.CompilerParams(vmem_limit_bytes=grant),
        cost_estimate=pl.CostEstimate(flops=flops, bytes_accessed=moved, transcendentals=exps),
        name=name,
    )


def unpack_items(held, which, regions, per_device, owner):
    width = held.shape[3] // HEADS
    aligned = per_device % regions == 0
    items = []
    for place in range(per_device):
        if aligned and place % regions:
            region = place % regions
        else:
            item = owner * per_device + place
            head = lax.div(item, regions)
            region = 0 if aligned else lax.rem(item, regions)
            start = pl.multiple_of(head * width, width)
            block = held[which, :, :, pl.ds(start, width)].astype(jnp.float32)
        value = block[:, 0, :]
        for other in range(1, regions):
            if aligned:
                value = block[:, other, :] if region == other else value
            else:
                value = jnp.where(region == other, block[:, other, :], value)
        items.append(value.astype(jnp.bfloat16))
    return items


def pack_kernel(
    regions, per_device, index_ref, query_ref, key_ref, value_ref, cot_ref, *refs
):
    held, ready, edges, sems = refs[-4:]
    edge_refs = refs[-6:-4]
    out_refs = refs[:-6]
    rows = cot_ref.shape[1]
    loads = [
        pltpu.make_async_copy(ref, held.at[which], sems.at[which])
        for which, ref in enumerate((query_ref, key_ref, value_ref))
    ]
    odd = lax.rem(index_ref[0], 2)
    for edge, row in enumerate(((1 - odd) * (rows - 1), odd * (rows - 1))):
        loads.append(pltpu.make_async_copy(cot_ref.at[:, row], edges.at[edge], sems.at[3 + edge]))
    for load in loads:
        load.start()
    stores = []
    for which in range(3):
        loads[which].wait()
        for number, ref in enumerate(out_refs):
            owner = lax.bitwise_xor(index_ref[0], number + 1)
            for place, value in enumerate(unpack_items(held, which, regions, per_device, owner)):
                ready[number, which, place] = value
            stores.append(
                pltpu.make_async_copy(
                    ready.at[number, which], ref.at[which], sems.at[7 + 3 * number + which]
                )
            )
            stores[-1].start()
        if which == 0:
            for edge, ref in enumerate(edge_refs):
                loads[3 + edge].wait()
                stores.append(pltpu.make_async_copy(edges.at[edge], ref, sems.at[5 + edge]))
                stores[-1].start()
    for store in stores:
        store.wait()


def own_kernel(regions, per_device, index_ref, query_ref, key_ref, value_ref, out_ref, held, sems):
    tokens, width = out_ref.shape[2:]
    span = max(1, per_device // regions) * width
    index = index_ref[0]
    start = lax.div(index * per_device, regions) * width
    loads = []
    for which, ref in enumerate((query_ref, key_ref, value_ref)):
        columns = pl.ds(pl.multiple_of(start, width), span)
        loads.append(
            pltpu.make_async_copy(ref.at[:, :, columns], held.at[which], sems.at[which])
        )
        loads[-1].start()
    for which, load in enumerate(loads):
        load.wait()
        for head in range(span // width):
            block = held[which, :, :, head * width : (head + 1) * width].astype(jnp.float32)
            if per_device % regions:
                value = block[:, 0, :]
                for other in range(1, regions):
                    value = jnp.where(lax.rem(index, regions) == other, block[:, other, :], value)
                out_ref[which, head] = value.astype(jnp.bfloat16)
            else:
                for region in range(regions):
                    out_ref[which, head * regions + region] = block[:, region, :].astype(
                        jnp.bfloat16
                    )


def attend_kernel(block_rows, group, order, index_ref, lengths_ref, *refs):
    chunks = dict(zip(order, refs))
    out_refs = refs[len(order) :]
    index = index_ref[0]
    sources = len(chunks)
    _, per_device, tokens, width = chunks[0].shape
    capacity = sources * tokens
    per_block = block_rows // tokens
    blocks = capacity // block_rows
    factor = math.log2(math.e) / math.sqrt(width)
    columns = lax.broadcasted_iota(jnp.int32, (1, capacity), 1)
    slots = columns
    for distance in range(sources):
        here = (columns >= distance * tokens) & (columns < (distance + 1) * tokens)
        moved = (lax.bitwise_xor(index, distance) - distance) * tokens
        slots = jnp.where(here, columns + moved, slots)

    def rows_of(which, item, distances):
        return jnp.concatenate([chunks[distance][which, item] for distance in distances], axis=0)

    def distances_of(block):
        return range(block * per_block, (block + 1) * per_block)

    def start_of(block, span):
        return lax.bitwise_xor(lax.div(index, span), block) * span

    def clear(item, block):
        for distance in distances_of(block):
            out_refs[distance][item] = jnp.zeros((tokens, width), jnp.bfloat16)

    def score(item, block):
        return lax.dot_general(
            rows_of(0, item, distances_of(block)),
            rows_of(1, item, range(sources)),
            (((1,), (1,)), ((), ())),
            preferred_element_type=jnp.float32,
        )

    def finish(item, block, scores, key_valid):
        scores = jnp.where(key_valid, scores * factor, -1e30)
        powers = jnp.exp2(scores - jnp.max(scores, axis=1, keepdims=True))
        totals = jnp.sum(powers, axis=1, keepdims=True)
        mixed = jnp.dot(
            powers.astype(jnp.bfloat16),
            rows_of(2, item, range(sources)),
            preferred_element_type=jnp.float32,
        )
        mixed = (mixed / totals).astype(jnp.bfloat16)
        for number, distance in enumerate(distances_of(block)):
            out_refs[distance][item] = mixed[number * tokens : (number + 1) * tokens]

    def attend(items, live, dead, length):
        key_valid = slots < length
        waiting = None
        for block in live:
            for item in items:
                scores = score(item, block)
                if waiting is not None:
                    finish(*waiting, key_valid)
                waiting = (item, block, scores)
        if waiting is not None:
            finish(*waiting, key_valid)
        for block in dead:
            for item in items:
                clear(item, block)

    for lead in range(group):
        length = lengths_ref[lead]
        items = list(range(lead, per_device, group))
        for block in range(0, blocks, 2):
            pair = list(range(block, min(block + 2, blocks)))
            alive = [length > start_of(one, per_block) * tokens for one in pair]
            for case in range(2 ** len(pair)):
                live = [one for bit, one in enumerate(pair) if case >> bit & 1]
                dead = [one for one in pair if one not in live]
                chosen = None
                for bit in range(len(pair)):
                    test = alive[bit] if case >> bit & 1 else jnp.logical_not(alive[bit])
                    chosen = test if chosen is None else chosen & test

                @pl.when(chosen)
                def _(items=items, live=live, dead=dead, length=length):
                    attend(items, live, dead, length)


def three_windows(padded, columns):
    return jnp.concatenate(
        [padded[RIM - 1 + shift : RIM - 1 + shift + columns].astype(jnp.bfloat16) for shift in range(3)],
        axis=1,
    )


def rows_at(place, rows):
    return pl.ds(pl.multiple_of(place * rows, rows), rows)


def around(odd, near, far):
    return jnp.where(odd == 1, near, far), jnp.where(odd == 1, far, near)


def turn_kernel(index_ref, cot_ref, near_ref, far_ref, out_ref):
    regions, rows, columns, width = cot_ref.shape
    for region in range(regions):
        before, after = around(lax.rem(index_ref[0], 2), near_ref[region], far_ref[region])
        for row in range(-1, rows + 1):
            value = before if row < 0 else after if row == rows else cot_ref[region, row]
            turned = value.T
            for down in range(3):
                image_row = row - 1 + down
                if 0 <= image_row < rows:
                    start = (region * rows + image_row) * columns
                    out_ref[down * width : (down + 1) * width, start : start + columns] = turned


def norm_kernel(lengths_ref, index_ref, quad_ref, gain_ref, turned_ref, *refs):
    attended, pixels, windows, grads = refs[-4:]
    sources = attended.shape[0]
    image_ref, near_ref, far_ref = refs[sources : sources + 3]
    grad_refs = refs[sources + 3 : -4]
    for distance, ref in enumerate(refs[:sources]):
        attended[lax.bitwise_xor(index_ref[0], distance)] = ref[...]
    heads = gain_ref.shape[0]
    regions = image_ref.shape[0]
    _, per_device, tokens, width = attended.shape

    def load(head, region):
        owner, place = divmod(head * regions + region, per_device)
        return attended[owner, place].astype(jnp.float32)

    columns = tokens * PATCH
    features = heads * width
    odd = lax.rem(index_ref[0], 2)
    position = index_ref[0] * tokens + lax.broadcasted_iota(jnp.int32, (tokens, 1), 0)
    pixels[:, :, :RIM, :] = jnp.zeros((regions, PATCH, RIM, width), jnp.float32)
    pixels[:, :, RIM + columns :, :] = jnp.zeros((regions, PATCH, RIM, width), jnp.float32)
    for region in range(regions):
        total = jnp.zeros((tokens, width), jnp.float32)
        for head in range(heads):
            total = total + load(head, region)
        mean = jnp.sum(total, axis=1, keepdims=True) * (1.0 / features)
        total = jnp.zeros((tokens, width), jnp.float32)
        for head in range(heads):
            centered = load(head, region) - mean
            total = total + centered * centered
        variance = jnp.sum(total, axis=1, keepdims=True) * (1.0 / features)
        spread = lax.rsqrt(variance + 1e-05)
        live = position < lengths_ref[region]
        for head in range(heads):
            centered = load(head, region) - mean
            normed = jnp.where(live, centered * spread * gain_ref[head : head + 1, :], 0.0)
            row, column = divmod(head, PATCH)
            pixels[region, row, pl.ds(RIM + column, tokens, stride=PATCH), :] = normed
        for row in range(PATCH):
            window = three_windows(pixels[region, row], columns)
            image_ref[region, row] = window[:, width : 2 * width]
            start = (region * PATCH + row) * columns
            windows[start : start + columns, :] = window
        near_ref[region] = image_ref[region, (1 - odd) * (PATCH - 1)]
        far_ref[region] = image_ref[region, odd * (PATCH - 1)]
        part = slice(region * PATCH * columns, (region + 1) * PATCH * columns)
        term = jnp.dot(turned_ref[:, part], windows[part, :], preferred_element_type=jnp.float32)
        product = term if region == 0 else product + term
    for down in range(3):
        for across in range(3):
            tap = 3 * down + across
            grads[tap * width : (tap + 1) * width, :] = product[
                down * width : (down + 1) * width, across * width : (across + 1) * width
            ].T
    filled = 9 * width
    if filled < grads.shape[0]:
        grads[filled:, :] = jnp.zeros((grads.shape[0] - filled, width), jnp.float32)
    for distance, ref in enumerate(grad_refs):
        rows = rows_at(lax.bitwise_xor(quad_ref[0], distance), ref.shape[0])
        ref[...] = grads[rows, :].astype(jnp.bfloat16)


def decode_kernel(index_ref, image_ref, near_ref, far_ref, weight_ref, out_ref, padded):
    regions, rows, columns, width = image_ref.shape
    padded[:RIM, :] = jnp.zeros((RIM, width), jnp.float32)
    padded[RIM + columns :, :] = jnp.zeros((RIM, width), jnp.float32)
    for region in range(regions):
        strips = []
        before, after = around(lax.rem(index_ref[0], 2), near_ref[region], far_ref[region])
        for row in range(-1, rows + 1):
            if row < 0:
                source = before
            elif row == rows:
                source = after
            else:
                source = image_ref[region, row]
            padded[RIM : RIM + columns, :] = source.astype(jnp.float32)
            strips.append(three_windows(padded[...], columns))
            if len(strips) == 3:
                total = jnp.dot(strips[0], weight_ref[0], preferred_element_type=jnp.float32)
                for down in (1, 2):
                    total = total + jnp.dot(
                        strips[down], weight_ref[down], preferred_element_type=jnp.float32
                    )
                out_ref[region, row - 1] = total.astype(jnp.bfloat16)
                strips.pop(0)


def add_pairs(terms):
    while len(terms) > 1:
        paired = [one + other for one, other in zip(terms[::2], terms[1::2])]
        terms = paired + terms[2 * len(paired) :]
    return terms[0]


def hold_kernel(value_ref, after_ref, out_ref):
    del after_ref
    out_ref[...] = value_ref[...]


def hold(value, after):
    return call(
        hold_kernel,
        "hold",
        jax.ShapeDtypeStruct(value.shape, value.dtype),
        [VMEM(), ANY()],
        moved=4 * value.size,
    )(value, after)


def sum_chips_kernel(core_ref, *refs):
    keep_ref, send_ref, total = refs[-3:]
    total[...] = add_pairs([ref[...].astype(jnp.float32) for ref in refs[:-3]])
    half = keep_ref.shape[0]
    keep_ref[...] = total[rows_at(core_ref[0], half), :]
    send_ref[...] = total[rows_at(1 - core_ref[0], half), :]


def sum_kernel(count, factor, *refs):
    total = add_pairs([ref[...].astype(jnp.float32) for ref in refs[:count]])
    refs[-1][...] = (total * factor).astype(jnp.bfloat16)


def join_kernel(core_ref, own_ref, other_ref, after_ref, out_ref):
    del after_ref
    half = own_ref.shape[0]
    out_ref[rows_at(core_ref[0], half), :] = own_ref[...]
    out_ref[rows_at(1 - core_ref[0], half), :] = other_ref[...]


def spread_kernel(quad_ref, *refs):
    out_ref = refs[-1]
    for distance, ref in enumerate(refs[:-1]):
        rows = rows_at(lax.bitwise_xor(quad_ref[0], distance), ref.shape[0])
        out_ref[rows, :] = ref[...].astype(jnp.float32)


def trade(values, distance):
    pairs = [(i, i ^ distance) for i in range(lax.axis_size("seq"))]
    return lax.ppermute(values, "seq", pairs)


def inner_size(seq_count):
    inner = 1
    while seq_count % (2 * inner) == 0 and (2 * inner) ** 2 <= seq_count:
        inner *= 2
    return inner


def trade_chips(values, distance, inner):
    seq_count = lax.axis_size("seq")
    pairs = []
    for outer in range(lax.axis_size("dp")):
        for seq in range(seq_count):
            chip, lane = divmod((outer // 2 * inner + seq % inner) ^ distance, inner)
            partner = (2 * chip + outer % 2) * seq_count + seq - seq % inner + lane
            pairs.append((outer * seq_count + seq, partner))
    return lax.ppermute(values, ("dp", "seq"), pairs)


def trade_cores(values):
    return lax.ppermute(values, "dp", [(i, i ^ 1) for i in range(lax.axis_size("dp"))])


def body(query_rows, key_rows, value_rows, region_lengths, norm_gain, conv_weight, cotangent):
    tokens, regions, model_width = query_rows.shape
    width = model_width // HEADS
    seq_count = lax.axis_size("seq")
    seq_index = lax.axis_index("seq")
    inner = inner_size(seq_count)
    quad_size = lax.axis_size("dp") // 2 * inner
    dp_index = lax.axis_index("dp")
    lane = lax.bitwise_and(seq_index, inner - 1)
    quad = (lax.shift_right_logical(dp_index, 1) * inner + lane).reshape(1)
    core = lax.bitwise_and(dp_index, 1).reshape(1)
    columns = tokens * PATCH
    capacity = seq_count * tokens
    per_device = regions * HEADS // seq_count
    far_pairs = [(i, i + 1) for i in range(1, seq_count - 1, 2)]
    far_pairs = far_pairs + [(j, i) for i, j in far_pairs]
    local_bytes = 2 * query_rows.size

    edge_shape = jax.ShapeDtypeStruct((regions, columns, width), jnp.bfloat16)
    chunk_shape = jax.ShapeDtypeStruct((3, per_device, tokens, width), jnp.bfloat16)
    index = seq_index.reshape(1)
    *leaving, cot_near, cot_far = call(
        functools.partial(pack_kernel, regions, per_device),
        "pack",
        [chunk_shape] * (seq_count - 1) + [edge_shape] * 2,
        [SMEM()] + [HBM()] * 4,
        out_specs=[HBM()] * (seq_count + 1),
        scratch=[
            pltpu.VMEM((3,) + query_rows.shape, jnp.bfloat16),
            pltpu.VMEM((seq_count - 1,) + chunk_shape.shape, jnp.bfloat16),
            pltpu.VMEM((2,) + edge_shape.shape, jnp.bfloat16),
            pltpu.SemaphoreType.DMA((7 + 3 * (seq_count - 1),)),
        ],
        moved=6 * local_bytes,
        grant=VMEM_WHOLE,
    )(index, query_rows, key_rows, value_rows, cotangent)
    order = list(range(1, seq_count)) + [0]
    packed = [trade(chunk, distance) for distance, chunk in zip(order, leaving)]
    own = call(
        functools.partial(own_kernel, regions, per_device),
        "own_chunk",
        chunk_shape,
        [SMEM()] + [HBM()] * 3,
        scratch=[
            pltpu.VMEM((3, tokens, regions, max(1, per_device // regions) * width), jnp.bfloat16),
            pltpu.SemaphoreType.DMA((3,)),
        ],
        moved=12 * chunk_shape.size,
    )(index, query_rows, key_rows, value_rows)
    cot_near = trade(cot_near, 1)
    cot_far = lax.ppermute(cot_far, "seq", far_pairs)

    items = seq_index * per_device + jnp.arange(per_device, dtype=jnp.int32)
    item_lengths = jnp.sum(
        jnp.where(
            (items % regions)[:, None] == jnp.arange(regions, dtype=jnp.int32)[None, :],
            region_lengths[None, :],
            0,
        ),
        axis=1,
    )
    block_rows = min(256, capacity)
    group = regions if per_device % regions == 0 else per_device
    mixed = call(
        functools.partial(attend_kernel, block_rows, group, order),
        "attend",
        [jax.ShapeDtypeStruct((per_device, tokens, width), jnp.bfloat16)] * seq_count,
        [SMEM(), SMEM()] + [VMEM()] * seq_count,
        flops=4 * per_device * capacity * capacity * width,
        moved=4 * local_bytes,
        exps=per_device * capacity * capacity,
    )(index, item_lengths, *packed, own)
    attended = [mixed[0]] + [trade(mixed[distance], distance) for distance in order[:-1]]

    turned = call(
        turn_kernel,
        "turn_cotangent",
        jax.ShapeDtypeStruct((3 * width, cotangent.size // width), jnp.bfloat16),
        [SMEM()] + [VMEM()] * 3,
        moved=8 * cotangent.size,
    )(index, cotangent, cot_near, cot_far)
    chunk_rows = -(-9 * width // (32 * quad_size)) * 32
    pixel_rows = regions * PATCH * columns
    conv_flops = 18 * pixel_rows * width * width
    chunk_moved = 8 * quad_size * chunk_rows * width
    image, near, far, *parts = call(
        norm_kernel,
        "norm_and_gradient",
        [jax.ShapeDtypeStruct((regions, PATCH, columns, width), jnp.bfloat16)]
        + [edge_shape] * 2
        + [jax.ShapeDtypeStruct((chunk_rows, width), jnp.bfloat16)] * quad_size,
        [SMEM()] * 3 + [VMEM()] * (2 + seq_count),
        scratch=[
            pltpu.VMEM((seq_count,) + mixed[0].shape, jnp.bfloat16),
            pltpu.VMEM((regions, PATCH, columns + 2 * RIM, width), jnp.float32),
            pltpu.VMEM((pixel_rows, 3 * width), jnp.bfloat16),
            pltpu.VMEM((quad_size * chunk_rows, width), jnp.float32),
        ],
        flops=conv_flops,
        moved=4 * local_bytes,
    )(region_lengths, index, quad, norm_gain.reshape(HEADS, width), turned, *attended)
    distances = range(1, quad_size)
    parts[1:] = [trade_chips(parts[distance], distance, inner) for distance in distances]
    half_shape = (chunk_rows // 2, width)
    near = trade(hold(near, parts[1]), 1)
    keep, send = call(
        sum_chips_kernel,
        "sum_chips",
        [jax.ShapeDtypeStruct(half_shape, jnp.float32)] * 2,
        [SMEM()] + [VMEM()] * quad_size,
        scratch=[pltpu.VMEM((chunk_rows, width), jnp.float32)],
        moved=chunk_moved,
    )(core, *parts)
    plane_sum = call(
        functools.partial(sum_kernel, 2, 1.0),
        "sum_cores",
        jax.ShapeDtypeStruct(half_shape, jnp.bfloat16),
        [VMEM()] * 2,
        moved=chunk_moved // quad_size,
    )(keep, trade_cores(send))
    plane_sums = [plane_sum] + [
        trade(plane_sum, distance) for distance in range(inner, seq_count, inner)
    ]
    far = lax.ppermute(hold(far, plane_sums[-1]), "seq", far_pairs)
    total = call(
        functools.partial(sum_kernel, len(plane_sums), 1.0 / math.sqrt(PATCH * columns)),
        "sum_planes",
        jax.ShapeDtypeStruct(half_shape, jnp.bfloat16),
        [VMEM()] * len(plane_sums) + [ANY()],
        moved=chunk_moved // quad_size,
    )(*plane_sums, near)
    joined = call(
        join_kernel,
        "join_cores",
        jax.ShapeDtypeStruct((chunk_rows, width), jnp.bfloat16),
        [SMEM()] + [VMEM()] * 2 + [ANY()],
        moved=chunk_moved // quad_size,
    )(core, total, trade_cores(total), far)
    totals = [joined] + [trade_chips(joined, distance, inner) for distance in distances]
    decoded = call(
        decode_kernel,
        "decode",
        jax.ShapeDtypeStruct(cotangent.shape, jnp.bfloat16),
        [SMEM()] + [VMEM()] * 4,
        scratch=[pltpu.VMEM((columns + 2 * RIM, width), jnp.float32)],
        flops=conv_flops,
        moved=2 * local_bytes,
    )(index, image, near, far, conv_weight.reshape(3, 3 * width, width))
    weight_grad = call(
        spread_kernel,
        "spread_sums",
        jax.ShapeDtypeStruct((quad_size * chunk_rows, width), jnp.float32),
        [SMEM()] + [VMEM()] * quad_size,
        moved=chunk_moved,
    )(quad, *totals)
    return (decoded, weight_grad[: 9 * width].reshape(conv_weight.shape))


def solution(mesh):
    placed = (
        P("seq", "dp", None),
        P("seq", "dp", None),
        P("seq", "dp", None),
        P("dp"),
        P(),
        P(),
        P("dp", "seq", None, None),
    )
    return jax.shard_map(
        body,
        mesh=mesh,
        in_specs=placed,
        out_specs=(P("dp", "seq", None, None), P()),
        check_vma=False,
    )
```

```python
import functools
import math

import jax
import jax.numpy as jnp
from jax import lax
from jax.experimental import pallas as pl
from jax.experimental.pallas import tpu as pltpu
from jax.sharding import PartitionSpec as P

HEADS = 16
PATCH = 4
RIM = 8
VMEM_LIMIT = 48 * 1024 * 1024
VMEM_WHOLE = 60 * 1024 * 1024

VMEM = functools.partial(pl.BlockSpec, memory_space=pltpu.VMEM)
HBM = functools.partial(pl.BlockSpec, memory_space=pltpu.HBM)
ANY = functools.partial(pl.BlockSpec, memory_space=pl.ANY)
SMEM = functools.partial(pl.BlockSpec, memory_space=pltpu.SMEM)


def call(kernel, name, out_shape, in_specs, out_specs=None, scratch=(), flops=0, moved=0, exps=0, grant=VMEM_LIMIT):
    many = isinstance(out_shape, (list, tuple))
    return pl.pallas_call(
        kernel,
        out_shape=out_shape,
        in_specs=in_specs,
        out_specs=out_specs or ([VMEM() for _ in out_shape] if many else VMEM()),
        scratch_shapes=list(scratch),
        compiler_params=pltpu.CompilerParams(vmem_limit_bytes=grant),
        cost_estimate=pl.CostEstimate(flops=flops, bytes_accessed=moved, transcendentals=exps),
        name=name,
    )


def unpack_items(held, which, regions, per_device, owner):
    width = held.shape[3] // HEADS
    aligned = per_device % regions == 0
    items = []
    for place in range(per_device):
        if aligned and place % regions:
            region = place % regions
        else:
            item = owner * per_device + place
            head = lax.div(item, regions)
            region = 0 if aligned else lax.rem(item, regions)
            start = pl.multiple_of(head * width, width)
            block = held[which, :, :, pl.ds(start, width)].astype(jnp.float32)
        value = block[:, 0, :]
        for other in range(1, regions):
            if aligned:
                value = block[:, other, :] if region == other else value
            else:
                value = jnp.where(region == other, block[:, other, :], value)
        items.append(value.astype(jnp.bfloat16))
    return items


def pack_kernel(
    regions, per_device, index_ref, query_ref, key_ref, value_ref, cot_ref, *refs
):
    held, ready, edges, sems = refs[-4:]
    edge_refs = refs[-6:-4]
    out_refs = refs[:-6]
    rows = cot_ref.shape[1]
    loads = [
        pltpu.make_async_copy(ref, held.at[which], sems.at[which])
        for which, ref in enumerate((query_ref, key_ref, value_ref))
    ]
    odd = lax.rem(index_ref[0], 2)
    for edge, row in enumerate(((1 - odd) * (rows - 1), odd * (rows - 1))):
        loads.append(pltpu.make_async_copy(cot_ref.at[:, row], edges.at[edge], sems.at[3 + edge]))
    for load in loads:
        load.start()
    stores = []
    for which in range(3):
        loads[which].wait()
        for number, ref in enumerate(out_refs):
            owner = lax.bitwise_xor(index_ref[0], number + 1)
            for place, value in enumerate(unpack_items(held, which, regions, per_device, owner)):
                ready[number, which, place] = value
            stores.append(
                pltpu.make_async_copy(
                    ready.at[number, which], ref.at[which], sems.at[7 + 3 * number + which]
                )
            )
            stores[-1].start()
        if which == 0:
            for edge, ref in enumerate(edge_refs):
                loads[3 + edge].wait()
                stores.append(pltpu.make_async_copy(edges.at[edge], ref, sems.at[5 + edge]))
                stores[-1].start()
    for store in stores:
        store.wait()


def own_kernel(regions, per_device, index_ref, query_ref, key_ref, value_ref, out_ref, held, sems):
    tokens, width = out_ref.shape[2:]
    span = max(1, per_device // regions) * width
    index = index_ref[0]
    start = lax.div(index * per_device, regions) * width
    loads = []
    for which, ref in enumerate((query_ref, key_ref, value_ref)):
        columns = pl.ds(pl.multiple_of(start, width), span)
        loads.append(
            pltpu.make_async_copy(ref.at[:, :, columns], held.at[which], sems.at[which])
        )
        loads[-1].start()
    for which, load in enumerate(loads):
        load.wait()
        for head in range(span // width):
            block = held[which, :, :, head * width : (head + 1) * width].astype(jnp.float32)
            if per_device % regions:
                value = block[:, 0, :]
                for other in range(1, regions):
                    value = jnp.where(lax.rem(index, regions) == other, block[:, other, :], value)
                out_ref[which, head] = value.astype(jnp.bfloat16)
            else:
                for region in range(regions):
                    out_ref[which, head * regions + region] = block[:, region, :].astype(
                        jnp.bfloat16
                    )


def attend_kernel(block_rows, group, order, index_ref, lengths_ref, *refs):
    chunks = dict(zip(order, refs))
    out_refs = refs[len(order) :]
    index = index_ref[0]
    sources = len(chunks)
    _, per_device, tokens, width = chunks[0].shape
    capacity = sources * tokens
    per_block = block_rows // tokens
    blocks = capacity // block_rows
    factor = math.log2(math.e) / math.sqrt(width)
    columns = lax.broadcasted_iota(jnp.int32, (1, capacity), 1)
    slots = columns
    for distance in range(sources):
        here = (columns >= distance * tokens) & (columns < (distance + 1) * tokens)
        moved = (lax.bitwise_xor(index, distance) - distance) * tokens
        slots = jnp.where(here, columns + moved, slots)

    def rows_of(which, item, distances):
        return jnp.concatenate([chunks[distance][which, item] for distance in distances], axis=0)

    def distances_of(block):
        return range(block * per_block, (block + 1) * per_block)

    def start_of(block, span):
        return lax.bitwise_xor(lax.div(index, span), block) * span

    def clear(item, block):
        for distance in distances_of(block):
            out_refs[distance][item] = jnp.zeros((tokens, width), jnp.bfloat16)

    def score(item, block):
        return lax.dot_general(
            rows_of(0, item, distances_of(block)),
            rows_of(1, item, range(sources)),
            (((1,), (1,)), ((), ())),
            preferred_element_type=jnp.float32,
        )

    def finish(item, block, scores, key_valid):
        scores = jnp.where(key_valid, scores * factor, -1e30)
        powers = jnp.exp2(scores - jnp.max(scores, axis=1, keepdims=True))
        totals = jnp.sum(powers, axis=1, keepdims=True)
        mixed = jnp.dot(
            powers.astype(jnp.bfloat16),
            rows_of(2, item, range(sources)),
            preferred_element_type=jnp.float32,
        )
        mixed = (mixed / totals).astype(jnp.bfloat16)
        for number, distance in enumerate(distances_of(block)):
            out_refs[distance][item] = mixed[number * tokens : (number + 1) * tokens]

    def attend(items, live, dead, length):
        key_valid = slots < length
        waiting = None
        for block in live:
            for item in items:
                scores = score(item, block)
                if waiting is not None:
                    finish(*waiting, key_valid)
                waiting = (item, block, scores)
        if waiting is not None:
            finish(*waiting, key_valid)
        for block in dead:
            for item in items:
                clear(item, block)

    for lead in range(group):
        length = lengths_ref[lead]
        items = list(range(lead, per_device, group))
        for block in range(0, blocks, 2):
            pair = list(range(block, min(block + 2, blocks)))
            alive = [length > start_of(one, per_block) * tokens for one in pair]
            for case in range(2 ** len(pair)):
                live = [one for bit, one in enumerate(pair) if case >> bit & 1]
                dead = [one for one in pair if one not in live]
                chosen = None
                for bit in range(len(pair)):
                    test = alive[bit] if case >> bit & 1 else jnp.logical_not(alive[bit])
                    chosen = test if chosen is None else chosen & test

                @pl.when(chosen)
                def _(items=items, live=live, dead=dead, length=length):
                    attend(items, live, dead, length)


def three_windows(padded, columns):
    return jnp.concatenate(
        [padded[RIM - 1 + shift : RIM - 1 + shift + columns].astype(jnp.bfloat16) for shift in range(3)],
        axis=1,
    )


def rows_at(place, rows):
    return pl.ds(pl.multiple_of(place * rows, rows), rows)


def around(odd, near, far):
    return jnp.where(odd == 1, near, far), jnp.where(odd == 1, far, near)


def turn_kernel(index_ref, cot_ref, near_ref, far_ref, out_ref):
    regions, rows, columns, width = cot_ref.shape
    for region in range(regions):
        before, after = around(lax.rem(index_ref[0], 2), near_ref[region], far_ref[region])
        for row in range(-1, rows + 1):
            value = before if row < 0 else after if row == rows else cot_ref[region, row]
            turned = value.T
            for down in range(3):
                image_row = row - 1 + down
                if 0 <= image_row < rows:
                    start = (region * rows + image_row) * columns
                    out_ref[down * width : (down + 1) * width, start : start + columns] = turned


def norm_kernel(lengths_ref, index_ref, core_ref, gain_ref, turned_ref, *refs):
    image_ref, near_ref, far_ref, keep_ref, send_ref, attended, pixels, windows, grads = refs[-9:]
    for distance, ref in enumerate(refs[:-9]):
        attended[lax.bitwise_xor(index_ref[0], distance)] = ref[...]
    heads = gain_ref.shape[0]
    regions = image_ref.shape[0]
    _, per_device, tokens, width = attended.shape

    def load(head, region):
        owner, place = divmod(head * regions + region, per_device)
        return attended[owner, place].astype(jnp.float32)

    columns = tokens * PATCH
    features = heads * width
    odd = lax.rem(index_ref[0], 2)
    position = index_ref[0] * tokens + lax.broadcasted_iota(jnp.int32, (tokens, 1), 0)
    pixels[:, :, :RIM, :] = jnp.zeros((regions, PATCH, RIM, width), jnp.float32)
    pixels[:, :, RIM + columns :, :] = jnp.zeros((regions, PATCH, RIM, width), jnp.float32)
    for region in range(regions):
        total = jnp.zeros((tokens, width), jnp.float32)
        for head in range(heads):
            total = total + load(head, region)
        mean = jnp.sum(total, axis=1, keepdims=True) * (1.0 / features)
        total = jnp.zeros((tokens, width), jnp.float32)
        for head in range(heads):
            centered = load(head, region) - mean
            total = total + centered * centered
        variance = jnp.sum(total, axis=1, keepdims=True) * (1.0 / features)
        spread = lax.rsqrt(variance + 1e-05)
        live = position < lengths_ref[region]
        for head in range(heads):
            centered = load(head, region) - mean
            normed = jnp.where(live, centered * spread * gain_ref[head : head + 1, :], 0.0)
            row, column = divmod(head, PATCH)
            pixels[region, row, pl.ds(RIM + column, tokens, stride=PATCH), :] = normed
        for row in range(PATCH):
            window = three_windows(pixels[region, row], columns)
            image_ref[region, row] = window[:, width : 2 * width]
            start = (region * PATCH + row) * columns
            windows[start : start + columns, :] = window
        near_ref[region] = image_ref[region, (1 - odd) * (PATCH - 1)]
        far_ref[region] = image_ref[region, odd * (PATCH - 1)]
        part = slice(region * PATCH * columns, (region + 1) * PATCH * columns)
        term = jnp.dot(turned_ref[:, part], windows[part, :], preferred_element_type=jnp.float32)
        product = term if region == 0 else product + term
    for down in range(3):
        for across in range(3):
            tap = 3 * down + across
            grads[tap * width : (tap + 1) * width, :] = product[
                down * width : (down + 1) * width, across * width : (across + 1) * width
            ].T
    filled = 9 * width
    if filled < grads.shape[0]:
        grads[filled:, :] = jnp.zeros((grads.shape[0] - filled, width), jnp.float32)
    half = keep_ref.shape[0]
    keep_ref[...] = grads[rows_at(core_ref[0], half), :]
    send_ref[...] = grads[rows_at(1 - core_ref[0], half), :]


def decode_kernel(index_ref, image_ref, near_ref, far_ref, weight_ref, out_ref, done_ref, padded):
    done_ref[...] = jnp.zeros(done_ref.shape, jnp.float32)
    regions, rows, columns, width = image_ref.shape
    padded[:RIM, :] = jnp.zeros((RIM, width), jnp.float32)
    padded[RIM + columns :, :] = jnp.zeros((RIM, width), jnp.float32)
    for region in range(regions):
        strips = []
        before, after = around(lax.rem(index_ref[0], 2), near_ref[region], far_ref[region])
        for row in range(-1, rows + 1):
            if row < 0:
                source = before
            elif row == rows:
                source = after
            else:
                source = image_ref[region, row]
            padded[RIM : RIM + columns, :] = source.astype(jnp.float32)
            strips.append(three_windows(padded[...], columns))
            if len(strips) == 3:
                total = jnp.dot(strips[0], weight_ref[0], preferred_element_type=jnp.float32)
                for down in (1, 2):
                    total = total + jnp.dot(
                        strips[down], weight_ref[down], preferred_element_type=jnp.float32
                    )
                out_ref[region, row - 1] = total.astype(jnp.bfloat16)
                strips.pop(0)


def add_pairs(terms):
    while len(terms) > 1:
        paired = [one + other for one, other in zip(terms[::2], terms[1::2])]
        terms = paired + terms[2 * len(paired) :]
    return terms[0]


def sum_cores_kernel(quad_ref, keep_ref, other_ref, *refs):
    total = refs[-1]
    total[...] = keep_ref[...] + other_ref[...]
    for distance, ref in enumerate(refs[:-1]):
        rows = rows_at(lax.bitwise_xor(quad_ref[0], distance), ref.shape[0])
        ref[...] = total[rows, :].astype(jnp.bfloat16)


def sum_kernel(count, factor, *refs):
    total = add_pairs([ref[...].astype(jnp.float32) for ref in refs[:count]])
    refs[-1][...] = (total * factor).astype(jnp.bfloat16)


def join_kernel(quad_ref, *refs):
    for distance, ref in enumerate(refs[:-1]):
        rows = rows_at(lax.bitwise_xor(quad_ref[0], distance), ref.shape[0])
        refs[-1][rows, :] = ref[...]


def spread_kernel(core_ref, own_ref, other_ref, out_ref):
    half = own_ref.shape[0]
    out_ref[rows_at(core_ref[0], half), :] = own_ref[...].astype(jnp.float32)
    out_ref[rows_at(1 - core_ref[0], half), :] = other_ref[...].astype(jnp.float32)


def trade(values, distance):
    pairs = [(i, i ^ distance) for i in range(lax.axis_size("seq"))]
    return lax.ppermute(values, "seq", pairs)


def inner_size(seq_count):
    inner = 1
    while seq_count % (2 * inner) == 0 and (2 * inner) ** 2 <= seq_count:
        inner *= 2
    return inner


def trade_chips(values, distance, inner):
    seq_count = lax.axis_size("seq")
    pairs = []
    for outer in range(lax.axis_size("dp")):
        for seq in range(seq_count):
            chip, lane = divmod((outer // 2 * inner + seq % inner) ^ distance, inner)
            partner = (2 * chip + outer % 2) * seq_count + seq - seq % inner + lane
            pairs.append((outer * seq_count + seq, partner))
    return lax.ppermute(values, ("dp", "seq"), pairs)


def trade_cores(values):
    return lax.ppermute(values, "dp", [(i, i ^ 1) for i in range(lax.axis_size("dp"))])


def body(query_rows, key_rows, value_rows, region_lengths, norm_gain, conv_weight, cotangent):
    tokens, regions, model_width = query_rows.shape
    width = model_width // HEADS
    seq_count = lax.axis_size("seq")
    seq_index = lax.axis_index("seq")
    inner = inner_size(seq_count)
    quad_size = lax.axis_size("dp") // 2 * inner
    dp_index = lax.axis_index("dp")
    lane = lax.bitwise_and(seq_index, inner - 1)
    quad = (lax.shift_right_logical(dp_index, 1) * inner + lane).reshape(1)
    core = lax.bitwise_and(dp_index, 1).reshape(1)
    columns = tokens * PATCH
    capacity = seq_count * tokens
    per_device = regions * HEADS // seq_count
    far_pairs = [(i, i + 1) for i in range(1, seq_count - 1, 2)]
    far_pairs = far_pairs + [(j, i) for i, j in far_pairs]
    local_bytes = 2 * query_rows.size

    edge_shape = jax.ShapeDtypeStruct((regions, columns, width), jnp.bfloat16)
    chunk_shape = jax.ShapeDtypeStruct((3, per_device, tokens, width), jnp.bfloat16)
    index = seq_index.reshape(1)
    *leaving, cot_near, cot_far = call(
        functools.partial(pack_kernel, regions, per_device),
        "pack",
        [chunk_shape] * (seq_count - 1) + [edge_shape] * 2,
        [SMEM()] + [HBM()] * 4,
        out_specs=[HBM()] * (seq_count + 1),
        scratch=[
            pltpu.VMEM((3,) + query_rows.shape, jnp.bfloat16),
            pltpu.VMEM((seq_count - 1,) + chunk_shape.shape, jnp.bfloat16),
            pltpu.VMEM((2,) + edge_shape.shape, jnp.bfloat16),
            pltpu.SemaphoreType.DMA((7 + 3 * (seq_count - 1),)),
        ],
        moved=6 * local_bytes,
        grant=VMEM_WHOLE,
    )(index, query_rows, key_rows, value_rows, cotangent)
    order = list(range(1, seq_count)) + [0]
    packed = [trade(chunk, distance) for distance, chunk in zip(order, leaving)]
    own = call(
        functools.partial(own_kernel, regions, per_device),
        "own_chunk",
        chunk_shape,
        [SMEM()] + [HBM()] * 3,
        scratch=[
            pltpu.VMEM((3, tokens, regions, max(1, per_device // regions) * width), jnp.bfloat16),
            pltpu.SemaphoreType.DMA((3,)),
        ],
        moved=12 * chunk_shape.size,
    )(index, query_rows, key_rows, value_rows)
    cot_near = trade(cot_near, 1)
    cot_far = lax.ppermute(cot_far, "seq", far_pairs)

    items = seq_index * per_device + jnp.arange(per_device, dtype=jnp.int32)
    item_lengths = jnp.sum(
        jnp.where(
            (items % regions)[:, None] == jnp.arange(regions, dtype=jnp.int32)[None, :],
            region_lengths[None, :],
            0,
        ),
        axis=1,
    )
    block_rows = min(256, capacity)
    group = regions if per_device % regions == 0 else per_device
    mixed = call(
        functools.partial(attend_kernel, block_rows, group, order),
        "attend",
        [jax.ShapeDtypeStruct((per_device, tokens, width), jnp.bfloat16)] * seq_count,
        [SMEM(), SMEM()] + [VMEM()] * seq_count,
        flops=4 * per_device * capacity * capacity * width,
        moved=4 * local_bytes,
        exps=per_device * capacity * capacity,
    )(index, item_lengths, *packed, own)
    attended = [mixed[0]] + [trade(mixed[distance], distance) for distance in order[:-1]]

    turned = call(
        turn_kernel,
        "turn_cotangent",
        jax.ShapeDtypeStruct((3 * width, cotangent.size // width), jnp.bfloat16),
        [SMEM()] + [VMEM()] * 3,
        moved=8 * cotangent.size,
    )(index, cotangent, cot_near, cot_far)
    chunk_rows = -(-9 * width // (32 * quad_size)) * 16
    half_rows = quad_size * chunk_rows
    pixel_rows = regions * PATCH * columns
    conv_flops = 18 * pixel_rows * width * width
    chunk_moved = 8 * chunk_rows * width
    image, near, far, keep, send = call(
        norm_kernel,
        "norm_and_gradient",
        [jax.ShapeDtypeStruct((regions, PATCH, columns, width), jnp.bfloat16)]
        + [edge_shape] * 2
        + [jax.ShapeDtypeStruct((half_rows, width), jnp.float32)] * 2,
        [SMEM()] * 3 + [VMEM()] * (2 + seq_count),
        scratch=[
            pltpu.VMEM((seq_count,) + mixed[0].shape, jnp.bfloat16),
            pltpu.VMEM((regions, PATCH, columns + 2 * RIM, width), jnp.float32),
            pltpu.VMEM((pixel_rows, 3 * width), jnp.bfloat16),
            pltpu.VMEM((2 * half_rows, width), jnp.float32),
        ],
        flops=conv_flops,
        moved=4 * local_bytes,
    )(region_lengths, index, core, norm_gain.reshape(HEADS, width), turned, *attended)
    chunk_shape = jax.ShapeDtypeStruct((chunk_rows, width), jnp.bfloat16)
    parts = call(
        sum_cores_kernel,
        "sum_cores",
        [chunk_shape] * quad_size,
        [SMEM()] + [VMEM()] * 2,
        scratch=[pltpu.VMEM((half_rows, width), jnp.float32)],
        moved=quad_size * chunk_moved,
    )(quad, keep, trade_cores(send))
    near = trade(near, 1)
    far = lax.ppermute(far, "seq", far_pairs)
    distances = range(1, quad_size)
    plane_sum = call(
        functools.partial(sum_kernel, quad_size, 1.0),
        "sum_chips",
        chunk_shape,
        [VMEM()] * quad_size,
        moved=chunk_moved,
    )(parts[0], *[trade_chips(parts[distance], distance, inner) for distance in distances])
    plane_sums = [plane_sum] + [
        trade(plane_sum, distance) for distance in range(inner, seq_count, inner)
    ]
    decoded, done = call(
        decode_kernel,
        "decode",
        [
            jax.ShapeDtypeStruct(cotangent.shape, jnp.bfloat16),
            jax.ShapeDtypeStruct((8, width), jnp.float32),
        ],
        [SMEM()] + [VMEM()] * 4,
        scratch=[pltpu.VMEM((columns + 2 * RIM, width), jnp.float32)],
        flops=conv_flops,
        moved=2 * local_bytes,
    )(index, image, near, far, conv_weight.reshape(3, 3 * width, width))
    total = call(
        functools.partial(sum_kernel, len(plane_sums), 1.0 / math.sqrt(PATCH * columns)),
        "sum_planes",
        chunk_shape,
        [VMEM()] * len(plane_sums) + [ANY()],
        moved=chunk_moved,
    )(*plane_sums, done)
    joined = call(
        join_kernel,
        "join_chips",
        jax.ShapeDtypeStruct((half_rows, width), jnp.bfloat16),
        [SMEM()] + [VMEM()] * quad_size,
        moved=quad_size * chunk_moved,
    )(quad, total, *[trade_chips(total, distance, inner) for distance in distances])
    weight_grad = call(
        spread_kernel,
        "spread_sums",
        jax.ShapeDtypeStruct((2 * half_rows, width), jnp.float32),
        [SMEM()] + [VMEM()] * 2,
        moved=2 * quad_size * chunk_moved,
    )(core, joined, trade_cores(joined))
    return (decoded, weight_grad[: 9 * width].reshape(conv_weight.shape))


def solution(mesh):
    placed = (
        P("seq", "dp", None),
        P("seq", "dp", None),
        P("seq", "dp", None),
        P("dp"),
        P(),
        P(),
        P("dp", "seq", None, None),
    )
    return jax.shard_map(
        body,
        mesh=mesh,
        in_specs=placed,
        out_specs=(P("dp", "seq", None, None), P()),
        check_vma=False,
    )
```

```python
import functools
import math

import jax
import jax.numpy as jnp
from jax import lax
from jax.experimental import pallas as pl
from jax.experimental.pallas import tpu as pltpu
from jax.sharding import PartitionSpec as P

HEADS = 16
PATCH = 4
RIM = 8
VMEM_LIMIT = 48 * 1024 * 1024
VMEM_WHOLE = 60 * 1024 * 1024

VMEM = functools.partial(pl.BlockSpec, memory_space=pltpu.VMEM)
HBM = functools.partial(pl.BlockSpec, memory_space=pltpu.HBM)
ANY = functools.partial(pl.BlockSpec, memory_space=pl.ANY)
SMEM = functools.partial(pl.BlockSpec, memory_space=pltpu.SMEM)


def call(kernel, name, out_shape, in_specs, out_specs=None, scratch=(), flops=0, moved=0, exps=0, grant=VMEM_LIMIT):
    many = isinstance(out_shape, (list, tuple))
    return pl.pallas_call(
        kernel,
        out_shape=out_shape,
        in_specs=in_specs,
        out_specs=out_specs or ([VMEM() for _ in out_shape] if many else VMEM()),
        scratch_shapes=list(scratch),
        compiler_params=pltpu.CompilerParams(vmem_limit_bytes=grant),
        cost_estimate=pl.CostEstimate(flops=flops, bytes_accessed=moved, transcendentals=exps),
        name=name,
    )


def columns_of(index, distance, regions, per_device, width):
    owner = lax.bitwise_xor(index, distance)
    span = max(1, per_device // regions) * width
    start = lax.div(owner * per_device, regions) * width
    return owner, pl.ds(pl.multiple_of(start, width), span)


def take_items(held, owner, regions, per_device, width, out_ref):
    for head in range(held.shape[2] // width):
        block = held[:, :, head * width : (head + 1) * width].astype(jnp.float32)
        if per_device % regions:
            value = block[:, 0, :]
            for other in range(1, regions):
                value = jnp.where(lax.rem(owner, regions) == other, block[:, other, :], value)
            out_ref[head] = value.astype(jnp.bfloat16)
        else:
            for region in range(regions):
                out_ref[head * regions + region] = block[:, region, :].astype(jnp.bfloat16)


def pack_kernel(distances, regions, per_device, index_ref, query_ref, key_ref, value_ref, *refs):
    refs = refs[-len(distances) - 4 :]
    held, ready, load_sems, store_sems = refs[-4:]
    width = query_ref.shape[2] // HEADS
    loads = []
    for number, distance in enumerate(distances):
        owner, columns = columns_of(index_ref[0], distance, regions, per_device, width)
        for which, ref in enumerate((query_ref, key_ref, value_ref)):
            load = pltpu.make_async_copy(
                ref.at[:, :, columns], held.at[number, which], load_sems.at[3 * number + which]
            )
            load.start()
            loads.append((number, which, owner, load))
    stores = []
    for number, which, owner, load in loads:
        load.wait()
        take_items(
            held.at[number, which], owner, regions, per_device, width, ready.at[number, which]
        )
        if which == 2:
            store = pltpu.make_async_copy(ready.at[number], refs[number], store_sems.at[number])
            store.start()
            stores.append(store)
    for store in stores:
        store.wait()


def own_kernel(
    regions, per_device, index_ref, query_ref, key_ref, value_ref, out_ref, held, sems
):
    width = out_ref.shape[3]
    owner, columns = columns_of(index_ref[0], 0, regions, per_device, width)
    loads = []
    for which, ref in enumerate((query_ref, key_ref, value_ref)):
        loads.append(
            pltpu.make_async_copy(ref.at[:, :, columns], held.at[which], sems.at[which])
        )
        loads[-1].start()
    for which, load in enumerate(loads):
        load.wait()
        take_items(held.at[which], owner, regions, per_device, width, out_ref.at[which])


def attend_kernel(block_rows, group, order, index_ref, lengths_ref, *refs):
    chunks = dict(zip(order, refs))
    out_refs = refs[len(order) :]
    index = index_ref[0]
    sources = len(chunks)
    _, per_device, tokens, width = chunks[0].shape
    capacity = sources * tokens
    per_block = block_rows // tokens
    blocks = capacity // block_rows
    factor = math.log2(math.e) / math.sqrt(width)
    columns = lax.broadcasted_iota(jnp.int32, (1, capacity), 1)
    slots = columns
    for distance in range(sources):
        here = (columns >= distance * tokens) & (columns < (distance + 1) * tokens)
        moved = (lax.bitwise_xor(index, distance) - distance) * tokens
        slots = jnp.where(here, columns + moved, slots)

    def rows_of(which, item, distances):
        return jnp.concatenate([chunks[distance][which, item] for distance in distances], axis=0)

    def distances_of(block):
        return range(block * per_block, (block + 1) * per_block)

    def start_of(block, span):
        return lax.bitwise_xor(lax.div(index, span), block) * span

    def clear(item, block):
        for distance in distances_of(block):
            out_refs[distance][item] = jnp.zeros((tokens, width), jnp.bfloat16)

    def score(item, block):
        return lax.dot_general(
            rows_of(0, item, distances_of(block)),
            rows_of(1, item, range(sources)),
            (((1,), (1,)), ((), ())),
            preferred_element_type=jnp.float32,
        )

    def finish(item, block, scores, key_valid):
        scores = jnp.where(key_valid, scores * factor, -1e30)
        powers = jnp.exp2(scores - jnp.max(scores, axis=1, keepdims=True))
        totals = jnp.sum(powers, axis=1, keepdims=True)
        mixed = jnp.dot(
            powers.astype(jnp.bfloat16),
            rows_of(2, item, range(sources)),
            preferred_element_type=jnp.float32,
        )
        mixed = (mixed / totals).astype(jnp.bfloat16)
        for number, distance in enumerate(distances_of(block)):
            out_refs[distance][item] = mixed[number * tokens : (number + 1) * tokens]

    def attend(items, live, dead, length):
        key_valid = slots < length
        waiting = None
        for block in live:
            for item in items:
                scores = score(item, block)
                if waiting is not None:
                    finish(*waiting, key_valid)
                waiting = (item, block, scores)
        if waiting is not None:
            finish(*waiting, key_valid)
        for block in dead:
            for item in items:
                clear(item, block)

    for lead in range(group):
        length = lengths_ref[lead]
        items = list(range(lead, per_device, group))
        for block in range(0, blocks, 2):
            pair = list(range(block, min(block + 2, blocks)))
            alive = [length > start_of(one, per_block) * tokens for one in pair]
            for case in range(2 ** len(pair)):
                live = [one for bit, one in enumerate(pair) if case >> bit & 1]
                dead = [one for one in pair if one not in live]
                chosen = None
                for bit in range(len(pair)):
                    test = alive[bit] if case >> bit & 1 else jnp.logical_not(alive[bit])
                    chosen = test if chosen is None else chosen & test

                @pl.when(chosen)
                def _(items=items, live=live, dead=dead, length=length):
                    attend(items, live, dead, length)


def three_windows(padded, columns):
    return jnp.concatenate(
        [padded[RIM - 1 + shift : RIM - 1 + shift + columns].astype(jnp.bfloat16) for shift in range(3)],
        axis=1,
    )


def rows_at(place, rows):
    return pl.ds(pl.multiple_of(place * rows, rows), rows)


def around(odd, near, far):
    return jnp.where(odd == 1, near, far), jnp.where(odd == 1, far, near)


def turn_kernel(index_ref, cot_ref, near_ref, far_ref, out_ref):
    regions, rows, columns, width = cot_ref.shape
    for region in range(regions):
        before, after = around(lax.rem(index_ref[0], 2), near_ref[region], far_ref[region])
        for row in range(-1, rows + 1):
            value = before if row < 0 else after if row == rows else cot_ref[region, row]
            turned = value.T
            for down in range(3):
                image_row = row - 1 + down
                if 0 <= image_row < rows:
                    start = (region * rows + image_row) * columns
                    out_ref[down * width : (down + 1) * width, start : start + columns] = turned


def norm_kernel(lengths_ref, index_ref, core_ref, gain_ref, turned_ref, *refs):
    image_ref, near_ref, far_ref, keep_ref, send_ref, attended, pixels, windows, grads = refs[-9:]
    for distance, ref in enumerate(refs[:-9]):
        attended[lax.bitwise_xor(index_ref[0], distance)] = ref[...]
    heads = gain_ref.shape[0]
    regions = image_ref.shape[0]
    _, per_device, tokens, width = attended.shape

    def load(head, region):
        owner, place = divmod(head * regions + region, per_device)
        return attended[owner, place].astype(jnp.float32)

    columns = tokens * PATCH
    features = heads * width
    odd = lax.rem(index_ref[0], 2)
    position = index_ref[0] * tokens + lax.broadcasted_iota(jnp.int32, (tokens, 1), 0)
    pixels[:, :, :RIM, :] = jnp.zeros((regions, PATCH, RIM, width), jnp.float32)
    pixels[:, :, RIM + columns :, :] = jnp.zeros((regions, PATCH, RIM, width), jnp.float32)
    for region in range(regions):
        total = jnp.zeros((tokens, width), jnp.float32)
        for head in range(heads):
            total = total + load(head, region)
        mean = jnp.sum(total, axis=1, keepdims=True) * (1.0 / features)
        total = jnp.zeros((tokens, width), jnp.float32)
        for head in range(heads):
            centered = load(head, region) - mean
            total = total + centered * centered
        variance = jnp.sum(total, axis=1, keepdims=True) * (1.0 / features)
        spread = lax.rsqrt(variance + 1e-05)
        live = position < lengths_ref[region]
        for head in range(heads):
            centered = load(head, region) - mean
            normed = jnp.where(live, centered * spread * gain_ref[head : head + 1, :], 0.0)
            row, column = divmod(head, PATCH)
            pixels[region, row, pl.ds(RIM + column, tokens, stride=PATCH), :] = normed
        for row in range(PATCH):
            window = three_windows(pixels[region, row], columns)
            image_ref[region, row] = window[:, width : 2 * width]
            start = (region * PATCH + row) * columns
            windows[start : start + columns, :] = window
        near_ref[region] = image_ref[region, (1 - odd) * (PATCH - 1)]
        far_ref[region] = image_ref[region, odd * (PATCH - 1)]
        part = slice(region * PATCH * columns, (region + 1) * PATCH * columns)
        term = jnp.dot(turned_ref[:, part], windows[part, :], preferred_element_type=jnp.float32)
        product = term if region == 0 else product + term
    for down in range(3):
        for across in range(3):
            tap = 3 * down + across
            grads[tap * width : (tap + 1) * width, :] = product[
                down * width : (down + 1) * width, across * width : (across + 1) * width
            ].T
    filled = 9 * width
    if filled < grads.shape[0]:
        grads[filled:, :] = jnp.zeros((grads.shape[0] - filled, width), jnp.float32)
    half = keep_ref.shape[0]
    keep_ref[...] = grads[rows_at(core_ref[0], half), :]
    send_ref[...] = grads[rows_at(1 - core_ref[0], half), :]


def decode_kernel(index_ref, image_ref, near_ref, far_ref, weight_ref, out_ref, done_ref, padded):
    done_ref[...] = jnp.zeros(done_ref.shape, jnp.float32)
    regions, rows, columns, width = image_ref.shape
    padded[:RIM, :] = jnp.zeros((RIM, width), jnp.float32)
    padded[RIM + columns :, :] = jnp.zeros((RIM, width), jnp.float32)
    for region in range(regions):
        strips = []
        before, after = around(lax.rem(index_ref[0], 2), near_ref[region], far_ref[region])
        for row in range(-1, rows + 1):
            if row < 0:
                source = before
            elif row == rows:
                source = after
            else:
                source = image_ref[region, row]
            padded[RIM : RIM + columns, :] = source.astype(jnp.float32)
            strips.append(three_windows(padded[...], columns))
            if len(strips) == 3:
                total = jnp.dot(strips[0], weight_ref[0], preferred_element_type=jnp.float32)
                for down in (1, 2):
                    total = total + jnp.dot(
                        strips[down], weight_ref[down], preferred_element_type=jnp.float32
                    )
                out_ref[region, row - 1] = total.astype(jnp.bfloat16)
                strips.pop(0)


def add_pairs(terms):
    while len(terms) > 1:
        paired = [one + other for one, other in zip(terms[::2], terms[1::2])]
        terms = paired + terms[2 * len(paired) :]
    return terms[0]


def sum_cores_kernel(quad_ref, keep_ref, other_ref, *refs):
    total = refs[-1]
    total[...] = keep_ref[...] + other_ref[...]
    for distance, ref in enumerate(refs[:-1]):
        rows = rows_at(lax.bitwise_xor(quad_ref[0], distance), ref.shape[0])
        ref[...] = total[rows, :].astype(jnp.bfloat16)


def sum_kernel(count, factor, *refs):
    total = add_pairs([ref[...].astype(jnp.float32) for ref in refs[:count]])
    refs[-1][...] = (total * factor).astype(jnp.bfloat16)


def join_kernel(quad_ref, *refs):
    for distance, ref in enumerate(refs[:-1]):
        rows = rows_at(lax.bitwise_xor(quad_ref[0], distance), ref.shape[0])
        refs[-1][rows, :] = ref[...]


def spread_kernel(core_ref, own_ref, other_ref, out_ref):
    half = own_ref.shape[0]
    out_ref[rows_at(core_ref[0], half), :] = own_ref[...].astype(jnp.float32)
    out_ref[rows_at(1 - core_ref[0], half), :] = other_ref[...].astype(jnp.float32)


def trade(values, distance):
    pairs = [(i, i ^ distance) for i in range(lax.axis_size("seq"))]
    return lax.ppermute(values, "seq", pairs)


def inner_size(seq_count):
    inner = 1
    while seq_count % (2 * inner) == 0 and (2 * inner) ** 2 <= seq_count:
        inner *= 2
    return inner


def trade_chips(values, distance, inner):
    seq_count = lax.axis_size("seq")
    pairs = []
    for outer in range(lax.axis_size("dp")):
        for seq in range(seq_count):
            chip, lane = divmod((outer // 2 * inner + seq % inner) ^ distance, inner)
            partner = (2 * chip + outer % 2) * seq_count + seq - seq % inner + lane
            pairs.append((outer * seq_count + seq, partner))
    return lax.ppermute(values, ("dp", "seq"), pairs)


def trade_cores(values):
    return lax.ppermute(values, "dp", [(i, i ^ 1) for i in range(lax.axis_size("dp"))])


def body(query_rows, key_rows, value_rows, region_lengths, norm_gain, conv_weight, cotangent):
    tokens, regions, model_width = query_rows.shape
    width = model_width // HEADS
    seq_count = lax.axis_size("seq")
    seq_index = lax.axis_index("seq")
    inner = inner_size(seq_count)
    quad_size = lax.axis_size("dp") // 2 * inner
    dp_index = lax.axis_index("dp")
    lane = lax.bitwise_and(seq_index, inner - 1)
    quad = (lax.shift_right_logical(dp_index, 1) * inner + lane).reshape(1)
    core = lax.bitwise_and(dp_index, 1).reshape(1)
    columns = tokens * PATCH
    capacity = seq_count * tokens
    per_device = regions * HEADS // seq_count
    far_pairs = [(i, i + 1) for i in range(1, seq_count - 1, 2)]
    far_pairs = far_pairs + [(j, i) for i, j in far_pairs]
    local_bytes = 2 * query_rows.size

    edge_shape = jax.ShapeDtypeStruct((regions, columns, width), jnp.bfloat16)
    chunk_shape = jax.ShapeDtypeStruct((3, per_device, tokens, width), jnp.bfloat16)
    index = seq_index.reshape(1)
    odd = lax.bitwise_and(seq_index, 1) == 1
    cot_far = jnp.where(odd, cotangent[:, PATCH - 1], cotangent[:, 0])
    cot_far = lax.ppermute(cot_far, "seq", far_pairs)
    half = seq_count // 2
    early = [2, half, half + 1]
    late = [distance for distance in range(1, seq_count) if distance not in early]
    span = max(1, per_device // regions) * width

    def pack(name, distances, *after):
        return call(
            functools.partial(pack_kernel, distances, regions, per_device),
            name,
            [chunk_shape] * len(distances),
            [SMEM()] + [HBM()] * 3 + [ANY()] * len(after),
            out_specs=[HBM()] * len(distances),
            scratch=[
                pltpu.VMEM((len(distances), 3, tokens, regions, span), jnp.bfloat16),
                pltpu.VMEM((len(distances),) + chunk_shape.shape, jnp.bfloat16),
                pltpu.SemaphoreType.DMA((3 * len(distances),)),
                pltpu.SemaphoreType.DMA((len(distances),)),
            ],
            moved=4 * len(distances) * chunk_shape.size,
            grant=VMEM_WHOLE,
        )(index, query_rows, key_rows, value_rows, *after)

    packed = {}
    for distance, chunk in zip(early, pack("pack_early", early)):
        packed[distance] = trade(chunk, distance)
    for distance, chunk in zip(late, pack("pack_late", late, cot_far)):
        packed[distance] = trade(chunk, distance)
    order = list(range(1, seq_count)) + [0]
    packed[0] = call(
        functools.partial(own_kernel, regions, per_device),
        "own_chunk",
        chunk_shape,
        [SMEM()] + [HBM()] * 3,
        scratch=[
            pltpu.VMEM((3, tokens, regions, span), jnp.bfloat16),
            pltpu.SemaphoreType.DMA((3,)),
        ],
        moved=12 * chunk_shape.size,
    )(index, query_rows, key_rows, value_rows)
    cot_near = jnp.where(odd, cotangent[:, 0], cotangent[:, PATCH - 1])
    cot_near = trade(cot_near, 1)

    items = seq_index * per_device + jnp.arange(per_device, dtype=jnp.int32)
    item_lengths = jnp.sum(
        jnp.where(
            (items % regions)[:, None] == jnp.arange(regions, dtype=jnp.int32)[None, :],
            region_lengths[None, :],
            0,
        ),
        axis=1,
    )
    block_rows = min(256, capacity)
    group = regions if per_device % regions == 0 else per_device
    mixed = call(
        functools.partial(attend_kernel, block_rows, group, order),
        "attend",
        [jax.ShapeDtypeStruct((per_device, tokens, width), jnp.bfloat16)] * seq_count,
        [SMEM(), SMEM()] + [VMEM()] * seq_count,
        flops=4 * per_device * capacity * capacity * width,
        moved=4 * local_bytes,
        exps=per_device * capacity * capacity,
    )(index, item_lengths, *[packed[distance] for distance in order])
    attended = [mixed[0]] + [trade(mixed[distance], distance) for distance in order[:-1]]

    turned = call(
        turn_kernel,
        "turn_cotangent",
        jax.ShapeDtypeStruct((3 * width, cotangent.size // width), jnp.bfloat16),
        [SMEM()] + [VMEM()] * 3,
        moved=8 * cotangent.size,
    )(index, cotangent, cot_near, cot_far)
    chunk_rows = -(-9 * width // (32 * quad_size)) * 16
    half_rows = quad_size * chunk_rows
    pixel_rows = regions * PATCH * columns
    conv_flops = 18 * pixel_rows * width * width
    chunk_moved = 8 * chunk_rows * width
    image, near, far, keep, send = call(
        norm_kernel,
        "norm_and_gradient",
        [jax.ShapeDtypeStruct((regions, PATCH, columns, width), jnp.bfloat16)]
        + [edge_shape] * 2
        + [jax.ShapeDtypeStruct((half_rows, width), jnp.float32)] * 2,
        [SMEM()] * 3 + [VMEM()] * (2 + seq_count),
        scratch=[
            pltpu.VMEM((seq_count,) + mixed[0].shape, jnp.bfloat16),
            pltpu.VMEM((regions, PATCH, columns + 2 * RIM, width), jnp.float32),
            pltpu.VMEM((pixel_rows, 3 * width), jnp.bfloat16),
            pltpu.VMEM((2 * half_rows, width), jnp.float32),
        ],
        flops=conv_flops,
        moved=4 * local_bytes,
    )(region_lengths, index, core, norm_gain.reshape(HEADS, width), turned, *attended)
    chunk_shape = jax.ShapeDtypeStruct((chunk_rows, width), jnp.bfloat16)
    parts = call(
        sum_cores_kernel,
        "sum_cores",
        [chunk_shape] * quad_size,
        [SMEM()] + [VMEM()] * 2,
        scratch=[pltpu.VMEM((half_rows, width), jnp.float32)],
        moved=quad_size * chunk_moved,
    )(quad, keep, trade_cores(send))
    near = trade(near, 1)
    far = lax.ppermute(far, "seq", far_pairs)
    distances = range(1, quad_size)
    plane_sum = call(
        functools.partial(sum_kernel, quad_size, 1.0),
        "sum_chips",
        chunk_shape,
        [VMEM()] * quad_size,
        moved=chunk_moved,
    )(parts[0], *[trade_chips(parts[distance], distance, inner) for distance in distances])
    plane_sums = [plane_sum] + [
        trade(plane_sum, distance) for distance in range(inner, seq_count, inner)
    ]
    decoded, done = call(
        decode_kernel,
        "decode",
        [
            jax.ShapeDtypeStruct(cotangent.shape, jnp.bfloat16),
            jax.ShapeDtypeStruct((8, width), jnp.float32),
        ],
        [SMEM()] + [VMEM()] * 4,
        scratch=[pltpu.VMEM((columns + 2 * RIM, width), jnp.float32)],
        flops=conv_flops,
        moved=2 * local_bytes,
    )(index, image, near, far, conv_weight.reshape(3, 3 * width, width))
    total = call(
        functools.partial(sum_kernel, len(plane_sums), 1.0 / math.sqrt(PATCH * columns)),
        "sum_planes",
        chunk_shape,
        [VMEM()] * len(plane_sums) + [ANY()],
        moved=chunk_moved,
    )(*plane_sums, done)
    joined = call(
        join_kernel,
        "join_chips",
        jax.ShapeDtypeStruct((half_rows, width), jnp.bfloat16),
        [SMEM()] + [VMEM()] * quad_size,
        moved=quad_size * chunk_moved,
    )(quad, total, *[trade_chips(total, distance, inner) for distance in distances])
    weight_grad = call(
        spread_kernel,
        "spread_sums",
        jax.ShapeDtypeStruct((2 * half_rows, width), jnp.float32),
        [SMEM()] + [VMEM()] * 2,
        moved=2 * quad_size * chunk_moved,
    )(core, joined, trade_cores(joined))
    return (decoded, weight_grad[: 9 * width].reshape(conv_weight.shape))


def solution(mesh):
    placed = (
        P("seq", "dp", None),
        P("seq", "dp", None),
        P("seq", "dp", None),
        P("dp"),
        P(),
        P(),
        P("dp", "seq", None, None),
    )
    return jax.shard_map(
        body,
        mesh=mesh,
        in_specs=placed,
        out_specs=(P("dp", "seq", None, None), P()),
        check_vma=False,
    )
```

```python
import functools
import math

import jax
import jax.numpy as jnp
from jax import lax
from jax.experimental import pallas as pl
from jax.experimental.pallas import tpu as pltpu
from jax.sharding import PartitionSpec as P

HEADS = 16
PATCH = 4
RIM = 8
VMEM_LIMIT = 48 * 1024 * 1024
VMEM_WHOLE = 60 * 1024 * 1024

VMEM = functools.partial(pl.BlockSpec, memory_space=pltpu.VMEM)
HBM = functools.partial(pl.BlockSpec, memory_space=pltpu.HBM)
ANY = functools.partial(pl.BlockSpec, memory_space=pl.ANY)
SMEM = functools.partial(pl.BlockSpec, memory_space=pltpu.SMEM)


def call(kernel, name, out_shape, in_specs, out_specs=None, scratch=(), flops=0, moved=0, exps=0, grant=VMEM_LIMIT):
    many = isinstance(out_shape, (list, tuple))
    return pl.pallas_call(
        kernel,
        out_shape=out_shape,
        in_specs=in_specs,
        out_specs=out_specs or ([VMEM() for _ in out_shape] if many else VMEM()),
        scratch_shapes=list(scratch),
        compiler_params=pltpu.CompilerParams(vmem_limit_bytes=grant),
        cost_estimate=pl.CostEstimate(flops=flops, bytes_accessed=moved, transcendentals=exps),
        name=name,
    )


def columns_of(index, distance, regions, per_device, width):
    owner = lax.bitwise_xor(index, distance)
    span = max(1, per_device // regions) * width
    start = lax.div(owner * per_device, regions) * width
    return owner, pl.ds(pl.multiple_of(start, width), span)


def take_items(held, owner, regions, per_device, width, out_ref):
    for head in range(held.shape[2] // width):
        block = held[:, :, head * width : (head + 1) * width].astype(jnp.float32)
        if per_device % regions:
            value = block[:, 0, :]
            for other in range(1, regions):
                value = jnp.where(lax.rem(owner, regions) == other, block[:, other, :], value)
            out_ref[head] = value.astype(jnp.bfloat16)
        else:
            for region in range(regions):
                out_ref[head * regions + region] = block[:, region, :].astype(jnp.bfloat16)


def pack_kernel(distances, regions, per_device, index_ref, query_ref, key_ref, value_ref, *refs):
    refs = refs[-len(distances) - 4 :]
    held, ready, load_sems, store_sems = refs[-4:]
    width = query_ref.shape[2] // HEADS
    loads = []
    for number, distance in enumerate(distances):
        owner, columns = columns_of(index_ref[0], distance, regions, per_device, width)
        for which, ref in enumerate((query_ref, key_ref, value_ref)):
            load = pltpu.make_async_copy(
                ref.at[:, :, columns], held.at[number, which], load_sems.at[3 * number + which]
            )
            load.start()
            loads.append((number, which, owner, load))
    stores = []
    for number, which, owner, load in loads:
        load.wait()
        take_items(
            held.at[number, which], owner, regions, per_device, width, ready.at[number, which]
        )
        if which == 2:
            store = pltpu.make_async_copy(ready.at[number], refs[number], store_sems.at[number])
            store.start()
            stores.append(store)
    for store in stores:
        store.wait()


def own_kernel(
    regions, per_device, index_ref, query_ref, key_ref, value_ref, out_ref, held, sems
):
    width = out_ref.shape[3]
    owner, columns = columns_of(index_ref[0], 0, regions, per_device, width)
    loads = []
    for which, ref in enumerate((query_ref, key_ref, value_ref)):
        loads.append(
            pltpu.make_async_copy(ref.at[:, :, columns], held.at[which], sems.at[which])
        )
        loads[-1].start()
    for which, load in enumerate(loads):
        load.wait()
        take_items(held.at[which], owner, regions, per_device, width, out_ref.at[which])


def attend_kernel(block_rows, group, order, index_ref, lengths_ref, *refs):
    chunks = dict(zip(order, refs))
    out_refs = refs[len(order) :]
    index = index_ref[0]
    sources = len(chunks)
    _, per_device, tokens, width = chunks[0].shape
    capacity = sources * tokens
    per_block = block_rows // tokens
    blocks = capacity // block_rows
    factor = math.log2(math.e) / math.sqrt(width)
    columns = lax.broadcasted_iota(jnp.int32, (1, capacity), 1)
    slots = columns
    for distance in range(sources):
        here = (columns >= distance * tokens) & (columns < (distance + 1) * tokens)
        moved = (lax.bitwise_xor(index, distance) - distance) * tokens
        slots = jnp.where(here, columns + moved, slots)

    def rows_of(which, item, distances):
        return jnp.concatenate([chunks[distance][which, item] for distance in distances], axis=0)

    def distances_of(block):
        return range(block * per_block, (block + 1) * per_block)

    def start_of(block, span):
        return lax.bitwise_xor(lax.div(index, span), block) * span

    def clear(item, block):
        for distance in distances_of(block):
            out_refs[distance][item] = jnp.zeros((tokens, width), jnp.bfloat16)

    def score(item, block):
        return lax.dot_general(
            rows_of(0, item, distances_of(block)),
            rows_of(1, item, range(sources)),
            (((1,), (1,)), ((), ())),
            preferred_element_type=jnp.float32,
        )

    def finish(item, block, scores, key_valid):
        scores = jnp.where(key_valid, scores * factor, -1e30)
        powers = jnp.exp2(scores - jnp.max(scores, axis=1, keepdims=True))
        totals = jnp.sum(powers, axis=1, keepdims=True)
        mixed = jnp.dot(
            powers.astype(jnp.bfloat16),
            rows_of(2, item, range(sources)),
            preferred_element_type=jnp.float32,
        )
        mixed = (mixed / totals).astype(jnp.bfloat16)
        for number, distance in enumerate(distances_of(block)):
            out_refs[distance][item] = mixed[number * tokens : (number + 1) * tokens]

    def attend(items, live, dead, length):
        key_valid = slots < length
        waiting = None
        for block in live:
            for item in items:
                scores = score(item, block)
                if waiting is not None:
                    finish(*waiting, key_valid)
                waiting = (item, block, scores)
        if waiting is not None:
            finish(*waiting, key_valid)
        for block in dead:
            for item in items:
                clear(item, block)

    for lead in range(group):
        length = lengths_ref[lead]
        items = list(range(lead, per_device, group))
        for block in range(0, blocks, 2):
            pair = list(range(block, min(block + 2, blocks)))
            alive = [length > start_of(one, per_block) * tokens for one in pair]
            for case in range(2 ** len(pair)):
                live = [one for bit, one in enumerate(pair) if case >> bit & 1]
                dead = [one for one in pair if one not in live]
                chosen = None
                for bit in range(len(pair)):
                    test = alive[bit] if case >> bit & 1 else jnp.logical_not(alive[bit])
                    chosen = test if chosen is None else chosen & test

                @pl.when(chosen)
                def _(items=items, live=live, dead=dead, length=length):
                    attend(items, live, dead, length)


def three_windows(padded, columns):
    return jnp.concatenate(
        [padded[RIM - 1 + shift : RIM - 1 + shift + columns].astype(jnp.bfloat16) for shift in range(3)],
        axis=1,
    )


def rows_at(place, rows):
    return pl.ds(pl.multiple_of(place * rows, rows), rows)


def around(odd, near, far):
    return jnp.where(odd == 1, near, far), jnp.where(odd == 1, far, near)


def turn_kernel(index_ref, cot_ref, near_ref, far_ref, out_ref):
    regions, rows, columns, width = cot_ref.shape
    for region in range(regions):
        before, after = around(lax.rem(index_ref[0], 2), near_ref[region], far_ref[region])
        for row in range(-1, rows + 1):
            value = before if row < 0 else after if row == rows else cot_ref[region, row]
            turned = value.T
            for down in range(3):
                image_row = row - 1 + down
                if 0 <= image_row < rows:
                    start = (region * rows + image_row) * columns
                    out_ref[down * width : (down + 1) * width, start : start + columns] = turned


def norm_kernel(lengths_ref, index_ref, core_ref, gain_ref, turned_ref, *refs):
    image_ref, near_ref, far_ref, keep_ref, send_ref, attended, pixels, windows, grads = refs[-9:]
    for distance, ref in enumerate(refs[:-9]):
        attended[lax.bitwise_xor(index_ref[0], distance)] = ref[...]
    heads = gain_ref.shape[0]
    regions = image_ref.shape[0]
    _, per_device, tokens, width = attended.shape

    def load(head, region):
        owner, place = divmod(head * regions + region, per_device)
        return attended[owner, place].astype(jnp.float32)

    columns = tokens * PATCH
    features = heads * width
    odd = lax.rem(index_ref[0], 2)
    position = index_ref[0] * tokens + lax.broadcasted_iota(jnp.int32, (tokens, 1), 0)
    pixels[:, :, :RIM, :] = jnp.zeros((regions, PATCH, RIM, width), jnp.float32)
    pixels[:, :, RIM + columns :, :] = jnp.zeros((regions, PATCH, RIM, width), jnp.float32)
    for region in range(regions):
        total = jnp.zeros((tokens, width), jnp.float32)
        for head in range(heads):
            total = total + load(head, region)
        mean = jnp.sum(total, axis=1, keepdims=True) * (1.0 / features)
        total = jnp.zeros((tokens, width), jnp.float32)
        for head in range(heads):
            centered = load(head, region) - mean
            total = total + centered * centered
        variance = jnp.sum(total, axis=1, keepdims=True) * (1.0 / features)
        spread = lax.rsqrt(variance + 1e-05)
        live = position < lengths_ref[region]
        for head in range(heads):
            centered = load(head, region) - mean
            normed = jnp.where(live, centered * spread * gain_ref[head : head + 1, :], 0.0)
            row, column = divmod(head, PATCH)
            pixels[region, row, pl.ds(RIM + column, tokens, stride=PATCH), :] = normed
        for row in range(PATCH):
            window = three_windows(pixels[region, row], columns)
            image_ref[region, row] = window[:, width : 2 * width]
            start = (region * PATCH + row) * columns
            windows[start : start + columns, :] = window
        near_ref[region] = image_ref[region, (1 - odd) * (PATCH - 1)]
        far_ref[region] = image_ref[region, odd * (PATCH - 1)]
        part = slice(region * PATCH * columns, (region + 1) * PATCH * columns)
        term = jnp.dot(turned_ref[:, part], windows[part, :], preferred_element_type=jnp.float32)
        product = term if region == 0 else product + term
    for down in range(3):
        for across in range(3):
            tap = 3 * down + across
            grads[tap * width : (tap + 1) * width, :] = product[
                down * width : (down + 1) * width, across * width : (across + 1) * width
            ].T
    filled = 9 * width
    if filled < grads.shape[0]:
        grads[filled:, :] = jnp.zeros((grads.shape[0] - filled, width), jnp.float32)
    half = keep_ref.shape[0]
    keep_ref[...] = grads[rows_at(core_ref[0], half), :]
    send_ref[...] = grads[rows_at(1 - core_ref[0], half), :]


def decode_kernel(index_ref, image_ref, near_ref, far_ref, weight_ref, out_ref, done_ref, padded):
    done_ref[...] = jnp.zeros(done_ref.shape, jnp.float32)
    regions, rows, columns, width = image_ref.shape
    padded[:RIM, :] = jnp.zeros((RIM, width), jnp.float32)
    padded[RIM + columns :, :] = jnp.zeros((RIM, width), jnp.float32)
    for region in range(regions):
        strips = []
        before, after = around(lax.rem(index_ref[0], 2), near_ref[region], far_ref[region])
        for row in range(-1, rows + 1):
            if row < 0:
                source = before
            elif row == rows:
                source = after
            else:
                source = image_ref[region, row]
            padded[RIM : RIM + columns, :] = source.astype(jnp.float32)
            strips.append(three_windows(padded[...], columns))
            if len(strips) == 3:
                total = jnp.dot(strips[0], weight_ref[0], preferred_element_type=jnp.float32)
                for down in (1, 2):
                    total = total + jnp.dot(
                        strips[down], weight_ref[down], preferred_element_type=jnp.float32
                    )
                out_ref[region, row - 1] = total.astype(jnp.bfloat16)
                strips.pop(0)


def add_pairs(terms):
    while len(terms) > 1:
        paired = [one + other for one, other in zip(terms[::2], terms[1::2])]
        terms = paired + terms[2 * len(paired) :]
    return terms[0]


def sum_cores_kernel(quad_ref, keep_ref, other_ref, *refs):
    total = refs[-1]
    total[...] = keep_ref[...] + other_ref[...]
    for distance, ref in enumerate(refs[:-1]):
        rows = rows_at(lax.bitwise_xor(quad_ref[0], distance), ref.shape[0])
        ref[...] = total[rows, :].astype(jnp.bfloat16)


def sum_kernel(count, factor, *refs):
    total = add_pairs([ref[...].astype(jnp.float32) for ref in refs[:count]])
    refs[-1][...] = (total * factor).astype(jnp.bfloat16)


def join_kernel(quad_ref, *refs):
    for distance, ref in enumerate(refs[:-1]):
        rows = rows_at(lax.bitwise_xor(quad_ref[0], distance), ref.shape[0])
        refs[-1][rows, :] = ref[...]


def spread_kernel(core_ref, own_ref, other_ref, out_ref):
    half = own_ref.shape[0]
    out_ref[rows_at(core_ref[0], half), :] = own_ref[...].astype(jnp.float32)
    out_ref[rows_at(1 - core_ref[0], half), :] = other_ref[...].astype(jnp.float32)


def trade(values, distance):
    pairs = [(i, i ^ distance) for i in range(lax.axis_size("seq"))]
    return lax.ppermute(values, "seq", pairs)


def inner_size(seq_count):
    inner = 1
    while seq_count % (2 * inner) == 0 and (2 * inner) ** 2 <= seq_count:
        inner *= 2
    return inner


def trade_chips(values, distance, inner):
    seq_count = lax.axis_size("seq")
    pairs = []
    for outer in range(lax.axis_size("dp")):
        for seq in range(seq_count):
            chip, lane = divmod((outer // 2 * inner + seq % inner) ^ distance, inner)
            partner = (2 * chip + outer % 2) * seq_count + seq - seq % inner + lane
            pairs.append((outer * seq_count + seq, partner))
    return lax.ppermute(values, ("dp", "seq"), pairs)


def trade_cores(values):
    return lax.ppermute(values, "dp", [(i, i ^ 1) for i in range(lax.axis_size("dp"))])


def body(query_rows, key_rows, value_rows, region_lengths, norm_gain, conv_weight, cotangent):
    tokens, regions, model_width = query_rows.shape
    width = model_width // HEADS
    seq_count = lax.axis_size("seq")
    seq_index = lax.axis_index("seq")
    inner = inner_size(seq_count)
    quad_size = lax.axis_size("dp") // 2 * inner
    dp_index = lax.axis_index("dp")
    lane = lax.bitwise_and(seq_index, inner - 1)
    quad = (lax.shift_right_logical(dp_index, 1) * inner + lane).reshape(1)
    core = lax.bitwise_and(dp_index, 1).reshape(1)
    columns = tokens * PATCH
    capacity = seq_count * tokens
    per_device = regions * HEADS // seq_count
    far_pairs = [(i, i + 1) for i in range(1, seq_count - 1, 2)]
    far_pairs = far_pairs + [(j, i) for i, j in far_pairs]
    local_bytes = 2 * query_rows.size

    edge_shape = jax.ShapeDtypeStruct((regions, columns, width), jnp.bfloat16)
    chunk_shape = jax.ShapeDtypeStruct((3, per_device, tokens, width), jnp.bfloat16)
    index = seq_index.reshape(1)
    odd = lax.bitwise_and(seq_index, 1) == 1
    cot_far = jnp.where(odd, cotangent[:, PATCH - 1], cotangent[:, 0])
    cot_far = lax.ppermute(cot_far, "seq", far_pairs)
    half = seq_count // 2
    early = [half, half + 1]
    near_by, far_off = (list(range(1, half)), list(range(half + 2, seq_count)))
    late = far_off[:1] + near_by[:2] + far_off[1:] + near_by[2:]
    span = max(1, per_device // regions) * width

    def pack(name, distances, *after):
        return call(
            functools.partial(pack_kernel, distances, regions, per_device),
            name,
            [chunk_shape] * len(distances),
            [SMEM()] + [HBM()] * 3 + [ANY()] * len(after),
            out_specs=[HBM()] * len(distances),
            scratch=[
                pltpu.VMEM((len(distances), 3, tokens, regions, span), jnp.bfloat16),
                pltpu.VMEM((len(distances),) + chunk_shape.shape, jnp.bfloat16),
                pltpu.SemaphoreType.DMA((3 * len(distances),)),
                pltpu.SemaphoreType.DMA((len(distances),)),
            ],
            moved=4 * len(distances) * chunk_shape.size,
            grant=VMEM_WHOLE,
        )(index, query_rows, key_rows, value_rows, *after)

    packed = {}
    for distance, chunk in zip(early, pack("pack_early", early)):
        packed[distance] = trade(chunk, distance)
    for distance, chunk in zip(late, pack("pack_late", late, cot_far)):
        packed[distance] = trade(chunk, distance)
    order = early + late + [0]
    packed[0] = call(
        functools.partial(own_kernel, regions, per_device),
        "own_chunk",
        chunk_shape,
        [SMEM()] + [HBM()] * 3,
        scratch=[
            pltpu.VMEM((3, tokens, regions, span), jnp.bfloat16),
            pltpu.SemaphoreType.DMA((3,)),
        ],
        moved=12 * chunk_shape.size,
    )(index, query_rows, key_rows, value_rows)
    cot_near = jnp.where(odd, cotangent[:, 0], cotangent[:, PATCH - 1])
    cot_near = trade(cot_near, 1)

    items = seq_index * per_device + jnp.arange(per_device, dtype=jnp.int32)
    item_lengths = jnp.sum(
        jnp.where(
            (items % regions)[:, None] == jnp.arange(regions, dtype=jnp.int32)[None, :],
            region_lengths[None, :],
            0,
        ),
        axis=1,
    )
    block_rows = min(256, capacity)
    group = regions if per_device % regions == 0 else per_device
    mixed = call(
        functools.partial(attend_kernel, block_rows, group, order),
        "attend",
        [jax.ShapeDtypeStruct((per_device, tokens, width), jnp.bfloat16)] * seq_count,
        [SMEM(), SMEM()] + [VMEM()] * seq_count,
        flops=4 * per_device * capacity * capacity * width,
        moved=4 * local_bytes,
        exps=per_device * capacity * capacity,
    )(index, item_lengths, *[packed[distance] for distance in order])
    attended = [mixed[0]] + [trade(mixed[distance], distance) for distance in range(1, seq_count)]

    turned = call(
        turn_kernel,
        "turn_cotangent",
        jax.ShapeDtypeStruct((3 * width, cotangent.size // width), jnp.bfloat16),
        [SMEM()] + [VMEM()] * 3,
        moved=8 * cotangent.size,
    )(index, cotangent, cot_near, cot_far)
    chunk_rows = -(-9 * width // (32 * quad_size)) * 16
    half_rows = quad_size * chunk_rows
    pixel_rows = regions * PATCH * columns
    conv_flops = 18 * pixel_rows * width * width
    chunk_moved = 8 * chunk_rows * width
    image, near, far, keep, send = call(
        norm_kernel,
        "norm_and_gradient",
        [jax.ShapeDtypeStruct((regions, PATCH, columns, width), jnp.bfloat16)]
        + [edge_shape] * 2
        + [jax.ShapeDtypeStruct((half_rows, width), jnp.float32)] * 2,
        [SMEM()] * 3 + [VMEM()] * (2 + seq_count),
        scratch=[
            pltpu.VMEM((seq_count,) + mixed[0].shape, jnp.bfloat16),
            pltpu.VMEM((regions, PATCH, columns + 2 * RIM, width), jnp.float32),
            pltpu.VMEM((pixel_rows, 3 * width), jnp.bfloat16),
            pltpu.VMEM((2 * half_rows, width), jnp.float32),
        ],
        flops=conv_flops,
        moved=4 * local_bytes,
    )(region_lengths, index, core, norm_gain.reshape(HEADS, width), turned, *attended)
    chunk_shape = jax.ShapeDtypeStruct((chunk_rows, width), jnp.bfloat16)
    parts = call(
        sum_cores_kernel,
        "sum_cores",
        [chunk_shape] * quad_size,
        [SMEM()] + [VMEM()] * 2,
        scratch=[pltpu.VMEM((half_rows, width), jnp.float32)],
        moved=quad_size * chunk_moved,
    )(quad, keep, trade_cores(send))
    near = trade(near, 1)
    far = lax.ppermute(far, "seq", far_pairs)
    distances = range(1, quad_size)
    plane_sum = call(
        functools.partial(sum_kernel, quad_size, 1.0),
        "sum_chips",
        chunk_shape,
        [VMEM()] * quad_size,
        moved=chunk_moved,
    )(parts[0], *[trade_chips(parts[distance], distance, inner) for distance in distances])
    plane_sums = [plane_sum] + [
        trade(plane_sum, distance) for distance in range(inner, seq_count, inner)
    ]
    decoded, done = call(
        decode_kernel,
        "decode",
        [
            jax.ShapeDtypeStruct(cotangent.shape, jnp.bfloat16),
            jax.ShapeDtypeStruct((8, width), jnp.float32),
        ],
        [SMEM()] + [VMEM()] * 4,
        scratch=[pltpu.VMEM((columns + 2 * RIM, width), jnp.float32)],
        flops=conv_flops,
        moved=2 * local_bytes,
    )(index, image, near, far, conv_weight.reshape(3, 3 * width, width))
    total = call(
        functools.partial(sum_kernel, len(plane_sums), 1.0 / math.sqrt(PATCH * columns)),
        "sum_planes",
        chunk_shape,
        [VMEM()] * len(plane_sums) + [ANY()],
        moved=chunk_moved,
    )(*plane_sums, done)
    joined = call(
        join_kernel,
        "join_chips",
        jax.ShapeDtypeStruct((half_rows, width), jnp.bfloat16),
        [SMEM()] + [VMEM()] * quad_size,
        moved=quad_size * chunk_moved,
    )(quad, total, *[trade_chips(total, distance, inner) for distance in distances])
    weight_grad = call(
        spread_kernel,
        "spread_sums",
        jax.ShapeDtypeStruct((2 * half_rows, width), jnp.float32),
        [SMEM()] + [VMEM()] * 2,
        moved=2 * quad_size * chunk_moved,
    )(core, joined, trade_cores(joined))
    return (decoded, weight_grad[: 9 * width].reshape(conv_weight.shape))


def solution(mesh):
    placed = (
        P("seq", "dp", None),
        P("seq", "dp", None),
        P("seq", "dp", None),
        P("dp"),
        P(),
        P(),
        P("dp", "seq", None, None),
    )
    return jax.shard_map(
        body,
        mesh=mesh,
        in_specs=placed,
        out_specs=(P("dp", "seq", None, None), P()),
        check_vma=False,
    )
```

```python
import functools
import math

import jax
import jax.numpy as jnp
from jax import lax
from jax.experimental import pallas as pl
from jax.experimental.pallas import tpu as pltpu
from jax.sharding import PartitionSpec as P

HEADS = 16
PATCH = 4
RIM = 8
VMEM_LIMIT = 48 * 1024 * 1024
VMEM_WHOLE = 60 * 1024 * 1024

VMEM = functools.partial(pl.BlockSpec, memory_space=pltpu.VMEM)
HBM = functools.partial(pl.BlockSpec, memory_space=pltpu.HBM)
ANY = functools.partial(pl.BlockSpec, memory_space=pl.ANY)
SMEM = functools.partial(pl.BlockSpec, memory_space=pltpu.SMEM)


def call(kernel, name, out_shape, in_specs, out_specs=None, scratch=(), flops=0, moved=0, exps=0, grant=VMEM_LIMIT):
    many = isinstance(out_shape, (list, tuple))
    return pl.pallas_call(
        kernel,
        out_shape=out_shape,
        in_specs=in_specs,
        out_specs=out_specs or ([VMEM() for _ in out_shape] if many else VMEM()),
        scratch_shapes=list(scratch),
        compiler_params=pltpu.CompilerParams(vmem_limit_bytes=grant),
        cost_estimate=pl.CostEstimate(flops=flops, bytes_accessed=moved, transcendentals=exps),
        name=name,
    )


def columns_of(index, distance, regions, per_device, width):
    owner = lax.bitwise_xor(index, distance)
    span = max(1, per_device // regions) * width
    start = lax.div(owner * per_device, regions) * width
    return owner, pl.ds(pl.multiple_of(start, width), span)


def take_items(held, owner, regions, per_device, width, out_ref):
    for head in range(held.shape[2] // width):
        block = held[:, :, head * width : (head + 1) * width].astype(jnp.float32)
        if per_device % regions:
            value = block[:, 0, :]
            for other in range(1, regions):
                value = jnp.where(lax.rem(owner, regions) == other, block[:, other, :], value)
            out_ref[head] = value.astype(jnp.bfloat16)
        else:
            for region in range(regions):
                out_ref[head * regions + region] = block[:, region, :].astype(jnp.bfloat16)


def pack_kernel(distances, regions, per_device, index_ref, query_ref, key_ref, value_ref, *refs):
    held, ready, load_sems, store_sems = refs[-4:]
    width = query_ref.shape[2] // HEADS
    loads = []
    for number, distance in enumerate(distances):
        owner, columns = columns_of(index_ref[0], distance, regions, per_device, width)
        for which, ref in enumerate((query_ref, key_ref, value_ref)):
            load = pltpu.make_async_copy(
                ref.at[:, :, columns], held.at[number, which], load_sems.at[3 * number + which]
            )
            load.start()
            loads.append((number, which, owner, load))
    stores = []
    for number, which, owner, load in loads:
        load.wait()
        take_items(
            held.at[number, which], owner, regions, per_device, width, ready.at[number, which]
        )
        if which == 2:
            store = pltpu.make_async_copy(ready.at[number], refs[number], store_sems.at[number])
            store.start()
            stores.append(store)
    for store in stores:
        store.wait()


def own_kernel(
    regions,
    per_device,
    index_ref,
    query_ref,
    key_ref,
    value_ref,
    near_ref,
    far_ref,
    out_ref,
    near_out_ref,
    far_out_ref,
    held,
    sems,
):
    near_out_ref[...] = near_ref[...]
    far_out_ref[...] = far_ref[...]
    width = out_ref.shape[3]
    owner, columns = columns_of(index_ref[0], 0, regions, per_device, width)
    loads = []
    for which, ref in enumerate((query_ref, key_ref, value_ref)):
        loads.append(
            pltpu.make_async_copy(ref.at[:, :, columns], held.at[which], sems.at[which])
        )
        loads[-1].start()
    for which, load in enumerate(loads):
        load.wait()
        take_items(held.at[which], owner, regions, per_device, width, out_ref.at[which])


def attend_kernel(block_rows, group, order, index_ref, lengths_ref, *refs):
    chunks = dict(zip(order, refs))
    out_refs = refs[len(order) :]
    index = index_ref[0]
    sources = len(chunks)
    _, per_device, tokens, width = chunks[0].shape
    capacity = sources * tokens
    per_block = block_rows // tokens
    blocks = capacity // block_rows
    factor = math.log2(math.e) / math.sqrt(width)
    columns = lax.broadcasted_iota(jnp.int32, (1, capacity), 1)
    slots = columns
    for distance in range(sources):
        here = (columns >= distance * tokens) & (columns < (distance + 1) * tokens)
        moved = (lax.bitwise_xor(index, distance) - distance) * tokens
        slots = jnp.where(here, columns + moved, slots)

    def rows_of(which, item, distances):
        return jnp.concatenate([chunks[distance][which, item] for distance in distances], axis=0)

    def distances_of(block):
        return range(block * per_block, (block + 1) * per_block)

    def start_of(block, span):
        return lax.bitwise_xor(lax.div(index, span), block) * span

    def clear(item, block):
        for distance in distances_of(block):
            out_refs[distance][item] = jnp.zeros((tokens, width), jnp.bfloat16)

    def score(item, block):
        return lax.dot_general(
            rows_of(0, item, distances_of(block)),
            rows_of(1, item, range(sources)),
            (((1,), (1,)), ((), ())),
            preferred_element_type=jnp.float32,
        )

    def finish(item, block, scores, key_valid):
        scores = jnp.where(key_valid, scores * factor, -1e30)
        powers = jnp.exp2(scores - jnp.max(scores, axis=1, keepdims=True))
        totals = jnp.sum(powers, axis=1, keepdims=True)
        mixed = jnp.dot(
            powers.astype(jnp.bfloat16),
            rows_of(2, item, range(sources)),
            preferred_element_type=jnp.float32,
        )
        mixed = (mixed / totals).astype(jnp.bfloat16)
        for number, distance in enumerate(distances_of(block)):
            out_refs[distance][item] = mixed[number * tokens : (number + 1) * tokens]

    def attend(items, live, dead, length):
        key_valid = slots < length
        waiting = None
        for block in live:
            for item in items:
                scores = score(item, block)
                if waiting is not None:
                    finish(*waiting, key_valid)
                waiting = (item, block, scores)
        if waiting is not None:
            finish(*waiting, key_valid)
        for block in dead:
            for item in items:
                clear(item, block)

    for lead in range(group):
        length = lengths_ref[lead]
        items = list(range(lead, per_device, group))
        for block in range(0, blocks, 2):
            pair = list(range(block, min(block + 2, blocks)))
            alive = [length > start_of(one, per_block) * tokens for one in pair]
            for case in range(2 ** len(pair)):
                live = [one for bit, one in enumerate(pair) if case >> bit & 1]
                dead = [one for one in pair if one not in live]
                chosen = None
                for bit in range(len(pair)):
                    test = alive[bit] if case >> bit & 1 else jnp.logical_not(alive[bit])
                    chosen = test if chosen is None else chosen & test

                @pl.when(chosen)
                def _(items=items, live=live, dead=dead, length=length):
                    attend(items, live, dead, length)


def three_windows(padded, columns):
    return jnp.concatenate(
        [padded[RIM - 1 + shift : RIM - 1 + shift + columns].astype(jnp.bfloat16) for shift in range(3)],
        axis=1,
    )


def rows_at(place, rows):
    return pl.ds(pl.multiple_of(place * rows, rows), rows)


def around(odd, near, far):
    return jnp.where(odd == 1, near, far), jnp.where(odd == 1, far, near)


def turn_kernel(index_ref, cot_ref, near_ref, far_ref, out_ref):
    regions, rows, columns, width = cot_ref.shape
    for region in range(regions):
        before, after = around(lax.rem(index_ref[0], 2), near_ref[region], far_ref[region])
        for row in range(-1, rows + 1):
            value = before if row < 0 else after if row == rows else cot_ref[region, row]
            turned = value.T
            for down in range(3):
                image_row = row - 1 + down
                if 0 <= image_row < rows:
                    start = (region * rows + image_row) * columns
                    out_ref[down * width : (down + 1) * width, start : start + columns] = turned


def norm_kernel(lengths_ref, index_ref, core_ref, gain_ref, turned_ref, *refs):
    image_ref, near_ref, far_ref, keep_ref, send_ref, attended, pixels, windows, grads = refs[-9:]
    for distance, ref in enumerate(refs[:-9]):
        attended[lax.bitwise_xor(index_ref[0], distance)] = ref[...]
    heads = gain_ref.shape[0]
    regions = image_ref.shape[0]
    _, per_device, tokens, width = attended.shape

    def load(head, region):
        owner, place = divmod(head * regions + region, per_device)
        return attended[owner, place].astype(jnp.float32)

    columns = tokens * PATCH
    features = heads * width
    odd = lax.rem(index_ref[0], 2)
    position = index_ref[0] * tokens + lax.broadcasted_iota(jnp.int32, (tokens, 1), 0)
    pixels[:, :, :RIM, :] = jnp.zeros((regions, PATCH, RIM, width), jnp.float32)
    pixels[:, :, RIM + columns :, :] = jnp.zeros((regions, PATCH, RIM, width), jnp.float32)
    for region in range(regions):
        total = jnp.zeros((tokens, width), jnp.float32)
        for head in range(heads):
            total = total + load(head, region)
        mean = jnp.sum(total, axis=1, keepdims=True) * (1.0 / features)
        total = jnp.zeros((tokens, width), jnp.float32)
        for head in range(heads):
            centered = load(head, region) - mean
            total = total + centered * centered
        variance = jnp.sum(total, axis=1, keepdims=True) * (1.0 / features)
        spread = lax.rsqrt(variance + 1e-05)
        live = position < lengths_ref[region]
        for head in range(heads):
            centered = load(head, region) - mean
            normed = jnp.where(live, centered * spread * gain_ref[head : head + 1, :], 0.0)
            row, column = divmod(head, PATCH)
            pixels[region, row, pl.ds(RIM + column, tokens, stride=PATCH), :] = normed
        for row in range(PATCH):
            window = three_windows(pixels[region, row], columns)
            image_ref[region, row] = window[:, width : 2 * width]
            start = (region * PATCH + row) * columns
            windows[start : start + columns, :] = window
        near_ref[region] = image_ref[region, (1 - odd) * (PATCH - 1)]
        far_ref[region] = image_ref[region, odd * (PATCH - 1)]
        part = slice(region * PATCH * columns, (region + 1) * PATCH * columns)
        term = jnp.dot(turned_ref[:, part], windows[part, :], preferred_element_type=jnp.float32)
        product = term if region == 0 else product + term
    for down in range(3):
        for across in range(3):
            tap = 3 * down + across
            grads[tap * width : (tap + 1) * width, :] = product[
                down * width : (down + 1) * width, across * width : (across + 1) * width
            ].T
    filled = 9 * width
    if filled < grads.shape[0]:
        grads[filled:, :] = jnp.zeros((grads.shape[0] - filled, width), jnp.float32)
    half = keep_ref.shape[0]
    keep_ref[...] = grads[rows_at(core_ref[0], half), :]
    send_ref[...] = grads[rows_at(1 - core_ref[0], half), :]


def decode_kernel(index_ref, image_ref, near_ref, far_ref, weight_ref, out_ref, done_ref, padded):
    done_ref[...] = jnp.zeros(done_ref.shape, jnp.float32)
    regions, rows, columns, width = image_ref.shape
    padded[:RIM, :] = jnp.zeros((RIM, width), jnp.float32)
    padded[RIM + columns :, :] = jnp.zeros((RIM, width), jnp.float32)
    for region in range(regions):
        strips = []
        before, after = around(lax.rem(index_ref[0], 2), near_ref[region], far_ref[region])
        for row in range(-1, rows + 1):
            if row < 0:
                source = before
            elif row == rows:
                source = after
            else:
                source = image_ref[region, row]
            padded[RIM : RIM + columns, :] = source.astype(jnp.float32)
            strips.append(three_windows(padded[...], columns))
            if len(strips) == 3:
                total = jnp.dot(strips[0], weight_ref[0], preferred_element_type=jnp.float32)
                for down in (1, 2):
                    total = total + jnp.dot(
                        strips[down], weight_ref[down], preferred_element_type=jnp.float32
                    )
                out_ref[region, row - 1] = total.astype(jnp.bfloat16)
                strips.pop(0)


def add_pairs(terms):
    while len(terms) > 1:
        paired = [one + other for one, other in zip(terms[::2], terms[1::2])]
        terms = paired + terms[2 * len(paired) :]
    return terms[0]


def sum_cores_kernel(quad_ref, keep_ref, other_ref, *refs):
    total = refs[-1]
    total[...] = keep_ref[...] + other_ref[...]
    for distance, ref in enumerate(refs[:-1]):
        rows = rows_at(lax.bitwise_xor(quad_ref[0], distance), ref.shape[0])
        ref[...] = total[rows, :].astype(jnp.bfloat16)


def sum_kernel(factor, *refs):
    total = add_pairs([ref[...].astype(jnp.float32) for ref in refs[:-1]])
    refs[-1][...] = (total * factor).astype(jnp.bfloat16)


def join_kernel(quad_ref, done_ref, *refs):
    del done_ref
    for distance, ref in enumerate(refs[:-1]):
        rows = rows_at(lax.bitwise_xor(quad_ref[0], distance), ref.shape[0])
        refs[-1][rows, :] = ref[...]


def spread_kernel(core_ref, own_ref, other_ref, out_ref):
    half = own_ref.shape[0]
    out_ref[rows_at(core_ref[0], half), :] = own_ref[...].astype(jnp.float32)
    out_ref[rows_at(1 - core_ref[0], half), :] = other_ref[...].astype(jnp.float32)


def trade(values, distance):
    pairs = [(i, i ^ distance) for i in range(lax.axis_size("seq"))]
    return lax.ppermute(values, "seq", pairs)


def inner_size(seq_count):
    inner = 1
    while seq_count % (2 * inner) == 0 and (2 * inner) ** 2 <= seq_count:
        inner *= 2
    return inner


def trade_chips(values, distance, inner):
    seq_count = lax.axis_size("seq")
    pairs = []
    for outer in range(lax.axis_size("dp")):
        for seq in range(seq_count):
            chip, lane = divmod((outer // 2 * inner + seq % inner) ^ distance, inner)
            partner = (2 * chip + outer % 2) * seq_count + seq - seq % inner + lane
            pairs.append((outer * seq_count + seq, partner))
    return lax.ppermute(values, ("dp", "seq"), pairs)


def trade_cores(values):
    return lax.ppermute(values, "dp", [(i, i ^ 1) for i in range(lax.axis_size("dp"))])


def body(query_rows, key_rows, value_rows, region_lengths, norm_gain, conv_weight, cotangent):
    tokens, regions, model_width = query_rows.shape
    width = model_width // HEADS
    seq_count = lax.axis_size("seq")
    seq_index = lax.axis_index("seq")
    inner = inner_size(seq_count)
    quad_size = lax.axis_size("dp") // 2 * inner
    dp_index = lax.axis_index("dp")
    lane = lax.bitwise_and(seq_index, inner - 1)
    quad = (lax.shift_right_logical(dp_index, 1) * inner + lane).reshape(1)
    core = lax.bitwise_and(dp_index, 1).reshape(1)
    columns = tokens * PATCH
    capacity = seq_count * tokens
    per_device = regions * HEADS // seq_count
    far_pairs = [(i, i + 1) for i in range(1, seq_count - 1, 2)]
    far_pairs = far_pairs + [(j, i) for i, j in far_pairs]
    local_bytes = 2 * query_rows.size

    edge_shape = jax.ShapeDtypeStruct((regions, columns, width), jnp.bfloat16)
    chunk_shape = jax.ShapeDtypeStruct((3, per_device, tokens, width), jnp.bfloat16)
    index = seq_index.reshape(1)
    odd = lax.bitwise_and(seq_index, 1) == 1
    cot_far = jnp.where(odd, cotangent[:, PATCH - 1], cotangent[:, 0])
    cot_near = jnp.where(odd, cotangent[:, 0], cotangent[:, PATCH - 1])
    half = seq_count // 2
    early = [2, half, half + 1]
    late = [distance for distance in range(1, seq_count) if distance not in early]
    span = max(1, per_device // regions) * width

    def pack(name, distances):
        return call(
            functools.partial(pack_kernel, distances, regions, per_device),
            name,
            [chunk_shape] * len(distances),
            [SMEM()] + [HBM()] * 3,
            out_specs=[HBM()] * len(distances),
            scratch=[
                pltpu.VMEM((len(distances), 3, tokens, regions, span), jnp.bfloat16),
                pltpu.VMEM((len(distances),) + chunk_shape.shape, jnp.bfloat16),
                pltpu.SemaphoreType.DMA((3 * len(distances),)),
                pltpu.SemaphoreType.DMA((len(distances),)),
            ],
            moved=4 * len(distances) * chunk_shape.size,
            grant=VMEM_WHOLE,
        )(index, query_rows, key_rows, value_rows)

    packed = {}
    for distance, chunk in zip(early, pack("pack_early", early)):
        packed[distance] = trade(chunk, distance)
    for distance, chunk in zip(late, pack("pack_late", late)):
        packed[distance] = trade(chunk, distance)
    order = list(range(1, seq_count)) + [0]
    packed[0], cot_near, cot_far = call(
        functools.partial(own_kernel, regions, per_device),
        "own_chunk",
        [chunk_shape, edge_shape, edge_shape],
        [SMEM()] + [HBM()] * 3 + [VMEM()] * 2,
        scratch=[
            pltpu.VMEM((3, tokens, regions, span), jnp.bfloat16),
            pltpu.SemaphoreType.DMA((3,)),
        ],
        moved=12 * chunk_shape.size,
    )(index, query_rows, key_rows, value_rows, cot_near, cot_far)
    cot_near = trade(cot_near, 1)
    cot_far = lax.ppermute(cot_far, "seq", far_pairs)

    items = seq_index * per_device + jnp.arange(per_device, dtype=jnp.int32)
    item_lengths = jnp.sum(
        jnp.where(
            (items % regions)[:, None] == jnp.arange(regions, dtype=jnp.int32)[None, :],
            region_lengths[None, :],
            0,
        ),
        axis=1,
    )
    block_rows = min(256, capacity)
    group = regions if per_device % regions == 0 else per_device
    mixed = call(
        functools.partial(attend_kernel, block_rows, group, order),
        "attend",
        [jax.ShapeDtypeStruct((per_device, tokens, width), jnp.bfloat16)] * seq_count,
        [SMEM(), SMEM()] + [VMEM()] * seq_count,
        flops=4 * per_device * capacity * capacity * width,
        moved=4 * local_bytes,
        exps=per_device * capacity * capacity,
    )(index, item_lengths, *[packed[distance] for distance in order])
    attended = [mixed[0]] + [trade(mixed[distance], distance) for distance in order[:-1]]

    turned = call(
        turn_kernel,
        "turn_cotangent",
        jax.ShapeDtypeStruct((3 * width, cotangent.size // width), jnp.bfloat16),
        [SMEM()] + [VMEM()] * 3,
        moved=8 * cotangent.size,
    )(index, cotangent, cot_near, cot_far)
    chunk_rows = -(-9 * width // (32 * quad_size)) * 16
    half_rows = quad_size * chunk_rows
    pixel_rows = regions * PATCH * columns
    conv_flops = 18 * pixel_rows * width * width
    chunk_moved = 8 * chunk_rows * width
    image, near, far, keep, send = call(
        norm_kernel,
        "norm_and_gradient",
        [jax.ShapeDtypeStruct((regions, PATCH, columns, width), jnp.bfloat16)]
        + [edge_shape] * 2
        + [jax.ShapeDtypeStruct((half_rows, width), jnp.float32)] * 2,
        [SMEM()] * 3 + [VMEM()] * (2 + seq_count),
        scratch=[
            pltpu.VMEM((seq_count,) + mixed[0].shape, jnp.bfloat16),
            pltpu.VMEM((regions, PATCH, columns + 2 * RIM, width), jnp.float32),
            pltpu.VMEM((pixel_rows, 3 * width), jnp.bfloat16),
            pltpu.VMEM((2 * half_rows, width), jnp.float32),
        ],
        flops=conv_flops,
        moved=4 * local_bytes,
    )(region_lengths, index, core, norm_gain.reshape(HEADS, width), turned, *attended)
    chunk_shape = jax.ShapeDtypeStruct((chunk_rows, width), jnp.bfloat16)
    parts = call(
        sum_cores_kernel,
        "sum_cores",
        [chunk_shape] * quad_size,
        [SMEM()] + [VMEM()] * 2,
        scratch=[pltpu.VMEM((half_rows, width), jnp.float32)],
        moved=quad_size * chunk_moved,
    )(quad, keep, trade_cores(send))
    near = trade(near, 1)
    far = lax.ppermute(far, "seq", far_pairs)
    distances = range(1, quad_size)
    plane_sum = call(
        functools.partial(sum_kernel, 1.0),
        "sum_chips",
        chunk_shape,
        [VMEM()] * quad_size,
        moved=chunk_moved,
    )(parts[0], *[trade_chips(parts[distance], distance, inner) for distance in distances])
    plane_sums = [plane_sum] + [
        trade(plane_sum, distance) for distance in range(inner, seq_count, inner)
    ]
    decoded, done = call(
        decode_kernel,
        "decode",
        [
            jax.ShapeDtypeStruct(cotangent.shape, jnp.bfloat16),
            jax.ShapeDtypeStruct((8, width), jnp.float32),
        ],
        [SMEM()] + [VMEM()] * 4,
        scratch=[pltpu.VMEM((columns + 2 * RIM, width), jnp.float32)],
        flops=conv_flops,
        moved=2 * local_bytes,
    )(index, image, near, far, conv_weight.reshape(3, 3 * width, width))
    total = call(
        functools.partial(sum_kernel, 1.0 / math.sqrt(PATCH * columns)),
        "sum_planes",
        chunk_shape,
        [VMEM()] * len(plane_sums),
        moved=chunk_moved,
    )(*plane_sums)
    joined = call(
        join_kernel,
        "join_chips",
        jax.ShapeDtypeStruct((half_rows, width), jnp.bfloat16),
        [SMEM(), ANY()] + [VMEM()] * quad_size,
        moved=quad_size * chunk_moved,
    )(quad, done, total, *[trade_chips(total, distance, inner) for distance in distances])
    weight_grad = call(
        spread_kernel,
        "spread_sums",
        jax.ShapeDtypeStruct((2 * half_rows, width), jnp.float32),
        [SMEM()] + [VMEM()] * 2,
        moved=2 * quad_size * chunk_moved,
    )(core, joined, trade_cores(joined))
    return (decoded, weight_grad[: 9 * width].reshape(conv_weight.shape))


def solution(mesh):
    placed = (
        P("seq", "dp", None),
        P("seq", "dp", None),
        P("seq", "dp", None),
        P("dp"),
        P(),
        P(),
        P("dp", "seq", None, None),
    )
    return jax.shard_map(
        body,
        mesh=mesh,
        in_specs=placed,
        out_specs=(P("dp", "seq", None, None), P()),
        check_vma=False,
    )
```

```python
import functools
import math

import jax
import jax.numpy as jnp
from jax import lax
from jax.experimental import pallas as pl
from jax.experimental.pallas import tpu as pltpu
from jax.sharding import PartitionSpec as P

HEADS = 16
PATCH = 4
RIM = 8
VMEM_LIMIT = 48 * 1024 * 1024
VMEM_WHOLE = 60 * 1024 * 1024

VMEM = functools.partial(pl.BlockSpec, memory_space=pltpu.VMEM)
HBM = functools.partial(pl.BlockSpec, memory_space=pltpu.HBM)
ANY = functools.partial(pl.BlockSpec, memory_space=pl.ANY)
SMEM = functools.partial(pl.BlockSpec, memory_space=pltpu.SMEM)


def call(kernel, name, out_shape, in_specs, out_specs=None, scratch=(), flops=0, moved=0, exps=0, grant=VMEM_LIMIT):
    many = isinstance(out_shape, (list, tuple))
    return pl.pallas_call(
        kernel,
        out_shape=out_shape,
        in_specs=in_specs,
        out_specs=out_specs or ([VMEM() for _ in out_shape] if many else VMEM()),
        scratch_shapes=list(scratch),
        compiler_params=pltpu.CompilerParams(vmem_limit_bytes=grant),
        cost_estimate=pl.CostEstimate(flops=flops, bytes_accessed=moved, transcendentals=exps),
        name=name,
    )


def columns_of(index, distance, regions, per_device, width):
    owner = lax.bitwise_xor(index, distance)
    span = max(1, per_device // regions) * width
    start = lax.div(owner * per_device, regions) * width
    return owner, pl.ds(pl.multiple_of(start, width), span)


def take_items(held, owner, regions, per_device, width, out_ref):
    for head in range(held.shape[2] // width):
        block = held[:, :, head * width : (head + 1) * width].astype(jnp.float32)
        if per_device % regions:
            value = block[:, 0, :]
            for other in range(1, regions):
                value = jnp.where(lax.rem(owner, regions) == other, block[:, other, :], value)
            out_ref[head] = value.astype(jnp.bfloat16)
        else:
            for region in range(regions):
                out_ref[head * regions + region] = block[:, region, :].astype(jnp.bfloat16)


def pack_kernel(distances, regions, per_device, index_ref, query_ref, key_ref, value_ref, *refs):
    held, ready, load_sems, store_sems = refs[-4:]
    width = query_ref.shape[2] // HEADS
    loads = []
    for number, distance in enumerate(distances):
        owner, columns = columns_of(index_ref[0], distance, regions, per_device, width)
        for which, ref in enumerate((query_ref, key_ref, value_ref)):
            load = pltpu.make_async_copy(
                ref.at[:, :, columns], held.at[number, which], load_sems.at[3 * number + which]
            )
            load.start()
            loads.append((number, which, owner, load))
    stores = []
    for number, which, owner, load in loads:
        load.wait()
        take_items(
            held.at[number, which], owner, regions, per_device, width, ready.at[number, which]
        )
        if which == 2:
            store = pltpu.make_async_copy(ready.at[number], refs[number], store_sems.at[number])
            store.start()
            stores.append(store)
    for store in stores:
        store.wait()


def own_kernel(
    regions,
    per_device,
    index_ref,
    query_ref,
    key_ref,
    value_ref,
    near_ref,
    far_ref,
    out_ref,
    near_out_ref,
    far_out_ref,
    held,
    sems,
):
    near_out_ref[...] = near_ref[...]
    far_out_ref[...] = far_ref[...]
    width = out_ref.shape[3]
    owner, columns = columns_of(index_ref[0], 0, regions, per_device, width)
    loads = []
    for which, ref in enumerate((query_ref, key_ref, value_ref)):
        loads.append(
            pltpu.make_async_copy(ref.at[:, :, columns], held.at[which], sems.at[which])
        )
        loads[-1].start()
    for which, load in enumerate(loads):
        load.wait()
        take_items(held.at[which], owner, regions, per_device, width, out_ref.at[which])


def attend_kernel(block_rows, group, order, index_ref, lengths_ref, *refs):
    chunks = dict(zip(order, refs))
    out_refs = refs[len(order) :]
    index = index_ref[0]
    sources = len(chunks)
    _, per_device, tokens, width = chunks[0].shape
    capacity = sources * tokens
    per_block = block_rows // tokens
    blocks = capacity // block_rows
    factor = math.log2(math.e) / math.sqrt(width)
    columns = lax.broadcasted_iota(jnp.int32, (1, capacity), 1)
    slots = columns
    for distance in range(sources):
        here = (columns >= distance * tokens) & (columns < (distance + 1) * tokens)
        moved = (lax.bitwise_xor(index, distance) - distance) * tokens
        slots = jnp.where(here, columns + moved, slots)

    def rows_of(which, item, distances):
        return jnp.concatenate([chunks[distance][which, item] for distance in distances], axis=0)

    def distances_of(block):
        return range(block * per_block, (block + 1) * per_block)

    def start_of(block, span):
        return lax.bitwise_xor(lax.div(index, span), block) * span

    def clear(item, block):
        for distance in distances_of(block):
            out_refs[distance][item] = jnp.zeros((tokens, width), jnp.bfloat16)

    def score(item, block):
        return lax.dot_general(
            rows_of(0, item, distances_of(block)),
            rows_of(1, item, range(sources)),
            (((1,), (1,)), ((), ())),
            preferred_element_type=jnp.float32,
        )

    def finish(item, block, scores, key_valid):
        scores = jnp.where(key_valid, scores * factor, -1e30)
        powers = jnp.exp2(scores - jnp.max(scores, axis=1, keepdims=True))
        totals = jnp.sum(powers, axis=1, keepdims=True)
        mixed = jnp.dot(
            powers.astype(jnp.bfloat16),
            rows_of(2, item, range(sources)),
            preferred_element_type=jnp.float32,
        )
        mixed = (mixed / totals).astype(jnp.bfloat16)
        for number, distance in enumerate(distances_of(block)):
            out_refs[distance][item] = mixed[number * tokens : (number + 1) * tokens]

    def attend(items, live, dead, length):
        key_valid = slots < length
        waiting = None
        for block in live:
            for item in items:
                scores = score(item, block)
                if waiting is not None:
                    finish(*waiting, key_valid)
                waiting = (item, block, scores)
        if waiting is not None:
            finish(*waiting, key_valid)
        for block in dead:
            for item in items:
                clear(item, block)

    for lead in range(group):
        length = lengths_ref[lead]
        items = list(range(lead, per_device, group))
        for block in range(0, blocks, 2):
            pair = list(range(block, min(block + 2, blocks)))
            alive = [length > start_of(one, per_block) * tokens for one in pair]
            for case in range(2 ** len(pair)):
                live = [one for bit, one in enumerate(pair) if case >> bit & 1]
                dead = [one for one in pair if one not in live]
                chosen = None
                for bit in range(len(pair)):
                    test = alive[bit] if case >> bit & 1 else jnp.logical_not(alive[bit])
                    chosen = test if chosen is None else chosen & test

                @pl.when(chosen)
                def _(items=items, live=live, dead=dead, length=length):
                    attend(items, live, dead, length)


def three_windows(padded, columns):
    return jnp.concatenate(
        [padded[RIM - 1 + shift : RIM - 1 + shift + columns].astype(jnp.bfloat16) for shift in range(3)],
        axis=1,
    )


def rows_at(place, rows):
    return pl.ds(pl.multiple_of(place * rows, rows), rows)


def around(odd, near, far):
    return jnp.where(odd == 1, near, far), jnp.where(odd == 1, far, near)


def turn_kernel(index_ref, cot_ref, near_ref, far_ref, out_ref):
    regions, rows, columns, width = cot_ref.shape
    for region in range(regions):
        before, after = around(lax.rem(index_ref[0], 2), near_ref[region], far_ref[region])
        for row in range(-1, rows + 1):
            value = before if row < 0 else after if row == rows else cot_ref[region, row]
            turned = value.T
            for down in range(3):
                image_row = row - 1 + down
                if 0 <= image_row < rows:
                    start = (region * rows + image_row) * columns
                    out_ref[down * width : (down + 1) * width, start : start + columns] = turned


def norm_kernel(lengths_ref, index_ref, core_ref, gain_ref, turned_ref, *refs):
    image_ref, near_ref, far_ref, keep_ref, send_ref, attended, pixels, windows, grads = refs[-9:]
    for distance, ref in enumerate(refs[:-9]):
        attended[lax.bitwise_xor(index_ref[0], distance)] = ref[...]
    heads = gain_ref.shape[0]
    regions = image_ref.shape[0]
    _, per_device, tokens, width = attended.shape

    def load(head, region):
        owner, place = divmod(head * regions + region, per_device)
        return attended[owner, place].astype(jnp.float32)

    columns = tokens * PATCH
    features = heads * width
    odd = lax.rem(index_ref[0], 2)
    position = index_ref[0] * tokens + lax.broadcasted_iota(jnp.int32, (tokens, 1), 0)
    pixels[:, :, :RIM, :] = jnp.zeros((regions, PATCH, RIM, width), jnp.float32)
    pixels[:, :, RIM + columns :, :] = jnp.zeros((regions, PATCH, RIM, width), jnp.float32)
    for region in range(regions):
        total = jnp.zeros((tokens, width), jnp.float32)
        for head in range(heads):
            total = total + load(head, region)
        mean = jnp.sum(total, axis=1, keepdims=True) * (1.0 / features)
        total = jnp.zeros((tokens, width), jnp.float32)
        for head in range(heads):
            centered = load(head, region) - mean
            total = total + centered * centered
        variance = jnp.sum(total, axis=1, keepdims=True) * (1.0 / features)
        spread = lax.rsqrt(variance + 1e-05)
        live = position < lengths_ref[region]
        for head in range(heads):
            centered = load(head, region) - mean
            normed = jnp.where(live, centered * spread * gain_ref[head : head + 1, :], 0.0)
            row, column = divmod(head, PATCH)
            pixels[region, row, pl.ds(RIM + column, tokens, stride=PATCH), :] = normed
        for row in range(PATCH):
            window = three_windows(pixels[region, row], columns)
            image_ref[region, row] = window[:, width : 2 * width]
            start = (region * PATCH + row) * columns
            windows[start : start + columns, :] = window
        near_ref[region] = image_ref[region, (1 - odd) * (PATCH - 1)]
        far_ref[region] = image_ref[region, odd * (PATCH - 1)]
        part = slice(region * PATCH * columns, (region + 1) * PATCH * columns)
        term = jnp.dot(turned_ref[:, part], windows[part, :], preferred_element_type=jnp.float32)
        product = term if region == 0 else product + term
    for down in range(3):
        for across in range(3):
            tap = 3 * down + across
            grads[tap * width : (tap + 1) * width, :] = product[
                down * width : (down + 1) * width, across * width : (across + 1) * width
            ].T
    filled = 9 * width
    if filled < grads.shape[0]:
        grads[filled:, :] = jnp.zeros((grads.shape[0] - filled, width), jnp.float32)
    half = keep_ref.shape[0]
    keep_ref[...] = grads[rows_at(core_ref[0], half), :]
    send_ref[...] = grads[rows_at(1 - core_ref[0], half), :]


def decode_kernel(index_ref, image_ref, near_ref, far_ref, weight_ref, out_ref, done_ref, padded):
    done_ref[...] = jnp.zeros(done_ref.shape, jnp.float32)
    regions, rows, columns, width = image_ref.shape
    padded[:RIM, :] = jnp.zeros((RIM, width), jnp.float32)
    padded[RIM + columns :, :] = jnp.zeros((RIM, width), jnp.float32)
    for region in range(regions):
        strips = []
        before, after = around(lax.rem(index_ref[0], 2), near_ref[region], far_ref[region])
        for row in range(-1, rows + 1):
            if row < 0:
                source = before
            elif row == rows:
                source = after
            else:
                source = image_ref[region, row]
            padded[RIM : RIM + columns, :] = source.astype(jnp.float32)
            strips.append(three_windows(padded[...], columns))
            if len(strips) == 3:
                total = jnp.dot(strips[0], weight_ref[0], preferred_element_type=jnp.float32)
                for down in (1, 2):
                    total = total + jnp.dot(
                        strips[down], weight_ref[down], preferred_element_type=jnp.float32
                    )
                out_ref[region, row - 1] = total.astype(jnp.bfloat16)
                strips.pop(0)


def add_pairs(terms):
    while len(terms) > 1:
        paired = [one + other for one, other in zip(terms[::2], terms[1::2])]
        terms = paired + terms[2 * len(paired) :]
    return terms[0]


def hold_kernel(value_ref, after_ref, out_ref):
    del after_ref
    out_ref[...] = value_ref[...]


def hold(value, after):
    return call(
        hold_kernel,
        "hold",
        jax.ShapeDtypeStruct(value.shape, value.dtype),
        [VMEM(), ANY()],
        moved=4 * value.size,
    )(value, after)


def sum_cores_kernel(quad_ref, keep_ref, other_ref, *refs):
    total = refs[-1]
    total[...] = keep_ref[...] + other_ref[...]
    for distance, ref in enumerate(refs[:-1]):
        rows = rows_at(lax.bitwise_xor(quad_ref[0], distance), ref.shape[0])
        ref[...] = total[rows, :].astype(jnp.bfloat16)


def sum_kernel(factor, *refs):
    total = add_pairs([ref[...].astype(jnp.float32) for ref in refs[:-1]])
    refs[-1][...] = (total * factor).astype(jnp.bfloat16)


def join_kernel(quad_ref, done_ref, *refs):
    del done_ref
    for distance, ref in enumerate(refs[:-1]):
        rows = rows_at(lax.bitwise_xor(quad_ref[0], distance), ref.shape[0])
        refs[-1][rows, :] = ref[...]


def spread_kernel(core_ref, own_ref, other_ref, out_ref):
    half = own_ref.shape[0]
    out_ref[rows_at(core_ref[0], half), :] = own_ref[...].astype(jnp.float32)
    out_ref[rows_at(1 - core_ref[0], half), :] = other_ref[...].astype(jnp.float32)


def trade(values, distance):
    pairs = [(i, i ^ distance) for i in range(lax.axis_size("seq"))]
    return lax.ppermute(values, "seq", pairs)


def inner_size(seq_count):
    inner = 1
    while seq_count % (2 * inner) == 0 and (2 * inner) ** 2 <= seq_count:
        inner *= 2
    return inner


def trade_chips(values, distance, inner):
    seq_count = lax.axis_size("seq")
    pairs = []
    for outer in range(lax.axis_size("dp")):
        for seq in range(seq_count):
            chip, lane = divmod((outer // 2 * inner + seq % inner) ^ distance, inner)
            partner = (2 * chip + outer % 2) * seq_count + seq - seq % inner + lane
            pairs.append((outer * seq_count + seq, partner))
    return lax.ppermute(values, ("dp", "seq"), pairs)


def trade_cores(values):
    return lax.ppermute(values, "dp", [(i, i ^ 1) for i in range(lax.axis_size("dp"))])


def body(query_rows, key_rows, value_rows, region_lengths, norm_gain, conv_weight, cotangent):
    tokens, regions, model_width = query_rows.shape
    width = model_width // HEADS
    seq_count = lax.axis_size("seq")
    seq_index = lax.axis_index("seq")
    inner = inner_size(seq_count)
    quad_size = lax.axis_size("dp") // 2 * inner
    dp_index = lax.axis_index("dp")
    lane = lax.bitwise_and(seq_index, inner - 1)
    quad = (lax.shift_right_logical(dp_index, 1) * inner + lane).reshape(1)
    core = lax.bitwise_and(dp_index, 1).reshape(1)
    columns = tokens * PATCH
    capacity = seq_count * tokens
    per_device = regions * HEADS // seq_count
    far_pairs = [(i, i + 1) for i in range(1, seq_count - 1, 2)]
    far_pairs = far_pairs + [(j, i) for i, j in far_pairs]
    local_bytes = 2 * query_rows.size

    edge_shape = jax.ShapeDtypeStruct((regions, columns, width), jnp.bfloat16)
    chunk_shape = jax.ShapeDtypeStruct((3, per_device, tokens, width), jnp.bfloat16)
    index = seq_index.reshape(1)
    odd = lax.bitwise_and(seq_index, 1) == 1
    cot_far = jnp.where(odd, cotangent[:, PATCH - 1], cotangent[:, 0])
    cot_near = jnp.where(odd, cotangent[:, 0], cotangent[:, PATCH - 1])
    half = seq_count // 2
    early = [2, half, half + 1]
    late = [distance for distance in range(1, seq_count) if distance not in early]
    span = max(1, per_device // regions) * width

    def pack(name, distances):
        return call(
            functools.partial(pack_kernel, distances, regions, per_device),
            name,
            [chunk_shape] * len(distances),
            [SMEM()] + [HBM()] * 3,
            out_specs=[HBM()] * len(distances),
            scratch=[
                pltpu.VMEM((len(distances), 3, tokens, regions, span), jnp.bfloat16),
                pltpu.VMEM((len(distances),) + chunk_shape.shape, jnp.bfloat16),
                pltpu.SemaphoreType.DMA((3 * len(distances),)),
                pltpu.SemaphoreType.DMA((len(distances),)),
            ],
            moved=4 * len(distances) * chunk_shape.size,
            grant=VMEM_WHOLE,
        )(index, query_rows, key_rows, value_rows)

    packed = {}
    for distance, chunk in zip(early, pack("pack_early", early)):
        packed[distance] = trade(chunk, distance)
    for distance, chunk in zip(late, pack("pack_late", late)):
        packed[distance] = trade(chunk, distance)
    order = list(range(1, seq_count)) + [0]
    packed[0], cot_near, cot_far = call(
        functools.partial(own_kernel, regions, per_device),
        "own_chunk",
        [chunk_shape, edge_shape, edge_shape],
        [SMEM()] + [HBM()] * 3 + [VMEM()] * 2,
        scratch=[
            pltpu.VMEM((3, tokens, regions, span), jnp.bfloat16),
            pltpu.SemaphoreType.DMA((3,)),
        ],
        moved=12 * chunk_shape.size,
    )(index, query_rows, key_rows, value_rows, cot_near, cot_far)
    cot_near = trade(cot_near, 1)
    cot_far = lax.ppermute(cot_far, "seq", far_pairs)

    items = seq_index * per_device + jnp.arange(per_device, dtype=jnp.int32)
    item_lengths = jnp.sum(
        jnp.where(
            (items % regions)[:, None] == jnp.arange(regions, dtype=jnp.int32)[None, :],
            region_lengths[None, :],
            0,
        ),
        axis=1,
    )
    block_rows = min(256, capacity)
    group = regions if per_device % regions == 0 else per_device
    mixed = call(
        functools.partial(attend_kernel, block_rows, group, order),
        "attend",
        [jax.ShapeDtypeStruct((per_device, tokens, width), jnp.bfloat16)] * seq_count,
        [SMEM(), SMEM()] + [VMEM()] * seq_count,
        flops=4 * per_device * capacity * capacity * width,
        moved=4 * local_bytes,
        exps=per_device * capacity * capacity,
    )(index, item_lengths, *[packed[distance] for distance in order])
    attended = [mixed[0]] + [trade(mixed[distance], distance) for distance in order[:-1]]

    turned = call(
        turn_kernel,
        "turn_cotangent",
        jax.ShapeDtypeStruct((3 * width, cotangent.size // width), jnp.bfloat16),
        [SMEM()] + [VMEM()] * 3,
        moved=8 * cotangent.size,
    )(index, cotangent, cot_near, cot_far)
    chunk_rows = -(-9 * width // (32 * quad_size)) * 16
    half_rows = quad_size * chunk_rows
    pixel_rows = regions * PATCH * columns
    conv_flops = 18 * pixel_rows * width * width
    chunk_moved = 8 * chunk_rows * width
    image, near, far, keep, send = call(
        norm_kernel,
        "norm_and_gradient",
        [jax.ShapeDtypeStruct((regions, PATCH, columns, width), jnp.bfloat16)]
        + [edge_shape] * 2
        + [jax.ShapeDtypeStruct((half_rows, width), jnp.float32)] * 2,
        [SMEM()] * 3 + [VMEM()] * (2 + seq_count),
        scratch=[
            pltpu.VMEM((seq_count,) + mixed[0].shape, jnp.bfloat16),
            pltpu.VMEM((regions, PATCH, columns + 2 * RIM, width), jnp.float32),
            pltpu.VMEM((pixel_rows, 3 * width), jnp.bfloat16),
            pltpu.VMEM((2 * half_rows, width), jnp.float32),
        ],
        flops=conv_flops,
        moved=4 * local_bytes,
    )(region_lengths, index, core, norm_gain.reshape(HEADS, width), turned, *attended)
    chunk_shape = jax.ShapeDtypeStruct((chunk_rows, width), jnp.bfloat16)
    parts = call(
        sum_cores_kernel,
        "sum_cores",
        [chunk_shape] * quad_size,
        [SMEM()] + [VMEM()] * 2,
        scratch=[pltpu.VMEM((half_rows, width), jnp.float32)],
        moved=quad_size * chunk_moved,
    )(quad, keep, trade_cores(send))
    near = trade(near, 1)
    distances = range(1, quad_size)
    parts = [parts[0]] + [trade_chips(parts[distance], distance, inner) for distance in distances]
    plane_sum = call(
        functools.partial(sum_kernel, 1.0),
        "sum_chips",
        chunk_shape,
        [VMEM()] * quad_size,
        moved=chunk_moved,
    )(*parts)
    far = lax.ppermute(hold(far, plane_sum), "seq", far_pairs)
    plane_sums = [plane_sum] + [
        trade(plane_sum, distance) for distance in range(inner, seq_count, inner)
    ]
    decoded, done = call(
        decode_kernel,
        "decode",
        [
            jax.ShapeDtypeStruct(cotangent.shape, jnp.bfloat16),
            jax.ShapeDtypeStruct((8, width), jnp.float32),
        ],
        [SMEM()] + [VMEM()] * 4,
        scratch=[pltpu.VMEM((columns + 2 * RIM, width), jnp.float32)],
        flops=conv_flops,
        moved=2 * local_bytes,
    )(index, image, near, far, conv_weight.reshape(3, 3 * width, width))
    total = call(
        functools.partial(sum_kernel, 1.0 / math.sqrt(PATCH * columns)),
        "sum_planes",
        chunk_shape,
        [VMEM()] * len(plane_sums),
        moved=chunk_moved,
    )(*plane_sums)
    joined = call(
        join_kernel,
        "join_chips",
        jax.ShapeDtypeStruct((half_rows, width), jnp.bfloat16),
        [SMEM(), ANY()] + [VMEM()] * quad_size,
        moved=quad_size * chunk_moved,
    )(quad, done, total, *[trade_chips(total, distance, inner) for distance in distances])
    weight_grad = call(
        spread_kernel,
        "spread_sums",
        jax.ShapeDtypeStruct((2 * half_rows, width), jnp.float32),
        [SMEM()] + [VMEM()] * 2,
        moved=2 * quad_size * chunk_moved,
    )(core, joined, trade_cores(joined))
    return (decoded, weight_grad[: 9 * width].reshape(conv_weight.shape))


def solution(mesh):
    placed = (
        P("seq", "dp", None),
        P("seq", "dp", None),
        P("seq", "dp", None),
        P("dp"),
        P(),
        P(),
        P("dp", "seq", None, None),
    )
    return jax.shard_map(
        body,
        mesh=mesh,
        in_specs=placed,
        out_specs=(P("dp", "seq", None, None), P()),
        check_vma=False,
    )
```

```python
import functools
import math

import jax
import jax.numpy as jnp
from jax import lax
from jax.experimental import pallas as pl
from jax.experimental.pallas import tpu as pltpu
from jax.sharding import PartitionSpec as P

HEADS = 16
PATCH = 4
RIM = 8
VMEM_LIMIT = 48 * 1024 * 1024
VMEM_WHOLE = 60 * 1024 * 1024

VMEM = functools.partial(pl.BlockSpec, memory_space=pltpu.VMEM)
HBM = functools.partial(pl.BlockSpec, memory_space=pltpu.HBM)
ANY = functools.partial(pl.BlockSpec, memory_space=pl.ANY)
SMEM = functools.partial(pl.BlockSpec, memory_space=pltpu.SMEM)


def call(kernel, name, out_shape, in_specs, out_specs=None, scratch=(), flops=0, moved=0, exps=0, grant=VMEM_LIMIT):
    many = isinstance(out_shape, (list, tuple))
    return pl.pallas_call(
        kernel,
        out_shape=out_shape,
        in_specs=in_specs,
        out_specs=out_specs or ([VMEM() for _ in out_shape] if many else VMEM()),
        scratch_shapes=list(scratch),
        compiler_params=pltpu.CompilerParams(vmem_limit_bytes=grant),
        cost_estimate=pl.CostEstimate(flops=flops, bytes_accessed=moved, transcendentals=exps),
        name=name,
    )


def columns_of(index, distance, regions, per_device, width):
    owner = lax.bitwise_xor(index, distance)
    span = max(1, per_device // regions) * width
    start = lax.div(owner * per_device, regions) * width
    return owner, pl.ds(pl.multiple_of(start, width), span)


def take_items(held, owner, regions, per_device, width, out_ref):
    for head in range(held.shape[2] // width):
        block = held[:, :, head * width : (head + 1) * width].astype(jnp.float32)
        if per_device % regions:
            value = block[:, 0, :]
            for other in range(1, regions):
                value = jnp.where(lax.rem(owner, regions) == other, block[:, other, :], value)
            out_ref[head] = value.astype(jnp.bfloat16)
        else:
            for region in range(regions):
                out_ref[head * regions + region] = block[:, region, :].astype(jnp.bfloat16)


def pack_kernel(distances, regions, per_device, index_ref, query_ref, key_ref, value_ref, *refs):
    held, ready, load_sems, store_sems = refs[-4:]
    width = query_ref.shape[2] // HEADS
    loads = []
    for number, distance in enumerate(distances):
        owner, columns = columns_of(index_ref[0], distance, regions, per_device, width)
        for which, ref in enumerate((query_ref, key_ref, value_ref)):
            load = pltpu.make_async_copy(
                ref.at[:, :, columns], held.at[number, which], load_sems.at[3 * number + which]
            )
            load.start()
            loads.append((number, which, owner, load))
    stores = []
    for number, which, owner, load in loads:
        load.wait()
        take_items(
            held.at[number, which], owner, regions, per_device, width, ready.at[number, which]
        )
        if which == 2:
            store = pltpu.make_async_copy(ready.at[number], refs[number], store_sems.at[number])
            store.start()
            stores.append(store)
    for store in stores:
        store.wait()


def own_kernel(
    regions,
    per_device,
    index_ref,
    query_ref,
    key_ref,
    value_ref,
    near_ref,
    far_ref,
    out_ref,
    near_out_ref,
    far_out_ref,
    held,
    sems,
):
    near_out_ref[...] = near_ref[...]
    far_out_ref[...] = far_ref[...]
    width = out_ref.shape[3]
    owner, columns = columns_of(index_ref[0], 0, regions, per_device, width)
    loads = []
    for which, ref in enumerate((query_ref, key_ref, value_ref)):
        loads.append(
            pltpu.make_async_copy(ref.at[:, :, columns], held.at[which], sems.at[which])
        )
        loads[-1].start()
    for which, load in enumerate(loads):
        load.wait()
        take_items(held.at[which], owner, regions, per_device, width, out_ref.at[which])


def attend_kernel(block_rows, group, order, index_ref, lengths_ref, *refs):
    chunks = dict(zip(order, refs))
    out_refs = refs[len(order) :]
    index = index_ref[0]
    sources = len(chunks)
    _, per_device, tokens, width = chunks[0].shape
    capacity = sources * tokens
    per_block = block_rows // tokens
    blocks = capacity // block_rows
    factor = math.log2(math.e) / math.sqrt(width)
    columns = lax.broadcasted_iota(jnp.int32, (1, capacity), 1)
    slots = columns
    for distance in range(sources):
        here = (columns >= distance * tokens) & (columns < (distance + 1) * tokens)
        moved = (lax.bitwise_xor(index, distance) - distance) * tokens
        slots = jnp.where(here, columns + moved, slots)

    def rows_of(which, item, distances):
        return jnp.concatenate([chunks[distance][which, item] for distance in distances], axis=0)

    def distances_of(block):
        return range(block * per_block, (block + 1) * per_block)

    def start_of(block, span):
        return lax.bitwise_xor(lax.div(index, span), block) * span

    def clear(item, block):
        for distance in distances_of(block):
            out_refs[distance][item] = jnp.zeros((tokens, width), jnp.bfloat16)

    def score(item, block):
        return lax.dot_general(
            rows_of(0, item, distances_of(block)),
            rows_of(1, item, range(sources)),
            (((1,), (1,)), ((), ())),
            preferred_element_type=jnp.float32,
        )

    def finish(item, block, scores, key_valid):
        scores = jnp.where(key_valid, scores * factor, -1e30)
        powers = jnp.exp2(scores - jnp.max(scores, axis=1, keepdims=True))
        totals = jnp.sum(powers, axis=1, keepdims=True)
        mixed = jnp.dot(
            powers.astype(jnp.bfloat16),
            rows_of(2, item, range(sources)),
            preferred_element_type=jnp.float32,
        )
        mixed = (mixed / totals).astype(jnp.bfloat16)
        for number, distance in enumerate(distances_of(block)):
            out_refs[distance][item] = mixed[number * tokens : (number + 1) * tokens]

    def attend(items, live, dead, length):
        key_valid = slots < length
        waiting = None
        for block in live:
            for item in items:
                scores = score(item, block)
                if waiting is not None:
                    finish(*waiting, key_valid)
                waiting = (item, block, scores)
        if waiting is not None:
            finish(*waiting, key_valid)
        for block in dead:
            for item in items:
                clear(item, block)

    for lead in range(group):
        length = lengths_ref[lead]
        items = list(range(lead, per_device, group))
        for block in range(0, blocks, 2):
            pair = list(range(block, min(block + 2, blocks)))
            alive = [length > start_of(one, per_block) * tokens for one in pair]
            for case in range(2 ** len(pair)):
                live = [one for bit, one in enumerate(pair) if case >> bit & 1]
                dead = [one for one in pair if one not in live]
                chosen = None
                for bit in range(len(pair)):
                    test = alive[bit] if case >> bit & 1 else jnp.logical_not(alive[bit])
                    chosen = test if chosen is None else chosen & test

                @pl.when(chosen)
                def _(items=items, live=live, dead=dead, length=length):
                    attend(items, live, dead, length)


def three_windows(padded, columns):
    return jnp.concatenate(
        [padded[RIM - 1 + shift : RIM - 1 + shift + columns].astype(jnp.bfloat16) for shift in range(3)],
        axis=1,
    )


def rows_at(place, rows):
    return pl.ds(pl.multiple_of(place * rows, rows), rows)


def around(odd, near, far):
    return jnp.where(odd == 1, near, far), jnp.where(odd == 1, far, near)


def turn_kernel(index_ref, cot_ref, near_ref, far_ref, out_ref):
    regions, rows, columns, width = cot_ref.shape
    for region in range(regions):
        before, after = around(lax.rem(index_ref[0], 2), near_ref[region], far_ref[region])
        for row in range(-1, rows + 1):
            value = before if row < 0 else after if row == rows else cot_ref[region, row]
            turned = value.T
            for down in range(3):
                image_row = row - 1 + down
                if 0 <= image_row < rows:
                    start = (region * rows + image_row) * columns
                    out_ref[down * width : (down + 1) * width, start : start + columns] = turned


def norm_kernel(order, lengths_ref, index_ref, core_ref, gain_ref, turned_ref, *refs):
    image_ref, near_ref, far_ref, keep_ref, send_ref, attended, pixels, windows, grads = refs[-9:]
    for distance, ref in zip(order, refs):
        attended[lax.bitwise_xor(index_ref[0], distance)] = ref[...]
    heads = gain_ref.shape[0]
    regions = image_ref.shape[0]
    _, per_device, tokens, width = attended.shape

    def load(head, region):
        owner, place = divmod(head * regions + region, per_device)
        return attended[owner, place].astype(jnp.float32)

    columns = tokens * PATCH
    features = heads * width
    odd = lax.rem(index_ref[0], 2)
    position = index_ref[0] * tokens + lax.broadcasted_iota(jnp.int32, (tokens, 1), 0)
    pixels[:, :, :RIM, :] = jnp.zeros((regions, PATCH, RIM, width), jnp.float32)
    pixels[:, :, RIM + columns :, :] = jnp.zeros((regions, PATCH, RIM, width), jnp.float32)
    for region in range(regions):
        total = jnp.zeros((tokens, width), jnp.float32)
        for head in range(heads):
            total = total + load(head, region)
        mean = jnp.sum(total, axis=1, keepdims=True) * (1.0 / features)
        total = jnp.zeros((tokens, width), jnp.float32)
        for head in range(heads):
            centered = load(head, region) - mean
            total = total + centered * centered
        variance = jnp.sum(total, axis=1, keepdims=True) * (1.0 / features)
        spread = lax.rsqrt(variance + 1e-05)
        live = position < lengths_ref[region]
        for head in range(heads):
            centered = load(head, region) - mean
            normed = jnp.where(live, centered * spread * gain_ref[head : head + 1, :], 0.0)
            row, column = divmod(head, PATCH)
            pixels[region, row, pl.ds(RIM + column, tokens, stride=PATCH), :] = normed
        for row in range(PATCH):
            window = three_windows(pixels[region, row], columns)
            image_ref[region, row] = window[:, width : 2 * width]
            start = (region * PATCH + row) * columns
            windows[start : start + columns, :] = window
        near_ref[region] = image_ref[region, (1 - odd) * (PATCH - 1)]
        far_ref[region] = image_ref[region, odd * (PATCH - 1)]
        part = slice(region * PATCH * columns, (region + 1) * PATCH * columns)
        term = jnp.dot(turned_ref[:, part], windows[part, :], preferred_element_type=jnp.float32)
        product = term if region == 0 else product + term
    for down in range(3):
        for across in range(3):
            tap = 3 * down + across
            grads[tap * width : (tap + 1) * width, :] = product[
                down * width : (down + 1) * width, across * width : (across + 1) * width
            ].T
    filled = 9 * width
    if filled < grads.shape[0]:
        grads[filled:, :] = jnp.zeros((grads.shape[0] - filled, width), jnp.float32)
    half = keep_ref.shape[0]
    keep_ref[...] = grads[rows_at(core_ref[0], half), :]
    send_ref[...] = grads[rows_at(1 - core_ref[0], half), :]


def decode_kernel(index_ref, image_ref, near_ref, far_ref, weight_ref, out_ref, done_ref, padded):
    done_ref[...] = jnp.zeros(done_ref.shape, jnp.float32)
    regions, rows, columns, width = image_ref.shape
    padded[:RIM, :] = jnp.zeros((RIM, width), jnp.float32)
    padded[RIM + columns :, :] = jnp.zeros((RIM, width), jnp.float32)
    for region in range(regions):
        strips = []
        before, after = around(lax.rem(index_ref[0], 2), near_ref[region], far_ref[region])
        for row in range(-1, rows + 1):
            if row < 0:
                source = before
            elif row == rows:
                source = after
            else:
                source = image_ref[region, row]
            padded[RIM : RIM + columns, :] = source.astype(jnp.float32)
            strips.append(three_windows(padded[...], columns))
            if len(strips) == 3:
                total = jnp.dot(strips[0], weight_ref[0], preferred_element_type=jnp.float32)
                for down in (1, 2):
                    total = total + jnp.dot(
                        strips[down], weight_ref[down], preferred_element_type=jnp.float32
                    )
                out_ref[region, row - 1] = total.astype(jnp.bfloat16)
                strips.pop(0)


def add_pairs(terms):
    while len(terms) > 1:
        paired = [one + other for one, other in zip(terms[::2], terms[1::2])]
        terms = paired + terms[2 * len(paired) :]
    return terms[0]


def sum_cores_kernel(quad_ref, keep_ref, other_ref, *refs):
    total = refs[-1]
    total[...] = keep_ref[...] + other_ref[...]
    for distance, ref in enumerate(refs[:-1]):
        rows = rows_at(lax.bitwise_xor(quad_ref[0], distance), ref.shape[0])
        ref[...] = total[rows, :].astype(jnp.bfloat16)


def sum_kernel(factor, *refs):
    total = add_pairs([ref[...].astype(jnp.float32) for ref in refs[:-1]])
    refs[-1][...] = (total * factor).astype(jnp.bfloat16)


def join_kernel(quad_ref, done_ref, *refs):
    del done_ref
    for distance, ref in enumerate(refs[:-1]):
        rows = rows_at(lax.bitwise_xor(quad_ref[0], distance), ref.shape[0])
        refs[-1][rows, :] = ref[...]


def spread_kernel(core_ref, own_ref, other_ref, out_ref):
    half = own_ref.shape[0]
    out_ref[rows_at(core_ref[0], half), :] = own_ref[...].astype(jnp.float32)
    out_ref[rows_at(1 - core_ref[0], half), :] = other_ref[...].astype(jnp.float32)


def trade(values, distance):
    pairs = [(i, i ^ distance) for i in range(lax.axis_size("seq"))]
    return lax.ppermute(values, "seq", pairs)


def inner_size(seq_count):
    inner = 1
    while seq_count % (2 * inner) == 0 and (2 * inner) ** 2 <= seq_count:
        inner *= 2
    return inner


def trade_chips(values, distance, inner):
    seq_count = lax.axis_size("seq")
    pairs = []
    for outer in range(lax.axis_size("dp")):
        for seq in range(seq_count):
            chip, lane = divmod((outer // 2 * inner + seq % inner) ^ distance, inner)
            partner = (2 * chip + outer % 2) * seq_count + seq - seq % inner + lane
            pairs.append((outer * seq_count + seq, partner))
    return lax.ppermute(values, ("dp", "seq"), pairs)


def trade_cores(values):
    return lax.ppermute(values, "dp", [(i, i ^ 1) for i in range(lax.axis_size("dp"))])


def body(query_rows, key_rows, value_rows, region_lengths, norm_gain, conv_weight, cotangent):
    tokens, regions, model_width = query_rows.shape
    width = model_width // HEADS
    seq_count = lax.axis_size("seq")
    seq_index = lax.axis_index("seq")
    inner = inner_size(seq_count)
    quad_size = lax.axis_size("dp") // 2 * inner
    dp_index = lax.axis_index("dp")
    lane = lax.bitwise_and(seq_index, inner - 1)
    quad = (lax.shift_right_logical(dp_index, 1) * inner + lane).reshape(1)
    core = lax.bitwise_and(dp_index, 1).reshape(1)
    columns = tokens * PATCH
    capacity = seq_count * tokens
    per_device = regions * HEADS // seq_count
    far_pairs = [(i, i + 1) for i in range(1, seq_count - 1, 2)]
    far_pairs = far_pairs + [(j, i) for i, j in far_pairs]
    local_bytes = 2 * query_rows.size

    edge_shape = jax.ShapeDtypeStruct((regions, columns, width), jnp.bfloat16)
    chunk_shape = jax.ShapeDtypeStruct((3, per_device, tokens, width), jnp.bfloat16)
    index = seq_index.reshape(1)
    odd = lax.bitwise_and(seq_index, 1) == 1
    cot_far = jnp.where(odd, cotangent[:, PATCH - 1], cotangent[:, 0])
    cot_near = jnp.where(odd, cotangent[:, 0], cotangent[:, PATCH - 1])
    half = seq_count // 2
    early = [2, half, half + 1]
    late = [distance for distance in range(1, seq_count) if distance not in early]
    span = max(1, per_device // regions) * width

    def pack(name, distances):
        return call(
            functools.partial(pack_kernel, distances, regions, per_device),
            name,
            [chunk_shape] * len(distances),
            [SMEM()] + [HBM()] * 3,
            out_specs=[HBM()] * len(distances),
            scratch=[
                pltpu.VMEM((len(distances), 3, tokens, regions, span), jnp.bfloat16),
                pltpu.VMEM((len(distances),) + chunk_shape.shape, jnp.bfloat16),
                pltpu.SemaphoreType.DMA((3 * len(distances),)),
                pltpu.SemaphoreType.DMA((len(distances),)),
            ],
            moved=4 * len(distances) * chunk_shape.size,
            grant=VMEM_WHOLE,
        )(index, query_rows, key_rows, value_rows)

    packed = {}
    for distance, chunk in zip(early, pack("pack_early", early)):
        packed[distance] = trade(chunk, distance)
    for distance, chunk in zip(late, pack("pack_late", late)):
        packed[distance] = trade(chunk, distance)
    order = list(range(1, seq_count)) + [0]
    packed[0], cot_near, cot_far = call(
        functools.partial(own_kernel, regions, per_device),
        "own_chunk",
        [chunk_shape, edge_shape, edge_shape],
        [SMEM()] + [HBM()] * 3 + [VMEM()] * 2,
        scratch=[
            pltpu.VMEM((3, tokens, regions, span), jnp.bfloat16),
            pltpu.SemaphoreType.DMA((3,)),
        ],
        moved=12 * chunk_shape.size,
    )(index, query_rows, key_rows, value_rows, cot_near, cot_far)
    cot_near = trade(cot_near, 1)
    cot_far = lax.ppermute(cot_far, "seq", far_pairs)

    items = seq_index * per_device + jnp.arange(per_device, dtype=jnp.int32)
    item_lengths = jnp.sum(
        jnp.where(
            (items % regions)[:, None] == jnp.arange(regions, dtype=jnp.int32)[None, :],
            region_lengths[None, :],
            0,
        ),
        axis=1,
    )
    block_rows = min(256, capacity)
    group = regions if per_device % regions == 0 else per_device
    mixed = call(
        functools.partial(attend_kernel, block_rows, group, order),
        "attend",
        [jax.ShapeDtypeStruct((per_device, tokens, width), jnp.bfloat16)] * seq_count,
        [SMEM(), SMEM()] + [VMEM()] * seq_count,
        flops=4 * per_device * capacity * capacity * width,
        moved=4 * local_bytes,
        exps=per_device * capacity * capacity,
    )(index, item_lengths, *[packed[distance] for distance in order])
    back = list(range(half, seq_count)) + list(range(2, half)) + [1]
    attended = [trade(mixed[distance], distance) for distance in back] + [mixed[0]]

    turned = call(
        turn_kernel,
        "turn_cotangent",
        jax.ShapeDtypeStruct((3 * width, cotangent.size // width), jnp.bfloat16),
        [SMEM()] + [VMEM()] * 3,
        moved=8 * cotangent.size,
    )(index, cotangent, cot_near, cot_far)
    chunk_rows = -(-9 * width // (32 * quad_size)) * 16
    half_rows = quad_size * chunk_rows
    pixel_rows = regions * PATCH * columns
    conv_flops = 18 * pixel_rows * width * width
    chunk_moved = 8 * chunk_rows * width
    image, near, far, keep, send = call(
        functools.partial(norm_kernel, back + [0]),
        "norm_and_gradient",
        [jax.ShapeDtypeStruct((regions, PATCH, columns, width), jnp.bfloat16)]
        + [edge_shape] * 2
        + [jax.ShapeDtypeStruct((half_rows, width), jnp.float32)] * 2,
        [SMEM()] * 3 + [VMEM()] * (2 + seq_count),
        scratch=[
            pltpu.VMEM((seq_count,) + mixed[0].shape, jnp.bfloat16),
            pltpu.VMEM((regions, PATCH, columns + 2 * RIM, width), jnp.float32),
            pltpu.VMEM((pixel_rows, 3 * width), jnp.bfloat16),
            pltpu.VMEM((2 * half_rows, width), jnp.float32),
        ],
        flops=conv_flops,
        moved=4 * local_bytes,
    )(region_lengths, index, core, norm_gain.reshape(HEADS, width), turned, *attended)
    chunk_shape = jax.ShapeDtypeStruct((chunk_rows, width), jnp.bfloat16)
    parts = call(
        sum_cores_kernel,
        "sum_cores",
        [chunk_shape] * quad_size,
        [SMEM()] + [VMEM()] * 2,
        scratch=[pltpu.VMEM((half_rows, width), jnp.float32)],
        moved=quad_size * chunk_moved,
    )(quad, keep, trade_cores(send))
    near = trade(near, 1)
    far = lax.ppermute(far, "seq", far_pairs)
    distances = range(1, quad_size)
    plane_sum = call(
        functools.partial(sum_kernel, 1.0),
        "sum_chips",
        chunk_shape,
        [VMEM()] * quad_size,
        moved=chunk_moved,
    )(parts[0], *[trade_chips(parts[distance], distance, inner) for distance in distances])
    plane_sums = [plane_sum] + [
        trade(plane_sum, distance) for distance in range(inner, seq_count, inner)
    ]
    decoded, done = call(
        decode_kernel,
        "decode",
        [
            jax.ShapeDtypeStruct(cotangent.shape, jnp.bfloat16),
            jax.ShapeDtypeStruct((8, width), jnp.float32),
        ],
        [SMEM()] + [VMEM()] * 4,
        scratch=[pltpu.VMEM((columns + 2 * RIM, width), jnp.float32)],
        flops=conv_flops,
        moved=2 * local_bytes,
    )(index, image, near, far, conv_weight.reshape(3, 3 * width, width))
    total = call(
        functools.partial(sum_kernel, 1.0 / math.sqrt(PATCH * columns)),
        "sum_planes",
        chunk_shape,
        [VMEM()] * len(plane_sums),
        moved=chunk_moved,
    )(*plane_sums)
    joined = call(
        join_kernel,
        "join_chips",
        jax.ShapeDtypeStruct((half_rows, width), jnp.bfloat16),
        [SMEM(), ANY()] + [VMEM()] * quad_size,
        moved=quad_size * chunk_moved,
    )(quad, done, total, *[trade_chips(total, distance, inner) for distance in distances])
    weight_grad = call(
        spread_kernel,
        "spread_sums",
        jax.ShapeDtypeStruct((2 * half_rows, width), jnp.float32),
        [SMEM()] + [VMEM()] * 2,
        moved=2 * quad_size * chunk_moved,
    )(core, joined, trade_cores(joined))
    return (decoded, weight_grad[: 9 * width].reshape(conv_weight.shape))


def solution(mesh):
    placed = (
        P("seq", "dp", None),
        P("seq", "dp", None),
        P("seq", "dp", None),
        P("dp"),
        P(),
        P(),
        P("dp", "seq", None, None),
    )
    return jax.shard_map(
        body,
        mesh=mesh,
        in_specs=placed,
        out_specs=(P("dp", "seq", None, None), P()),
        check_vma=False,
    )
```

```python
import functools
import math

import jax
import jax.numpy as jnp
from jax import lax
from jax.experimental import pallas as pl
from jax.experimental.pallas import tpu as pltpu
from jax.sharding import PartitionSpec as P

HEADS = 16
PATCH = 4
RIM = 8
VMEM_LIMIT = 48 * 1024 * 1024
VMEM_WHOLE = 60 * 1024 * 1024

VMEM = functools.partial(pl.BlockSpec, memory_space=pltpu.VMEM)
HBM = functools.partial(pl.BlockSpec, memory_space=pltpu.HBM)
ANY = functools.partial(pl.BlockSpec, memory_space=pl.ANY)
SMEM = functools.partial(pl.BlockSpec, memory_space=pltpu.SMEM)


def call(kernel, name, out_shape, in_specs, out_specs=None, scratch=(), flops=0, moved=0, exps=0, grant=VMEM_LIMIT):
    many = isinstance(out_shape, (list, tuple))
    return pl.pallas_call(
        kernel,
        out_shape=out_shape,
        in_specs=in_specs,
        out_specs=out_specs or ([VMEM() for _ in out_shape] if many else VMEM()),
        scratch_shapes=list(scratch),
        compiler_params=pltpu.CompilerParams(vmem_limit_bytes=grant),
        cost_estimate=pl.CostEstimate(flops=flops, bytes_accessed=moved, transcendentals=exps),
        name=name,
    )


def columns_of(index, distance, regions, per_device, width):
    owner = lax.bitwise_xor(index, distance)
    span = max(1, per_device // regions) * width
    start = lax.div(owner * per_device, regions) * width
    return owner, pl.ds(pl.multiple_of(start, width), span)


def take_items(held, owner, regions, per_device, width, out_ref):
    for head in range(held.shape[2] // width):
        block = held[:, :, head * width : (head + 1) * width].astype(jnp.float32)
        if per_device % regions:
            value = block[:, 0, :]
            for other in range(1, regions):
                value = jnp.where(lax.rem(owner, regions) == other, block[:, other, :], value)
            out_ref[head] = value.astype(jnp.bfloat16)
        else:
            for region in range(regions):
                out_ref[head * regions + region] = block[:, region, :].astype(jnp.bfloat16)


def pack_kernel(distances, regions, per_device, index_ref, query_ref, key_ref, value_ref, *refs):
    held, ready, load_sems, store_sems = refs[-4:]
    width = query_ref.shape[2] // HEADS
    loads = []
    for number, distance in enumerate(distances):
        owner, columns = columns_of(index_ref[0], distance, regions, per_device, width)
        for which, ref in enumerate((query_ref, key_ref, value_ref)):
            load = pltpu.make_async_copy(
                ref.at[:, :, columns], held.at[number, which], load_sems.at[3 * number + which]
            )
            load.start()
            loads.append((number, which, owner, load))
    stores = []
    for number, which, owner, load in loads:
        load.wait()
        take_items(
            held.at[number, which], owner, regions, per_device, width, ready.at[number, which]
        )
        if which == 2:
            store = pltpu.make_async_copy(ready.at[number], refs[number], store_sems.at[number])
            store.start()
            stores.append(store)
    for store in stores:
        store.wait()


def own_kernel(
    regions,
    per_device,
    index_ref,
    query_ref,
    key_ref,
    value_ref,
    near_ref,
    far_ref,
    out_ref,
    near_out_ref,
    far_out_ref,
    held,
    sems,
):
    near_out_ref[...] = near_ref[...]
    far_out_ref[...] = far_ref[...]
    width = out_ref.shape[3]
    owner, columns = columns_of(index_ref[0], 0, regions, per_device, width)
    loads = []
    for which, ref in enumerate((query_ref, key_ref, value_ref)):
        loads.append(
            pltpu.make_async_copy(ref.at[:, :, columns], held.at[which], sems.at[which])
        )
        loads[-1].start()
    for which, load in enumerate(loads):
        load.wait()
        take_items(held.at[which], owner, regions, per_device, width, out_ref.at[which])


def attend_kernel(block_rows, group, order, index_ref, lengths_ref, *refs):
    chunks = dict(zip(order, refs))
    out_refs = refs[len(order) :]
    index = index_ref[0]
    sources = len(chunks)
    _, per_device, tokens, width = chunks[0].shape
    capacity = sources * tokens
    per_block = block_rows // tokens
    blocks = capacity // block_rows
    factor = math.log2(math.e) / math.sqrt(width)
    columns = lax.broadcasted_iota(jnp.int32, (1, capacity), 1)
    slots = columns
    for distance in range(sources):
        here = (columns >= distance * tokens) & (columns < (distance + 1) * tokens)
        moved = (lax.bitwise_xor(index, distance) - distance) * tokens
        slots = jnp.where(here, columns + moved, slots)

    def rows_of(which, item, distances):
        return jnp.concatenate([chunks[distance][which, item] for distance in distances], axis=0)

    def distances_of(block):
        return range(block * per_block, (block + 1) * per_block)

    def start_of(block, span):
        return lax.bitwise_xor(lax.div(index, span), block) * span

    def clear(item, block):
        for distance in distances_of(block):
            out_refs[distance][item] = jnp.zeros((tokens, width), jnp.bfloat16)

    def score(item, block):
        return lax.dot_general(
            rows_of(0, item, distances_of(block)),
            rows_of(1, item, range(sources)),
            (((1,), (1,)), ((), ())),
            preferred_element_type=jnp.float32,
        )

    def finish(item, block, scores, key_valid):
        scores = jnp.where(key_valid, scores * factor, -1e30)
        powers = jnp.exp2(scores - jnp.max(scores, axis=1, keepdims=True))
        totals = jnp.sum(powers, axis=1, keepdims=True)
        mixed = jnp.dot(
            powers.astype(jnp.bfloat16),
            rows_of(2, item, range(sources)),
            preferred_element_type=jnp.float32,
        )
        mixed = (mixed / totals).astype(jnp.bfloat16)
        for number, distance in enumerate(distances_of(block)):
            out_refs[distance][item] = mixed[number * tokens : (number + 1) * tokens]

    def attend(items, live, dead, length):
        key_valid = slots < length
        waiting = None
        for block in live:
            for item in items:
                scores = score(item, block)
                if waiting is not None:
                    finish(*waiting, key_valid)
                waiting = (item, block, scores)
        if waiting is not None:
            finish(*waiting, key_valid)
        for block in dead:
            for item in items:
                clear(item, block)

    for lead in range(group):
        length = lengths_ref[lead]
        items = list(range(lead, per_device, group))
        for block in range(0, blocks, 2):
            pair = list(range(block, min(block + 2, blocks)))
            alive = [length > start_of(one, per_block) * tokens for one in pair]
            for case in range(2 ** len(pair)):
                live = [one for bit, one in enumerate(pair) if case >> bit & 1]
                dead = [one for one in pair if one not in live]
                chosen = None
                for bit in range(len(pair)):
                    test = alive[bit] if case >> bit & 1 else jnp.logical_not(alive[bit])
                    chosen = test if chosen is None else chosen & test

                @pl.when(chosen)
                def _(items=items, live=live, dead=dead, length=length):
                    attend(items, live, dead, length)


def three_windows(padded, columns):
    return jnp.concatenate(
        [padded[RIM - 1 + shift : RIM - 1 + shift + columns].astype(jnp.bfloat16) for shift in range(3)],
        axis=1,
    )


def rows_at(place, rows):
    return pl.ds(pl.multiple_of(place * rows, rows), rows)


def around(odd, near, far):
    return jnp.where(odd == 1, near, far), jnp.where(odd == 1, far, near)


def turn_kernel(index_ref, cot_ref, near_ref, far_ref, out_ref):
    regions, rows, columns, width = cot_ref.shape
    for region in range(regions):
        before, after = around(lax.rem(index_ref[0], 2), near_ref[region], far_ref[region])
        for row in range(-1, rows + 1):
            value = before if row < 0 else after if row == rows else cot_ref[region, row]
            turned = value.T
            for down in range(3):
                image_row = row - 1 + down
                if 0 <= image_row < rows:
                    start = (region * rows + image_row) * columns
                    out_ref[down * width : (down + 1) * width, start : start + columns] = turned


def norm_kernel(order, lengths_ref, index_ref, core_ref, gain_ref, turned_ref, *refs):
    image_ref, near_ref, far_ref, keep_ref, send_ref, attended, pixels, windows, grads = refs[-9:]
    for distance, ref in zip(order, refs):
        attended[lax.bitwise_xor(index_ref[0], distance)] = ref[...]
    heads = gain_ref.shape[0]
    regions = image_ref.shape[0]
    _, per_device, tokens, width = attended.shape

    def load(head, region):
        owner, place = divmod(head * regions + region, per_device)
        return attended[owner, place].astype(jnp.float32)

    columns = tokens * PATCH
    features = heads * width
    odd = lax.rem(index_ref[0], 2)
    position = index_ref[0] * tokens + lax.broadcasted_iota(jnp.int32, (tokens, 1), 0)
    pixels[:, :, :RIM, :] = jnp.zeros((regions, PATCH, RIM, width), jnp.float32)
    pixels[:, :, RIM + columns :, :] = jnp.zeros((regions, PATCH, RIM, width), jnp.float32)
    for region in range(regions):
        total = jnp.zeros((tokens, width), jnp.float32)
        for head in range(heads):
            total = total + load(head, region)
        mean = jnp.sum(total, axis=1, keepdims=True) * (1.0 / features)
        total = jnp.zeros((tokens, width), jnp.float32)
        for head in range(heads):
            centered = load(head, region) - mean
            total = total + centered * centered
        variance = jnp.sum(total, axis=1, keepdims=True) * (1.0 / features)
        spread = lax.rsqrt(variance + 1e-05)
        live = position < lengths_ref[region]
        for head in range(heads):
            centered = load(head, region) - mean
            normed = jnp.where(live, centered * spread * gain_ref[head : head + 1, :], 0.0)
            row, column = divmod(head, PATCH)
            pixels[region, row, pl.ds(RIM + column, tokens, stride=PATCH), :] = normed
        for row in range(PATCH):
            window = three_windows(pixels[region, row], columns)
            image_ref[region, row] = window[:, width : 2 * width]
            start = (region * PATCH + row) * columns
            windows[start : start + columns, :] = window
        near_ref[region] = image_ref[region, (1 - odd) * (PATCH - 1)]
        far_ref[region] = image_ref[region, odd * (PATCH - 1)]
        part = slice(region * PATCH * columns, (region + 1) * PATCH * columns)
        term = jnp.dot(turned_ref[:, part], windows[part, :], preferred_element_type=jnp.float32)
        product = term if region == 0 else product + term
    for down in range(3):
        for across in range(3):
            tap = 3 * down + across
            grads[tap * width : (tap + 1) * width, :] = product[
                down * width : (down + 1) * width, across * width : (across + 1) * width
            ].T
    filled = 9 * width
    if filled < grads.shape[0]:
        grads[filled:, :] = jnp.zeros((grads.shape[0] - filled, width), jnp.float32)
    half = keep_ref.shape[0]
    keep_ref[...] = grads[rows_at(core_ref[0], half), :]
    send_ref[...] = grads[rows_at(1 - core_ref[0], half), :]


def decode_kernel(index_ref, image_ref, near_ref, far_ref, weight_ref, out_ref, done_ref, padded):
    done_ref[...] = jnp.zeros(done_ref.shape, jnp.float32)
    regions, rows, columns, width = image_ref.shape
    padded[:RIM, :] = jnp.zeros((RIM, width), jnp.float32)
    padded[RIM + columns :, :] = jnp.zeros((RIM, width), jnp.float32)
    for region in range(regions):
        strips = []
        before, after = around(lax.rem(index_ref[0], 2), near_ref[region], far_ref[region])
        for row in range(-1, rows + 1):
            if row < 0:
                source = before
            elif row == rows:
                source = after
            else:
                source = image_ref[region, row]
            padded[RIM : RIM + columns, :] = source.astype(jnp.float32)
            strips.append(three_windows(padded[...], columns))
            if len(strips) == 3:
                total = jnp.dot(strips[0], weight_ref[0], preferred_element_type=jnp.float32)
                for down in (1, 2):
                    total = total + jnp.dot(
                        strips[down], weight_ref[down], preferred_element_type=jnp.float32
                    )
                out_ref[region, row - 1] = total.astype(jnp.bfloat16)
                strips.pop(0)


def add_pairs(terms):
    while len(terms) > 1:
        paired = [one + other for one, other in zip(terms[::2], terms[1::2])]
        terms = paired + terms[2 * len(paired) :]
    return terms[0]


def hold_kernel(value_ref, after_ref, out_ref):
    del after_ref
    out_ref[...] = value_ref[...]


def hold(value, after):
    return call(
        hold_kernel,
        "hold",
        jax.ShapeDtypeStruct(value.shape, value.dtype),
        [VMEM(), ANY()],
        moved=4 * value.size,
    )(value, after)


def sum_cores_kernel(quad_ref, keep_ref, other_ref, *refs):
    total = refs[-1]
    total[...] = keep_ref[...] + other_ref[...]
    for distance, ref in enumerate(refs[:-1]):
        rows = rows_at(lax.bitwise_xor(quad_ref[0], distance), ref.shape[0])
        ref[...] = total[rows, :].astype(jnp.bfloat16)


def sum_kernel(factor, *refs):
    total = add_pairs([ref[...].astype(jnp.float32) for ref in refs[:-1]])
    refs[-1][...] = (total * factor).astype(jnp.bfloat16)


def join_kernel(quad_ref, done_ref, *refs):
    del done_ref
    for distance, ref in enumerate(refs[:-1]):
        rows = rows_at(lax.bitwise_xor(quad_ref[0], distance), ref.shape[0])
        refs[-1][rows, :] = ref[...]


def spread_kernel(core_ref, own_ref, other_ref, out_ref):
    half = own_ref.shape[0]
    out_ref[rows_at(core_ref[0], half), :] = own_ref[...].astype(jnp.float32)
    out_ref[rows_at(1 - core_ref[0], half), :] = other_ref[...].astype(jnp.float32)


def trade(values, distance):
    pairs = [(i, i ^ distance) for i in range(lax.axis_size("seq"))]
    return lax.ppermute(values, "seq", pairs)


def inner_size(seq_count):
    inner = 1
    while seq_count % (2 * inner) == 0 and (2 * inner) ** 2 <= seq_count:
        inner *= 2
    return inner


def trade_chips(values, distance, inner):
    seq_count = lax.axis_size("seq")
    pairs = []
    for outer in range(lax.axis_size("dp")):
        for seq in range(seq_count):
            chip, lane = divmod((outer // 2 * inner + seq % inner) ^ distance, inner)
            partner = (2 * chip + outer % 2) * seq_count + seq - seq % inner + lane
            pairs.append((outer * seq_count + seq, partner))
    return lax.ppermute(values, ("dp", "seq"), pairs)


def trade_cores(values):
    return lax.ppermute(values, "dp", [(i, i ^ 1) for i in range(lax.axis_size("dp"))])


def body(query_rows, key_rows, value_rows, region_lengths, norm_gain, conv_weight, cotangent):
    tokens, regions, model_width = query_rows.shape
    width = model_width // HEADS
    seq_count = lax.axis_size("seq")
    seq_index = lax.axis_index("seq")
    inner = inner_size(seq_count)
    quad_size = lax.axis_size("dp") // 2 * inner
    dp_index = lax.axis_index("dp")
    lane = lax.bitwise_and(seq_index, inner - 1)
    quad = (lax.shift_right_logical(dp_index, 1) * inner + lane).reshape(1)
    core = lax.bitwise_and(dp_index, 1).reshape(1)
    columns = tokens * PATCH
    capacity = seq_count * tokens
    per_device = regions * HEADS // seq_count
    far_pairs = [(i, i + 1) for i in range(1, seq_count - 1, 2)]
    far_pairs = far_pairs + [(j, i) for i, j in far_pairs]
    local_bytes = 2 * query_rows.size

    edge_shape = jax.ShapeDtypeStruct((regions, columns, width), jnp.bfloat16)
    chunk_shape = jax.ShapeDtypeStruct((3, per_device, tokens, width), jnp.bfloat16)
    index = seq_index.reshape(1)
    odd = lax.bitwise_and(seq_index, 1) == 1
    cot_far = jnp.where(odd, cotangent[:, PATCH - 1], cotangent[:, 0])
    cot_near = jnp.where(odd, cotangent[:, 0], cotangent[:, PATCH - 1])
    half = seq_count // 2
    early = [2, half, half + 1]
    late = [distance for distance in range(1, seq_count) if distance not in early]
    span = max(1, per_device // regions) * width

    def pack(name, distances):
        return call(
            functools.partial(pack_kernel, distances, regions, per_device),
            name,
            [chunk_shape] * len(distances),
            [SMEM()] + [HBM()] * 3,
            out_specs=[HBM()] * len(distances),
            scratch=[
                pltpu.VMEM((len(distances), 3, tokens, regions, span), jnp.bfloat16),
                pltpu.VMEM((len(distances),) + chunk_shape.shape, jnp.bfloat16),
                pltpu.SemaphoreType.DMA((3 * len(distances),)),
                pltpu.SemaphoreType.DMA((len(distances),)),
            ],
            moved=4 * len(distances) * chunk_shape.size,
            grant=VMEM_WHOLE,
        )(index, query_rows, key_rows, value_rows)

    packed = {}
    for distance, chunk in zip(early, pack("pack_early", early)):
        packed[distance] = trade(chunk, distance)
    for distance, chunk in zip(late, pack("pack_late", late)):
        packed[distance] = trade(chunk, distance)
    order = list(range(1, seq_count)) + [0]
    packed[0], cot_near, cot_far = call(
        functools.partial(own_kernel, regions, per_device),
        "own_chunk",
        [chunk_shape, edge_shape, edge_shape],
        [SMEM()] + [HBM()] * 3 + [VMEM()] * 2,
        scratch=[
            pltpu.VMEM((3, tokens, regions, span), jnp.bfloat16),
            pltpu.SemaphoreType.DMA((3,)),
        ],
        moved=12 * chunk_shape.size,
    )(index, query_rows, key_rows, value_rows, cot_near, cot_far)
    cot_near = trade(cot_near, 1)
    cot_far = lax.ppermute(cot_far, "seq", far_pairs)

    items = seq_index * per_device + jnp.arange(per_device, dtype=jnp.int32)
    item_lengths = jnp.sum(
        jnp.where(
            (items % regions)[:, None] == jnp.arange(regions, dtype=jnp.int32)[None, :],
            region_lengths[None, :],
            0,
        ),
        axis=1,
    )
    block_rows = min(256, capacity)
    group = regions if per_device % regions == 0 else per_device
    mixed = call(
        functools.partial(attend_kernel, block_rows, group, order),
        "attend",
        [jax.ShapeDtypeStruct((per_device, tokens, width), jnp.bfloat16)] * seq_count,
        [SMEM(), SMEM()] + [VMEM()] * seq_count,
        flops=4 * per_device * capacity * capacity * width,
        moved=4 * local_bytes,
        exps=per_device * capacity * capacity,
    )(index, item_lengths, *[packed[distance] for distance in order])
    back = list(range(half, seq_count)) + list(range(2, half)) + [1]
    attended = [trade(mixed[distance], distance) for distance in back] + [mixed[0]]

    turned = call(
        turn_kernel,
        "turn_cotangent",
        jax.ShapeDtypeStruct((3 * width, cotangent.size // width), jnp.bfloat16),
        [SMEM()] + [VMEM()] * 3,
        moved=8 * cotangent.size,
    )(index, cotangent, cot_near, cot_far)
    chunk_rows = -(-9 * width // (32 * quad_size)) * 16
    half_rows = quad_size * chunk_rows
    pixel_rows = regions * PATCH * columns
    conv_flops = 18 * pixel_rows * width * width
    chunk_moved = 8 * chunk_rows * width
    image, near, far, keep, send = call(
        functools.partial(norm_kernel, back + [0]),
        "norm_and_gradient",
        [jax.ShapeDtypeStruct((regions, PATCH, columns, width), jnp.bfloat16)]
        + [edge_shape] * 2
        + [jax.ShapeDtypeStruct((half_rows, width), jnp.float32)] * 2,
        [SMEM()] * 3 + [VMEM()] * (2 + seq_count),
        scratch=[
            pltpu.VMEM((seq_count,) + mixed[0].shape, jnp.bfloat16),
            pltpu.VMEM((regions, PATCH, columns + 2 * RIM, width), jnp.float32),
            pltpu.VMEM((pixel_rows, 3 * width), jnp.bfloat16),
            pltpu.VMEM((2 * half_rows, width), jnp.float32),
        ],
        flops=conv_flops,
        moved=4 * local_bytes,
    )(region_lengths, index, core, norm_gain.reshape(HEADS, width), turned, *attended)
    chunk_shape = jax.ShapeDtypeStruct((chunk_rows, width), jnp.bfloat16)
    parts = call(
        sum_cores_kernel,
        "sum_cores",
        [chunk_shape] * quad_size,
        [SMEM()] + [VMEM()] * 2,
        scratch=[pltpu.VMEM((half_rows, width), jnp.float32)],
        moved=quad_size * chunk_moved,
    )(quad, keep, trade_cores(send))
    far = lax.ppermute(far, "seq", far_pairs)
    distances = range(1, quad_size)
    plane_sum = call(
        functools.partial(sum_kernel, 1.0),
        "sum_chips",
        chunk_shape,
        [VMEM()] * quad_size,
        moved=chunk_moved,
    )(parts[0], *[trade_chips(parts[distance], distance, inner) for distance in distances])
    near = trade(hold(near, plane_sum), 1)
    plane_sums = [plane_sum] + [
        trade(plane_sum, distance) for distance in range(inner, seq_count, inner)
    ]
    decoded, done = call(
        decode_kernel,
        "decode",
        [
            jax.ShapeDtypeStruct(cotangent.shape, jnp.bfloat16),
            jax.ShapeDtypeStruct((8, width), jnp.float32),
        ],
        [SMEM()] + [VMEM()] * 4,
        scratch=[pltpu.VMEM((columns + 2 * RIM, width), jnp.float32)],
        flops=conv_flops,
        moved=2 * local_bytes,
    )(index, image, near, far, conv_weight.reshape(3, 3 * width, width))
    total = call(
        functools.partial(sum_kernel, 1.0 / math.sqrt(PATCH * columns)),
        "sum_planes",
        chunk_shape,
        [VMEM()] * len(plane_sums),
        moved=chunk_moved,
    )(*plane_sums)
    joined = call(
        join_kernel,
        "join_chips",
        jax.ShapeDtypeStruct((half_rows, width), jnp.bfloat16),
        [SMEM(), ANY()] + [VMEM()] * quad_size,
        moved=quad_size * chunk_moved,
    )(quad, done, total, *[trade_chips(total, distance, inner) for distance in distances])
    weight_grad = call(
        spread_kernel,
        "spread_sums",
        jax.ShapeDtypeStruct((2 * half_rows, width), jnp.float32),
        [SMEM()] + [VMEM()] * 2,
        moved=2 * quad_size * chunk_moved,
    )(core, joined, trade_cores(joined))
    return (decoded, weight_grad[: 9 * width].reshape(conv_weight.shape))


def solution(mesh):
    placed = (
        P("seq", "dp", None),
        P("seq", "dp", None),
        P("seq", "dp", None),
        P("dp"),
        P(),
        P(),
        P("dp", "seq", None, None),
    )
    return jax.shard_map(
        body,
        mesh=mesh,
        in_specs=placed,
        out_specs=(P("dp", "seq", None, None), P()),
        check_vma=False,
    )
```

```python
import functools
import math

import jax
import jax.numpy as jnp
from jax import lax
from jax.experimental import pallas as pl
from jax.experimental.pallas import tpu as pltpu
from jax.sharding import PartitionSpec as P

HEADS = 16
PATCH = 4
RIM = 8
VMEM_LIMIT = 48 * 1024 * 1024
VMEM_WHOLE = 60 * 1024 * 1024

VMEM = functools.partial(pl.BlockSpec, memory_space=pltpu.VMEM)
HBM = functools.partial(pl.BlockSpec, memory_space=pltpu.HBM)
ANY = functools.partial(pl.BlockSpec, memory_space=pl.ANY)
SMEM = functools.partial(pl.BlockSpec, memory_space=pltpu.SMEM)


def call(kernel, name, out_shape, in_specs, out_specs=None, scratch=(), flops=0, moved=0, exps=0, grant=VMEM_LIMIT):
    many = isinstance(out_shape, (list, tuple))
    return pl.pallas_call(
        kernel,
        out_shape=out_shape,
        in_specs=in_specs,
        out_specs=out_specs or ([VMEM() for _ in out_shape] if many else VMEM()),
        scratch_shapes=list(scratch),
        compiler_params=pltpu.CompilerParams(vmem_limit_bytes=grant),
        cost_estimate=pl.CostEstimate(flops=flops, bytes_accessed=moved, transcendentals=exps),
        name=name,
    )


def columns_of(index, distance, regions, per_device, width):
    owner = lax.bitwise_xor(index, distance)
    span = max(1, per_device // regions) * width
    start = lax.div(owner * per_device, regions) * width
    return owner, pl.ds(pl.multiple_of(start, width), span)


def take_items(held, owner, regions, per_device, width, out_ref):
    for head in range(held.shape[2] // width):
        block = held[:, :, head * width : (head + 1) * width].astype(jnp.float32)
        if per_device % regions:
            value = block[:, 0, :]
            for other in range(1, regions):
                value = jnp.where(lax.rem(owner, regions) == other, block[:, other, :], value)
            out_ref[head] = value.astype(jnp.bfloat16)
        else:
            for region in range(regions):
                out_ref[head * regions + region] = block[:, region, :].astype(jnp.bfloat16)


def pack_kernel(distances, regions, per_device, index_ref, query_ref, key_ref, value_ref, *refs):
    held, ready, load_sems, store_sems = refs[-4:]
    width = query_ref.shape[2] // HEADS
    loads = []
    for number, distance in enumerate(distances):
        owner, columns = columns_of(index_ref[0], distance, regions, per_device, width)
        for which, ref in enumerate((query_ref, key_ref, value_ref)):
            load = pltpu.make_async_copy(
                ref.at[:, :, columns], held.at[number, which], load_sems.at[3 * number + which]
            )
            load.start()
            loads.append((number, which, owner, load))
    stores = []
    for number, which, owner, load in loads:
        load.wait()
        take_items(
            held.at[number, which], owner, regions, per_device, width, ready.at[number, which]
        )
        if which == 2:
            store = pltpu.make_async_copy(ready.at[number], refs[number], store_sems.at[number])
            store.start()
            stores.append(store)
    for store in stores:
        store.wait()


def own_kernel(
    regions,
    per_device,
    index_ref,
    query_ref,
    key_ref,
    value_ref,
    near_ref,
    far_ref,
    out_ref,
    near_out_ref,
    far_out_ref,
    held,
    sems,
):
    near_out_ref[...] = near_ref[...]
    far_out_ref[...] = far_ref[...]
    width = out_ref.shape[3]
    owner, columns = columns_of(index_ref[0], 0, regions, per_device, width)
    loads = []
    for which, ref in enumerate((query_ref, key_ref, value_ref)):
        loads.append(
            pltpu.make_async_copy(ref.at[:, :, columns], held.at[which], sems.at[which])
        )
        loads[-1].start()
    for which, load in enumerate(loads):
        load.wait()
        take_items(held.at[which], owner, regions, per_device, width, out_ref.at[which])


def attend_kernel(block_rows, group, order, index_ref, lengths_ref, *refs):
    chunks = dict(zip(order, refs))
    out_refs = refs[len(order) :]
    index = index_ref[0]
    sources = len(chunks)
    _, per_device, tokens, width = chunks[0].shape
    capacity = sources * tokens
    per_block = block_rows // tokens
    blocks = capacity // block_rows
    factor = math.log2(math.e) / math.sqrt(width)
    columns = lax.broadcasted_iota(jnp.int32, (1, capacity), 1)
    slots = columns
    for distance in range(sources):
        here = (columns >= distance * tokens) & (columns < (distance + 1) * tokens)
        moved = (lax.bitwise_xor(index, distance) - distance) * tokens
        slots = jnp.where(here, columns + moved, slots)

    def rows_of(which, item, distances):
        return jnp.concatenate([chunks[distance][which, item] for distance in distances], axis=0)

    def distances_of(block):
        return range(block * per_block, (block + 1) * per_block)

    def start_of(block, span):
        return lax.bitwise_xor(lax.div(index, span), block) * span

    def clear(item, block):
        for distance in distances_of(block):
            out_refs[distance][item] = jnp.zeros((tokens, width), jnp.bfloat16)

    def score(item, block):
        return lax.dot_general(
            rows_of(0, item, distances_of(block)),
            rows_of(1, item, range(sources)),
            (((1,), (1,)), ((), ())),
            preferred_element_type=jnp.float32,
        )

    def finish(item, block, scores, key_valid):
        scores = jnp.where(key_valid, scores * factor, -1e30)
        powers = jnp.exp2(scores - jnp.max(scores, axis=1, keepdims=True))
        totals = jnp.sum(powers, axis=1, keepdims=True)
        mixed = jnp.dot(
            powers.astype(jnp.bfloat16),
            rows_of(2, item, range(sources)),
            preferred_element_type=jnp.float32,
        )
        mixed = (mixed / totals).astype(jnp.bfloat16)
        for number, distance in enumerate(distances_of(block)):
            out_refs[distance][item] = mixed[number * tokens : (number + 1) * tokens]

    def attend(items, live, dead, length):
        key_valid = slots < length
        waiting = None
        for block in live:
            for item in items:
                scores = score(item, block)
                if waiting is not None:
                    finish(*waiting, key_valid)
                waiting = (item, block, scores)
        if waiting is not None:
            finish(*waiting, key_valid)
        for block in dead:
            for item in items:
                clear(item, block)

    for lead in range(group):
        length = lengths_ref[lead]
        items = list(range(lead, per_device, group))
        for block in range(0, blocks, 2):
            pair = list(range(block, min(block + 2, blocks)))
            alive = [length > start_of(one, per_block) * tokens for one in pair]
            for case in range(2 ** len(pair)):
                live = [one for bit, one in enumerate(pair) if case >> bit & 1]
                dead = [one for one in pair if one not in live]
                chosen = None
                for bit in range(len(pair)):
                    test = alive[bit] if case >> bit & 1 else jnp.logical_not(alive[bit])
                    chosen = test if chosen is None else chosen & test

                @pl.when(chosen)
                def _(items=items, live=live, dead=dead, length=length):
                    attend(items, live, dead, length)


def three_windows(padded, columns):
    return jnp.concatenate(
        [padded[RIM - 1 + shift : RIM - 1 + shift + columns].astype(jnp.bfloat16) for shift in range(3)],
        axis=1,
    )


def rows_at(place, rows):
    return pl.ds(pl.multiple_of(place * rows, rows), rows)


def around(odd, near, far):
    return jnp.where(odd == 1, near, far), jnp.where(odd == 1, far, near)


def turn_kernel(index_ref, cot_ref, near_ref, far_ref, out_ref):
    regions, rows, columns, width = cot_ref.shape
    for region in range(regions):
        before, after = around(lax.rem(index_ref[0], 2), near_ref[region], far_ref[region])
        for row in range(-1, rows + 1):
            value = before if row < 0 else after if row == rows else cot_ref[region, row]
            turned = value.T
            for down in range(3):
                image_row = row - 1 + down
                if 0 <= image_row < rows:
                    start = (region * rows + image_row) * columns
                    out_ref[down * width : (down + 1) * width, start : start + columns] = turned


def norm_kernel(order, lengths_ref, index_ref, core_ref, gain_ref, turned_ref, *refs):
    image_ref, near_ref, far_ref, keep_ref, send_ref, attended, pixels, windows, grads = refs[-9:]
    for distance, ref in zip(order, refs):
        attended[lax.bitwise_xor(index_ref[0], distance)] = ref[...]
    heads = gain_ref.shape[0]
    regions = image_ref.shape[0]
    _, per_device, tokens, width = attended.shape

    def load(head, region):
        owner, place = divmod(head * regions + region, per_device)
        return attended[owner, place].astype(jnp.float32)

    columns = tokens * PATCH
    features = heads * width
    odd = lax.rem(index_ref[0], 2)
    position = index_ref[0] * tokens + lax.broadcasted_iota(jnp.int32, (tokens, 1), 0)
    pixels[:, :, :RIM, :] = jnp.zeros((regions, PATCH, RIM, width), jnp.float32)
    pixels[:, :, RIM + columns :, :] = jnp.zeros((regions, PATCH, RIM, width), jnp.float32)
    for region in range(regions):
        total = jnp.zeros((tokens, width), jnp.float32)
        for head in range(heads):
            total = total + load(head, region)
        mean = jnp.sum(total, axis=1, keepdims=True) * (1.0 / features)
        total = jnp.zeros((tokens, width), jnp.float32)
        for head in range(heads):
            centered = load(head, region) - mean
            total = total + centered * centered
        variance = jnp.sum(total, axis=1, keepdims=True) * (1.0 / features)
        spread = lax.rsqrt(variance + 1e-05)
        live = position < lengths_ref[region]
        for head in range(heads):
            centered = load(head, region) - mean
            normed = jnp.where(live, centered * spread * gain_ref[head : head + 1, :], 0.0)
            row, column = divmod(head, PATCH)
            pixels[region, row, pl.ds(RIM + column, tokens, stride=PATCH), :] = normed
        for row in range(PATCH):
            window = three_windows(pixels[region, row], columns)
            image_ref[region, row] = window[:, width : 2 * width]
            start = (region * PATCH + row) * columns
            windows[start : start + columns, :] = window
        near_ref[region] = image_ref[region, (1 - odd) * (PATCH - 1)]
        far_ref[region] = image_ref[region, odd * (PATCH - 1)]
        part = slice(region * PATCH * columns, (region + 1) * PATCH * columns)
        term = jnp.dot(turned_ref[:, part], windows[part, :], preferred_element_type=jnp.float32)
        product = term if region == 0 else product + term
    for down in range(3):
        for across in range(3):
            tap = 3 * down + across
            grads[tap * width : (tap + 1) * width, :] = product[
                down * width : (down + 1) * width, across * width : (across + 1) * width
            ].T
    filled = 9 * width
    if filled < grads.shape[0]:
        grads[filled:, :] = jnp.zeros((grads.shape[0] - filled, width), jnp.float32)
    half = keep_ref.shape[0]
    keep_ref[...] = grads[rows_at(core_ref[0], half), :]
    send_ref[...] = grads[rows_at(1 - core_ref[0], half), :]


def decode_kernel(index_ref, image_ref, near_ref, far_ref, weight_ref, out_ref, done_ref, padded):
    done_ref[...] = jnp.zeros(done_ref.shape, jnp.float32)
    regions, rows, columns, width = image_ref.shape
    padded[:RIM, :] = jnp.zeros((RIM, width), jnp.float32)
    padded[RIM + columns :, :] = jnp.zeros((RIM, width), jnp.float32)
    for region in range(regions):
        strips = []
        before, after = around(lax.rem(index_ref[0], 2), near_ref[region], far_ref[region])
        for row in range(-1, rows + 1):
            if row < 0:
                source = before
            elif row == rows:
                source = after
            else:
                source = image_ref[region, row]
            padded[RIM : RIM + columns, :] = source.astype(jnp.float32)
            strips.append(three_windows(padded[...], columns))
            if len(strips) == 3:
                total = jnp.dot(strips[0], weight_ref[0], preferred_element_type=jnp.float32)
                for down in (1, 2):
                    total = total + jnp.dot(
                        strips[down], weight_ref[down], preferred_element_type=jnp.float32
                    )
                out_ref[region, row - 1] = total.astype(jnp.bfloat16)
                strips.pop(0)


def add_pairs(terms):
    while len(terms) > 1:
        paired = [one + other for one, other in zip(terms[::2], terms[1::2])]
        terms = paired + terms[2 * len(paired) :]
    return terms[0]


def hold_kernel(value_ref, after_ref, out_ref):
    del after_ref
    out_ref[...] = value_ref[...]


def hold(value, after):
    return call(
        hold_kernel,
        "hold",
        jax.ShapeDtypeStruct(value.shape, value.dtype),
        [VMEM(), ANY()],
        moved=4 * value.size,
    )(value, after)


def sum_cores_kernel(quad_ref, keep_ref, other_ref, *refs):
    total = refs[-1]
    total[...] = keep_ref[...] + other_ref[...]
    for distance, ref in enumerate(refs[:-1]):
        rows = rows_at(lax.bitwise_xor(quad_ref[0], distance), ref.shape[0])
        ref[...] = total[rows, :].astype(jnp.bfloat16)


def sum_kernel(factor, *refs):
    total = add_pairs([ref[...].astype(jnp.float32) for ref in refs[:-1]])
    refs[-1][...] = (total * factor).astype(jnp.bfloat16)


def join_kernel(quad_ref, done_ref, *refs):
    del done_ref
    for distance, ref in enumerate(refs[:-1]):
        rows = rows_at(lax.bitwise_xor(quad_ref[0], distance), ref.shape[0])
        refs[-1][rows, :] = ref[...]


def spread_kernel(core_ref, own_ref, other_ref, out_ref):
    half = own_ref.shape[0]
    out_ref[rows_at(core_ref[0], half), :] = own_ref[...].astype(jnp.float32)
    out_ref[rows_at(1 - core_ref[0], half), :] = other_ref[...].astype(jnp.float32)


def trade(values, distance):
    pairs = [(i, i ^ distance) for i in range(lax.axis_size("seq"))]
    return lax.ppermute(values, "seq", pairs)


def inner_size(seq_count):
    inner = 1
    while seq_count % (2 * inner) == 0 and (2 * inner) ** 2 <= seq_count:
        inner *= 2
    return inner


def trade_chips(values, distance, inner):
    seq_count = lax.axis_size("seq")
    pairs = []
    for outer in range(lax.axis_size("dp")):
        for seq in range(seq_count):
            chip, lane = divmod((outer // 2 * inner + seq % inner) ^ distance, inner)
            partner = (2 * chip + outer % 2) * seq_count + seq - seq % inner + lane
            pairs.append((outer * seq_count + seq, partner))
    return lax.ppermute(values, ("dp", "seq"), pairs)


def trade_cores(values):
    return lax.ppermute(values, "dp", [(i, i ^ 1) for i in range(lax.axis_size("dp"))])


def body(query_rows, key_rows, value_rows, region_lengths, norm_gain, conv_weight, cotangent):
    tokens, regions, model_width = query_rows.shape
    width = model_width // HEADS
    seq_count = lax.axis_size("seq")
    seq_index = lax.axis_index("seq")
    inner = inner_size(seq_count)
    quad_size = lax.axis_size("dp") // 2 * inner
    dp_index = lax.axis_index("dp")
    lane = lax.bitwise_and(seq_index, inner - 1)
    quad = (lax.shift_right_logical(dp_index, 1) * inner + lane).reshape(1)
    core = lax.bitwise_and(dp_index, 1).reshape(1)
    columns = tokens * PATCH
    capacity = seq_count * tokens
    per_device = regions * HEADS // seq_count
    far_pairs = [(i, i + 1) for i in range(1, seq_count - 1, 2)]
    far_pairs = far_pairs + [(j, i) for i, j in far_pairs]
    local_bytes = 2 * query_rows.size

    edge_shape = jax.ShapeDtypeStruct((regions, columns, width), jnp.bfloat16)
    chunk_shape = jax.ShapeDtypeStruct((3, per_device, tokens, width), jnp.bfloat16)
    index = seq_index.reshape(1)
    odd = lax.bitwise_and(seq_index, 1) == 1
    cot_far = jnp.where(odd, cotangent[:, PATCH - 1], cotangent[:, 0])
    cot_near = jnp.where(odd, cotangent[:, 0], cotangent[:, PATCH - 1])
    half = seq_count // 2
    early = [2, half, half + 1]
    late = [distance for distance in range(1, seq_count) if distance not in early]
    span = max(1, per_device // regions) * width

    def pack(name, distances):
        return call(
            functools.partial(pack_kernel, distances, regions, per_device),
            name,
            [chunk_shape] * len(distances),
            [SMEM()] + [HBM()] * 3,
            out_specs=[HBM()] * len(distances),
            scratch=[
                pltpu.VMEM((len(distances), 3, tokens, regions, span), jnp.bfloat16),
                pltpu.VMEM((len(distances),) + chunk_shape.shape, jnp.bfloat16),
                pltpu.SemaphoreType.DMA((3 * len(distances),)),
                pltpu.SemaphoreType.DMA((len(distances),)),
            ],
            moved=4 * len(distances) * chunk_shape.size,
            grant=VMEM_WHOLE,
        )(index, query_rows, key_rows, value_rows)

    packed = {}
    for distance, chunk in zip(early, pack("pack_early", early)):
        packed[distance] = trade(chunk, distance)
    for distance, chunk in zip(late, pack("pack_late", late)):
        packed[distance] = trade(chunk, distance)
    order = list(range(1, seq_count)) + [0]
    packed[0], cot_near, cot_far = call(
        functools.partial(own_kernel, regions, per_device),
        "own_chunk",
        [chunk_shape, edge_shape, edge_shape],
        [SMEM()] + [HBM()] * 3 + [VMEM()] * 2,
        scratch=[
            pltpu.VMEM((3, tokens, regions, span), jnp.bfloat16),
            pltpu.SemaphoreType.DMA((3,)),
        ],
        moved=12 * chunk_shape.size,
    )(index, query_rows, key_rows, value_rows, cot_near, cot_far)
    cot_near = trade(cot_near, 1)
    cot_far = lax.ppermute(cot_far, "seq", far_pairs)

    items = seq_index * per_device + jnp.arange(per_device, dtype=jnp.int32)
    item_lengths = jnp.sum(
        jnp.where(
            (items % regions)[:, None] == jnp.arange(regions, dtype=jnp.int32)[None, :],
            region_lengths[None, :],
            0,
        ),
        axis=1,
    )
    block_rows = min(256, capacity)
    group = regions if per_device % regions == 0 else per_device
    mixed = call(
        functools.partial(attend_kernel, block_rows, group, order),
        "attend",
        [jax.ShapeDtypeStruct((per_device, tokens, width), jnp.bfloat16)] * seq_count,
        [SMEM(), SMEM()] + [VMEM()] * seq_count,
        flops=4 * per_device * capacity * capacity * width,
        moved=4 * local_bytes,
        exps=per_device * capacity * capacity,
    )(index, item_lengths, *[packed[distance] for distance in order])
    back = list(range(half, seq_count)) + list(range(2, half)) + [1]
    attended = [trade(mixed[distance], distance) for distance in back] + [mixed[0]]

    turned = call(
        turn_kernel,
        "turn_cotangent",
        jax.ShapeDtypeStruct((3 * width, cotangent.size // width), jnp.bfloat16),
        [SMEM()] + [VMEM()] * 3,
        moved=8 * cotangent.size,
    )(index, cotangent, cot_near, cot_far)
    chunk_rows = -(-9 * width // (32 * quad_size)) * 16
    half_rows = quad_size * chunk_rows
    pixel_rows = regions * PATCH * columns
    conv_flops = 18 * pixel_rows * width * width
    chunk_moved = 8 * chunk_rows * width
    image, near, far, keep, send = call(
        functools.partial(norm_kernel, back + [0]),
        "norm_and_gradient",
        [jax.ShapeDtypeStruct((regions, PATCH, columns, width), jnp.bfloat16)]
        + [edge_shape] * 2
        + [jax.ShapeDtypeStruct((half_rows, width), jnp.float32)] * 2,
        [SMEM()] * 3 + [VMEM()] * (2 + seq_count),
        scratch=[
            pltpu.VMEM((seq_count,) + mixed[0].shape, jnp.bfloat16),
            pltpu.VMEM((regions, PATCH, columns + 2 * RIM, width), jnp.float32),
            pltpu.VMEM((pixel_rows, 3 * width), jnp.bfloat16),
            pltpu.VMEM((2 * half_rows, width), jnp.float32),
        ],
        flops=conv_flops,
        moved=4 * local_bytes,
    )(region_lengths, index, core, norm_gain.reshape(HEADS, width), turned, *attended)
    chunk_shape = jax.ShapeDtypeStruct((chunk_rows, width), jnp.bfloat16)
    parts = call(
        sum_cores_kernel,
        "sum_cores",
        [chunk_shape] * quad_size,
        [SMEM()] + [VMEM()] * 2,
        scratch=[pltpu.VMEM((half_rows, width), jnp.float32)],
        moved=quad_size * chunk_moved,
    )(quad, keep, trade_cores(send))
    distances = range(1, quad_size)
    plane_sum = call(
        functools.partial(sum_kernel, 1.0),
        "sum_chips",
        chunk_shape,
        [VMEM()] * quad_size,
        moved=chunk_moved,
    )(parts[0], *[trade_chips(parts[distance], distance, inner) for distance in distances])
    near = trade(hold(near, plane_sum), 1)
    plane_sums = [plane_sum] + [
        trade(plane_sum, distance) for distance in range(inner, seq_count, inner)
    ]
    total = call(
        functools.partial(sum_kernel, 1.0 / math.sqrt(PATCH * columns)),
        "sum_planes",
        chunk_shape,
        [VMEM()] * len(plane_sums),
        moved=chunk_moved,
    )(*plane_sums)
    far = lax.ppermute(hold(far, total), "seq", far_pairs)
    decoded, done = call(
        decode_kernel,
        "decode",
        [
            jax.ShapeDtypeStruct(cotangent.shape, jnp.bfloat16),
            jax.ShapeDtypeStruct((8, width), jnp.float32),
        ],
        [SMEM()] + [VMEM()] * 4,
        scratch=[pltpu.VMEM((columns + 2 * RIM, width), jnp.float32)],
        flops=conv_flops,
        moved=2 * local_bytes,
    )(index, image, near, far, conv_weight.reshape(3, 3 * width, width))
    joined = call(
        join_kernel,
        "join_chips",
        jax.ShapeDtypeStruct((half_rows, width), jnp.bfloat16),
        [SMEM(), ANY()] + [VMEM()] * quad_size,
        moved=quad_size * chunk_moved,
    )(quad, done, total, *[trade_chips(total, distance, inner) for distance in distances])
    weight_grad = call(
        spread_kernel,
        "spread_sums",
        jax.ShapeDtypeStruct((2 * half_rows, width), jnp.float32),
        [SMEM()] + [VMEM()] * 2,
        moved=2 * quad_size * chunk_moved,
    )(core, joined, trade_cores(joined))
    return (decoded, weight_grad[: 9 * width].reshape(conv_weight.shape))


def solution(mesh):
    placed = (
        P("seq", "dp", None),
        P("seq", "dp", None),
        P("seq", "dp", None),
        P("dp"),
        P(),
        P(),
        P("dp", "seq", None, None),
    )
    return jax.shard_map(
        body,
        mesh=mesh,
        in_specs=placed,
        out_specs=(P("dp", "seq", None, None), P()),
        check_vma=False,
    )
```

```python
import functools
import math

import jax
import jax.numpy as jnp
from jax import lax
from jax.experimental import pallas as pl
from jax.experimental.pallas import tpu as pltpu
from jax.sharding import PartitionSpec as P

HEADS = 16
PATCH = 4
RIM = 8
VMEM_LIMIT = 48 * 1024 * 1024
VMEM_WHOLE = 60 * 1024 * 1024

VMEM = functools.partial(pl.BlockSpec, memory_space=pltpu.VMEM)
HBM = functools.partial(pl.BlockSpec, memory_space=pltpu.HBM)
ANY = functools.partial(pl.BlockSpec, memory_space=pl.ANY)
SMEM = functools.partial(pl.BlockSpec, memory_space=pltpu.SMEM)


def call(kernel, name, out_shape, in_specs, out_specs=None, scratch=(), flops=0, moved=0, exps=0, grant=VMEM_LIMIT):
    many = isinstance(out_shape, (list, tuple))
    return pl.pallas_call(
        kernel,
        out_shape=out_shape,
        in_specs=in_specs,
        out_specs=out_specs or ([VMEM() for _ in out_shape] if many else VMEM()),
        scratch_shapes=list(scratch),
        compiler_params=pltpu.CompilerParams(vmem_limit_bytes=grant),
        cost_estimate=pl.CostEstimate(flops=flops, bytes_accessed=moved, transcendentals=exps),
        name=name,
    )


def columns_of(index, distance, regions, per_device, width):
    owner = lax.bitwise_xor(index, distance)
    span = max(1, per_device // regions) * width
    start = lax.div(owner * per_device, regions) * width
    return owner, pl.ds(pl.multiple_of(start, width), span)


def take_items(held, owner, regions, per_device, width, out_ref):
    for head in range(held.shape[2] // width):
        block = held[:, :, head * width : (head + 1) * width].astype(jnp.float32)
        if per_device % regions:
            value = block[:, 0, :]
            for other in range(1, regions):
                value = jnp.where(lax.rem(owner, regions) == other, block[:, other, :], value)
            out_ref[head] = value.astype(jnp.bfloat16)
        else:
            for region in range(regions):
                out_ref[head * regions + region] = block[:, region, :].astype(jnp.bfloat16)


def pack_kernel(distances, regions, per_device, index_ref, query_ref, key_ref, value_ref, *refs):
    held, ready, load_sems, store_sems = refs[-4:]
    width = query_ref.shape[2] // HEADS
    loads = []
    for number, distance in enumerate(distances):
        owner, columns = columns_of(index_ref[0], distance, regions, per_device, width)
        for which, ref in enumerate((query_ref, key_ref, value_ref)):
            load = pltpu.make_async_copy(
                ref.at[:, :, columns], held.at[number, which], load_sems.at[3 * number + which]
            )
            load.start()
            loads.append((number, which, owner, load))
    stores = []
    for number, which, owner, load in loads:
        load.wait()
        take_items(
            held.at[number, which], owner, regions, per_device, width, ready.at[number, which]
        )
        if which == 2:
            store = pltpu.make_async_copy(ready.at[number], refs[number], store_sems.at[number])
            store.start()
            stores.append(store)
    for store in stores:
        store.wait()


def own_kernel(
    regions,
    per_device,
    index_ref,
    query_ref,
    key_ref,
    value_ref,
    near_ref,
    far_ref,
    out_ref,
    near_out_ref,
    far_out_ref,
    held,
    sems,
):
    near_out_ref[...] = near_ref[...]
    far_out_ref[...] = far_ref[...]
    width = out_ref.shape[3]
    owner, columns = columns_of(index_ref[0], 0, regions, per_device, width)
    loads = []
    for which, ref in enumerate((query_ref, key_ref, value_ref)):
        loads.append(
            pltpu.make_async_copy(ref.at[:, :, columns], held.at[which], sems.at[which])
        )
        loads[-1].start()
    for which, load in enumerate(loads):
        load.wait()
        take_items(held.at[which], owner, regions, per_device, width, out_ref.at[which])


def attend_kernel(block_rows, group, order, index_ref, lengths_ref, *refs):
    chunks = dict(zip(order, refs))
    out_refs = refs[len(order) :]
    index = index_ref[0]
    sources = len(chunks)
    _, per_device, tokens, width = chunks[0].shape
    capacity = sources * tokens
    per_block = block_rows // tokens
    blocks = capacity // block_rows
    factor = math.log2(math.e) / math.sqrt(width)
    columns = lax.broadcasted_iota(jnp.int32, (1, capacity), 1)
    slots = columns
    for distance in range(sources):
        here = (columns >= distance * tokens) & (columns < (distance + 1) * tokens)
        moved = (lax.bitwise_xor(index, distance) - distance) * tokens
        slots = jnp.where(here, columns + moved, slots)

    def rows_of(which, item, distances):
        return jnp.concatenate([chunks[distance][which, item] for distance in distances], axis=0)

    def distances_of(block):
        return range(block * per_block, (block + 1) * per_block)

    def start_of(block, span):
        return lax.bitwise_xor(lax.div(index, span), block) * span

    def clear(item, block):
        for distance in distances_of(block):
            out_refs[distance][item] = jnp.zeros((tokens, width), jnp.bfloat16)

    def score(item, block):
        return lax.dot_general(
            rows_of(0, item, distances_of(block)),
            rows_of(1, item, range(sources)),
            (((1,), (1,)), ((), ())),
            preferred_element_type=jnp.float32,
        )

    def finish(item, block, scores, key_valid):
        scores = jnp.where(key_valid, scores * factor, -1e30)
        powers = jnp.exp2(scores - jnp.max(scores, axis=1, keepdims=True))
        totals = jnp.sum(powers, axis=1, keepdims=True)
        mixed = jnp.dot(
            powers.astype(jnp.bfloat16),
            rows_of(2, item, range(sources)),
            preferred_element_type=jnp.float32,
        )
        mixed = (mixed / totals).astype(jnp.bfloat16)
        for number, distance in enumerate(distances_of(block)):
            out_refs[distance][item] = mixed[number * tokens : (number + 1) * tokens]

    def attend(items, live, dead, length):
        key_valid = slots < length
        waiting = None
        for block in live:
            for item in items:
                scores = score(item, block)
                if waiting is not None:
                    finish(*waiting, key_valid)
                waiting = (item, block, scores)
        if waiting is not None:
            finish(*waiting, key_valid)
        for block in dead:
            for item in items:
                clear(item, block)

    for lead in range(group):
        length = lengths_ref[lead]
        items = list(range(lead, per_device, group))
        for block in range(0, blocks, 2):
            pair = list(range(block, min(block + 2, blocks)))
            alive = [length > start_of(one, per_block) * tokens for one in pair]
            for case in range(2 ** len(pair)):
                live = [one for bit, one in enumerate(pair) if case >> bit & 1]
                dead = [one for one in pair if one not in live]
                chosen = None
                for bit in range(len(pair)):
                    test = alive[bit] if case >> bit & 1 else jnp.logical_not(alive[bit])
                    chosen = test if chosen is None else chosen & test

                @pl.when(chosen)
                def _(items=items, live=live, dead=dead, length=length):
                    attend(items, live, dead, length)


def three_windows(padded, columns):
    return jnp.concatenate(
        [padded[RIM - 1 + shift : RIM - 1 + shift + columns].astype(jnp.bfloat16) for shift in range(3)],
        axis=1,
    )


def rows_at(place, rows):
    return pl.ds(pl.multiple_of(place * rows, rows), rows)


def around(odd, near, far):
    return jnp.where(odd == 1, near, far), jnp.where(odd == 1, far, near)


def turn_kernel(index_ref, cot_ref, near_ref, far_ref, out_ref):
    regions, rows, columns, width = cot_ref.shape
    for region in range(regions):
        before, after = around(lax.rem(index_ref[0], 2), near_ref[region], far_ref[region])
        for row in range(-1, rows + 1):
            value = before if row < 0 else after if row == rows else cot_ref[region, row]
            turned = value.T
            for down in range(3):
                image_row = row - 1 + down
                if 0 <= image_row < rows:
                    start = (region * rows + image_row) * columns
                    out_ref[down * width : (down + 1) * width, start : start + columns] = turned


def norm_kernel(order, lengths_ref, index_ref, core_ref, gain_ref, turned_ref, *refs):
    image_ref, near_ref, far_ref, keep_ref, send_ref, attended, pixels, windows, grads = refs[-9:]
    for distance, ref in zip(order, refs):
        attended[lax.bitwise_xor(index_ref[0], distance)] = ref[...]
    heads = gain_ref.shape[0]
    regions = image_ref.shape[0]
    _, per_device, tokens, width = attended.shape

    def load(head, region):
        owner, place = divmod(head * regions + region, per_device)
        return attended[owner, place].astype(jnp.float32)

    columns = tokens * PATCH
    features = heads * width
    odd = lax.rem(index_ref[0], 2)
    position = index_ref[0] * tokens + lax.broadcasted_iota(jnp.int32, (tokens, 1), 0)
    pixels[:, :, :RIM, :] = jnp.zeros((regions, PATCH, RIM, width), jnp.float32)
    pixels[:, :, RIM + columns :, :] = jnp.zeros((regions, PATCH, RIM, width), jnp.float32)
    for region in range(regions):
        total = jnp.zeros((tokens, width), jnp.float32)
        for head in range(heads):
            total = total + load(head, region)
        mean = jnp.sum(total, axis=1, keepdims=True) * (1.0 / features)
        total = jnp.zeros((tokens, width), jnp.float32)
        for head in range(heads):
            centered = load(head, region) - mean
            total = total + centered * centered
        variance = jnp.sum(total, axis=1, keepdims=True) * (1.0 / features)
        spread = lax.rsqrt(variance + 1e-05)
        live = position < lengths_ref[region]
        for head in range(heads):
            centered = load(head, region) - mean
            normed = jnp.where(live, centered * spread * gain_ref[head : head + 1, :], 0.0)
            row, column = divmod(head, PATCH)
            pixels[region, row, pl.ds(RIM + column, tokens, stride=PATCH), :] = normed
        for row in range(PATCH):
            window = three_windows(pixels[region, row], columns)
            image_ref[region, row] = window[:, width : 2 * width]
            start = (region * PATCH + row) * columns
            windows[start : start + columns, :] = window
        near_ref[region] = image_ref[region, (1 - odd) * (PATCH - 1)]
        far_ref[region] = image_ref[region, odd * (PATCH - 1)]
        part = slice(region * PATCH * columns, (region + 1) * PATCH * columns)
        term = jnp.dot(turned_ref[:, part], windows[part, :], preferred_element_type=jnp.float32)
        product = term if region == 0 else product + term
    for down in range(3):
        for across in range(3):
            tap = 3 * down + across
            grads[tap * width : (tap + 1) * width, :] = product[
                down * width : (down + 1) * width, across * width : (across + 1) * width
            ].T
    filled = 9 * width
    if filled < grads.shape[0]:
        grads[filled:, :] = jnp.zeros((grads.shape[0] - filled, width), jnp.float32)
    half = keep_ref.shape[0]
    keep_ref[...] = grads[rows_at(core_ref[0], half), :]
    send_ref[...] = grads[rows_at(1 - core_ref[0], half), :]


def decode_kernel(index_ref, image_ref, near_ref, far_ref, weight_ref, out_ref, padded):
    regions, rows, columns, width = image_ref.shape
    padded[:RIM, :] = jnp.zeros((RIM, width), jnp.float32)
    padded[RIM + columns :, :] = jnp.zeros((RIM, width), jnp.float32)
    for region in range(regions):
        strips = []
        before, after = around(lax.rem(index_ref[0], 2), near_ref[region], far_ref[region])
        for row in range(-1, rows + 1):
            if row < 0:
                source = before
            elif row == rows:
                source = after
            else:
                source = image_ref[region, row]
            padded[RIM : RIM + columns, :] = source.astype(jnp.float32)
            strips.append(three_windows(padded[...], columns))
            if len(strips) == 3:
                total = jnp.dot(strips[0], weight_ref[0], preferred_element_type=jnp.float32)
                for down in (1, 2):
                    total = total + jnp.dot(
                        strips[down], weight_ref[down], preferred_element_type=jnp.float32
                    )
                out_ref[region, row - 1] = total.astype(jnp.bfloat16)
                strips.pop(0)


def add_pairs(terms):
    while len(terms) > 1:
        paired = [one + other for one, other in zip(terms[::2], terms[1::2])]
        terms = paired + terms[2 * len(paired) :]
    return terms[0]


def hold_kernel(value_ref, after_ref, out_ref):
    del after_ref
    out_ref[...] = value_ref[...]


def hold(value, after):
    return call(
        hold_kernel,
        "hold",
        jax.ShapeDtypeStruct(value.shape, value.dtype),
        [VMEM(), ANY()],
        moved=4 * value.size,
    )(value, after)


def sum_cores_kernel(quad_ref, keep_ref, other_ref, *refs):
    total = refs[-1]
    total[...] = keep_ref[...] + other_ref[...]
    for distance, ref in enumerate(refs[:-1]):
        rows = rows_at(lax.bitwise_xor(quad_ref[0], distance), ref.shape[0])
        ref[...] = total[rows, :].astype(jnp.bfloat16)


def sum_kernel(factor, *refs):
    total = add_pairs([ref[...].astype(jnp.float32) for ref in refs[:-1]])
    refs[-1][...] = (total * factor).astype(jnp.bfloat16)


def join_kernel(quad_ref, *refs):
    for distance, ref in enumerate(refs[:-1]):
        rows = rows_at(lax.bitwise_xor(quad_ref[0], distance), ref.shape[0])
        refs[-1][rows, :] = ref[...]


def spread_kernel(core_ref, own_ref, other_ref, out_ref):
    half = own_ref.shape[0]
    out_ref[rows_at(core_ref[0], half), :] = own_ref[...].astype(jnp.float32)
    out_ref[rows_at(1 - core_ref[0], half), :] = other_ref[...].astype(jnp.float32)


def trade(values, distance):
    pairs = [(i, i ^ distance) for i in range(lax.axis_size("seq"))]
    return lax.ppermute(values, "seq", pairs)


def inner_size(seq_count):
    inner = 1
    while seq_count % (2 * inner) == 0 and (2 * inner) ** 2 <= seq_count:
        inner *= 2
    return inner


def trade_chips(values, distance, inner):
    seq_count = lax.axis_size("seq")
    pairs = []
    for outer in range(lax.axis_size("dp")):
        for seq in range(seq_count):
            chip, lane = divmod((outer // 2 * inner + seq % inner) ^ distance, inner)
            partner = (2 * chip + outer % 2) * seq_count + seq - seq % inner + lane
            pairs.append((outer * seq_count + seq, partner))
    return lax.ppermute(values, ("dp", "seq"), pairs)


def trade_cores(values):
    return lax.ppermute(values, "dp", [(i, i ^ 1) for i in range(lax.axis_size("dp"))])


def body(query_rows, key_rows, value_rows, region_lengths, norm_gain, conv_weight, cotangent):
    tokens, regions, model_width = query_rows.shape
    width = model_width // HEADS
    seq_count = lax.axis_size("seq")
    seq_index = lax.axis_index("seq")
    inner = inner_size(seq_count)
    quad_size = lax.axis_size("dp") // 2 * inner
    dp_index = lax.axis_index("dp")
    lane = lax.bitwise_and(seq_index, inner - 1)
    quad = (lax.shift_right_logical(dp_index, 1) * inner + lane).reshape(1)
    core = lax.bitwise_and(dp_index, 1).reshape(1)
    columns = tokens * PATCH
    capacity = seq_count * tokens
    per_device = regions * HEADS // seq_count
    far_pairs = [(i, i + 1) for i in range(1, seq_count - 1, 2)]
    far_pairs = far_pairs + [(j, i) for i, j in far_pairs]
    local_bytes = 2 * query_rows.size

    edge_shape = jax.ShapeDtypeStruct((regions, columns, width), jnp.bfloat16)
    chunk_shape = jax.ShapeDtypeStruct((3, per_device, tokens, width), jnp.bfloat16)
    index = seq_index.reshape(1)
    odd = lax.bitwise_and(seq_index, 1) == 1
    cot_far = jnp.where(odd, cotangent[:, PATCH - 1], cotangent[:, 0])
    cot_near = jnp.where(odd, cotangent[:, 0], cotangent[:, PATCH - 1])
    half = seq_count // 2
    early = [2, half, half + 1]
    late = [distance for distance in range(1, seq_count) if distance not in early]
    span = max(1, per_device // regions) * width

    def pack(name, distances):
        return call(
            functools.partial(pack_kernel, distances, regions, per_device),
            name,
            [chunk_shape] * len(distances),
            [SMEM()] + [HBM()] * 3,
            out_specs=[HBM()] * len(distances),
            scratch=[
                pltpu.VMEM((len(distances), 3, tokens, regions, span), jnp.bfloat16),
                pltpu.VMEM((len(distances),) + chunk_shape.shape, jnp.bfloat16),
                pltpu.SemaphoreType.DMA((3 * len(distances),)),
                pltpu.SemaphoreType.DMA((len(distances),)),
            ],
            moved=4 * len(distances) * chunk_shape.size,
            grant=VMEM_WHOLE,
        )(index, query_rows, key_rows, value_rows)

    packed = {}
    for distance, chunk in zip(early, pack("pack_early", early)):
        packed[distance] = trade(chunk, distance)
    for distance, chunk in zip(late, pack("pack_late", late)):
        packed[distance] = trade(chunk, distance)
    order = list(range(1, seq_count)) + [0]
    packed[0], cot_near, cot_far = call(
        functools.partial(own_kernel, regions, per_device),
        "own_chunk",
        [chunk_shape, edge_shape, edge_shape],
        [SMEM()] + [HBM()] * 3 + [VMEM()] * 2,
        scratch=[
            pltpu.VMEM((3, tokens, regions, span), jnp.bfloat16),
            pltpu.SemaphoreType.DMA((3,)),
        ],
        moved=12 * chunk_shape.size,
    )(index, query_rows, key_rows, value_rows, cot_near, cot_far)
    cot_near = trade(cot_near, 1)
    cot_far = lax.ppermute(cot_far, "seq", far_pairs)

    items = seq_index * per_device + jnp.arange(per_device, dtype=jnp.int32)
    item_lengths = jnp.sum(
        jnp.where(
            (items % regions)[:, None] == jnp.arange(regions, dtype=jnp.int32)[None, :],
            region_lengths[None, :],
            0,
        ),
        axis=1,
    )
    block_rows = min(256, capacity)
    group = regions if per_device % regions == 0 else per_device
    mixed = call(
        functools.partial(attend_kernel, block_rows, group, order),
        "attend",
        [jax.ShapeDtypeStruct((per_device, tokens, width), jnp.bfloat16)] * seq_count,
        [SMEM(), SMEM()] + [VMEM()] * seq_count,
        flops=4 * per_device * capacity * capacity * width,
        moved=4 * local_bytes,
        exps=per_device * capacity * capacity,
    )(index, item_lengths, *[packed[distance] for distance in order])
    back = list(range(half, seq_count)) + list(range(2, half)) + [1]
    attended = [trade(mixed[distance], distance) for distance in back] + [mixed[0]]

    turned = call(
        turn_kernel,
        "turn_cotangent",
        jax.ShapeDtypeStruct((3 * width, cotangent.size // width), jnp.bfloat16),
        [SMEM()] + [VMEM()] * 3,
        moved=8 * cotangent.size,
    )(index, cotangent, cot_near, cot_far)
    chunk_rows = -(-9 * width // (32 * quad_size)) * 16
    half_rows = quad_size * chunk_rows
    pixel_rows = regions * PATCH * columns
    conv_flops = 18 * pixel_rows * width * width
    chunk_moved = 8 * chunk_rows * width
    image, near, far, keep, send = call(
        functools.partial(norm_kernel, back + [0]),
        "norm_and_gradient",
        [jax.ShapeDtypeStruct((regions, PATCH, columns, width), jnp.bfloat16)]
        + [edge_shape] * 2
        + [jax.ShapeDtypeStruct((half_rows, width), jnp.float32)] * 2,
        [SMEM()] * 3 + [VMEM()] * (2 + seq_count),
        scratch=[
            pltpu.VMEM((seq_count,) + mixed[0].shape, jnp.bfloat16),
            pltpu.VMEM((regions, PATCH, columns + 2 * RIM, width), jnp.float32),
            pltpu.VMEM((pixel_rows, 3 * width), jnp.bfloat16),
            pltpu.VMEM((2 * half_rows, width), jnp.float32),
        ],
        flops=conv_flops,
        moved=4 * local_bytes,
    )(region_lengths, index, core, norm_gain.reshape(HEADS, width), turned, *attended)
    chunk_shape = jax.ShapeDtypeStruct((chunk_rows, width), jnp.bfloat16)
    parts = call(
        sum_cores_kernel,
        "sum_cores",
        [chunk_shape] * quad_size,
        [SMEM()] + [VMEM()] * 2,
        scratch=[pltpu.VMEM((half_rows, width), jnp.float32)],
        moved=quad_size * chunk_moved,
    )(quad, keep, trade_cores(send))
    distances = range(1, quad_size)
    plane_sum = call(
        functools.partial(sum_kernel, 1.0),
        "sum_chips",
        chunk_shape,
        [VMEM()] * quad_size,
        moved=chunk_moved,
    )(parts[0], *[trade_chips(parts[distance], distance, inner) for distance in distances])
    near = trade(hold(near, plane_sum), 1)
    far = lax.ppermute(hold(far, plane_sum), "seq", far_pairs)
    plane_sums = [plane_sum] + [
        trade(plane_sum, distance) for distance in range(inner, seq_count, inner)
    ]
    decoded = call(
        decode_kernel,
        "decode",
        jax.ShapeDtypeStruct(cotangent.shape, jnp.bfloat16),
        [SMEM()] + [VMEM()] * 4,
        scratch=[pltpu.VMEM((columns + 2 * RIM, width), jnp.float32)],
        flops=conv_flops,
        moved=2 * local_bytes,
    )(index, image, near, far, conv_weight.reshape(3, 3 * width, width))
    total = call(
        functools.partial(sum_kernel, 1.0 / math.sqrt(PATCH * columns)),
        "sum_planes",
        chunk_shape,
        [VMEM()] * len(plane_sums),
        moved=chunk_moved,
    )(*plane_sums)
    joined = call(
        join_kernel,
        "join_chips",
        jax.ShapeDtypeStruct((half_rows, width), jnp.bfloat16),
        [SMEM()] + [VMEM()] * quad_size,
        moved=quad_size * chunk_moved,
    )(quad, total, *[trade_chips(total, distance, inner) for distance in distances])
    weight_grad = call(
        spread_kernel,
        "spread_sums",
        jax.ShapeDtypeStruct((2 * half_rows, width), jnp.float32),
        [SMEM()] + [VMEM()] * 2,
        moved=2 * quad_size * chunk_moved,
    )(core, joined, trade_cores(joined))
    return (decoded, weight_grad[: 9 * width].reshape(conv_weight.shape))


def solution(mesh):
    placed = (
        P("seq", "dp", None),
        P("seq", "dp", None),
        P("seq", "dp", None),
        P("dp"),
        P(),
        P(),
        P("dp", "seq", None, None),
    )
    return jax.shard_map(
        body,
        mesh=mesh,
        in_specs=placed,
        out_specs=(P("dp", "seq", None, None), P()),
        check_vma=False,
    )
```

```python
import functools
import math

import jax
import jax.numpy as jnp
from jax import lax
from jax.experimental import pallas as pl
from jax.experimental.pallas import tpu as pltpu
from jax.sharding import PartitionSpec as P

HEADS = 16
PATCH = 4
RIM = 8
VMEM_LIMIT = 48 * 1024 * 1024
VMEM_WHOLE = 60 * 1024 * 1024

VMEM = functools.partial(pl.BlockSpec, memory_space=pltpu.VMEM)
HBM = functools.partial(pl.BlockSpec, memory_space=pltpu.HBM)
ANY = functools.partial(pl.BlockSpec, memory_space=pl.ANY)
SMEM = functools.partial(pl.BlockSpec, memory_space=pltpu.SMEM)


def call(kernel, name, out_shape, in_specs, out_specs=None, scratch=(), flops=0, moved=0, exps=0, grant=VMEM_LIMIT):
    many = isinstance(out_shape, (list, tuple))
    return pl.pallas_call(
        kernel,
        out_shape=out_shape,
        in_specs=in_specs,
        out_specs=out_specs or ([VMEM() for _ in out_shape] if many else VMEM()),
        scratch_shapes=list(scratch),
        compiler_params=pltpu.CompilerParams(vmem_limit_bytes=grant),
        cost_estimate=pl.CostEstimate(flops=flops, bytes_accessed=moved, transcendentals=exps),
        name=name,
    )


def columns_of(index, distance, regions, per_device, width):
    owner = lax.bitwise_xor(index, distance)
    span = max(1, per_device // regions) * width
    start = lax.div(owner * per_device, regions) * width
    return owner, pl.ds(pl.multiple_of(start, width), span)


def take_items(held, owner, regions, per_device, width, out_ref):
    for head in range(held.shape[2] // width):
        block = held[:, :, head * width : (head + 1) * width].astype(jnp.float32)
        if per_device % regions:
            value = block[:, 0, :]
            for other in range(1, regions):
                value = jnp.where(lax.rem(owner, regions) == other, block[:, other, :], value)
            out_ref[head] = value.astype(jnp.bfloat16)
        else:
            for region in range(regions):
                out_ref[head * regions + region] = block[:, region, :].astype(jnp.bfloat16)


def pack_kernel(distances, regions, per_device, index_ref, query_ref, key_ref, value_ref, *refs):
    held, ready, load_sems, store_sems = refs[-4:]
    width = query_ref.shape[2] // HEADS
    loads = []
    for number, distance in enumerate(distances):
        owner, columns = columns_of(index_ref[0], distance, regions, per_device, width)
        for which, ref in enumerate((query_ref, key_ref, value_ref)):
            load = pltpu.make_async_copy(
                ref.at[:, :, columns], held.at[number, which], load_sems.at[3 * number + which]
            )
            load.start()
            loads.append((number, which, owner, load))
    stores = []
    for number, which, owner, load in loads:
        load.wait()
        take_items(
            held.at[number, which], owner, regions, per_device, width, ready.at[number, which]
        )
        if which == 2:
            store = pltpu.make_async_copy(ready.at[number], refs[number], store_sems.at[number])
            store.start()
            stores.append(store)
    for store in stores:
        store.wait()


def own_kernel(
    regions,
    per_device,
    index_ref,
    query_ref,
    key_ref,
    value_ref,
    near_ref,
    far_ref,
    out_ref,
    near_out_ref,
    far_out_ref,
    held,
    sems,
):
    near_out_ref[...] = near_ref[...]
    far_out_ref[...] = far_ref[...]
    width = out_ref.shape[3]
    owner, columns = columns_of(index_ref[0], 0, regions, per_device, width)
    loads = []
    for which, ref in enumerate((query_ref, key_ref, value_ref)):
        loads.append(
            pltpu.make_async_copy(ref.at[:, :, columns], held.at[which], sems.at[which])
        )
        loads[-1].start()
    for which, load in enumerate(loads):
        load.wait()
        take_items(held.at[which], owner, regions, per_device, width, out_ref.at[which])


def attend_kernel(block_rows, group, order, index_ref, lengths_ref, *refs):
    chunks = dict(zip(order, refs))
    out_refs = refs[len(order) :]
    index = index_ref[0]
    sources = len(chunks)
    _, per_device, tokens, width = chunks[0].shape
    capacity = sources * tokens
    per_block = block_rows // tokens
    blocks = capacity // block_rows
    factor = math.log2(math.e) / math.sqrt(width)
    columns = lax.broadcasted_iota(jnp.int32, (1, capacity), 1)
    slots = columns
    for distance in range(sources):
        here = (columns >= distance * tokens) & (columns < (distance + 1) * tokens)
        moved = (lax.bitwise_xor(index, distance) - distance) * tokens
        slots = jnp.where(here, columns + moved, slots)

    def rows_of(which, item, distances):
        return jnp.concatenate([chunks[distance][which, item] for distance in distances], axis=0)

    def distances_of(block):
        return range(block * per_block, (block + 1) * per_block)

    def start_of(block, span):
        return lax.bitwise_xor(lax.div(index, span), block) * span

    def clear(item, block):
        for distance in distances_of(block):
            out_refs[distance][item] = jnp.zeros((tokens, width), jnp.bfloat16)

    def score(item, block):
        return lax.dot_general(
            rows_of(0, item, distances_of(block)),
            rows_of(1, item, range(sources)),
            (((1,), (1,)), ((), ())),
            preferred_element_type=jnp.float32,
        )

    def finish(item, block, scores, key_valid):
        scores = jnp.where(key_valid, scores * factor, -1e30)
        powers = jnp.exp2(scores - jnp.max(scores, axis=1, keepdims=True))
        totals = jnp.sum(powers, axis=1, keepdims=True)
        mixed = jnp.dot(
            powers.astype(jnp.bfloat16),
            rows_of(2, item, range(sources)),
            preferred_element_type=jnp.float32,
        )
        mixed = (mixed / totals).astype(jnp.bfloat16)
        for number, distance in enumerate(distances_of(block)):
            out_refs[distance][item] = mixed[number * tokens : (number + 1) * tokens]

    def attend(items, live, dead, length):
        key_valid = slots < length
        waiting = None
        for block in live:
            for item in items:
                scores = score(item, block)
                if waiting is not None:
                    finish(*waiting, key_valid)
                waiting = (item, block, scores)
        if waiting is not None:
            finish(*waiting, key_valid)
        for block in dead:
            for item in items:
                clear(item, block)

    for lead in range(group):
        length = lengths_ref[lead]
        items = list(range(lead, per_device, group))
        for block in range(0, blocks, 2):
            pair = list(range(block, min(block + 2, blocks)))
            alive = [length > start_of(one, per_block) * tokens for one in pair]
            for case in range(2 ** len(pair)):
                live = [one for bit, one in enumerate(pair) if case >> bit & 1]
                dead = [one for one in pair if one not in live]
                chosen = None
                for bit in range(len(pair)):
                    test = alive[bit] if case >> bit & 1 else jnp.logical_not(alive[bit])
                    chosen = test if chosen is None else chosen & test

                @pl.when(chosen)
                def _(items=items, live=live, dead=dead, length=length):
                    attend(items, live, dead, length)


def three_windows(padded, columns):
    return jnp.concatenate(
        [padded[RIM - 1 + shift : RIM - 1 + shift + columns].astype(jnp.bfloat16) for shift in range(3)],
        axis=1,
    )


def rows_at(place, rows):
    return pl.ds(pl.multiple_of(place * rows, rows), rows)


def around(odd, near, far):
    return jnp.where(odd == 1, near, far), jnp.where(odd == 1, far, near)


def turn_kernel(index_ref, cot_ref, near_ref, far_ref, out_ref):
    regions, rows, columns, width = cot_ref.shape
    for region in range(regions):
        before, after = around(lax.rem(index_ref[0], 2), near_ref[region], far_ref[region])
        for row in range(-1, rows + 1):
            value = before if row < 0 else after if row == rows else cot_ref[region, row]
            turned = value.T
            for down in range(3):
                image_row = row - 1 + down
                if 0 <= image_row < rows:
                    start = (region * rows + image_row) * columns
                    out_ref[down * width : (down + 1) * width, start : start + columns] = turned


def norm_kernel(order, lengths_ref, index_ref, core_ref, gain_ref, turned_ref, *refs):
    image_ref, near_ref, far_ref, keep_ref, send_ref, attended, pixels, windows, grads = refs[-9:]
    for distance, ref in zip(order, refs):
        attended[lax.bitwise_xor(index_ref[0], distance)] = ref[...]
    heads = gain_ref.shape[0]
    regions = image_ref.shape[0]
    _, per_device, tokens, width = attended.shape

    def load(head, region):
        owner, place = divmod(head * regions + region, per_device)
        return attended[owner, place].astype(jnp.float32)

    columns = tokens * PATCH
    features = heads * width
    odd = lax.rem(index_ref[0], 2)
    position = index_ref[0] * tokens + lax.broadcasted_iota(jnp.int32, (tokens, 1), 0)
    pixels[:, :, :RIM, :] = jnp.zeros((regions, PATCH, RIM, width), jnp.float32)
    pixels[:, :, RIM + columns :, :] = jnp.zeros((regions, PATCH, RIM, width), jnp.float32)
    for region in range(regions):
        total = jnp.zeros((tokens, width), jnp.float32)
        for head in range(heads):
            total = total + load(head, region)
        mean = jnp.sum(total, axis=1, keepdims=True) * (1.0 / features)
        total = jnp.zeros((tokens, width), jnp.float32)
        for head in range(heads):
            centered = load(head, region) - mean
            total = total + centered * centered
        variance = jnp.sum(total, axis=1, keepdims=True) * (1.0 / features)
        spread = lax.rsqrt(variance + 1e-05)
        live = position < lengths_ref[region]
        for head in range(heads):
            centered = load(head, region) - mean
            normed = jnp.where(live, centered * spread * gain_ref[head : head + 1, :], 0.0)
            row, column = divmod(head, PATCH)
            pixels[region, row, pl.ds(RIM + column, tokens, stride=PATCH), :] = normed
        for row in range(PATCH):
            window = three_windows(pixels[region, row], columns)
            image_ref[region, row] = window[:, width : 2 * width]
            start = (region * PATCH + row) * columns
            windows[start : start + columns, :] = window
        near_ref[region] = image_ref[region, (1 - odd) * (PATCH - 1)]
        far_ref[region] = image_ref[region, odd * (PATCH - 1)]
        part = slice(region * PATCH * columns, (region + 1) * PATCH * columns)
        term = jnp.dot(turned_ref[:, part], windows[part, :], preferred_element_type=jnp.float32)
        product = term if region == 0 else product + term
    for down in range(3):
        for across in range(3):
            tap = 3 * down + across
            grads[tap * width : (tap + 1) * width, :] = product[
                down * width : (down + 1) * width, across * width : (across + 1) * width
            ].T
    filled = 9 * width
    if filled < grads.shape[0]:
        grads[filled:, :] = jnp.zeros((grads.shape[0] - filled, width), jnp.float32)
    half = keep_ref.shape[0]
    keep_ref[...] = grads[rows_at(core_ref[0], half), :]
    send_ref[...] = grads[rows_at(1 - core_ref[0], half), :]


def decode_kernel(index_ref, image_ref, near_ref, far_ref, weight_ref, out_ref, padded):
    regions, rows, columns, width = image_ref.shape
    padded[:RIM, :] = jnp.zeros((RIM, width), jnp.float32)
    padded[RIM + columns :, :] = jnp.zeros((RIM, width), jnp.float32)
    for region in range(regions):
        strips = []
        before, after = around(lax.rem(index_ref[0], 2), near_ref[region], far_ref[region])
        for row in range(-1, rows + 1):
            if row < 0:
                source = before
            elif row == rows:
                source = after
            else:
                source = image_ref[region, row]
            padded[RIM : RIM + columns, :] = source.astype(jnp.float32)
            strips.append(three_windows(padded[...], columns))
            if len(strips) == 3:
                total = jnp.dot(strips[0], weight_ref[0], preferred_element_type=jnp.float32)
                for down in (1, 2):
                    total = total + jnp.dot(
                        strips[down], weight_ref[down], preferred_element_type=jnp.float32
                    )
                out_ref[region, row - 1] = total.astype(jnp.bfloat16)
                strips.pop(0)


def add_pairs(terms):
    while len(terms) > 1:
        paired = [one + other for one, other in zip(terms[::2], terms[1::2])]
        terms = paired + terms[2 * len(paired) :]
    return terms[0]


def hold_kernel(value_ref, after_ref, out_ref):
    del after_ref
    out_ref[...] = value_ref[...]


def hold(value, after):
    return call(
        hold_kernel,
        "hold",
        jax.ShapeDtypeStruct(value.shape, value.dtype),
        [VMEM(), ANY()],
        moved=4 * value.size,
    )(value, after)


def sum_cores_kernel(quad_ref, keep_ref, other_ref, *refs):
    total = refs[-1]
    total[...] = keep_ref[...] + other_ref[...]
    for distance, ref in enumerate(refs[:-1]):
        rows = rows_at(lax.bitwise_xor(quad_ref[0], distance), ref.shape[0])
        ref[...] = total[rows, :].astype(jnp.bfloat16)


def sum_kernel(factor, *refs):
    total = add_pairs([ref[...].astype(jnp.float32) for ref in refs[:-1]])
    refs[-1][...] = (total * factor).astype(jnp.bfloat16)


def join_kernel(quad_ref, *refs):
    for distance, ref in enumerate(refs[:-1]):
        rows = rows_at(lax.bitwise_xor(quad_ref[0], distance), ref.shape[0])
        refs[-1][rows, :] = ref[...]


def spread_kernel(core_ref, own_ref, other_ref, out_ref):
    half = own_ref.shape[0]
    out_ref[rows_at(core_ref[0], half), :] = own_ref[...].astype(jnp.float32)
    out_ref[rows_at(1 - core_ref[0], half), :] = other_ref[...].astype(jnp.float32)


def trade(values, distance):
    pairs = [(i, i ^ distance) for i in range(lax.axis_size("seq"))]
    return lax.ppermute(values, "seq", pairs)


def inner_size(seq_count):
    inner = 1
    while seq_count % (2 * inner) == 0 and (2 * inner) ** 2 <= seq_count:
        inner *= 2
    return inner


def trade_chips(values, distance, inner):
    seq_count = lax.axis_size("seq")
    pairs = []
    for outer in range(lax.axis_size("dp")):
        for seq in range(seq_count):
            chip, lane = divmod((outer // 2 * inner + seq % inner) ^ distance, inner)
            partner = (2 * chip + outer % 2) * seq_count + seq - seq % inner + lane
            pairs.append((outer * seq_count + seq, partner))
    return lax.ppermute(values, ("dp", "seq"), pairs)


def trade_cores(values):
    return lax.ppermute(values, "dp", [(i, i ^ 1) for i in range(lax.axis_size("dp"))])


def body(query_rows, key_rows, value_rows, region_lengths, norm_gain, conv_weight, cotangent):
    tokens, regions, model_width = query_rows.shape
    width = model_width // HEADS
    seq_count = lax.axis_size("seq")
    seq_index = lax.axis_index("seq")
    inner = inner_size(seq_count)
    quad_size = lax.axis_size("dp") // 2 * inner
    dp_index = lax.axis_index("dp")
    lane = lax.bitwise_and(seq_index, inner - 1)
    quad = (lax.shift_right_logical(dp_index, 1) * inner + lane).reshape(1)
    core = lax.bitwise_and(dp_index, 1).reshape(1)
    columns = tokens * PATCH
    capacity = seq_count * tokens
    per_device = regions * HEADS // seq_count
    far_pairs = [(i, i + 1) for i in range(1, seq_count - 1, 2)]
    far_pairs = far_pairs + [(j, i) for i, j in far_pairs]
    local_bytes = 2 * query_rows.size

    edge_shape = jax.ShapeDtypeStruct((regions, columns, width), jnp.bfloat16)
    chunk_shape = jax.ShapeDtypeStruct((3, per_device, tokens, width), jnp.bfloat16)
    index = seq_index.reshape(1)
    odd = lax.bitwise_and(seq_index, 1) == 1
    cot_far = jnp.where(odd, cotangent[:, PATCH - 1], cotangent[:, 0])
    cot_near = jnp.where(odd, cotangent[:, 0], cotangent[:, PATCH - 1])
    half = seq_count // 2
    early = [2, half, half + 1]
    late = [distance for distance in range(1, seq_count) if distance not in early]
    span = max(1, per_device // regions) * width

    def pack(name, distances):
        return call(
            functools.partial(pack_kernel, distances, regions, per_device),
            name,
            [chunk_shape] * len(distances),
            [SMEM()] + [HBM()] * 3,
            out_specs=[HBM()] * len(distances),
            scratch=[
                pltpu.VMEM((len(distances), 3, tokens, regions, span), jnp.bfloat16),
                pltpu.VMEM((len(distances),) + chunk_shape.shape, jnp.bfloat16),
                pltpu.SemaphoreType.DMA((3 * len(distances),)),
                pltpu.SemaphoreType.DMA((len(distances),)),
            ],
            moved=4 * len(distances) * chunk_shape.size,
            grant=VMEM_WHOLE,
        )(index, query_rows, key_rows, value_rows)

    packed = {}
    for distance, chunk in zip(early, pack("pack_early", early)):
        packed[distance] = trade(chunk, distance)
    for distance, chunk in zip(late, pack("pack_late", late)):
        packed[distance] = trade(chunk, distance)
    order = list(range(1, seq_count)) + [0]
    packed[0], cot_near, cot_far = call(
        functools.partial(own_kernel, regions, per_device),
        "own_chunk",
        [chunk_shape, edge_shape, edge_shape],
        [SMEM()] + [HBM()] * 3 + [VMEM()] * 2,
        scratch=[
            pltpu.VMEM((3, tokens, regions, span), jnp.bfloat16),
            pltpu.SemaphoreType.DMA((3,)),
        ],
        moved=12 * chunk_shape.size,
    )(index, query_rows, key_rows, value_rows, cot_near, cot_far)
    cot_near = trade(cot_near, 1)
    cot_far = lax.ppermute(cot_far, "seq", far_pairs)

    items = seq_index * per_device + jnp.arange(per_device, dtype=jnp.int32)
    item_lengths = jnp.sum(
        jnp.where(
            (items % regions)[:, None] == jnp.arange(regions, dtype=jnp.int32)[None, :],
            region_lengths[None, :],
            0,
        ),
        axis=1,
    )
    block_rows = min(256, capacity)
    group = regions if per_device % regions == 0 else per_device
    mixed = call(
        functools.partial(attend_kernel, block_rows, group, order),
        "attend",
        [jax.ShapeDtypeStruct((per_device, tokens, width), jnp.bfloat16)] * seq_count,
        [SMEM(), SMEM()] + [VMEM()] * seq_count,
        flops=4 * per_device * capacity * capacity * width,
        moved=4 * local_bytes,
        exps=per_device * capacity * capacity,
    )(index, item_lengths, *[packed[distance] for distance in order])
    back = list(range(half, seq_count)) + list(range(2, half)) + [1]
    attended = [trade(mixed[distance], distance) for distance in back] + [mixed[0]]

    turned = call(
        turn_kernel,
        "turn_cotangent",
        jax.ShapeDtypeStruct((3 * width, cotangent.size // width), jnp.bfloat16),
        [SMEM()] + [VMEM()] * 3,
        moved=8 * cotangent.size,
    )(index, cotangent, cot_near, cot_far)
    chunk_rows = -(-9 * width // (32 * quad_size)) * 16
    half_rows = quad_size * chunk_rows
    pixel_rows = regions * PATCH * columns
    conv_flops = 18 * pixel_rows * width * width
    chunk_moved = 8 * chunk_rows * width
    image, near, far, keep, send = call(
        functools.partial(norm_kernel, back + [0]),
        "norm_and_gradient",
        [jax.ShapeDtypeStruct((regions, PATCH, columns, width), jnp.bfloat16)]
        + [edge_shape] * 2
        + [jax.ShapeDtypeStruct((half_rows, width), jnp.float32)] * 2,
        [SMEM()] * 3 + [VMEM()] * (2 + seq_count),
        scratch=[
            pltpu.VMEM((seq_count,) + mixed[0].shape, jnp.bfloat16),
            pltpu.VMEM((regions, PATCH, columns + 2 * RIM, width), jnp.float32),
            pltpu.VMEM((pixel_rows, 3 * width), jnp.bfloat16),
            pltpu.VMEM((2 * half_rows, width), jnp.float32),
        ],
        flops=conv_flops,
        moved=4 * local_bytes,
    )(region_lengths, index, core, norm_gain.reshape(HEADS, width), turned, *attended)
    chunk_shape = jax.ShapeDtypeStruct((chunk_rows, width), jnp.bfloat16)
    parts = call(
        sum_cores_kernel,
        "sum_cores",
        [chunk_shape] * quad_size,
        [SMEM()] + [VMEM()] * 2,
        scratch=[pltpu.VMEM((half_rows, width), jnp.float32)],
        moved=quad_size * chunk_moved,
    )(quad, keep, trade_cores(send))
    far = lax.ppermute(far, "seq", far_pairs)
    distances = range(1, quad_size)
    plane_sum = call(
        functools.partial(sum_kernel, 1.0),
        "sum_chips",
        chunk_shape,
        [VMEM()] * quad_size,
        moved=chunk_moved,
    )(parts[0], *[trade_chips(parts[distance], distance, inner) for distance in distances])
    near = trade(hold(near, plane_sum), 1)
    plane_sums = [plane_sum] + [
        trade(plane_sum, distance) for distance in range(inner, seq_count, inner)
    ]
    decoded = call(
        decode_kernel,
        "decode",
        jax.ShapeDtypeStruct(cotangent.shape, jnp.bfloat16),
        [SMEM()] + [VMEM()] * 4,
        scratch=[pltpu.VMEM((columns + 2 * RIM, width), jnp.float32)],
        flops=conv_flops,
        moved=2 * local_bytes,
    )(index, image, near, far, conv_weight.reshape(3, 3 * width, width))
    total = call(
        functools.partial(sum_kernel, 1.0 / math.sqrt(PATCH * columns)),
        "sum_planes",
        chunk_shape,
        [VMEM()] * len(plane_sums),
        moved=chunk_moved,
    )(*plane_sums)
    joined = call(
        join_kernel,
        "join_chips",
        jax.ShapeDtypeStruct((half_rows, width), jnp.bfloat16),
        [SMEM()] + [VMEM()] * quad_size,
        moved=quad_size * chunk_moved,
    )(quad, total, *[trade_chips(total, distance, inner) for distance in distances])
    weight_grad = call(
        spread_kernel,
        "spread_sums",
        jax.ShapeDtypeStruct((2 * half_rows, width), jnp.float32),
        [SMEM()] + [VMEM()] * 2,
        moved=2 * quad_size * chunk_moved,
    )(core, joined, trade_cores(joined))
    return (decoded, weight_grad[: 9 * width].reshape(conv_weight.shape))


def solution(mesh):
    placed = (
        P("seq", "dp", None),
        P("seq", "dp", None),
        P("seq", "dp", None),
        P("dp"),
        P(),
        P(),
        P("dp", "seq", None, None),
    )
    return jax.shard_map(
        body,
        mesh=mesh,
        in_specs=placed,
        out_specs=(P("dp", "seq", None, None), P()),
        check_vma=False,
    )
```

```python
import functools
import math

import jax
import jax.numpy as jnp
from jax import lax
from jax.experimental import pallas as pl
from jax.experimental.pallas import tpu as pltpu
from jax.sharding import PartitionSpec as P

HEADS = 16
PATCH = 4
RIM = 8
VMEM_LIMIT = 48 * 1024 * 1024
VMEM_WHOLE = 60 * 1024 * 1024

VMEM = functools.partial(pl.BlockSpec, memory_space=pltpu.VMEM)
HBM = functools.partial(pl.BlockSpec, memory_space=pltpu.HBM)
ANY = functools.partial(pl.BlockSpec, memory_space=pl.ANY)
SMEM = functools.partial(pl.BlockSpec, memory_space=pltpu.SMEM)


def call(kernel, name, out_shape, in_specs, out_specs=None, scratch=(), flops=0, moved=0, exps=0, grant=VMEM_LIMIT):
    many = isinstance(out_shape, (list, tuple))
    return pl.pallas_call(
        kernel,
        out_shape=out_shape,
        in_specs=in_specs,
        out_specs=out_specs or ([VMEM() for _ in out_shape] if many else VMEM()),
        scratch_shapes=list(scratch),
        compiler_params=pltpu.CompilerParams(vmem_limit_bytes=grant),
        cost_estimate=pl.CostEstimate(flops=flops, bytes_accessed=moved, transcendentals=exps),
        name=name,
    )


def columns_of(index, distance, regions, per_device, width):
    owner = lax.bitwise_xor(index, distance)
    span = max(1, per_device // regions) * width
    start = lax.div(owner * per_device, regions) * width
    return owner, pl.ds(pl.multiple_of(start, width), span)


def take_items(held, owner, regions, per_device, width, out_ref):
    for head in range(held.shape[2] // width):
        block = held[:, :, head * width : (head + 1) * width].astype(jnp.float32)
        if per_device % regions:
            value = block[:, 0, :]
            for other in range(1, regions):
                value = jnp.where(lax.rem(owner, regions) == other, block[:, other, :], value)
            out_ref[head] = value.astype(jnp.bfloat16)
        else:
            for region in range(regions):
                out_ref[head * regions + region] = block[:, region, :].astype(jnp.bfloat16)


def pack_kernel(distances, regions, per_device, index_ref, query_ref, key_ref, value_ref, *refs):
    held, ready, load_sems, store_sems = refs[-4:]
    width = query_ref.shape[2] // HEADS
    loads = []
    for number, distance in enumerate(distances):
        owner, columns = columns_of(index_ref[0], distance, regions, per_device, width)
        for which, ref in enumerate((query_ref, key_ref, value_ref)):
            load = pltpu.make_async_copy(
                ref.at[:, :, columns], held.at[number, which], load_sems.at[3 * number + which]
            )
            load.start()
            loads.append((number, which, owner, load))
    stores = []
    for number, which, owner, load in loads:
        load.wait()
        take_items(
            held.at[number, which], owner, regions, per_device, width, ready.at[number, which]
        )
        if which == 2:
            store = pltpu.make_async_copy(ready.at[number], refs[number], store_sems.at[number])
            store.start()
            stores.append(store)
    for store in stores:
        store.wait()


def own_kernel(
    regions,
    per_device,
    index_ref,
    query_ref,
    key_ref,
    value_ref,
    near_ref,
    far_ref,
    out_ref,
    near_out_ref,
    far_out_ref,
    held,
    sems,
):
    near_out_ref[...] = near_ref[...]
    far_out_ref[...] = far_ref[...]
    width = out_ref.shape[3]
    owner, columns = columns_of(index_ref[0], 0, regions, per_device, width)
    loads = []
    for which, ref in enumerate((query_ref, key_ref, value_ref)):
        loads.append(
            pltpu.make_async_copy(ref.at[:, :, columns], held.at[which], sems.at[which])
        )
        loads[-1].start()
    for which, load in enumerate(loads):
        load.wait()
        take_items(held.at[which], owner, regions, per_device, width, out_ref.at[which])


def attend_kernel(block_rows, group, order, index_ref, lengths_ref, *refs):
    chunks = dict(zip(order, refs))
    out_refs = refs[len(order) :]
    index = index_ref[0]
    sources = len(chunks)
    _, per_device, tokens, width = chunks[0].shape
    capacity = sources * tokens
    per_block = block_rows // tokens
    blocks = capacity // block_rows
    factor = math.log2(math.e) / math.sqrt(width)
    columns = lax.broadcasted_iota(jnp.int32, (1, capacity), 1)
    slots = columns
    for distance in range(sources):
        here = (columns >= distance * tokens) & (columns < (distance + 1) * tokens)
        moved = (lax.bitwise_xor(index, distance) - distance) * tokens
        slots = jnp.where(here, columns + moved, slots)

    def rows_of(which, item, distances):
        return jnp.concatenate([chunks[distance][which, item] for distance in distances], axis=0)

    def distances_of(block):
        return range(block * per_block, (block + 1) * per_block)

    def start_of(block, span):
        return lax.bitwise_xor(lax.div(index, span), block) * span

    def clear(item, block):
        for distance in distances_of(block):
            out_refs[distance][item] = jnp.zeros((tokens, width), jnp.bfloat16)

    def score(item, block):
        return lax.dot_general(
            rows_of(0, item, distances_of(block)),
            rows_of(1, item, range(sources)),
            (((1,), (1,)), ((), ())),
            preferred_element_type=jnp.float32,
        )

    def finish(item, block, scores, key_valid):
        scores = jnp.where(key_valid, scores * factor, -1e30)
        powers = jnp.exp2(scores - jnp.max(scores, axis=1, keepdims=True))
        totals = jnp.sum(powers, axis=1, keepdims=True)
        mixed = jnp.dot(
            powers.astype(jnp.bfloat16),
            rows_of(2, item, range(sources)),
            preferred_element_type=jnp.float32,
        )
        mixed = (mixed / totals).astype(jnp.bfloat16)
        for number, distance in enumerate(distances_of(block)):
            out_refs[distance][item] = mixed[number * tokens : (number + 1) * tokens]

    def attend(items, live, dead, length):
        key_valid = slots < length
        waiting = None
        for block in live:
            for item in items:
                scores = score(item, block)
                if waiting is not None:
                    finish(*waiting, key_valid)
                waiting = (item, block, scores)
        if waiting is not None:
            finish(*waiting, key_valid)
        for block in dead:
            for item in items:
                clear(item, block)

    for lead in range(group):
        length = lengths_ref[lead]
        items = list(range(lead, per_device, group))
        for block in range(0, blocks, 2):
            pair = list(range(block, min(block + 2, blocks)))
            alive = [length > start_of(one, per_block) * tokens for one in pair]
            for case in range(2 ** len(pair)):
                live = [one for bit, one in enumerate(pair) if case >> bit & 1]
                dead = [one for one in pair if one not in live]
                chosen = None
                for bit in range(len(pair)):
                    test = alive[bit] if case >> bit & 1 else jnp.logical_not(alive[bit])
                    chosen = test if chosen is None else chosen & test

                @pl.when(chosen)
                def _(items=items, live=live, dead=dead, length=length):
                    attend(items, live, dead, length)


def three_windows(padded, columns):
    return jnp.concatenate(
        [padded[RIM - 1 + shift : RIM - 1 + shift + columns].astype(jnp.bfloat16) for shift in range(3)],
        axis=1,
    )


def rows_at(place, rows):
    return pl.ds(pl.multiple_of(place * rows, rows), rows)


def around(odd, near, far):
    return jnp.where(odd == 1, near, far), jnp.where(odd == 1, far, near)


def turn_kernel(index_ref, cot_ref, near_ref, far_ref, out_ref):
    regions, rows, columns, width = cot_ref.shape
    for region in range(regions):
        before, after = around(lax.rem(index_ref[0], 2), near_ref[region], far_ref[region])
        for row in range(-1, rows + 1):
            value = before if row < 0 else after if row == rows else cot_ref[region, row]
            turned = value.T
            for down in range(3):
                image_row = row - 1 + down
                if 0 <= image_row < rows:
                    start = (region * rows + image_row) * columns
                    out_ref[down * width : (down + 1) * width, start : start + columns] = turned


def norm_kernel(order, lengths_ref, index_ref, core_ref, gain_ref, turned_ref, *refs):
    image_ref, near_ref, far_ref, keep_ref, send_ref, attended, pixels, windows, grads = refs[-9:]
    for distance, ref in zip(order, refs):
        attended[lax.bitwise_xor(index_ref[0], distance)] = ref[...]
    heads = gain_ref.shape[0]
    regions = image_ref.shape[0]
    _, per_device, tokens, width = attended.shape

    def load(head, region):
        owner, place = divmod(head * regions + region, per_device)
        return attended[owner, place].astype(jnp.float32)

    columns = tokens * PATCH
    features = heads * width
    odd = lax.rem(index_ref[0], 2)
    position = index_ref[0] * tokens + lax.broadcasted_iota(jnp.int32, (tokens, 1), 0)
    pixels[:, :, :RIM, :] = jnp.zeros((regions, PATCH, RIM, width), jnp.float32)
    pixels[:, :, RIM + columns :, :] = jnp.zeros((regions, PATCH, RIM, width), jnp.float32)
    for region in range(regions):
        total = jnp.zeros((tokens, width), jnp.float32)
        for head in range(heads):
            total = total + load(head, region)
        mean = jnp.sum(total, axis=1, keepdims=True) * (1.0 / features)
        total = jnp.zeros((tokens, width), jnp.float32)
        for head in range(heads):
            centered = load(head, region) - mean
            total = total + centered * centered
        variance = jnp.sum(total, axis=1, keepdims=True) * (1.0 / features)
        spread = lax.rsqrt(variance + 1e-05)
        live = position < lengths_ref[region]
        for head in range(heads):
            centered = load(head, region) - mean
            normed = jnp.where(live, centered * spread * gain_ref[head : head + 1, :], 0.0)
            row, column = divmod(head, PATCH)
            pixels[region, row, pl.ds(RIM + column, tokens, stride=PATCH), :] = normed
        for row in range(PATCH):
            window = three_windows(pixels[region, row], columns)
            image_ref[region, row] = window[:, width : 2 * width]
            start = (region * PATCH + row) * columns
            windows[start : start + columns, :] = window
        near_ref[region] = image_ref[region, (1 - odd) * (PATCH - 1)]
        far_ref[region] = image_ref[region, odd * (PATCH - 1)]
        part = slice(region * PATCH * columns, (region + 1) * PATCH * columns)
        term = jnp.dot(turned_ref[:, part], windows[part, :], preferred_element_type=jnp.float32)
        product = term if region == 0 else product + term
    for down in range(3):
        for across in range(3):
            tap = 3 * down + across
            grads[tap * width : (tap + 1) * width, :] = product[
                down * width : (down + 1) * width, across * width : (across + 1) * width
            ].T
    filled = 9 * width
    if filled < grads.shape[0]:
        grads[filled:, :] = jnp.zeros((grads.shape[0] - filled, width), jnp.float32)
    half = keep_ref.shape[0]
    keep_ref[...] = grads[rows_at(core_ref[0], half), :]
    send_ref[...] = grads[rows_at(1 - core_ref[0], half), :]


def decode_kernel(index_ref, image_ref, near_ref, far_ref, weight_ref, out_ref, done_ref, padded):
    done_ref[...] = jnp.zeros(done_ref.shape, jnp.float32)
    regions, rows, columns, width = image_ref.shape
    padded[:RIM, :] = jnp.zeros((RIM, width), jnp.float32)
    padded[RIM + columns :, :] = jnp.zeros((RIM, width), jnp.float32)
    for region in range(regions):
        strips = []
        before, after = around(lax.rem(index_ref[0], 2), near_ref[region], far_ref[region])
        for row in range(-1, rows + 1):
            if row < 0:
                source = before
            elif row == rows:
                source = after
            else:
                source = image_ref[region, row]
            padded[RIM : RIM + columns, :] = source.astype(jnp.float32)
            strips.append(three_windows(padded[...], columns))
            if len(strips) == 3:
                total = jnp.dot(strips[0], weight_ref[0], preferred_element_type=jnp.float32)
                for down in (1, 2):
                    total = total + jnp.dot(
                        strips[down], weight_ref[down], preferred_element_type=jnp.float32
                    )
                out_ref[region, row - 1] = total.astype(jnp.bfloat16)
                strips.pop(0)


def add_pairs(terms):
    while len(terms) > 1:
        paired = [one + other for one, other in zip(terms[::2], terms[1::2])]
        terms = paired + terms[2 * len(paired) :]
    return terms[0]


def hold_kernel(value_ref, after_ref, out_ref):
    del after_ref
    out_ref[...] = value_ref[...]


def hold(value, after):
    return call(
        hold_kernel,
        "hold",
        jax.ShapeDtypeStruct(value.shape, value.dtype),
        [VMEM(), ANY()],
        moved=4 * value.size,
    )(value, after)


def sum_cores_kernel(quad_ref, keep_ref, other_ref, *refs):
    total = refs[-1]
    total[...] = keep_ref[...] + other_ref[...]
    for distance, ref in enumerate(refs[:-1]):
        rows = rows_at(lax.bitwise_xor(quad_ref[0], distance), ref.shape[0])
        ref[...] = total[rows, :].astype(jnp.bfloat16)


def sum_kernel(factor, *refs):
    total = add_pairs([ref[...].astype(jnp.float32) for ref in refs[:-1]])
    refs[-1][...] = (total * factor).astype(jnp.bfloat16)


def join_kernel(quad_ref, done_ref, *refs):
    del done_ref
    for distance, ref in enumerate(refs[:-1]):
        rows = rows_at(lax.bitwise_xor(quad_ref[0], distance), ref.shape[0])
        refs[-1][rows, :] = ref[...]


def spread_kernel(core_ref, own_ref, other_ref, out_ref, wide, sems):
    half = own_ref.shape[0]
    stores = []
    for number, (place, ref) in enumerate(((core_ref[0], own_ref), (1 - core_ref[0], other_ref))):
        wide[number] = ref[...].astype(jnp.float32)
        stores.append(
            pltpu.make_async_copy(wide.at[number], out_ref.at[rows_at(place, half)], sems.at[number])
        )
        stores[-1].start()
    for store in stores:
        store.wait()


def trade(values, distance):
    pairs = [(i, i ^ distance) for i in range(lax.axis_size("seq"))]
    return lax.ppermute(values, "seq", pairs)


def inner_size(seq_count):
    inner = 1
    while seq_count % (2 * inner) == 0 and (2 * inner) ** 2 <= seq_count:
        inner *= 2
    return inner


def trade_chips(values, distance, inner):
    seq_count = lax.axis_size("seq")
    pairs = []
    for outer in range(lax.axis_size("dp")):
        for seq in range(seq_count):
            chip, lane = divmod((outer // 2 * inner + seq % inner) ^ distance, inner)
            partner = (2 * chip + outer % 2) * seq_count + seq - seq % inner + lane
            pairs.append((outer * seq_count + seq, partner))
    return lax.ppermute(values, ("dp", "seq"), pairs)


def trade_cores(values):
    return lax.ppermute(values, "dp", [(i, i ^ 1) for i in range(lax.axis_size("dp"))])


def body(query_rows, key_rows, value_rows, region_lengths, norm_gain, conv_weight, cotangent):
    tokens, regions, model_width = query_rows.shape
    width = model_width // HEADS
    seq_count = lax.axis_size("seq")
    seq_index = lax.axis_index("seq")
    inner = inner_size(seq_count)
    quad_size = lax.axis_size("dp") // 2 * inner
    dp_index = lax.axis_index("dp")
    lane = lax.bitwise_and(seq_index, inner - 1)
    quad = (lax.shift_right_logical(dp_index, 1) * inner + lane).reshape(1)
    core = lax.bitwise_and(dp_index, 1).reshape(1)
    columns = tokens * PATCH
    capacity = seq_count * tokens
    per_device = regions * HEADS // seq_count
    far_pairs = [(i, i + 1) for i in range(1, seq_count - 1, 2)]
    far_pairs = far_pairs + [(j, i) for i, j in far_pairs]
    local_bytes = 2 * query_rows.size

    edge_shape = jax.ShapeDtypeStruct((regions, columns, width), jnp.bfloat16)
    chunk_shape = jax.ShapeDtypeStruct((3, per_device, tokens, width), jnp.bfloat16)
    index = seq_index.reshape(1)
    odd = lax.bitwise_and(seq_index, 1) == 1
    cot_far = jnp.where(odd, cotangent[:, PATCH - 1], cotangent[:, 0])
    cot_near = jnp.where(odd, cotangent[:, 0], cotangent[:, PATCH - 1])
    half = seq_count // 2
    early = [2, half, half + 1]
    late = [distance for distance in range(1, seq_count) if distance not in early]
    span = max(1, per_device // regions) * width

    def pack(name, distances):
        return call(
            functools.partial(pack_kernel, distances, regions, per_device),
            name,
            [chunk_shape] * len(distances),
            [SMEM()] + [HBM()] * 3,
            out_specs=[HBM()] * len(distances),
            scratch=[
                pltpu.VMEM((len(distances), 3, tokens, regions, span), jnp.bfloat16),
                pltpu.VMEM((len(distances),) + chunk_shape.shape, jnp.bfloat16),
                pltpu.SemaphoreType.DMA((3 * len(distances),)),
                pltpu.SemaphoreType.DMA((len(distances),)),
            ],
            moved=4 * len(distances) * chunk_shape.size,
            grant=VMEM_WHOLE,
        )(index, query_rows, key_rows, value_rows)

    packed = {}
    for distance, chunk in zip(early, pack("pack_early", early)):
        packed[distance] = trade(chunk, distance)
    for distance, chunk in zip(late, pack("pack_late", late)):
        packed[distance] = trade(chunk, distance)
    order = list(range(1, seq_count)) + [0]
    packed[0], cot_near, cot_far = call(
        functools.partial(own_kernel, regions, per_device),
        "own_chunk",
        [chunk_shape, edge_shape, edge_shape],
        [SMEM()] + [HBM()] * 3 + [VMEM()] * 2,
        scratch=[
            pltpu.VMEM((3, tokens, regions, span), jnp.bfloat16),
            pltpu.SemaphoreType.DMA((3,)),
        ],
        moved=12 * chunk_shape.size,
    )(index, query_rows, key_rows, value_rows, cot_near, cot_far)
    cot_near = trade(cot_near, 1)
    cot_far = lax.ppermute(cot_far, "seq", far_pairs)

    items = seq_index * per_device + jnp.arange(per_device, dtype=jnp.int32)
    item_lengths = jnp.sum(
        jnp.where(
            (items % regions)[:, None] == jnp.arange(regions, dtype=jnp.int32)[None, :],
            region_lengths[None, :],
            0,
        ),
        axis=1,
    )
    block_rows = min(256, capacity)
    group = regions if per_device % regions == 0 else per_device
    mixed = call(
        functools.partial(attend_kernel, block_rows, group, order),
        "attend",
        [jax.ShapeDtypeStruct((per_device, tokens, width), jnp.bfloat16)] * seq_count,
        [SMEM(), SMEM()] + [VMEM()] * seq_count,
        flops=4 * per_device * capacity * capacity * width,
        moved=4 * local_bytes,
        exps=per_device * capacity * capacity,
    )(index, item_lengths, *[packed[distance] for distance in order])
    back = list(range(half, seq_count)) + list(range(2, half)) + [1]
    attended = [trade(mixed[distance], distance) for distance in back] + [mixed[0]]

    turned = call(
        turn_kernel,
        "turn_cotangent",
        jax.ShapeDtypeStruct((3 * width, cotangent.size // width), jnp.bfloat16),
        [SMEM()] + [VMEM()] * 3,
        moved=8 * cotangent.size,
    )(index, cotangent, cot_near, cot_far)
    chunk_rows = -(-9 * width // (32 * quad_size)) * 16
    half_rows = quad_size * chunk_rows
    pixel_rows = regions * PATCH * columns
    conv_flops = 18 * pixel_rows * width * width
    chunk_moved = 8 * chunk_rows * width
    image, near, far, keep, send = call(
        functools.partial(norm_kernel, back + [0]),
        "norm_and_gradient",
        [jax.ShapeDtypeStruct((regions, PATCH, columns, width), jnp.bfloat16)]
        + [edge_shape] * 2
        + [jax.ShapeDtypeStruct((half_rows, width), jnp.float32)] * 2,
        [SMEM()] * 3 + [VMEM()] * (2 + seq_count),
        scratch=[
            pltpu.VMEM((seq_count,) + mixed[0].shape, jnp.bfloat16),
            pltpu.VMEM((regions, PATCH, columns + 2 * RIM, width), jnp.float32),
            pltpu.VMEM((pixel_rows, 3 * width), jnp.bfloat16),
            pltpu.VMEM((2 * half_rows, width), jnp.float32),
        ],
        flops=conv_flops,
        moved=4 * local_bytes,
    )(region_lengths, index, core, norm_gain.reshape(HEADS, width), turned, *attended)
    chunk_shape = jax.ShapeDtypeStruct((chunk_rows, width), jnp.bfloat16)
    parts = call(
        sum_cores_kernel,
        "sum_cores",
        [chunk_shape] * quad_size,
        [SMEM()] + [VMEM()] * 2,
        scratch=[pltpu.VMEM((half_rows, width), jnp.float32)],
        moved=quad_size * chunk_moved,
    )(quad, keep, trade_cores(send))
    far = lax.ppermute(far, "seq", far_pairs)
    distances = range(1, quad_size)
    plane_sum = call(
        functools.partial(sum_kernel, 1.0),
        "sum_chips",
        chunk_shape,
        [VMEM()] * quad_size,
        moved=chunk_moved,
    )(parts[0], *[trade_chips(parts[distance], distance, inner) for distance in distances])
    near = trade(hold(near, plane_sum), 1)
    plane_sums = [plane_sum] + [
        trade(plane_sum, distance) for distance in range(inner, seq_count, inner)
    ]
    decoded, done = call(
        decode_kernel,
        "decode",
        [
            jax.ShapeDtypeStruct(cotangent.shape, jnp.bfloat16),
            jax.ShapeDtypeStruct((8, width), jnp.float32),
        ],
        [SMEM()] + [VMEM()] * 4,
        scratch=[pltpu.VMEM((columns + 2 * RIM, width), jnp.float32)],
        flops=conv_flops,
        moved=2 * local_bytes,
    )(index, image, near, far, conv_weight.reshape(3, 3 * width, width))
    total = call(
        functools.partial(sum_kernel, 1.0 / math.sqrt(PATCH * columns)),
        "sum_planes",
        chunk_shape,
        [VMEM()] * len(plane_sums),
        moved=chunk_moved,
    )(*plane_sums)
    joined = call(
        join_kernel,
        "join_chips",
        jax.ShapeDtypeStruct((half_rows, width), jnp.bfloat16),
        [SMEM(), ANY()] + [VMEM()] * quad_size,
        moved=quad_size * chunk_moved,
    )(quad, done, total, *[trade_chips(total, distance, inner) for distance in distances])
    weight_grad = call(
        spread_kernel,
        "spread_sums",
        jax.ShapeDtypeStruct((2 * half_rows, width), jnp.float32),
        [SMEM()] + [VMEM()] * 2,
        out_specs=HBM(),
        scratch=[
            pltpu.VMEM((2, half_rows, width), jnp.float32),
            pltpu.SemaphoreType.DMA((2,)),
        ],
        moved=2 * quad_size * chunk_moved,
    )(core, joined, trade_cores(joined))
    return (decoded, weight_grad[: 9 * width].reshape(conv_weight.shape))


def solution(mesh):
    placed = (
        P("seq", "dp", None),
        P("seq", "dp", None),
        P("seq", "dp", None),
        P("dp"),
        P(),
        P(),
        P("dp", "seq", None, None),
    )
    return jax.shard_map(
        body,
        mesh=mesh,
        in_specs=placed,
        out_specs=(P("dp", "seq", None, None), P()),
        check_vma=False,
    )
```
